32 devices in a mesh: groups: 2 (over y), dp: 4 (over x, core), tensor: 4 (over z).
Axes of the slice: x: 2, y: 2, z: 4, core: 2. Of those that a mesh axis runs over, the one named last changes fastest.
Arguments:
- query_states: bfloat16 [128, 64, 5120], P(('groups', 'dp'), None, 'tensor'), parts along dimension 0, may hold values from -9 to 9
- key_states: bfloat16 [128, 64, 1024], P(('groups', 'dp'), None, 'tensor'), parts along dimension 0, may hold values from -6 to 6
- value_states: bfloat16 [128, 64, 1024], P(('groups', 'dp'), None, 'tensor'), parts along dimension 0, may hold values from -6 to 6
- residual: bfloat16 [128, 64, 5120], P(('groups', 'dp'), None, 'tensor'), parts along dimension 0, may hold values from -13 to 13
- returns: bfloat16 [128, 64], P(('groups', 'dp')), parts along dimension 0, may hold values from -5 to 5
- lengths: int32 [128], P('groups'), parts along dimension 0, may hold values from 8 to 64, as said below
- balance_list: int32 [128], P('groups'), parts along dimension 0, may hold values from 0 to 63, as said below
- out_weight: bfloat16 [5120, 5120], P('tensor'), may hold values from -0.078125 to 0.078125
- norm_gain: float32 [5120], P('tensor'), may hold values from 0.5 to 1.5
- value_weight: float32 [5120], P('tensor'), may hold values from -0.0009765625 to 0.0015625
Outputs:
- critic_values: bfloat16 [4608], P(('groups', 'dp')), parts along dimension 0
- query_grads: bfloat16 [4608, 5120], P(('groups', 'dp'), 'tensor'), parts along dimension 0
- key_grads: bfloat16 [4608, 1024], P(('groups', 'dp'), 'tensor'), parts along dimension 0
- value_grads: bfloat16 [4608, 1024], P(('groups', 'dp'), 'tensor'), parts along dimension 0
- residual_grads: bfloat16 [4608, 5120], P(('groups', 'dp'), 'tensor'), parts along dimension 0
- out_weight_grad: float32 [10240, 5120], P(('groups', 'dp'), 'tensor'), parts along dimension 0
- gain_grad: float32 [10240], P(('groups', 'tensor')), parts along dimension 0
- value_weight_grad: float32 [10240], P(('groups', 'tensor')), parts along dimension 0
The draws below stay inside these ranges and needn't reach their ends.
There are 2 independent parts, one for each index of `groups`. The reference program is written for one: setup_inputs(seed, part) draws one part's arguments, and reference() takes and returns one part's arrays. A program takes and returns all parts, laid end to end along the dimension named above; an argument that names none is the same for every part. Nothing has to cross between parts.
Inputs may be any that keep to these rules, and one draw needn't show every extreme that they name: `lengths`: the largest length is exactly 64; under balance_list every replica's 16 rollouts hold exactly 576 tokens together. `balance_list`: A permutation of the 64 home slots (home slot r lies on replica r // 16). Of the 16 rollouts that one replica works on, no home replica supplies more than 4, and every replica takes exactly 4 from some home replica.
All inputs are finite; a program needn't handle non-finite values.
Results may differ from the reference program's by a relative error of at most 0.015.
Values may be sent and summed in bfloat16 or wider, within the bound.
No kernel may reach another device: no remote copies, remote signals or barrier semaphores. Data moves between devices by JAX's collectives and lax.ppermute only.
A program may use at most 192 MiB of HBM per device.

```python
import math
import jax
import jax.numpy as jnp
from jax import lax

D = 5120
H = 40
KVH = 8
HD = 128
LMAX = 64
RPD = 16
CAPB = 576
NROLL = 64
TOKENS = 2304
N_DP = 4
N_TENSOR = 4


ALIGN_MEAN = 1.2


HEAD_SCALE = 1.5


def rollout_plan(key):
    plan_keys = jax.random.split(key, 5)
    pair_total = LMAX * 9 // 8
    half_count = RPD // 2
    first_len = jax.random.randint(plan_keys[0], (N_DP, half_count), pair_total - LMAX, LMAX + 1)
    first_len = first_len.at[0, 0].set(LMAX)
    group_len = jnp.concatenate([first_len, pair_total - first_len], axis=1)
    column_ids = jnp.arange(RPD, dtype=jnp.int32)
    shuffle_key = jax.random.randint(plan_keys[1], (N_DP, RPD), 0, 1 << 20) * RPD + column_ids[None, :]
    group_len = jnp.take_along_axis(group_len, jnp.argsort(shuffle_key, axis=1), axis=1)
    shifts = jax.random.permutation(plan_keys[2], N_DP)[column_ids % N_DP]
    base_perm = jax.random.permutation(plan_keys[3], N_DP)
    replica_ids = jnp.arange(N_DP, dtype=jnp.int32)
    home_rep = base_perm[(replica_ids[:, None] + shifts[None, :]) % N_DP]
    place_key = jax.random.randint(plan_keys[4], (N_DP, RPD), 0, 1 << 20) * RPD + column_ids[None, :]
    place_order = jnp.argsort(place_key, axis=1)
    home_pos = place_order[home_rep, column_ids[None, :]]
    balance = (home_rep * RPD + home_pos).reshape(N_DP * RPD).astype(jnp.int32)
    lengths = jnp.zeros((N_DP * RPD,), jnp.int32).at[balance].set(group_len.reshape(N_DP * RPD).astype(jnp.int32))
    return (lengths, balance)


def draw_lengths(key, part):
    plan = rollout_plan(key)
    return plan[0]


def draw_balance_list(key, part):
    plan = rollout_plan(key)
    return plan[1]


def drawn_keys(key):
    align_keys = jax.random.split(key, 1)
    key_base = jnp.clip(jax.random.normal(align_keys[0], (NROLL, LMAX, KVH, HD), jnp.float32), -6.0, 6.0)
    return key_base


def row_offsets(key):
    offset_key = jax.random.fold_in(key, 21)
    return jax.random.uniform(offset_key, (NROLL, LMAX, 1), jnp.float32, -1.5, 1.5)


def draw_key_states(key, part):
    key_base = drawn_keys(key)
    return key_base.reshape(NROLL, LMAX, KVH * HD).astype(jnp.bfloat16)


def draw_query_states(key, part):
    key = jax.random.fold_in(key, 12)
    query_base = jnp.clip(jax.random.normal(key, (NROLL, LMAX, KVH, H // KVH, HD), jnp.float32), -6.0, 6.0)
    return query_base.reshape(NROLL, LMAX, H * HD).astype(jnp.bfloat16)


def draw_residual(key, part):
    offsets = row_offsets(key)
    key = jax.random.fold_in(key, 13)
    draw_keys = jax.random.split(key, 1)
    return (jnp.clip(jax.random.normal(draw_keys[0], (NROLL, LMAX, D), jnp.float32), -4.0, 4.0) + offsets).astype(jnp.bfloat16)


def draw_returns(key, part):
    offsets = row_offsets(key)[:, :, 0]
    key = jax.random.fold_in(key, 15)
    estimate = ALIGN_MEAN * HEAD_SCALE * offsets / jnp.sqrt(offsets * offsets + 1.09)
    jitter = jnp.clip(jax.random.normal(key, (NROLL, LMAX), jnp.float32), -3.0, 3.0)
    return (estimate + jitter).astype(jnp.bfloat16)


def draw_value_weight(key, part):
    key = jax.random.fold_in(key, 16)
    spread = jnp.clip(jax.random.normal(key, (D,), jnp.float32), -4.0, 4.0)
    return HEAD_SCALE * (ALIGN_MEAN + spread) / D


def shard_levels(key, shape, pieces, least, largest):
    level, own = 1.0, jax.random.fold_in(key, 6)
    for dim, parts in pieces:
        heights = jnp.exp(jax.random.uniform(jax.random.fold_in(own, dim), (parts,), jnp.float32, least / len(pieces), largest / len(pieces)))
        level = level * jnp.repeat(heights, shape[dim] // parts).reshape([-1 if axis == dim else 1 for axis in range(len(shape))])
    return level


def gaussian(rng, extent, width, bound, cuts=(), held_as=jnp.bfloat16):
    entries = width * jax.random.normal(rng, extent, jnp.float32)
    if cuts:
        entries = entries * shard_levels(rng, extent, cuts, -0.22, 0.18)
    return jnp.clip(entries, -bound, bound).astype(held_as)


def setup_inputs(seed: int = 0, part: int = 0) -> dict:
    streams_of = jax.random.split(jax.random.key(seed), 11)
    part_splits = jax.random.split(jax.random.fold_in(streams_of[10], part), 11)
    query_states = draw_query_states(jax.random.fold_in(jax.random.fold_in(streams_of[10], part), 71), part)
    key_states = draw_key_states(jax.random.fold_in(jax.random.fold_in(streams_of[10], part), 71), part)
    value_states = gaussian(part_splits[2], (NROLL, LMAX, KVH * HD), 1.0, 6.0, ((0, 4), (2, 4)))
    residual = draw_residual(jax.random.fold_in(jax.random.fold_in(streams_of[10], part), 71), part)
    returns = draw_returns(jax.random.fold_in(jax.random.fold_in(streams_of[10], part), 71), part)
    lengths = draw_lengths(jax.random.fold_in(jax.random.fold_in(streams_of[10], part), 71), part)
    balance_list = draw_balance_list(jax.random.fold_in(jax.random.fold_in(streams_of[10], part), 71), part)
    out_weight = gaussian(streams_of[7], (H * HD, D), (H * HD) ** -0.5, 0.078125, ((0, 4),))
    norm_gain = jnp.clip(1.0 + 0.1 * jax.random.normal(streams_of[8], (D,), jnp.float32), 0.5, 1.5)
    value_weight = draw_value_weight(jax.random.fold_in(streams_of[10], 71), part)
    return {"query_states": query_states, "key_states": key_states, "value_states": value_states, "residual": residual, "returns": returns, "lengths": lengths, "balance_list": balance_list, "out_weight": out_weight, "norm_gain": norm_gain, "value_weight": value_weight}


EPS = 1e-06

def rollout_pass(query_rows, key_rows, value_rows, resid_rows, target_rows, length, out_weight, norm_gain, value_weight):
    seq_len = query_rows.shape[0]
    group_ratio = H // KVH
    score_scale = 1.0 / math.sqrt(HD)
    positions = jnp.arange(seq_len, dtype=jnp.int32)
    live_rows = positions < length
    allowed = (positions[None, :] <= positions[:, None]) & (positions[None, :] < length)
    query_heads = query_rows.astype(jnp.float32).reshape(seq_len, KVH, group_ratio, HD)
    key_heads = key_rows.astype(jnp.float32).reshape(seq_len, KVH, HD)
    value_heads = value_rows.astype(jnp.float32).reshape(seq_len, KVH, HD)
    scores = jnp.einsum('sgrd,ugd->grsu', query_heads, key_heads) * score_scale
    scores = jnp.where(allowed, scores, -jnp.inf)
    softmax_w = jax.nn.softmax(scores, axis=-1)
    softmax_low = lax.optimization_barrier(softmax_w.astype(jnp.bfloat16)).astype(jnp.float32)
    context = jnp.einsum('grsu,ugd->sgrd', softmax_low, value_heads).reshape(seq_len, H * HD).astype(jnp.bfloat16)
    head_groups = context.astype(jnp.float32).reshape(seq_len, N_TENSOR, H * HD // N_TENSOR)
    weight_groups = out_weight.astype(jnp.float32).reshape(N_TENSOR, H * HD // N_TENSOR, D)
    partial_value = jnp.einsum('sck,ckd->csd', head_groups, weight_groups)
    partial_value = lax.optimization_barrier(partial_value.astype(jnp.bfloat16)).astype(jnp.float32)
    hidden = resid_rows.astype(jnp.float32) + lax.optimization_barrier(jnp.sum(partial_value, axis=0))
    square_sum = lax.optimization_barrier(jnp.sum(hidden * hidden, axis=1))
    value_dot = lax.optimization_barrier(jnp.sum(hidden * norm_gain * value_weight, axis=1))
    inv_rms = lax.rsqrt(square_sum / D + EPS)
    critic = inv_rms * value_dot
    value_err = jnp.where(live_rows, critic - target_rows.astype(jnp.float32), 0.0)
    hidden_grad = (inv_rms * value_err)[:, None] * (norm_gain * value_weight) - hidden * (inv_rms ** 3 * value_err * value_dot / D)[:, None]
    grad_low = hidden_grad.astype(jnp.bfloat16)
    gain_part = lax.optimization_barrier(jnp.sum((inv_rms * value_err)[:, None] * hidden, axis=0))
    weight_part = jnp.dot(grad_low.T, context, preferred_element_type=jnp.float32)
    context_grad = jnp.dot(grad_low, out_weight.T, preferred_element_type=jnp.float32).astype(jnp.bfloat16)
    grad_heads = context_grad.astype(jnp.float32).reshape(seq_len, KVH, group_ratio, HD)
    prob_grad = jnp.einsum('sgrd,ugd->grsu', grad_heads, value_heads)
    row_dot = lax.optimization_barrier(jnp.sum(softmax_w * prob_grad, axis=-1, keepdims=True))
    score_grad = lax.optimization_barrier((softmax_w * (prob_grad - row_dot) * score_scale).astype(jnp.bfloat16)).astype(jnp.float32)
    query_grad = jnp.einsum('grsu,ugd->sgrd', score_grad, key_heads).reshape(seq_len, H * HD).astype(jnp.bfloat16)
    key_grad = jnp.einsum('grsu,sgrd->ugd', score_grad, query_heads).reshape(seq_len, KVH * HD).astype(jnp.bfloat16)
    value_grad = jnp.einsum('grsu,sgrd->ugd', softmax_low, grad_heads).reshape(seq_len, KVH * HD).astype(jnp.bfloat16)
    return (critic.astype(jnp.bfloat16), query_grad, key_grad, value_grad, grad_low, weight_part, gain_part)

def reference(query_states, key_states, value_states, residual, returns, lengths, balance_list, out_weight, norm_gain, value_weight):

    def visit_slot(totals, rollout):
        query_rows, key_rows, value_rows, resid_rows, target_rows, length = rollout
        outs_here = rollout_pass(query_rows, key_rows, value_rows, resid_rows, target_rows, length, out_weight, norm_gain, value_weight)
        return ((totals[0] + outs_here[5], totals[1] + outs_here[6]), outs_here[:5])
    initial = (jnp.zeros((D, H * HD), jnp.float32), jnp.zeros((D,), jnp.float32))
    (weight_grad, gain_sum), per_slot = lax.scan(visit_slot, initial, (query_states, key_states, value_states, residual, returns, lengths))
    chosen = jnp.take(lengths, balance_list.astype(jnp.int32)).reshape(N_DP, RPD).astype(jnp.int32)
    starts = (jnp.cumsum(chosen, axis=1) - chosen).astype(jnp.int32)
    token_ids = jnp.arange(TOKENS, dtype=jnp.int32)
    replica = (token_ids // CAPB).astype(jnp.int32)
    within = (token_ids % CAPB).astype(jnp.int32)
    my_starts = jnp.take(starts, replica, axis=0)
    member = (lax.optimization_barrier(jnp.sum((within[:, None] >= my_starts).astype(jnp.int32), axis=1)) - 1).astype(jnp.int32)
    offset = (within - jnp.take_along_axis(my_starts, member[:, None], axis=1)[:, 0]).astype(jnp.int32)
    source = jnp.take(balance_list, (replica * RPD + member).astype(jnp.int32)).astype(jnp.int32)
    flat_row = (source * LMAX + offset).astype(jnp.int32)

    def arrange(per_token):
        flattened = per_token.reshape((NROLL * LMAX,) + per_token.shape[2:])
        return jnp.take(flattened, flat_row, axis=0)
    critic_values = arrange(per_slot[0])
    query_grads = arrange(per_slot[1])
    key_grads = arrange(per_slot[2])
    value_grads = arrange(per_slot[3])
    residual_grads = arrange(per_slot[4])
    return (critic_values, query_grads, key_grads, value_grads, residual_grads, weight_grad, value_weight * gain_sum, norm_gain * gain_sum)
```

```python
import functools
import math

import jax
import jax.numpy as jnp
from jax import lax
from jax.experimental import pallas as pl
from jax.experimental.pallas import tpu as pltpu
from jax.sharding import PartitionSpec as P

H = 40
KVH = 8
HD = 128
RATIO = H // KVH
CAPB = 576
EPS = 1e-06
NEG = -1e30
CW = 256
LAG = 3
F32 = jnp.float32
BF16 = jnp.bfloat16
VMEM = pl.BlockSpec(memory_space=pltpu.VMEM)
SMEM = pl.BlockSpec(memory_space=pltpu.SMEM)
ANY = pl.BlockSpec(memory_space=pl.ANY)


def params(mib):
    return pltpu.CompilerParams(vmem_limit_bytes=mib * 1024 * 1024)


def mm(a, b, dims):
    return lax.dot_general(a, b, (dims, ((), ())), preferred_element_type=F32)


def route_kernel(n_dp, per_dev, me_ref, len_ref, bal_ref, pick_ref, start_ref, size_ref, cnt_ref):
    cap = per_dev // n_dp
    me = me_ref[0]
    for d in range(n_dp):
        target = jnp.bitwise_xor(me, d)

        def outgoing(s, count):
            b = bal_ref[target * per_dev + s]
            home = lax.div(b, per_dev)

            @pl.when(home == me)
            def _():
                pick_ref[d * cap + count] = lax.rem(b, per_dev)

            return count + (home == me).astype(jnp.int32)

        lax.fori_loop(0, per_dev, outgoing, jnp.int32(0))
        cnt_ref[d] = jnp.int32(0)

    def incoming(s, run):
        b = bal_ref[me * per_dev + s]
        d = jnp.bitwise_xor(lax.div(b, per_dev), me)
        count = cnt_ref[d]
        size = len_ref[b]
        start_ref[d * cap + count] = run
        size_ref[d * cap + count] = size
        cnt_ref[d] = count + 1
        return run + size

    lax.fori_loop(0, per_dev, incoming, jnp.int32(0))


def route(me, lengths, balance_list, n_dp, per_dev):
    table = jax.ShapeDtypeStruct((per_dev,), jnp.int32)
    return pl.pallas_call(
        functools.partial(route_kernel, n_dp, per_dev),
        out_shape=(table, table, table),
        in_specs=[SMEM] * 3,
        out_specs=(SMEM, SMEM, SMEM),
        scratch_shapes=[pltpu.SMEM((n_dp,), jnp.int32)],
        name="route",
    )(me, lengths, balance_list)


def gather_kernel(n_dp, cap, widths, pick_ref, *refs):
    parts = refs[: len(widths)]
    outs = refs[len(widths) : len(widths) + n_dp]
    sems = refs[-1]
    order = list(range(1, n_dp)) + [0]
    for d in order:
        for i in range(cap):
            row = pick_ref[d * cap + i]
            col = 0
            for part, width in zip(parts, widths):
                pltpu.make_async_copy(
                    part.at[row], outs[d].at[i, :, pl.ds(col, width)], sems.at[d]
                ).start()
                col += width
    for d in order:
        pltpu.make_async_copy(outs[d], outs[d], sems.at[d]).wait()


def gather_rollouts(pick, parts, n_dp):
    per_dev, seq_len = parts[0].shape[:2]
    cap = per_dev // n_dp
    widths = tuple(p.shape[2] for p in parts)
    out = jax.ShapeDtypeStruct((cap, seq_len, sum(widths)), BF16)
    return pl.pallas_call(
        functools.partial(gather_kernel, n_dp, cap, widths),
        out_shape=(out,) * n_dp,
        in_specs=[SMEM] + [ANY] * len(parts),
        out_specs=(ANY,) * n_dp,
        scratch_shapes=[pltpu.SemaphoreType.DMA((n_dp,))],
        name="gather_rollouts",
    )(pick, *parts)


def xor_move(value, d, n_dp):
    return lax.ppermute(value, "dp", [(i, i ^ d) for i in range(n_dp)])


def exchange(blocks, n_dp):
    order = sorted(range(1, n_dp), key=lambda d: d < 2)
    moved = {d: xor_move(blocks[d], d, n_dp) for d in order}
    return [blocks[0]] + [moved[d] for d in range(1, n_dp)]


def window(start, size, seq_len):
    tall = seq_len + 8
    base = pl.multiple_of(lax.div(start, 8) * 8, 8)
    shift = start - base
    fill = lambda shape, axis: lax.broadcasted_iota(jnp.int32, shape, axis)
    place = (fill((tall, seq_len), 0) - shift == fill((tall, seq_len), 1)) & (
        fill((tall, seq_len), 1) < size
    )
    fetch = (fill((seq_len, tall), 1) - shift == fill((seq_len, tall), 0)) & (
        fill((seq_len, tall), 0) < size
    )
    return pl.ds(base, tall), place.astype(BF16), fetch.astype(BF16)


def pack_kernel(n_dp, cap, seq_len, start_ref, size_ref, *refs):
    blocks, out, room = refs[:n_dp], refs[n_dp], refs[n_dp + 1]
    room[...] = jnp.zeros_like(room)
    for d in range(n_dp):

        def step(i, _):
            spot, place, _ = window(start_ref[d * cap + i], size_ref[d * cap + i], seq_len)
            room[spot, :] += mm(place, blocks[d][i], ((1,), (0,)))
            return 0

        lax.fori_loop(0, cap, step, 0)
    out[...] = room[:CAPB, :].astype(BF16)


def pack(start, size, blocks):
    cap, seq_len, width = blocks[0].shape
    n_dp = len(blocks)
    return pl.pallas_call(
        functools.partial(pack_kernel, n_dp, cap, seq_len),
        out_shape=jax.ShapeDtypeStruct((CAPB, width), BF16),
        in_specs=[SMEM, SMEM] + [VMEM] * n_dp,
        out_specs=VMEM,
        scratch_shapes=[pltpu.VMEM((CAPB + seq_len, width), F32)],
        compiler_params=params(32),
        name="pack",
    )(start, size, *blocks)


def heads_of(rows, first):
    return jnp.concatenate(
        [rows[:, (first + r) * HD : (first + r + 1) * HD] for r in range(RATIO)], axis=0
    )


def forward_kernel(n_dp, cap, seq_len, kv, start_ref, size_ref, *refs):
    blocks, out, probs_ref, room = refs[:n_dp], refs[n_dp], refs[n_dp + 1], refs[n_dp + 2]
    qw = kv * RATIO * HD
    scale = 1.0 / math.sqrt(HD)
    span = RATIO * seq_len
    room[...] = jnp.zeros_like(room)
    at_u = lax.broadcasted_iota(jnp.int32, (seq_len, span), 0)
    at_t = lax.rem(lax.broadcasted_iota(jnp.int32, (seq_len, span), 1), seq_len)
    at_t1 = lax.rem(lax.broadcasted_iota(jnp.int32, (1, span), 1), seq_len)
    causal = at_u <= at_t
    for d in range(n_dp):

        def step(i, _):
            size = size_ref[d * cap + i]
            spot, place, _ = window(start_ref[d * cap + i], size, seq_len)
            keep = causal & (at_u < size)
            parts = []
            for g in range(kv):
                queries = heads_of(blocks[d][i, :, g * RATIO * HD : (g + 1) * RATIO * HD], 0)
                keys = blocks[d][i, :, qw + g * HD : qw + (g + 1) * HD]
                values = blocks[d][i, :, qw + (kv + g) * HD : qw + (kv + g + 1) * HD]
                scores = jnp.where(keep, mm(keys, queries, ((1,), (1,))) * scale, NEG)
                top = jnp.max(scores, axis=0, keepdims=True)
                weights = jnp.exp(scores - top)
                total = jnp.sum(weights, axis=0, keepdims=True)
                probs = (weights * jnp.where(at_t1 < size, 1.0 / total, 0.0)).astype(BF16)
                probs_ref[d * cap + i, g] = probs
                mixed = mm(probs, values, ((0,), (0,)))
                parts += [mixed[r * seq_len : (r + 1) * seq_len] for r in range(RATIO)]
            mixed = jnp.concatenate(parts, axis=1).astype(BF16)
            room[spot, :] += mm(place, mixed, ((1,), (0,)))
            return 0

        lax.fori_loop(0, cap, step, 0)
    out[...] = room[:CAPB, :].astype(BF16)


def attention_forward(start, size, blocks, kv):
    cap, seq_len, _ = blocks[0].shape
    n_dp = len(blocks)
    width = kv * RATIO * HD
    return pl.pallas_call(
        functools.partial(forward_kernel, n_dp, cap, seq_len, kv),
        out_shape=(
            jax.ShapeDtypeStruct((CAPB, width), BF16),
            jax.ShapeDtypeStruct((n_dp * cap, kv, seq_len, RATIO * seq_len), BF16),
        ),
        in_specs=[SMEM, SMEM] + [VMEM] * n_dp,
        out_specs=(VMEM, VMEM),
        scratch_shapes=[pltpu.VMEM((CAPB + seq_len, width), F32)],
        compiler_params=params(40),
        name="attention_forward",
    )(start, size, *blocks)


def backward_kernel(
    n_dp, cap, seq_len, kv, start_ref, size_ref, a_ref, b_ref, wgw_ref, acc_ref, probs_ref, *refs
):
    blocks = refs[:n_dp]
    dq_out, dk_out, dv_out = refs[n_dp : n_dp + 3]
    grads, dq_room, dk_room, dv_room = refs[n_dp + 3 :]
    qw = kv * RATIO * HD
    scale = 1.0 / math.sqrt(HD)
    for room in (dq_room, dk_room, dv_room):
        room[...] = jnp.zeros_like(room)
    grads[:CAPB, :] = a_ref[...] * wgw_ref[...] - b_ref[...] * acc_ref[...]
    grads[CAPB:, :] = jnp.zeros((seq_len, qw), F32)
    for d in range(n_dp):

        def step(i, _):
            spot, place, fetch = window(start_ref[d * cap + i], size_ref[d * cap + i], seq_len)
            mine = mm(fetch, grads[spot, :].astype(BF16), ((1,), (0,))).astype(BF16)
            dq_parts, dk_parts, dv_parts = [], [], []
            for g in range(kv):
                cols = slice(g * RATIO * HD, (g + 1) * RATIO * HD)
                queries = heads_of(blocks[d][i, :, cols], 0)
                keys = blocks[d][i, :, qw + g * HD : qw + (g + 1) * HD]
                values = blocks[d][i, :, qw + (kv + g) * HD : qw + (kv + g + 1) * HD]
                out_grad = heads_of(mine[:, cols], 0)
                probs_low = probs_ref[d * cap + i, g]
                probs = probs_low.astype(F32)
                prob_grad = mm(values, out_grad, ((1,), (1,)))
                row_dot = jnp.sum(probs * prob_grad, axis=0, keepdims=True)
                score_grad = (probs * (prob_grad - row_dot) * scale).astype(BF16)
                dq = mm(score_grad, keys, ((0,), (0,)))
                dq_parts += [dq[r * seq_len : (r + 1) * seq_len] for r in range(RATIO)]
                dk_parts.append(mm(score_grad, queries, ((1,), (0,))))
                dv_parts.append(mm(probs_low, out_grad, ((1,), (0,))))
            for room, parts in ((dq_room, dq_parts), (dk_room, dk_parts), (dv_room, dv_parts)):
                rows = jnp.concatenate(parts, axis=1).astype(BF16)
                room[spot, :] += mm(place, rows, ((1,), (0,)))
            return 0

        lax.fori_loop(0, cap, step, 0)
    dq_out[...] = dq_room[:CAPB, :].astype(BF16)
    dk_out[...] = dk_room[:CAPB, :].astype(BF16)
    dv_out[...] = dv_room[:CAPB, :].astype(BF16)


def attention_backward(start, size, a, b, wgw, acc, probs, blocks, kv):
    cap, seq_len, _ = blocks[0].shape
    n_dp = len(blocks)
    qw, kw = kv * RATIO * HD, kv * HD
    tall = CAPB + seq_len
    return pl.pallas_call(
        functools.partial(backward_kernel, n_dp, cap, seq_len, kv),
        out_shape=tuple(jax.ShapeDtypeStruct((CAPB, w), BF16) for w in (qw, kw, kw)),
        in_specs=[SMEM, SMEM] + [VMEM] * (5 + n_dp),
        out_specs=(VMEM,) * 3,
        scratch_shapes=[pltpu.VMEM((tall, w), F32) for w in (qw, qw, kw, kw)],
        compiler_params=params(48),
        name="attention_backward",
    )(start, size, a, b, wgw, acc, probs, *blocks)


def select(index, options):
    out = options[0]
    for k in range(1, len(options)):
        out = jnp.where(index == k, options[k], out)
    return out


def round_kernel(n_blk, first, last, model_width, pos_ref, *refs):
    refs = list(refs)
    take = lambda n: [refs.pop(0) for _ in range(n)]
    sent, got, weights, gains = take(n_blk), take(n_blk), take(n_blk), take(n_blk)
    acc_in, sq_in, vd_in = (None, None, None) if first else take(3)
    (target,) = take(1) if last else (None,)
    acc, sq, vd, own = take(4)
    pays = take(n_blk)
    me, col, mid = pos_ref[0], pos_ref[1], pos_ref[2] == 1
    pieces = [jnp.where(mid, s[...], g[...]) for s, g in zip(sent, got)]
    own[...] = select(col, pieces)
    for d in range(n_blk):
        pays[d][...] = select(jnp.bitwise_xor(me, d), pieces)
    squares = 0.0 if first else sq_in[...]
    dots = 0.0 if first else vd_in[...]
    for piece, gain in zip(pieces, gains):
        wide = piece.astype(F32)
        squares = squares + jnp.sum(wide * wide, axis=1, keepdims=True)
        dots = dots + jnp.sum(wide * gain[...], axis=1, keepdims=True)
    if last:
        inv_rms = lax.rsqrt(squares / model_width + EPS)
        critic = inv_rms * dots
        err = critic - target[...]
        sq[...] = inv_rms * err
        vd[...] = inv_rms * inv_rms * inv_rms * err * dots / model_width
        refs[0][...] = critic
    else:
        sq[...] = squares
        vd[...] = dots
    rows = 192
    for r in range(CAPB // rows):
        part = slice(r * rows, (r + 1) * rows)
        total = None if first else acc_in[part, :]
        for piece, weight in zip(pieces, weights):
            term = mm(piece[part, :], weight[...], ((1,), (1,)))
            total = term if total is None else total + term
        acc[part, :] = total


def round_step(r, per_block, pos, sent, got, out_weight, gw_row, state, target):
    n_blk = len(sent)
    depth, model_width = out_weight.shape
    first, last = state is None, target is not None
    at = lambda j: (lambda i: (0, j * per_block + r))
    whole = lambda shape: pl.BlockSpec(shape, lambda i: (0, 0))
    column, piece, square = (CAPB, 1), (CAPB, CW), (CAPB, depth)
    ins = [SMEM] + [whole(piece)] * (2 * n_blk)
    ins += [pl.BlockSpec((depth, CW), at(j)) for j in range(n_blk)]
    ins += [pl.BlockSpec((1, CW), at(j)) for j in range(n_blk)]
    args = [pos, *sent, *got] + [out_weight] * n_blk + [gw_row] * n_blk
    if not first:
        ins += [whole(square), whole(column), whole(column)]
        args += list(state)
    if last:
        ins.append(whole(column))
        args.append(target)
    shapes = [(square, F32), (column, F32), (column, F32)] + [(piece, BF16)] * (1 + n_blk)
    if last:
        shapes.append((column, F32))
    flops = 2 * CAPB * n_blk * CW * depth
    return pl.pallas_call(
        functools.partial(round_kernel, n_blk, first, last, model_width),
        grid=(1,),
        out_shape=tuple(jax.ShapeDtypeStruct(s, t) for s, t in shapes),
        in_specs=ins,
        out_specs=tuple(whole(s) for s, _ in shapes),
        compiler_params=params(48),
        cost_estimate=pl.CostEstimate(flops=flops, bytes_accessed=12_000_000, transcendentals=0),
        name="row_round",
    )(*args)


def finish_kernel(n_piece, a_ref, b_ref, gw_ref, ctx_ref, *refs):
    pieces, out, sums = refs[:n_piece], refs[n_piece], refs[n_piece + 1]
    a, b = a_ref[...], b_ref[...]
    width = pieces[0].shape[1]
    for k in range(n_piece):
        cols = slice(k * width, (k + 1) * width)
        hidden = pieces[k][...].astype(F32)
        out[:, cols] = (a * gw_ref[:, cols] - b * hidden).astype(BF16)
        sums[0:1, cols] = jnp.sum(a * hidden, axis=0, keepdims=True)
    sums[1:2, :] = jnp.sum(a * ctx_ref[...].astype(F32), axis=0, keepdims=True)


def finish(a, b, gw_own, context, pieces):
    width = context.shape[1]
    return pl.pallas_call(
        functools.partial(finish_kernel, len(pieces)),
        out_shape=(
            jax.ShapeDtypeStruct((CAPB, width), BF16),
            jax.ShapeDtypeStruct((2, width), F32),
        ),
        in_specs=[VMEM] * (4 + len(pieces)),
        out_specs=(VMEM, VMEM),
        compiler_params=params(32),
        name="finish",
    )(a, b, gw_own, context, *pieces)


def weight_kernel(n_dp, n_piece, gw_ref, va_ref, *refs):
    bs, ctxs = refs[:n_dp], refs[n_dp : 2 * n_dp]
    pieces = refs[2 * n_dp : 2 * n_dp + n_dp * n_piece]
    out, scaled = refs[-2], refs[-1]
    for d in range(n_dp):
        scaled[d * CAPB : (d + 1) * CAPB, :] = (bs[d][...] * ctxs[d][...].astype(F32)).astype(BF16)
    width = pieces[0].shape[1]
    for r in range(n_piece):
        rows = slice(r * width, (r + 1) * width)
        total = gw_ref[rows, :] * va_ref[...]
        for d in range(n_dp):
            total = total - mm(
                pieces[d * n_piece + r][...], scaled[d * CAPB : (d + 1) * CAPB, :], ((0,), (0,))
            )
        out[rows, :] = total


def weight_grad(gw_col, va, bs, ctxs, pieces):
    n_dp, n_piece = len(bs), len(pieces[0])
    width = ctxs[0].shape[1]
    flat = [p for group in pieces for p in group]
    height = n_piece * flat[0].shape[1]
    return pl.pallas_call(
        functools.partial(weight_kernel, n_dp, n_piece),
        out_shape=jax.ShapeDtypeStruct((height, width), F32),
        in_specs=[VMEM] * (2 + 2 * n_dp + len(flat)),
        out_specs=VMEM,
        scratch_shapes=[pltpu.VMEM((n_dp * CAPB, width), BF16)],
        compiler_params=params(56),
        name="weight_grad",
    )(gw_col, va, *bs, *ctxs, *flat)


def line_sum(context, resid, out_weight, is_mid, col, ready):
    edge = [(0, 1), (1, 0), (2, 3), (3, 2)]
    middle = [(1, 2), (2, 1)]
    width = resid.shape[1]
    per_block = width // CW
    early, late = [(j, r) for r in range(per_block) for j in (1, 2)], [
        (j, r) for r in range(per_block) for j in (0, 3)
    ]
    order = early[:4] + late[:2]
    rest_early, rest_late = early[4:], late[2:]
    while rest_early or rest_late:
        order += rest_early[:2] + rest_late[:2]
        rest_early, rest_late = rest_early[2:], rest_late[2:]
    n = len(order)
    parts, totals = [], []
    done = {}
    for s in range(n + LAG):
        payload = None
        if s < n:
            j, r = order[s]
            lo = j * width + r * CW
            part = jnp.dot(context, out_weight[:, lo : lo + CW], preferred_element_type=F32)
            own = jnp.where(col == j, resid[:, r * CW : (r + 1) * CW].astype(F32), 0.0)
            parts.append((part + own).astype(BF16))
            payload = parts[s]
        if s >= LAG:
            total = totals[s - LAG]
            payload = total if payload is None else jnp.where(is_mid, total, payload)
        got = lax.ppermute(payload, "tensor", edge)
        if s < n:
            joined = (parts[s].astype(F32) + got.astype(F32)).astype(BF16)
            other = lax.ppermute(joined, "tensor", middle)
            totals.append((joined.astype(F32) + other.astype(F32)).astype(BF16))
        if s >= LAG:
            done[order[s - LAG]] = (payload, got)
            ready(order[s - LAG], done)


def butterfly(value, n_dp):
    step = 1
    while step < n_dp:
        value = value + xor_move(value, step, n_dp)
        step *= 2
    return value


def target_rows(me, lengths, balance_list, returns, per_dev):
    seq_len = returns.shape[1]
    slots = lax.dynamic_slice_in_dim(balance_list, me * per_dev, per_dev)
    homes = jnp.arange(lengths.shape[0], dtype=jnp.int32)
    is_home = slots[:, None] == homes[None, :]
    sizes = jnp.sum(jnp.where(is_home, lengths[None, :], 0), axis=1)
    starts = jnp.cumsum(sizes) - sizes
    every = lax.all_gather(returns, "dp", axis=0, tiled=True)
    mine = jnp.dot(is_home.astype(BF16), every, preferred_element_type=F32)
    tokens = jnp.arange(CAPB, dtype=jnp.int32)
    offset = tokens[:, None] - starts[None, :]
    inside = (offset >= 0) & (offset < sizes[None, :])
    spread = jnp.dot(inside.astype(BF16), mine.astype(BF16), preferred_element_type=F32)
    place = jnp.sum(jnp.where(inside, offset, 0), axis=1, keepdims=True)
    at = jnp.arange(seq_len, dtype=jnp.int32)[None, :] == place
    return jnp.sum(jnp.where(at, spread, 0.0), axis=1, keepdims=True)


def on_device(
    query_states,
    key_states,
    value_states,
    residual,
    returns,
    lengths,
    balance_list,
    out_weight,
    norm_gain,
    value_weight,
):
    n_dp, n_tensor = lax.axis_size("dp"), lax.axis_size("tensor")
    me, col = lax.axis_index("dp"), lax.axis_index("tensor")
    per_dev = query_states.shape[0]
    width = query_states.shape[2]
    model_width = out_weight.shape[1]
    kv = key_states.shape[2] // HD

    pick, start, size = route(me.reshape(1), lengths, balance_list, n_dp, per_dev)
    sent = gather_rollouts(pick, (query_states, key_states, value_states), n_dp)
    blocks = exchange(sent, n_dp)
    resid_blocks = exchange(gather_rollouts(pick, (residual,), n_dp), n_dp)
    context, probs = attention_forward(start, size, blocks, kv)
    resid = pack(start, size, resid_blocks)
    contexts = [context] + [xor_move(context, d, n_dp) for d in range(1, n_dp)]

    target = target_rows(me, lengths, balance_list, returns, per_dev)
    gw_own = norm_gain * value_weight
    gw = lax.all_gather(gw_own, "tensor", axis=0, tiled=True)
    gw_high = gw.astype(BF16)
    gw_low = (gw - gw_high.astype(F32)).astype(BF16)
    pair = jnp.stack([gw_high, gw_low])
    wgw = jnp.sum(mm(pair, out_weight, ((1,), (1,))), axis=0, keepdims=True)
    block = model_width // n_dp
    gw_col = lax.dynamic_slice_in_dim(gw, me * block, block).reshape(block, 1)

    if n_tensor == 4 and n_dp == 4:
        is_mid = (col == 1) | (col == 2)
        pos = jnp.stack([me, col, is_mid.astype(jnp.int32)]).astype(jnp.int32)
        per_block = width // CW
        gw_row = gw.reshape(1, model_width)
        state, own, pieces, critic = None, [], [[] for _ in range(n_dp)], None

        def ready(key, done):
            nonlocal state, critic
            r = key[1]
            if any((j, r) not in done for j in range(n_tensor)):
                return
            out = round_step(
                r,
                per_block,
                pos,
                [done[j, r][0] for j in range(n_tensor)],
                [done[j, r][1] for j in range(n_tensor)],
                out_weight,
                gw_row,
                state,
                target if r == per_block - 1 else None,
            )
            state = out[:3]
            own.append(out[3])
            pays = out[4 : 4 + n_dp]
            pieces[0].append(pays[0])
            for d in range(1, n_dp):
                pieces[d].append(xor_move(pays[d], d, n_dp))
            if r == per_block - 1:
                critic = out[-1]

        line_sum(context, resid, out_weight, is_mid, col, ready)
        acc, a, b = state
    else:
        part = jnp.dot(context, out_weight, preferred_element_type=F32)
        mine = lax.dynamic_slice_in_dim(part, col * width, width, axis=1) + resid.astype(F32)
        part = lax.dynamic_update_slice_in_dim(part, mine, col * width, axis=1)
        hidden = lax.psum(part.astype(BF16), "tensor")
        wide = hidden.astype(F32)
        inv_rms = lax.rsqrt(jnp.sum(wide * wide, axis=1, keepdims=True) / model_width + EPS)
        dots = jnp.sum(wide * gw[None, :], axis=1, keepdims=True)
        critic = inv_rms * dots
        err = critic - target
        a, b = inv_rms * err, inv_rms**3 * err * dots / model_width
        acc = mm(hidden, out_weight, ((1,), (1,)))
        own = [lax.dynamic_slice_in_dim(hidden, col * width, width, axis=1)]
        part_for = lambda d: lax.dynamic_slice_in_dim(hidden, (me ^ d) * block, block, axis=1)
        pieces = [[part_for(0)]] + [[xor_move(part_for(d), d, n_dp)] for d in range(1, n_dp)]

    resid_out, sums = finish(a, b, gw_own.reshape(1, width), context, own)
    sums = butterfly(sums, n_dp)
    bs = [b] + [xor_move(b.reshape(CAPB), d, n_dp).reshape(CAPB, 1) for d in range(1, n_dp)]
    query_out, key_out, value_out = attention_backward(
        start, size, a, b, wgw, acc, probs, blocks, kv
    )
    weight_out = weight_grad(gw_col, sums[1:2], bs, contexts, pieces)
    gain_sum = sums[0]
    return (
        critic.reshape(CAPB).astype(BF16),
        query_out,
        key_out,
        value_out,
        resid_out,
        weight_out,
        value_weight * gain_sum,
        norm_gain * gain_sum,
    )


def solution(mesh):
    rows = P(("groups", "dp"), None, "tensor")
    packed = P(("groups", "dp"), "tensor")
    placed = (rows, rows, rows, rows, P(("groups", "dp"), None), P("groups"), P("groups"))
    placed += (P("tensor", None), P("tensor"), P("tensor"))
    return jax.shard_map(
        on_device,
        mesh=mesh,
        in_specs=placed,
        out_specs=(
            P(("groups", "dp")),
            packed,
            packed,
            packed,
            packed,
            packed,
            P(("groups", "tensor")),
            P(("groups", "tensor")),
        ),
        check_vma=False,
    )
```

```python
import functools
import math

import jax
import jax.numpy as jnp
from jax import lax
from jax.experimental import pallas as pl
from jax.experimental.pallas import tpu as pltpu
from jax.sharding import PartitionSpec as P

H = 40
KVH = 8
HD = 128
RATIO = H // KVH
CAPB = 576
EPS = 1e-06
NEG = -1e30
CW = 256
TAIL = 16
F32 = jnp.float32
BF16 = jnp.bfloat16
VMEM = pl.BlockSpec(memory_space=pltpu.VMEM)
SMEM = pl.BlockSpec(memory_space=pltpu.SMEM)
ANY = pl.BlockSpec(memory_space=pl.ANY)


def params(mib):
    return pltpu.CompilerParams(vmem_limit_bytes=mib * 1024 * 1024)


def mm(a, b, dims):
    return lax.dot_general(a, b, (dims, ((), ())), preferred_element_type=F32)


def route_kernel(n_dp, per_dev, me_ref, len_ref, bal_ref, pick_ref, start_ref, size_ref, cnt_ref):
    cap = per_dev // n_dp
    me = me_ref[0]
    for d in range(n_dp):
        target = jnp.bitwise_xor(me, d)

        def outgoing(s, count):
            b = bal_ref[target * per_dev + s]
            home = lax.div(b, per_dev)

            @pl.when(home == me)
            def _():
                pick_ref[d * cap + count] = lax.rem(b, per_dev)

            return count + (home == me).astype(jnp.int32)

        lax.fori_loop(0, per_dev, outgoing, jnp.int32(0))
        cnt_ref[d] = jnp.int32(0)

    def incoming(s, run):
        b = bal_ref[me * per_dev + s]
        d = jnp.bitwise_xor(lax.div(b, per_dev), me)
        count = cnt_ref[d]
        size = len_ref[b]
        start_ref[d * cap + count] = run
        size_ref[d * cap + count] = size
        cnt_ref[d] = count + 1
        return run + size

    lax.fori_loop(0, per_dev, incoming, jnp.int32(0))


def route(me, lengths, balance_list, n_dp, per_dev):
    table = jax.ShapeDtypeStruct((per_dev,), jnp.int32)
    return pl.pallas_call(
        functools.partial(route_kernel, n_dp, per_dev),
        out_shape=(table, table, table),
        in_specs=[SMEM] * 3,
        out_specs=(SMEM, SMEM, SMEM),
        scratch_shapes=[pltpu.SMEM((n_dp,), jnp.int32)],
        name="route",
    )(me, lengths, balance_list)


def gather_kernel(n_dp, cap, seq_len, spans, pick_ref, *refs):
    parts = refs[: len(spans)]
    returns = refs[len(spans)] if len(refs) > len(spans) + n_dp else None
    outs = refs[-n_dp:]
    for d in range(n_dp):
        for i in range(cap):
            row = pick_ref[d * cap + i]
            col = 0
            for part, (lo, hi) in zip(parts, spans):
                outs[d][i * seq_len : (i + 1) * seq_len, col : col + hi - lo] = part[row, :, lo:hi]
                col += hi - lo
        if returns is not None:
            rows = returns[...].astype(F32)
            at = lax.broadcasted_iota(jnp.int32, rows.shape, 0)
            picked = [
                jnp.sum(jnp.where(at == pick_ref[d * cap + i], rows, 0.0), axis=0, keepdims=True)
                for i in range(cap)
            ]
            picked += [jnp.zeros((TAIL - cap, seq_len), F32)]
            outs[d][cap * seq_len :, :seq_len] = jnp.concatenate(picked, axis=0).astype(BF16)
            outs[d][cap * seq_len :, seq_len:] = jnp.zeros(
                (TAIL, outs[d].shape[1] - seq_len), BF16
            )


def gather_rollouts(pick, parts, spans, returns, n_dp):
    per_dev, seq_len = parts[0].shape[:2]
    cap = per_dev // n_dp
    rows = cap * seq_len + (TAIL if returns is not None else 0)
    out = jax.ShapeDtypeStruct((rows, sum(hi - lo for lo, hi in spans)), BF16)
    extra = [] if returns is None else [returns]
    return pl.pallas_call(
        functools.partial(gather_kernel, n_dp, cap, seq_len, spans),
        out_shape=(out,) * n_dp,
        in_specs=[SMEM] + [VMEM] * (len(parts) + len(extra)),
        out_specs=(VMEM,) * n_dp,
        compiler_params=params(40),
        name="gather_rollouts",
    )(pick, *parts, *extra)


def xor_move(value, d, n_dp):
    return lax.ppermute(value, "dp", [(i, i ^ d) for i in range(n_dp)])


def exchange(blocks, n_dp):
    order = sorted(range(1, n_dp), key=lambda d: d < 2)
    moved = {d: xor_move(blocks[d], d, n_dp) for d in order}
    return [blocks[0]] + [moved[d] for d in range(1, n_dp)]


def window(start, size, seq_len):
    tall = seq_len + 8
    base = pl.multiple_of(lax.div(start, 8) * 8, 8)
    shift = start - base
    fill = lambda shape, axis: lax.broadcasted_iota(jnp.int32, shape, axis)
    place = (fill((tall, seq_len), 0) - shift == fill((tall, seq_len), 1)) & (
        fill((tall, seq_len), 1) < size
    )
    fetch = (fill((seq_len, tall), 1) - shift == fill((seq_len, tall), 0)) & (
        fill((seq_len, tall), 0) < size
    )
    return pl.ds(base, tall), place.astype(BF16), fetch.astype(BF16)


def pack_kernel(n_dp, cap, seq_len, lo, hi, with_target, start_ref, size_ref, *refs):
    blocks = refs[:n_dp]
    out, other, room = refs[-3:]
    room[...] = jnp.zeros_like(room)
    if with_target:
        other[...] = jnp.zeros_like(other)
    else:
        other[...] = refs[n_dp][...]
    for d in range(n_dp):
        for i in range(cap):
            spot, place, _ = window(start_ref[d * cap + i], size_ref[d * cap + i], seq_len)
            room[spot, :] += mm(place, blocks[d][i * seq_len : (i + 1) * seq_len, lo:hi], ((1,), (0,)))
            if with_target:
                at = cap * seq_len
                row = blocks[d][at : at + TAIL, :seq_len].astype(F32)[i : i + 1, :]
                other[spot, :] += jnp.sum(place.astype(F32) * row, axis=1, keepdims=True)
    out[...] = room[:CAPB, :].astype(BF16)


def pack(start, size, blocks, seq_len, cap, span, context):
    n_dp = len(blocks)
    lo, hi = span
    with_target = context is None
    tall = CAPB + seq_len
    second = ((tall, 1), F32) if with_target else (context.shape, BF16)
    extra = [] if with_target else [context]
    return pl.pallas_call(
        functools.partial(pack_kernel, n_dp, cap, seq_len, lo, hi, with_target),
        out_shape=(
            jax.ShapeDtypeStruct((CAPB, hi - lo), BF16),
            jax.ShapeDtypeStruct(*second),
        ),
        in_specs=[SMEM, SMEM] + [VMEM] * (n_dp + len(extra)),
        out_specs=(VMEM, VMEM),
        scratch_shapes=[pltpu.VMEM((tall, hi - lo), F32)],
        compiler_params=params(32),
        name="pack",
    )(start, size, *blocks, *extra)


def heads_of(rows, first):
    return jnp.concatenate(
        [rows[:, (first + r) * HD : (first + r + 1) * HD] for r in range(RATIO)], axis=0
    )


def forward_kernel(n_dp, cap, seq_len, kv, start_ref, size_ref, *refs):
    blocks = refs[:n_dp]
    out, probs_ref, room = refs[-3:]
    qw = kv * RATIO * HD
    scale = 1.0 / math.sqrt(HD)
    span = RATIO * seq_len
    room[...] = jnp.zeros_like(room)
    at_u = lax.broadcasted_iota(jnp.int32, (seq_len, span), 0)
    at_t = lax.rem(lax.broadcasted_iota(jnp.int32, (seq_len, span), 1), seq_len)
    at_t1 = lax.rem(lax.broadcasted_iota(jnp.int32, (1, span), 1), seq_len)
    causal = at_u <= at_t
    for d in range(n_dp):

        def step(i, _):
            size = size_ref[d * cap + i]
            spot, place, _ = window(start_ref[d * cap + i], size, seq_len)
            rows_i = pl.ds(pl.multiple_of(i * seq_len, seq_len), seq_len)
            keep = causal & (at_u < size)
            parts = []
            for g in range(kv):
                queries = heads_of(blocks[d][rows_i, g * RATIO * HD : (g + 1) * RATIO * HD], 0)
                keys = blocks[d][rows_i, qw + g * HD : qw + (g + 1) * HD]
                values = blocks[d][rows_i, qw + (kv + g) * HD : qw + (kv + g + 1) * HD]
                scores = jnp.where(keep, mm(keys, queries, ((1,), (1,))) * scale, NEG)
                top = jnp.max(scores, axis=0, keepdims=True)
                weights = jnp.exp(scores - top)
                total = jnp.sum(weights, axis=0, keepdims=True)
                probs = (weights * jnp.where(at_t1 < size, 1.0 / total, 0.0)).astype(BF16)
                probs_ref[d * cap + i, g] = probs
                mixed = mm(probs, values, ((0,), (0,)))
                parts += [mixed[r * seq_len : (r + 1) * seq_len] for r in range(RATIO)]
            mixed = jnp.concatenate(parts, axis=1).astype(BF16)
            room[spot, :] += mm(place, mixed, ((1,), (0,)))
            return 0

        lax.fori_loop(0, cap, step, 0)
    out[...] = room[:CAPB, :].astype(BF16)


def attention_forward(start, size, blocks, kv, seq_len, cap, ahead):
    n_dp = len(blocks)
    width = kv * RATIO * HD
    return pl.pallas_call(
        functools.partial(forward_kernel, n_dp, cap, seq_len, kv),
        out_shape=(
            jax.ShapeDtypeStruct((CAPB, width), BF16),
            jax.ShapeDtypeStruct((n_dp * cap, kv, seq_len, RATIO * seq_len), BF16),
        ),
        in_specs=[SMEM, SMEM] + [VMEM] * n_dp + [ANY] * len(ahead),
        out_specs=(VMEM, VMEM),
        scratch_shapes=[pltpu.VMEM((CAPB + seq_len, width), F32)],
        compiler_params=params(40),
        name="attention_forward",
    )(start, size, *blocks, *ahead)


def backward_kernel(
    n_dp, cap, seq_len, kv, start_ref, size_ref, a_ref, b_ref, wgw_ref, acc_ref, probs_ref, *refs
):
    blocks = refs[:n_dp]
    dq_out, dk_out, dv_out = refs[n_dp : n_dp + 3]
    grads, dq_room, dk_room, dv_room = refs[n_dp + 3 :]
    qw = kv * RATIO * HD
    scale = 1.0 / math.sqrt(HD)
    for room in (dq_room, dk_room, dv_room):
        room[...] = jnp.zeros_like(room)
    grads[:CAPB, :] = a_ref[...] * wgw_ref[...] - b_ref[...] * acc_ref[...]
    grads[CAPB:, :] = jnp.zeros((seq_len, qw), F32)
    for d in range(n_dp):

        def step(i, _):
            spot, place, fetch = window(start_ref[d * cap + i], size_ref[d * cap + i], seq_len)
            mine = mm(fetch, grads[spot, :].astype(BF16), ((1,), (0,))).astype(BF16)
            rows_i = pl.ds(pl.multiple_of(i * seq_len, seq_len), seq_len)
            dq_parts, dk_parts, dv_parts = [], [], []
            for g in range(kv):
                cols = slice(g * RATIO * HD, (g + 1) * RATIO * HD)
                queries = heads_of(blocks[d][rows_i, cols], 0)
                keys = blocks[d][rows_i, qw + g * HD : qw + (g + 1) * HD]
                values = blocks[d][rows_i, qw + (kv + g) * HD : qw + (kv + g + 1) * HD]
                out_grad = heads_of(mine[:, cols], 0)
                probs_low = probs_ref[d * cap + i, g]
                probs = probs_low.astype(F32)
                prob_grad = mm(values, out_grad, ((1,), (1,)))
                row_dot = jnp.sum(probs * prob_grad, axis=0, keepdims=True)
                score_grad = (probs * (prob_grad - row_dot) * scale).astype(BF16)
                dq = mm(score_grad, keys, ((0,), (0,)))
                dq_parts += [dq[r * seq_len : (r + 1) * seq_len] for r in range(RATIO)]
                dk_parts.append(mm(score_grad, queries, ((1,), (0,))))
                dv_parts.append(mm(probs_low, out_grad, ((1,), (0,))))
            for room, parts in ((dq_room, dq_parts), (dk_room, dk_parts), (dv_room, dv_parts)):
                rows = jnp.concatenate(parts, axis=1).astype(BF16)
                room[spot, :] += mm(place, rows, ((1,), (0,)))
            return 0

        lax.fori_loop(0, cap, step, 0)
    dq_out[...] = dq_room[:CAPB, :].astype(BF16)
    dk_out[...] = dk_room[:CAPB, :].astype(BF16)
    dv_out[...] = dv_room[:CAPB, :].astype(BF16)


def attention_backward(start, size, a, b, wgw, acc, probs, blocks, kv, seq_len, cap):
    n_dp = len(blocks)
    qw, kw = kv * RATIO * HD, kv * HD
    tall = CAPB + seq_len
    return pl.pallas_call(
        functools.partial(backward_kernel, n_dp, cap, seq_len, kv),
        out_shape=tuple(jax.ShapeDtypeStruct((CAPB, w), BF16) for w in (qw, kw, kw)),
        in_specs=[SMEM, SMEM] + [VMEM] * (5 + n_dp),
        out_specs=(VMEM,) * 3,
        scratch_shapes=[pltpu.VMEM((tall, w), F32) for w in (qw, qw, kw, kw)],
        compiler_params=params(48),
        name="attention_backward",
    )(start, size, a, b, wgw, acc, probs, *blocks)


def select(index, options):
    out = options[0]
    for k in range(1, len(options)):
        out = jnp.where(index == k, options[k], out)
    return out


def round_kernel(n_blk, first, last, model_width, pos_ref, *refs):
    refs = list(refs)
    take = lambda n: [refs.pop(0) for _ in range(n)]
    sent, got, weights, gains = take(n_blk), take(n_blk), take(n_blk), take(n_blk)
    acc_in, sq_in, vd_in = (None, None, None) if first else take(3)
    (target,) = take(1) if last else (None,)
    acc, sq, vd, own = take(4)
    pays = take(n_blk)
    me, col, mid = pos_ref[0], pos_ref[1], pos_ref[2] == 1
    pieces = [jnp.where(mid, s[...], g[...]) for s, g in zip(sent, got)]
    own[...] = select(col, pieces)
    for d in range(n_blk):
        pays[d][...] = select(jnp.bitwise_xor(me, d), pieces)
    squares = 0.0 if first else sq_in[...]
    dots = 0.0 if first else vd_in[...]
    for piece, gain in zip(pieces, gains):
        wide = piece.astype(F32)
        squares = squares + jnp.sum(wide * wide, axis=1, keepdims=True)
        dots = dots + jnp.sum(wide * gain[...], axis=1, keepdims=True)
    if last:
        inv_rms = lax.rsqrt(squares / model_width + EPS)
        critic = inv_rms * dots
        err = critic - target[...]
        sq[...] = inv_rms * err
        vd[...] = inv_rms * inv_rms * inv_rms * err * dots / model_width
        refs[0][...] = critic
    else:
        sq[...] = squares
        vd[...] = dots
    total = None if first else acc_in[...]
    for piece, weight in zip(pieces, weights):
        term = mm(piece, weight[...], ((1,), (1,)))
        total = term if total is None else total + term
    acc[...] = total


def round_step(r, per_block, pos, sent, got, out_weight, gw_row, state, target):
    n_blk = len(sent)
    depth, model_width = out_weight.shape
    first, last = state is None, target is not None
    at = lambda j: (lambda i: (0, j * per_block + r))
    tile = CAPB // 3
    whole = lambda shape: pl.BlockSpec((tile, shape[1]), lambda i: (i, 0))
    column, piece, square = (CAPB, 1), (CAPB, CW), (CAPB, depth)
    ins = [SMEM] + [whole(piece)] * (2 * n_blk)
    ins += [pl.BlockSpec((depth, CW), at(j)) for j in range(n_blk)]
    ins += [pl.BlockSpec((1, CW), at(j)) for j in range(n_blk)]
    args = [pos, *sent, *got] + [out_weight] * n_blk + [gw_row] * n_blk
    if not first:
        ins += [whole(square), whole(column), whole(column)]
        args += list(state)
    if last:
        ins.append(whole(column))
        args.append(target)
    shapes = [(square, F32), (column, F32), (column, F32)] + [(piece, BF16)] * (1 + n_blk)
    if last:
        shapes.append((column, F32))
    flops = 2 * CAPB * n_blk * CW * depth
    return pl.pallas_call(
        functools.partial(round_kernel, n_blk, first, last, model_width),
        grid=(CAPB // tile,),
        out_shape=tuple(jax.ShapeDtypeStruct(s, t) for s, t in shapes),
        in_specs=ins,
        out_specs=tuple(whole(s) for s, _ in shapes),
        compiler_params=params(48),
        cost_estimate=pl.CostEstimate(flops=flops, bytes_accessed=12_000_000, transcendentals=0),
        name="row_round",
    )(*args)


def row_of(column):
    return jnp.transpose(jnp.broadcast_to(column, (column.shape[0], 128)))[0:1, :]


def column_of(row):
    return jnp.transpose(jnp.broadcast_to(row, (128, row.shape[1])))[:, 0:1]


def finish_kernel(n_piece, a_ref, b_ref, critic_ref, gw_ref, ctx_ref, *refs):
    pieces = refs[:n_piece]
    out, sums, b_row, critic_row = refs[n_piece:]
    b_row[...] = row_of(b_ref[...])
    critic_row[...] = row_of(critic_ref[...])
    a, b = a_ref[...], b_ref[...]
    width = pieces[0].shape[1]
    for k in range(n_piece):
        cols = slice(k * width, (k + 1) * width)
        hidden = pieces[k][...].astype(F32)
        out[:, cols] = (a * gw_ref[:, cols] - b * hidden).astype(BF16)
        sums[0:1, cols] = jnp.sum(a * hidden, axis=0, keepdims=True)
    sums[1:2, :] = jnp.sum(a * ctx_ref[...].astype(F32), axis=0, keepdims=True)


def finish(a, b, critic, gw_own, context, pieces):
    width = context.shape[1]
    return pl.pallas_call(
        functools.partial(finish_kernel, len(pieces)),
        out_shape=(
            jax.ShapeDtypeStruct((CAPB, width), BF16),
            jax.ShapeDtypeStruct((2, width), F32),
            jax.ShapeDtypeStruct((1, CAPB), F32),
            jax.ShapeDtypeStruct((1, CAPB), F32),
        ),
        in_specs=[VMEM] * (5 + len(pieces)),
        out_specs=(VMEM,) * 4,
        compiler_params=params(32),
        name="finish",
    )(a, b, critic, gw_own, context, *pieces)


def weight_kernel(n_dp, n_piece, gw_ref, va_ref, *refs):
    bs, ctxs = refs[:n_dp], refs[n_dp : 2 * n_dp]
    pieces = refs[2 * n_dp : 2 * n_dp + n_dp * n_piece]
    out, scaled = refs[-2], refs[-1]
    for d in range(n_dp):
        factor = column_of(bs[d][...])
        scaled[d * CAPB : (d + 1) * CAPB, :] = (factor * ctxs[d][...].astype(F32)).astype(BF16)
    width = pieces[0].shape[1]
    for r in range(n_piece):
        rows = slice(r * width, (r + 1) * width)
        total = gw_ref[rows, :] * va_ref[...]
        for d in range(n_dp):
            total = total - mm(
                pieces[d * n_piece + r][...], scaled[d * CAPB : (d + 1) * CAPB, :], ((0,), (0,))
            )
        out[rows, :] = total


def weight_grad(gw_col, va, bs, ctxs, pieces):
    n_dp, n_piece = len(bs), len(pieces[0])
    width = ctxs[0].shape[1]
    flat = [p for group in pieces for p in group]
    height = n_piece * flat[0].shape[1]
    return pl.pallas_call(
        functools.partial(weight_kernel, n_dp, n_piece),
        out_shape=jax.ShapeDtypeStruct((height, width), F32),
        in_specs=[VMEM] * (2 + 2 * n_dp + len(flat)),
        out_specs=VMEM,
        scratch_shapes=[pltpu.VMEM((n_dp * CAPB, width), BF16)],
        compiler_params=params(56),
        name="weight_grad",
    )(gw_col, va, *bs, *ctxs, *flat)


def step_kernel(ends, begins, joins, totals, pos_ref, *refs):
    refs = list(refs)
    take = lambda: refs.pop(0)
    mid = pos_ref[2] == 1
    part_new = None
    if begins is not None:
        context, weight, resid = take(), take(), take()
        part_new = jnp.dot(context[...], weight[...], preferred_element_type=F32)
        own = jnp.where(pos_ref[1] == begins, resid[...].astype(F32), 0.0)
        part_new = (part_new + own).astype(BF16)
    if joins:
        joined = (take()[...].astype(F32) + take()[...].astype(F32)).astype(BF16)
    total = None
    if totals:
        total = (take()[...].astype(F32) + take()[...].astype(F32)).astype(BF16)
    refs = refs[ends:]
    if begins is not None:
        take()[...] = part_new
    if joins:
        take()[...] = joined
    if totals:
        take()[...] = total if part_new is None else jnp.where(mid, total, part_new)


def line_sum(context, resid_of, out_weight, pos, ready):
    edge = [(0, 1), (1, 0), (2, 3), (3, 2)]
    middle = [(1, 2), (2, 1)]
    width = context.shape[1]
    depth = out_weight.shape[0]
    per_block = width // CW
    order = [(j, r) for r in range(per_block) for j in (1, 2, 0, 3)]
    n = len(order)
    piece = jax.ShapeDtypeStruct((CAPB, CW), BF16)
    whole = lambda shape: pl.BlockSpec(shape, lambda i: (0, 0))
    parts, joined, from_edge, from_mid, payloads = {}, {}, {}, {}, {}
    done = {}
    tie = ()
    for s in range(-2, n + 2):
        begins, joins, totals = s + 2 < n, 0 <= s < n, s >= 2
        ins, args, outs = [SMEM], [pos], []
        j = None
        if begins:
            j, r = order[s + 2]
            resid, at = resid_of(r)
            ins += [whole(context.shape)]
            ins += [pl.BlockSpec((depth, CW), lambda i, c=j * per_block + r: (0, c))]
            ins += [pl.BlockSpec((CAPB, CW), lambda i, c=at: (0, c))]
            args += [context, out_weight, resid]
            outs.append("part")
        if joins:
            ins += [whole(piece.shape)] * 2
            args += [parts[s], from_edge[s]]
            outs.append("joined")
        if totals:
            ins += [whole(piece.shape)] * 2
            args += [joined[s - 2], from_mid[s - 2]]
            outs.append("payload")
        ins += [ANY] * len(tie)
        args += tie
        made = pl.pallas_call(
            functools.partial(step_kernel, len(tie), j, joins, totals),
            grid=(1,),
            out_shape=(piece,) * len(outs),
            in_specs=ins,
            out_specs=(whole(piece.shape),) * len(outs),
            compiler_params=params(32),
            cost_estimate=pl.CostEstimate(
                flops=2 * CAPB * CW * depth, bytes_accessed=4_000_000, transcendentals=0
            ),
            name="line_step",
        )(*args)
        made = dict(zip(outs, made))
        tie = ()
        if begins:
            parts[s + 2] = made["part"]
        payloads[s + 2] = made.get("payload", made.get("part"))
        if joins:
            joined[s] = made["joined"]
            from_mid[s] = lax.ppermute(joined[s], "tensor", middle)
        from_edge[s + 2] = lax.ppermute(payloads[s + 2], "tensor", edge)
        if s >= 4:
            done[order[s - 4]] = (payloads[s], from_edge[s])
            tie = ready(order[s - 4], done)
    for s in (n + 2, n + 3):
        done[order[s - 4]] = (payloads[s], from_edge[s])
        ready(order[s - 4], done)


def butterfly(value, n_dp):
    step = 1
    while step < n_dp:
        value = value + xor_move(value, step, n_dp)
        step *= 2
    return value


def on_device(
    query_states,
    key_states,
    value_states,
    residual,
    returns,
    lengths,
    balance_list,
    out_weight,
    norm_gain,
    value_weight,
):
    n_dp, n_tensor = lax.axis_size("dp"), lax.axis_size("tensor")
    me, col = lax.axis_index("dp"), lax.axis_index("tensor")
    per_dev = query_states.shape[0]
    width = query_states.shape[2]
    model_width = out_weight.shape[1]
    kv = key_states.shape[2] // HD

    seq_len = query_states.shape[1]
    cap = per_dev // n_dp
    qkv = width + 2 * kv * HD
    first = CW if width > CW else width
    pick, start, size = route(me.reshape(1), lengths, balance_list, n_dp, per_dev)
    sent = gather_rollouts(
        pick,
        (query_states, key_states, value_states, residual),
        ((0, width), (0, kv * HD), (0, kv * HD), (0, first)),
        returns,
        n_dp,
    )
    blocks = exchange(sent, n_dp)
    rest = exchange(
        gather_rollouts(pick, (residual,), ((first, width),), None, n_dp), n_dp
    )
    gw_own = norm_gain * value_weight
    gw = lax.all_gather(gw_own, "tensor", axis=0, tiled=True)
    gw_high = gw.astype(BF16)
    gw_low = (gw - gw_high.astype(F32)).astype(BF16)
    pair = jnp.stack([gw_high, gw_low])
    wgw = jnp.sum(mm(pair, out_weight, ((1,), (1,))), axis=0, keepdims=True)
    context, probs = attention_forward(start, size, blocks, kv, seq_len, cap, (wgw,))
    resid_first, target = pack(start, size, blocks, seq_len, cap, (qkv, qkv + first), None)
    resid_rest, context_copy = pack(start, size, rest, seq_len, cap, (0, width - first), context)
    contexts = [context] + [xor_move(context_copy, d, n_dp) for d in range(1, n_dp)]

    block = model_width // n_dp
    gw_col = lax.dynamic_slice_in_dim(gw, me * block, block).reshape(block, 1)

    if n_tensor == 4 and n_dp == 4:
        is_mid = (col == 1) | (col == 2)
        resid_of = lambda r: (resid_first, 0) if r == 0 else (resid_rest, r - 1)
        pos = jnp.stack([me, col, is_mid.astype(jnp.int32)]).astype(jnp.int32)
        per_block = width // CW
        gw_row = gw.reshape(1, model_width)
        state, own, pieces, critic = None, [], [[] for _ in range(n_dp)], None

        def ready(key, done):
            nonlocal state, critic
            r = key[1]
            if any((j, r) not in done for j in range(n_tensor)):
                return ()
            out = round_step(
                r,
                per_block,
                pos,
                [done[j, r][0] for j in range(n_tensor)],
                [done[j, r][1] for j in range(n_tensor)],
                out_weight,
                gw_row,
                state,
                target[:CAPB] if r == per_block - 1 else None,
            )
            state = out[:3]
            own.append(out[3])
            pays = out[4 : 4 + n_dp]
            pieces[0].append(pays[0])
            for d in range(1, n_dp):
                pieces[d].append(xor_move(pays[d], d, n_dp))
            if r == per_block - 1:
                critic = out[-1]
            return (out[1],)

        line_sum(context, resid_of, out_weight, pos, ready)
        acc, a, b = state
    else:
        resid = jnp.concatenate([resid_first, resid_rest], axis=1)
        part = jnp.dot(context, out_weight, preferred_element_type=F32)
        mine = lax.dynamic_slice_in_dim(part, col * width, width, axis=1) + resid.astype(F32)
        part = lax.dynamic_update_slice_in_dim(part, mine, col * width, axis=1)
        hidden = lax.psum(part.astype(BF16), "tensor")
        wide = hidden.astype(F32)
        inv_rms = lax.rsqrt(jnp.sum(wide * wide, axis=1, keepdims=True) / model_width + EPS)
        dots = jnp.sum(wide * gw[None, :], axis=1, keepdims=True)
        critic = inv_rms * dots
        err = critic - target[:CAPB]
        a, b = inv_rms * err, inv_rms**3 * err * dots / model_width
        acc = mm(hidden, out_weight, ((1,), (1,)))
        own = [lax.dynamic_slice_in_dim(hidden, col * width, width, axis=1)]
        part_for = lambda d: lax.dynamic_slice_in_dim(hidden, (me ^ d) * block, block, axis=1)
        pieces = [[part_for(0)]] + [[xor_move(part_for(d), d, n_dp)] for d in range(1, n_dp)]

    resid_out, sums, b_row, critic_row = finish(
        a, b, critic, gw_own.reshape(1, width), context, own
    )
    bs = [b_row] + [xor_move(b_row, d, n_dp) for d in range(1, n_dp)]
    sums = butterfly(sums, n_dp)
    query_out, key_out, value_out = attention_backward(
        start, size, a, b, wgw, acc, probs, blocks, kv, seq_len, cap
    )
    weight_out = weight_grad(gw_col, sums[1:2], bs, contexts, pieces)
    gain_sum = sums[0]
    return (
        critic_row.reshape(CAPB).astype(BF16),
        query_out,
        key_out,
        value_out,
        resid_out,
        weight_out,
        value_weight * gain_sum,
        norm_gain * gain_sum,
    )


def solution(mesh):
    rows = P(("groups", "dp"), None, "tensor")
    packed = P(("groups", "dp"), "tensor")
    placed = (rows, rows, rows, rows, P(("groups", "dp"), None), P("groups"), P("groups"))
    placed += (P("tensor", None), P("tensor"), P("tensor"))
    return jax.shard_map(
        on_device,
        mesh=mesh,
        in_specs=placed,
        out_specs=(
            P(("groups", "dp")),
            packed,
            packed,
            packed,
            packed,
            packed,
            P(("groups", "tensor")),
            P(("groups", "tensor")),
        ),
        check_vma=False,
    )
```

```python
import functools
import math

import jax
import jax.numpy as jnp
from jax import lax
from jax.experimental import pallas as pl
from jax.experimental.pallas import tpu as pltpu
from jax.sharding import PartitionSpec as P

H = 40
KVH = 8
HD = 128
RATIO = H // KVH
CAPB = 576
EPS = 1e-06
NEG = -1e30
CW = 256
TAIL = 16
F32 = jnp.float32
BF16 = jnp.bfloat16
VMEM = pl.BlockSpec(memory_space=pltpu.VMEM)
SMEM = pl.BlockSpec(memory_space=pltpu.SMEM)
ANY = pl.BlockSpec(memory_space=pl.ANY)
HBM = pl.BlockSpec(memory_space=pltpu.HBM)


def params(mib):
    return pltpu.CompilerParams(vmem_limit_bytes=mib * 1024 * 1024)


def mm(a, b, dims):
    return lax.dot_general(a, b, (dims, ((), ())), preferred_element_type=F32)


def route_kernel(n_dp, per_dev, me_ref, len_ref, bal_ref, pick_ref, start_ref, size_ref, cnt_ref):
    cap = per_dev // n_dp
    me = me_ref[0]
    for d in range(n_dp):
        target = jnp.bitwise_xor(me, d)

        def outgoing(s, count):
            b = bal_ref[target * per_dev + s]
            home = lax.div(b, per_dev)

            @pl.when(home == me)
            def _():
                pick_ref[d * cap + count] = lax.rem(b, per_dev)

            return count + (home == me).astype(jnp.int32)

        lax.fori_loop(0, per_dev, outgoing, jnp.int32(0))
        cnt_ref[d] = jnp.int32(0)

    def incoming(s, run):
        b = bal_ref[me * per_dev + s]
        d = jnp.bitwise_xor(lax.div(b, per_dev), me)
        count = cnt_ref[d]
        size = len_ref[b]
        start_ref[d * cap + count] = run
        size_ref[d * cap + count] = size
        cnt_ref[d] = count + 1
        return run + size

    lax.fori_loop(0, per_dev, incoming, jnp.int32(0))


def route(me, lengths, balance_list, n_dp, per_dev):
    table = jax.ShapeDtypeStruct((per_dev,), jnp.int32)
    return pl.pallas_call(
        functools.partial(route_kernel, n_dp, per_dev),
        out_shape=(table, table, table),
        in_specs=[SMEM] * 3,
        out_specs=(SMEM, SMEM, SMEM),
        scratch_shapes=[pltpu.SMEM((n_dp,), jnp.int32)],
        name="route",
    )(me, lengths, balance_list)


def gather_kernel(n_dp, cap, seq_len, spans, pick_ref, *refs):
    parts = refs[: len(spans)]
    returns = refs[len(spans)] if len(refs) > len(spans) + n_dp else None
    outs = refs[-n_dp:]
    for d in range(n_dp):
        for i in range(cap):
            row = pick_ref[d * cap + i]
            col = 0
            for part, (lo, hi) in zip(parts, spans):
                outs[d][i * seq_len : (i + 1) * seq_len, col : col + hi - lo] = part[row, :, lo:hi]
                col += hi - lo
        if returns is not None:
            rows = returns[...].astype(F32)
            at = lax.broadcasted_iota(jnp.int32, rows.shape, 0)
            picked = [
                jnp.sum(jnp.where(at == pick_ref[d * cap + i], rows, 0.0), axis=0, keepdims=True)
                for i in range(cap)
            ]
            picked += [jnp.zeros((TAIL - cap, seq_len), F32)]
            outs[d][cap * seq_len :, :seq_len] = jnp.concatenate(picked, axis=0).astype(BF16)
            outs[d][cap * seq_len :, seq_len:] = jnp.zeros(
                (TAIL, outs[d].shape[1] - seq_len), BF16
            )


def gather_rollouts(pick, parts, spans, returns, n_dp):
    per_dev, seq_len = parts[0].shape[:2]
    cap = per_dev // n_dp
    rows = cap * seq_len + (TAIL if returns is not None else 0)
    out = jax.ShapeDtypeStruct((rows, sum(hi - lo for lo, hi in spans)), BF16)
    extra = [] if returns is None else [returns]
    return pl.pallas_call(
        functools.partial(gather_kernel, n_dp, cap, seq_len, spans),
        out_shape=(out,) * n_dp,
        in_specs=[SMEM] + [VMEM] * (len(parts) + len(extra)),
        out_specs=(VMEM,) * n_dp,
        compiler_params=params(40),
        name="gather_rollouts",
    )(pick, *parts, *extra)


def xor_move(value, d, n_dp):
    return lax.ppermute(value, "dp", [(i, i ^ d) for i in range(n_dp)])


def exchange(blocks, n_dp):
    order = sorted(range(1, n_dp), key=lambda d: d < 2)
    moved = {d: xor_move(blocks[d], d, n_dp) for d in order}
    return [blocks[0]] + [moved[d] for d in range(1, n_dp)]


def window(start, size, seq_len):
    tall = seq_len + 8
    base = pl.multiple_of(lax.div(start, 8) * 8, 8)
    shift = start - base
    fill = lambda shape, axis: lax.broadcasted_iota(jnp.int32, shape, axis)
    place = (fill((tall, seq_len), 0) - shift == fill((tall, seq_len), 1)) & (
        fill((tall, seq_len), 1) < size
    )
    fetch = (fill((seq_len, tall), 1) - shift == fill((seq_len, tall), 0)) & (
        fill((seq_len, tall), 0) < size
    )
    return pl.ds(base, tall), place.astype(BF16), fetch.astype(BF16)


def pack_kernel(n_dp, cap, seq_len, lo, hi, with_target, start_ref, size_ref, *refs):
    blocks = refs[:n_dp]
    out, other, room = refs[-3:]
    room[...] = jnp.zeros_like(room)
    if with_target:
        other[...] = jnp.zeros_like(other)
    else:
        other[...] = refs[n_dp][...]
    for d in range(n_dp):
        for i in range(cap):
            spot, place, _ = window(start_ref[d * cap + i], size_ref[d * cap + i], seq_len)
            room[spot, :] += mm(place, blocks[d][i * seq_len : (i + 1) * seq_len, lo:hi], ((1,), (0,)))
            if with_target:
                at = cap * seq_len
                row = blocks[d][at : at + TAIL, :seq_len].astype(F32)[i : i + 1, :]
                other[spot, :] += jnp.sum(place.astype(F32) * row, axis=1, keepdims=True)
    out[...] = room[:CAPB, :].astype(BF16)


def pack(start, size, blocks, seq_len, cap, span, context):
    n_dp = len(blocks)
    lo, hi = span
    with_target = context is None
    tall = CAPB + seq_len
    second = ((tall, 1), F32) if with_target else (context.shape, BF16)
    extra = [] if with_target else [context]
    return pl.pallas_call(
        functools.partial(pack_kernel, n_dp, cap, seq_len, lo, hi, with_target),
        out_shape=(
            jax.ShapeDtypeStruct((CAPB, hi - lo), BF16),
            jax.ShapeDtypeStruct(*second),
        ),
        in_specs=[SMEM, SMEM] + [VMEM] * (n_dp + len(extra)),
        out_specs=(VMEM, VMEM),
        scratch_shapes=[pltpu.VMEM((tall, hi - lo), F32)],
        compiler_params=params(32),
        name="pack",
    )(start, size, *blocks, *extra)


def heads_of(rows, first):
    return jnp.concatenate(
        [rows[:, (first + r) * HD : (first + r + 1) * HD] for r in range(RATIO)], axis=0
    )


def forward_kernel(first, count, cap, seq_len, kv, start_ref, size_ref, *refs):
    blocks = refs[:count]
    if first == 0:
        probs_ref, room = refs[-2:]
    else:
        out, probs_ref, room = refs[-3:]
    qw = kv * RATIO * HD
    scale = 1.0 / math.sqrt(HD)
    span = RATIO * seq_len
    room[...] = jnp.zeros_like(room) if first == 0 else refs[count][...]
    at_u = lax.broadcasted_iota(jnp.int32, (seq_len, span), 0)
    at_t = lax.rem(lax.broadcasted_iota(jnp.int32, (seq_len, span), 1), seq_len)
    at_t1 = lax.rem(lax.broadcasted_iota(jnp.int32, (1, span), 1), seq_len)
    causal = at_u <= at_t
    for d in range(count):

        def step(i, _):
            size = size_ref[(first + d) * cap + i]
            spot, place, _ = window(start_ref[(first + d) * cap + i], size, seq_len)
            rows_i = pl.ds(pl.multiple_of(i * seq_len, seq_len), seq_len)
            keep = causal & (at_u < size)
            parts = []
            for g in range(kv):
                queries = heads_of(blocks[d][rows_i, g * RATIO * HD : (g + 1) * RATIO * HD], 0)
                keys = blocks[d][rows_i, qw + g * HD : qw + (g + 1) * HD]
                values = blocks[d][rows_i, qw + (kv + g) * HD : qw + (kv + g + 1) * HD]
                scores = jnp.where(keep, mm(keys, queries, ((1,), (1,))) * scale, NEG)
                top = jnp.max(scores, axis=0, keepdims=True)
                weights = jnp.exp(scores - top)
                total = jnp.sum(weights, axis=0, keepdims=True)
                probs = (weights * jnp.where(at_t1 < size, 1.0 / total, 0.0)).astype(BF16)
                probs_ref[d * cap + i, g] = probs
                mixed = mm(probs, values, ((0,), (0,)))
                parts += [mixed[r * seq_len : (r + 1) * seq_len] for r in range(RATIO)]
            mixed = jnp.concatenate(parts, axis=1).astype(BF16)
            room[spot, :] += mm(place, mixed, ((1,), (0,)))
            return 0

        lax.fori_loop(0, cap, step, 0)
    if first:
        out[...] = room[:CAPB, :].astype(BF16)


def attention_forward(start, size, blocks, kv, seq_len, cap, ahead):
    n_dp = len(blocks)
    half = n_dp // 2
    width = kv * RATIO * HD
    tall = CAPB + seq_len
    probs = jax.ShapeDtypeStruct((half * cap, kv, seq_len, RATIO * seq_len), BF16)
    call = lambda first, outs, scratch, before: pl.pallas_call(
        functools.partial(forward_kernel, first, half, cap, seq_len, kv),
        out_shape=outs,
        in_specs=[SMEM, SMEM] + [VMEM] * (half + (first > 0)) + [ANY] * (len(before) - (first > 0)),
        out_specs=(VMEM, VMEM),
        scratch_shapes=scratch,
        compiler_params=params(40),
        name="attention_forward",
    )(start, size, *blocks[first : first + half], *before)
    probs_low, room = call(0, (probs, jax.ShapeDtypeStruct((tall, width), F32)), [], ahead)
    context, probs_high = call(
        half,
        (jax.ShapeDtypeStruct((CAPB, width), BF16), probs),
        [pltpu.VMEM((tall, width), F32)],
        (room,),
    )
    return context, (probs_low, probs_high)


def backward_kernel(
    n_dp, cap, seq_len, kv, start_ref, size_ref, a_ref, b_ref, wgw_ref, acc_ref, *refs
):
    all_probs, refs = refs[:2], refs[2:]
    blocks = refs[:n_dp]
    dq_out, dk_out, dv_out = refs[n_dp : n_dp + 3]
    grads, dq_room, dk_room, dv_room = refs[n_dp + 3 :]
    qw = kv * RATIO * HD
    scale = 1.0 / math.sqrt(HD)
    half = n_dp // 2
    for room in (dq_room, dk_room, dv_room):
        room[...] = jnp.zeros_like(room)
    grads[:CAPB, :] = a_ref[...] * wgw_ref[...] - b_ref[...] * acc_ref[...]
    grads[CAPB:, :] = jnp.zeros((seq_len, qw), F32)
    for d in range(n_dp):

        def step(i, _):
            spot, place, fetch = window(start_ref[d * cap + i], size_ref[d * cap + i], seq_len)
            mine = mm(fetch, grads[spot, :].astype(BF16), ((1,), (0,))).astype(BF16)
            rows_i = pl.ds(pl.multiple_of(i * seq_len, seq_len), seq_len)
            dq_parts, dk_parts, dv_parts = [], [], []
            for g in range(kv):
                cols = slice(g * RATIO * HD, (g + 1) * RATIO * HD)
                queries = heads_of(blocks[d][rows_i, cols], 0)
                keys = blocks[d][rows_i, qw + g * HD : qw + (g + 1) * HD]
                values = blocks[d][rows_i, qw + (kv + g) * HD : qw + (kv + g + 1) * HD]
                out_grad = heads_of(mine[:, cols], 0)
                probs_low = all_probs[d // half][d % half * cap + i, g]
                probs = probs_low.astype(F32)
                prob_grad = mm(values, out_grad, ((1,), (1,)))
                row_dot = jnp.sum(probs * prob_grad, axis=0, keepdims=True)
                score_grad = (probs * (prob_grad - row_dot) * scale).astype(BF16)
                dq = mm(score_grad, keys, ((0,), (0,)))
                dq_parts += [dq[r * seq_len : (r + 1) * seq_len] for r in range(RATIO)]
                dk_parts.append(mm(score_grad, queries, ((1,), (0,))))
                dv_parts.append(mm(probs_low, out_grad, ((1,), (0,))))
            for room, parts in ((dq_room, dq_parts), (dk_room, dk_parts), (dv_room, dv_parts)):
                rows = jnp.concatenate(parts, axis=1).astype(BF16)
                room[spot, :] += mm(place, rows, ((1,), (0,)))
            return 0

        lax.fori_loop(0, cap, step, 0)
    dq_out[...] = dq_room[:CAPB, :].astype(BF16)
    dk_out[...] = dk_room[:CAPB, :].astype(BF16)
    dv_out[...] = dv_room[:CAPB, :].astype(BF16)


def attention_backward(start, size, a, b, wgw, acc, probs, blocks, kv, seq_len, cap):
    n_dp = len(blocks)
    qw, kw = kv * RATIO * HD, kv * HD
    tall = CAPB + seq_len
    return pl.pallas_call(
        functools.partial(backward_kernel, n_dp, cap, seq_len, kv),
        out_shape=tuple(jax.ShapeDtypeStruct((CAPB, w), BF16) for w in (qw, kw, kw)),
        in_specs=[SMEM, SMEM] + [VMEM] * (6 + n_dp),
        out_specs=(VMEM,) * 3,
        scratch_shapes=[pltpu.VMEM((tall, w), F32) for w in (qw, qw, kw, kw)],
        compiler_params=params(48),
        name="attention_backward",
    )(start, size, a, b, wgw, acc, *probs, *blocks)


def select(index, options):
    out = options[0]
    for k in range(1, len(options)):
        out = jnp.where(index == k, options[k], out)
    return out


def round_kernel(n_blk, first, last, model_width, starts, pos_ref, *refs):
    refs = list(refs)
    sems, weights = refs.pop(), refs.pop()
    take = lambda n: [refs.pop(0) for _ in range(n)]
    sent, got, (weight_hbm,), gains = take(n_blk), take(n_blk), take(1), take(n_blk)
    fetch = [
        pltpu.make_async_copy(weight_hbm.at[:, pl.ds(at, CW)], weights.at[j], sems.at[j])
        for j, at in enumerate(starts)
    ]

    @pl.when(pl.program_id(0) == 0)
    def _():
        for copy in fetch:
            copy.start()

    acc_in, sq_in, vd_in = (None, None, None) if first else take(3)
    (target,) = take(1) if last else (None,)
    acc, sq, vd, own = take(4)
    (pays,) = take(1)
    col, mid = pos_ref[1], pos_ref[2] == 1
    pieces = [jnp.where(mid, s[...], g[...]) for s, g in zip(sent, got)]
    own[...] = select(col, pieces)
    for j in range(n_blk):
        pays[j] = pieces[j]
    squares = 0.0 if first else sq_in[...]
    dots = 0.0 if first else vd_in[...]
    for piece, gain in zip(pieces, gains):
        wide = piece.astype(F32)
        squares = squares + jnp.sum(wide * wide, axis=1, keepdims=True)
        dots = dots + jnp.sum(wide * gain[...], axis=1, keepdims=True)
    if last:
        inv_rms = lax.rsqrt(squares / model_width + EPS)
        critic = inv_rms * dots
        err = critic - target[...]
        sq[...] = inv_rms * err
        vd[...] = inv_rms * inv_rms * inv_rms * err * dots / model_width
        refs[0][...] = critic
    else:
        sq[...] = squares
        vd[...] = dots

    @pl.when(pl.program_id(0) == 0)
    def _():
        for copy in fetch:
            copy.wait()

    total = None if first else acc_in[...]
    for j, piece in enumerate(pieces):
        term = mm(piece, weights[j], ((1,), (1,)))
        total = term if total is None else total + term
    acc[...] = total


def round_step(r, per_block, pos, sent, got, out_weight, gw_row, state, target):
    n_blk = len(sent)
    depth, model_width = out_weight.shape
    first, last = state is None, target is not None
    at = lambda j: (lambda i: (0, j * per_block + r))
    tile = CAPB // 3
    whole = lambda shape: pl.BlockSpec((tile, shape[1]), lambda i: (i, 0))
    column, piece, square = (CAPB, 1), (CAPB, CW), (CAPB, depth)
    ins = [SMEM] + [whole(piece)] * (2 * n_blk)
    ins += [HBM] + [pl.BlockSpec((1, CW), at(j)) for j in range(n_blk)]
    args = [pos, *sent, *got, out_weight] + [gw_row] * n_blk
    if not first:
        ins += [whole(square), whole(column), whole(column)]
        args += list(state)
    if last:
        ins.append(whole(column))
        args.append(target)
    shapes = [(square, F32), (column, F32), (column, F32), (piece, BF16)]
    shapes.append(((n_blk,) + piece, BF16))
    if last:
        shapes.append((column, F32))
    flops = 2 * CAPB * n_blk * CW * depth
    return pl.pallas_call(
        functools.partial(
            round_kernel, n_blk, first, last, model_width,
            [(j * per_block + r) * CW for j in range(n_blk)],
        ),
        grid=(CAPB // tile,),
        out_shape=tuple(jax.ShapeDtypeStruct(s, t) for s, t in shapes),
        in_specs=ins,
        out_specs=tuple(
            whole(s) if len(s) == 2 else pl.BlockSpec((n_blk, tile, CW), lambda i: (0, i, 0))
            for s, _ in shapes
        ),
        scratch_shapes=[
            pltpu.VMEM((n_blk, depth, CW), BF16),
            pltpu.SemaphoreType.DMA((n_blk,)),
        ],
        compiler_params=params(32),
        cost_estimate=pl.CostEstimate(flops=flops, bytes_accessed=12_000_000, transcendentals=0),
        name="row_round",
    )(*args)


def row_of(column):
    return jnp.transpose(jnp.broadcast_to(column, (column.shape[0], 128)))[0:1, :]


def column_of(row):
    return jnp.transpose(jnp.broadcast_to(row, (128, row.shape[1])))[:, 0:1]


def finish_kernel(n_piece, a_ref, b_ref, critic_ref, gw_ref, ctx_ref, *refs):
    pieces = refs[:n_piece]
    out, sums, b_row, critic_row = refs[n_piece:]
    b_row[...] = row_of(b_ref[...])
    critic_row[...] = row_of(critic_ref[...])
    a, b = a_ref[...], b_ref[...]
    width = pieces[0].shape[1]
    for k in range(n_piece):
        cols = slice(k * width, (k + 1) * width)
        hidden = pieces[k][...].astype(F32)
        out[:, cols] = (a * gw_ref[:, cols] - b * hidden).astype(BF16)
        sums[0:1, cols] = jnp.sum(a * hidden, axis=0, keepdims=True)
    sums[1:2, :] = jnp.sum(a * ctx_ref[...].astype(F32), axis=0, keepdims=True)


def finish(a, b, critic, gw_own, context, pieces):
    width = context.shape[1]
    return pl.pallas_call(
        functools.partial(finish_kernel, len(pieces)),
        out_shape=(
            jax.ShapeDtypeStruct((CAPB, width), BF16),
            jax.ShapeDtypeStruct((2, width), F32),
            jax.ShapeDtypeStruct((1, CAPB), F32),
            jax.ShapeDtypeStruct((1, CAPB), F32),
        ),
        in_specs=[VMEM] * (5 + len(pieces)),
        out_specs=(VMEM,) * 4,
        compiler_params=params(32),
        name="finish",
    )(a, b, critic, gw_own, context, *pieces)


def weight_kernel(n_dp, n_piece, pos_ref, gw_ref, va_ref, ctx_ref, *refs):
    bs, pieces = refs[:n_dp], refs[n_dp : n_dp + n_piece]
    out, scaled = refs[-2], refs[-1]
    me = pos_ref[0]
    for d in range(n_dp):
        factor = column_of(bs[d][...])
        rows = pl.ds(pl.multiple_of(jnp.bitwise_xor(me, d) * CAPB, CAPB), CAPB)
        scaled[rows, :] = (factor * ctx_ref[rows, :].astype(F32)).astype(BF16)
    width = pieces[0].shape[1]
    for r in range(n_piece):
        rows = slice(r * width, (r + 1) * width)
        out[rows, :] = gw_ref[rows, :] * va_ref[...] - mm(pieces[r][...], scaled[...], ((0,), (0,)))


def weight_grad(pos, gw_col, va, bs, contexts, pieces):
    width = contexts.shape[1]
    height = sum(p.shape[1] for p in pieces)
    return pl.pallas_call(
        functools.partial(weight_kernel, len(bs), len(pieces)),
        out_shape=jax.ShapeDtypeStruct((height, width), F32),
        in_specs=[SMEM] + [VMEM] * (3 + len(bs) + len(pieces)),
        out_specs=VMEM,
        scratch_shapes=[pltpu.VMEM(contexts.shape, BF16)],
        compiler_params=params(56),
        name="weight_grad",
    )(pos, gw_col, va, contexts, *bs, *pieces)


def step_kernel(ends, begins, start, joins, totals, pos_ref, *refs):
    refs = list(refs)
    sem, columns = refs.pop(), refs.pop()
    take = lambda: refs.pop(0)
    mid = pos_ref[2] == 1
    part_new = None
    if begins is not None:
        context, weight, resid = take(), take(), take()
        fetch = pltpu.make_async_copy(weight.at[:, pl.ds(start, CW)], columns, sem)
        fetch.start()
        fetch.wait()
        part_new = jnp.dot(context[...], columns[...], preferred_element_type=F32)
        own = jnp.where(pos_ref[1] == begins, resid[...].astype(F32), 0.0)
        part_new = (part_new + own).astype(BF16)
    if joins:
        joined = (take()[...].astype(F32) + take()[...].astype(F32)).astype(BF16)
    total = None
    if totals:
        total = (take()[...].astype(F32) + take()[...].astype(F32)).astype(BF16)
    refs = refs[ends:]
    if begins is not None:
        take()[...] = part_new
    if joins:
        take()[...] = joined
    if totals:
        take()[...] = total if part_new is None else jnp.where(mid, total, part_new)


def line_sum(context, resid_of, out_weight, pos, ready):
    edge = [(0, 1), (1, 0), (2, 3), (3, 2)]
    middle = [(1, 2), (2, 1)]
    width = context.shape[1]
    depth = out_weight.shape[0]
    per_block = width // CW
    order = [(j, r) for r in range(per_block) for j in (1, 2, 0, 3)]
    n = len(order)
    piece = jax.ShapeDtypeStruct((CAPB, CW), BF16)
    whole = lambda shape: pl.BlockSpec(shape, lambda i: (0, 0))
    parts, joined, from_edge, from_mid, payloads = {}, {}, {}, {}, {}
    done = {}
    tie = ()
    for s in range(-2, n + 2):
        begins, joins, totals = s + 2 < n, 0 <= s < n, s >= 2
        ins, args, outs = [SMEM], [pos], []
        j = start = None
        if begins:
            j, r = order[s + 2]
            start = (j * per_block + r) * CW
            resid, at = resid_of(r)
            ins += [whole(context.shape)]
            ins += [HBM]
            ins += [pl.BlockSpec((CAPB, CW), lambda i, c=at: (0, c))]
            args += [context, out_weight, resid]
            outs.append("part")
        if joins:
            ins += [whole(piece.shape)] * 2
            args += [parts[s], from_edge[s]]
            outs.append("joined")
        if totals:
            ins += [whole(piece.shape)] * 2
            args += [joined[s - 2], from_mid[s - 2]]
            outs.append("payload")
        ins += [ANY] * len(tie)
        args += tie
        made = pl.pallas_call(
            functools.partial(step_kernel, len(tie), j, start, joins, totals),
            grid=(1,),
            out_shape=(piece,) * len(outs),
            in_specs=ins,
            out_specs=(whole(piece.shape),) * len(outs),
            scratch_shapes=[pltpu.VMEM((depth, CW), BF16), pltpu.SemaphoreType.DMA(())],
            compiler_params=params(16),
            cost_estimate=pl.CostEstimate(
                flops=2 * CAPB * CW * depth, bytes_accessed=4_000_000, transcendentals=0
            ),
            name="line_step",
        )(*args)
        made = dict(zip(outs, made))
        tie = ()
        if begins:
            parts[s + 2] = made["part"]
        payloads[s + 2] = made.get("payload", made.get("part"))
        if joins:
            joined[s] = made["joined"]
            from_mid[s] = lax.ppermute(joined[s], "tensor", middle)
        from_edge[s + 2] = lax.ppermute(payloads[s + 2], "tensor", edge)
        if s >= 4:
            done[order[s - 4]] = (payloads[s], from_edge[s])
            tie = ready(order[s - 4], done)
    for s in (n + 2, n + 3):
        done[order[s - 4]] = (payloads[s], from_edge[s])
        ready(order[s - 4], done)


def butterfly(value, n_dp):
    step = 1
    while step < n_dp:
        value = value + xor_move(value, step, n_dp)
        step *= 2
    return value


def on_device(
    query_states,
    key_states,
    value_states,
    residual,
    returns,
    lengths,
    balance_list,
    out_weight,
    norm_gain,
    value_weight,
):
    n_dp, n_tensor = lax.axis_size("dp"), lax.axis_size("tensor")
    me, col = lax.axis_index("dp"), lax.axis_index("tensor")
    per_dev = query_states.shape[0]
    width = query_states.shape[2]
    model_width = out_weight.shape[1]
    kv = key_states.shape[2] // HD

    seq_len = query_states.shape[1]
    cap = per_dev // n_dp
    qkv = width + 2 * kv * HD
    first = CW if width > CW else width
    pick, start, size = route(me.reshape(1), lengths, balance_list, n_dp, per_dev)
    sent = gather_rollouts(
        pick,
        (query_states, key_states, value_states, residual),
        ((0, width), (0, kv * HD), (0, kv * HD), (0, first)),
        returns,
        n_dp,
    )
    blocks = exchange(sent, n_dp)
    rest = exchange(
        gather_rollouts(pick, (residual,), ((first, width),), None, n_dp), n_dp
    )
    gw_own = norm_gain * value_weight
    gw = lax.all_gather(gw_own, "tensor", axis=0, tiled=True)
    gw_high = gw.astype(BF16)
    gw_low = (gw - gw_high.astype(F32)).astype(BF16)
    pair = jnp.stack([gw_high, gw_low])
    wgw = jnp.sum(mm(pair, out_weight, ((1,), (1,))), axis=0, keepdims=True)
    context, probs = attention_forward(start, size, blocks, kv, seq_len, cap, (wgw,))
    resid_first, target = pack(start, size, blocks, seq_len, cap, (qkv, qkv + first), None)
    resid_rest, context_copy = pack(start, size, rest, seq_len, cap, (0, width - first), context)
    contexts = lax.all_gather(context_copy, "dp", axis=0, tiled=True)

    block = model_width // n_dp
    gw_col = lax.dynamic_slice_in_dim(gw, me * block, block).reshape(block, 1)

    is_mid = (col == 1) | (col == 2)
    pos = jnp.stack([me, col, is_mid.astype(jnp.int32)]).astype(jnp.int32)
    if n_tensor == 4 and n_dp == 4:
        resid_of = lambda r: (resid_first, 0) if r == 0 else (resid_rest, r - 1)
        per_block = width // CW
        gw_row = gw.reshape(1, model_width)
        state, own, pieces, critic = None, [], [], None

        def ready(key, done):
            nonlocal state, critic
            r = key[1]
            if any((j, r) not in done for j in range(n_tensor)):
                return ()
            out = round_step(
                r,
                per_block,
                pos,
                [done[j, r][0] for j in range(n_tensor)],
                [done[j, r][1] for j in range(n_tensor)],
                out_weight,
                gw_row,
                state,
                target[:CAPB] if r == per_block - 1 else None,
            )
            state = out[:3]
            own.append(out[3])
            moved = lax.all_to_all(out[4], "dp", split_axis=0, concat_axis=0, tiled=True)
            pieces.append(moved.reshape(n_dp * CAPB, CW))
            if r == per_block - 1:
                critic = out[-1]
            return (out[1],)

        line_sum(context, resid_of, out_weight, pos, ready)
        acc, a, b = state
    else:
        resid = jnp.concatenate([resid_first, resid_rest], axis=1)
        part = jnp.dot(context, out_weight, preferred_element_type=F32)
        mine = lax.dynamic_slice_in_dim(part, col * width, width, axis=1) + resid.astype(F32)
        part = lax.dynamic_update_slice_in_dim(part, mine, col * width, axis=1)
        hidden = lax.psum(part.astype(BF16), "tensor")
        wide = hidden.astype(F32)
        inv_rms = lax.rsqrt(jnp.sum(wide * wide, axis=1, keepdims=True) / model_width + EPS)
        dots = jnp.sum(wide * gw[None, :], axis=1, keepdims=True)
        critic = inv_rms * dots
        err = critic - target[:CAPB]
        a, b = inv_rms * err, inv_rms**3 * err * dots / model_width
        acc = mm(hidden, out_weight, ((1,), (1,)))
        own = [lax.dynamic_slice_in_dim(hidden, col * width, width, axis=1)]
        pieces = [lax.all_to_all(hidden, "dp", split_axis=1, concat_axis=0, tiled=True)]

    resid_out, sums, b_row, critic_row = finish(
        a, b, critic, gw_own.reshape(1, width), context, own
    )
    bs = [b_row] + [xor_move(b_row, d, n_dp) for d in range(1, n_dp)]
    sums = butterfly(sums, n_dp)
    query_out, key_out, value_out = attention_backward(
        start, size, a, b, wgw, acc, probs, blocks, kv, seq_len, cap
    )
    weight_out = weight_grad(pos, gw_col, sums[1:2], bs, contexts, pieces)
    gain_sum = sums[0]
    return (
        critic_row.reshape(CAPB).astype(BF16),
        query_out,
        key_out,
        value_out,
        resid_out,
        weight_out,
        value_weight * gain_sum,
        norm_gain * gain_sum,
    )


def solution(mesh):
    rows = P(("groups", "dp"), None, "tensor")
    packed = P(("groups", "dp"), "tensor")
    placed = (rows, rows, rows, rows, P(("groups", "dp"), None), P("groups"), P("groups"))
    placed += (P("tensor", None), P("tensor"), P("tensor"))
    return jax.shard_map(
        on_device,
        mesh=mesh,
        in_specs=placed,
        out_specs=(
            P(("groups", "dp")),
            packed,
            packed,
            packed,
            packed,
            packed,
            P(("groups", "tensor")),
            P(("groups", "tensor")),
        ),
        check_vma=False,
    )
```

```python
import functools
import math

import jax
import jax.numpy as jnp
from jax import lax
from jax.experimental import pallas as pl
from jax.experimental.pallas import tpu as pltpu
from jax.sharding import PartitionSpec as P

H = 40
KVH = 8
HD = 128
RATIO = H // KVH
CAPB = 576
EPS = 1e-06
NEG = -1e30
CW = 256
TAIL = 16
F32 = jnp.float32
BF16 = jnp.bfloat16
VMEM = pl.BlockSpec(memory_space=pltpu.VMEM)
SMEM = pl.BlockSpec(memory_space=pltpu.SMEM)
ANY = pl.BlockSpec(memory_space=pl.ANY)
HBM = pl.BlockSpec(memory_space=pltpu.HBM)


def params(mib):
    return pltpu.CompilerParams(vmem_limit_bytes=mib * 1024 * 1024)


def mm(a, b, dims):
    return lax.dot_general(a, b, (dims, ((), ())), preferred_element_type=F32)


def route_kernel(n_dp, per_dev, me_ref, len_ref, bal_ref, pick_ref, start_ref, size_ref, cnt_ref):
    cap = per_dev // n_dp
    me = me_ref[0]
    for d in range(n_dp):
        target = jnp.bitwise_xor(me, d)

        def outgoing(s, count):
            b = bal_ref[target * per_dev + s]
            home = lax.div(b, per_dev)

            @pl.when(home == me)
            def _():
                pick_ref[d * cap + count] = lax.rem(b, per_dev)

            return count + (home == me).astype(jnp.int32)

        lax.fori_loop(0, per_dev, outgoing, jnp.int32(0))
        cnt_ref[d] = jnp.int32(0)

    def incoming(s, run):
        b = bal_ref[me * per_dev + s]
        d = jnp.bitwise_xor(lax.div(b, per_dev), me)
        count = cnt_ref[d]
        size = len_ref[b]
        start_ref[d * cap + count] = run
        size_ref[d * cap + count] = size
        cnt_ref[d] = count + 1
        return run + size

    lax.fori_loop(0, per_dev, incoming, jnp.int32(0))


def route(me, lengths, balance_list, n_dp, per_dev):
    table = jax.ShapeDtypeStruct((per_dev,), jnp.int32)
    return pl.pallas_call(
        functools.partial(route_kernel, n_dp, per_dev),
        out_shape=(table, table, table),
        in_specs=[SMEM] * 3,
        out_specs=(SMEM, SMEM, SMEM),
        scratch_shapes=[pltpu.SMEM((n_dp,), jnp.int32)],
        name="route",
    )(me, lengths, balance_list)


def gather_kernel(n_dp, cap, seq_len, spans, pick_ref, *refs):
    parts = refs[: len(spans)]
    returns = refs[len(spans)] if len(refs) > len(spans) + n_dp + 1 else None
    outs, sems = refs[-n_dp - 1 : -1], refs[-1]
    copies = []
    for d in range(n_dp):
        for i in range(cap):
            row = pick_ref[d * cap + i]
            col = 0
            for p, (part, (lo, hi)) in enumerate(zip(parts, spans)):
                rows = pl.ds(i * seq_len, seq_len)
                copies.append(
                    pltpu.make_async_copy(
                        part.at[row, :, pl.ds(lo, hi - lo)],
                        outs[d].at[rows, pl.ds(col, hi - lo)],
                        sems.at[d * cap + i, p],
                    )
                )
                copies[-1].start()
                col += hi - lo
    for d in range(n_dp):
        if returns is not None:
            rows = returns[...].astype(F32)
            at = lax.broadcasted_iota(jnp.int32, rows.shape, 0)
            picked = [
                jnp.sum(jnp.where(at == pick_ref[d * cap + i], rows, 0.0), axis=0, keepdims=True)
                for i in range(cap)
            ]
            picked += [jnp.zeros((TAIL - cap, seq_len), F32)]
            outs[d][cap * seq_len :, :seq_len] = jnp.concatenate(picked, axis=0).astype(BF16)
            outs[d][cap * seq_len :, seq_len:] = jnp.zeros(
                (TAIL, outs[d].shape[1] - seq_len), BF16
            )
    for copy in copies:
        copy.wait()


def gather_rollouts(pick, parts, spans, returns, n_dp):
    per_dev, seq_len = parts[0].shape[:2]
    cap = per_dev // n_dp
    rows = cap * seq_len + (TAIL if returns is not None else 0)
    out = jax.ShapeDtypeStruct((rows, sum(hi - lo for lo, hi in spans)), BF16)
    extra = [] if returns is None else [returns]
    return pl.pallas_call(
        functools.partial(gather_kernel, n_dp, cap, seq_len, spans),
        out_shape=(out,) * n_dp,
        in_specs=[SMEM] + [ANY] * len(parts) + [VMEM] * len(extra),
        out_specs=(VMEM,) * n_dp,
        scratch_shapes=[pltpu.SemaphoreType.DMA((n_dp * cap, len(parts)))],
        compiler_params=params(60),
        name="gather_rollouts",
    )(pick, *parts, *extra)


def xor_move(value, d, n_dp):
    return lax.ppermute(value, "dp", [(i, i ^ d) for i in range(n_dp)])


def exchange(blocks, n_dp):
    order = sorted(range(1, n_dp), key=lambda d: d < 2)
    moved = {d: xor_move(blocks[d], d, n_dp) for d in order}
    return [blocks[0]] + [moved[d] for d in range(1, n_dp)]


def window(start, size, seq_len):
    tall = seq_len + 8
    base = pl.multiple_of(lax.div(start, 8) * 8, 8)
    shift = start - base
    fill = lambda shape, axis: lax.broadcasted_iota(jnp.int32, shape, axis)
    place = (fill((tall, seq_len), 0) - shift == fill((tall, seq_len), 1)) & (
        fill((tall, seq_len), 1) < size
    )
    fetch = (fill((seq_len, tall), 1) - shift == fill((seq_len, tall), 0)) & (
        fill((seq_len, tall), 0) < size
    )
    return pl.ds(base, tall), place.astype(BF16), fetch.astype(BF16)


def pack_kernel(n_dp, cap, seq_len, lo, hi, with_target, start_ref, size_ref, *refs):
    blocks = refs[:n_dp]
    out, other, room = refs[-3:]
    room[...] = jnp.zeros_like(room)
    if with_target:
        other[...] = jnp.zeros_like(other)
    else:
        other[...] = refs[n_dp][...]
    for d in range(n_dp):
        for i in range(cap):
            spot, place, _ = window(start_ref[d * cap + i], size_ref[d * cap + i], seq_len)
            room[spot, :] += mm(place, blocks[d][i * seq_len : (i + 1) * seq_len, lo:hi], ((1,), (0,)))
            if with_target:
                at = cap * seq_len
                row = blocks[d][at : at + TAIL, :seq_len].astype(F32)[i : i + 1, :]
                other[spot, :] += jnp.sum(place.astype(F32) * row, axis=1, keepdims=True)
    out[...] = room[:CAPB, :].astype(BF16)


def pack(start, size, blocks, seq_len, cap, span, context, tie=()):
    n_dp = len(blocks)
    lo, hi = span
    with_target = context is None
    tall = CAPB + seq_len
    second = ((tall, 1), F32) if with_target else (context.shape, BF16)
    extra = [] if with_target else [context]
    return pl.pallas_call(
        functools.partial(pack_kernel, n_dp, cap, seq_len, lo, hi, with_target),
        out_shape=(
            jax.ShapeDtypeStruct((CAPB, hi - lo), BF16),
            jax.ShapeDtypeStruct(*second),
        ),
        in_specs=[SMEM, SMEM] + [VMEM] * (n_dp + len(extra)) + [ANY] * len(tie),
        out_specs=(VMEM, VMEM),
        scratch_shapes=[pltpu.VMEM((tall, hi - lo), F32)],
        compiler_params=params(20),
        name="pack",
    )(start, size, *blocks, *extra, *tie)


def heads_of(rows, first):
    return jnp.concatenate(
        [rows[:, (first + r) * HD : (first + r + 1) * HD] for r in range(RATIO)], axis=0
    )


def forward_kernel(first, count, cap, seq_len, kv, start_ref, size_ref, *refs):
    blocks = refs[:count]
    if first == 0:
        probs_ref, room = refs[-2:]
    else:
        out, probs_ref, room = refs[-3:]
    qw = kv * RATIO * HD
    scale = 1.0 / math.sqrt(HD)
    span = RATIO * seq_len
    room[...] = jnp.zeros_like(room) if first == 0 else refs[count][...]
    at_u = lax.broadcasted_iota(jnp.int32, (seq_len, span), 0)
    at_t = lax.rem(lax.broadcasted_iota(jnp.int32, (seq_len, span), 1), seq_len)
    at_t1 = lax.rem(lax.broadcasted_iota(jnp.int32, (1, span), 1), seq_len)
    causal = at_u <= at_t
    for d in range(count):

        def step(i, _):
            size = size_ref[(first + d) * cap + i]
            spot, place, _ = window(start_ref[(first + d) * cap + i], size, seq_len)
            rows_i = pl.ds(pl.multiple_of(i * seq_len, seq_len), seq_len)
            keep = causal & (at_u < size)
            parts = []
            for g in range(kv):
                queries = heads_of(blocks[d][rows_i, g * RATIO * HD : (g + 1) * RATIO * HD], 0)
                keys = blocks[d][rows_i, qw + g * HD : qw + (g + 1) * HD]
                values = blocks[d][rows_i, qw + (kv + g) * HD : qw + (kv + g + 1) * HD]
                scores = jnp.where(keep, mm(keys, queries, ((1,), (1,))) * scale, NEG)
                top = jnp.max(scores, axis=0, keepdims=True)
                weights = jnp.exp(scores - top)
                total = jnp.sum(weights, axis=0, keepdims=True)
                probs = (weights * jnp.where(at_t1 < size, 1.0 / total, 0.0)).astype(BF16)
                probs_ref[d * cap + i, g] = probs
                mixed = mm(probs, values, ((0,), (0,)))
                parts += [mixed[r * seq_len : (r + 1) * seq_len] for r in range(RATIO)]
            mixed = jnp.concatenate(parts, axis=1).astype(BF16)
            room[spot, :] += mm(place, mixed, ((1,), (0,)))
            return 0

        lax.fori_loop(0, cap, step, 0)
    if first:
        out[...] = room[:CAPB, :].astype(BF16)


def attention_forward(start, size, blocks, kv, seq_len, cap, ahead):
    n_dp = len(blocks)
    half = n_dp // 2
    width = kv * RATIO * HD
    tall = CAPB + seq_len
    probs = jax.ShapeDtypeStruct((half * cap, kv, seq_len, RATIO * seq_len), BF16)
    call = lambda first, outs, scratch, before: pl.pallas_call(
        functools.partial(forward_kernel, first, half, cap, seq_len, kv),
        out_shape=outs,
        in_specs=[SMEM, SMEM] + [VMEM] * (half + (first > 0)) + [ANY] * (len(before) - (first > 0)),
        out_specs=(VMEM, VMEM),
        scratch_shapes=scratch,
        compiler_params=params(20),
        name="attention_forward",
    )(start, size, *blocks[first : first + half], *before)
    probs_low, room = call(0, (probs, jax.ShapeDtypeStruct((tall, width), F32)), [], ahead)
    context, probs_high = call(
        half,
        (jax.ShapeDtypeStruct((CAPB, width), BF16), probs),
        [pltpu.VMEM((tall, width), F32)],
        (room,),
    )
    return context, (probs_low, probs_high)


def backward_kernel(
    n_dp, cap, seq_len, kv, start_ref, size_ref, a_ref, b_ref, wgw_ref, acc_ref, *refs
):
    all_probs, refs = refs[:2], refs[2:]
    blocks = refs[:n_dp]
    dq_out, dk_out, dv_out = refs[n_dp : n_dp + 3]
    grads, dq_room, dk_room, dv_room = refs[n_dp + 3 :]
    qw = kv * RATIO * HD
    scale = 1.0 / math.sqrt(HD)
    half = n_dp // 2
    for room in (dq_room, dk_room, dv_room):
        room[...] = jnp.zeros_like(room)
    grads[:CAPB, :] = a_ref[...] * wgw_ref[...] - b_ref[...] * acc_ref[...]
    grads[CAPB:, :] = jnp.zeros((seq_len, qw), F32)
    lanes = 2 if cap % 2 == 0 else 1

    def rollout(d, i):
        spot, place, fetch = window(start_ref[d * cap + i], size_ref[d * cap + i], seq_len)
        mine = mm(fetch, grads[spot, :].astype(BF16), ((1,), (0,))).astype(BF16)
        rows_i = pl.ds(pl.multiple_of(i * seq_len, seq_len), seq_len)
        dq_parts, dk_parts, dv_parts = [], [], []
        for g in range(kv):
            cols = slice(g * RATIO * HD, (g + 1) * RATIO * HD)
            queries = heads_of(blocks[d][rows_i, cols], 0)
            keys = blocks[d][rows_i, qw + g * HD : qw + (g + 1) * HD]
            values = blocks[d][rows_i, qw + (kv + g) * HD : qw + (kv + g + 1) * HD]
            out_grad = heads_of(mine[:, cols], 0)
            probs_low = all_probs[d // half][d % half * cap + i, g]
            probs = probs_low.astype(F32)
            prob_grad = mm(values, out_grad, ((1,), (1,)))
            row_dot = jnp.sum(probs * prob_grad, axis=0, keepdims=True)
            score_grad = (probs * (prob_grad - row_dot) * scale).astype(BF16)
            dq = mm(score_grad, keys, ((0,), (0,)))
            dq_parts += [dq[r * seq_len : (r + 1) * seq_len] for r in range(RATIO)]
            dk_parts.append(mm(score_grad, queries, ((1,), (0,))))
            dv_parts.append(mm(probs_low, out_grad, ((1,), (0,))))
        wide = [jnp.concatenate(parts, axis=1).astype(BF16) for parts in (dq_parts, dk_parts, dv_parts)]
        return spot, [mm(place, rows, ((1,), (0,))) for rows in wide]

    for d in range(n_dp):

        def step(i, _):
            for spot, moved in [rollout(d, i * lanes + k) for k in range(lanes)]:
                for room, rows in zip((dq_room, dk_room, dv_room), moved):
                    room[spot, :] += rows
            return 0

        lax.fori_loop(0, cap // lanes, step, 0)
    dq_out[...] = dq_room[:CAPB, :].astype(BF16)
    dk_out[...] = dk_room[:CAPB, :].astype(BF16)
    dv_out[...] = dv_room[:CAPB, :].astype(BF16)


def attention_backward(start, size, a, b, wgw, acc, probs, blocks, kv, seq_len, cap):
    n_dp = len(blocks)
    qw, kw = kv * RATIO * HD, kv * HD
    tall = CAPB + seq_len
    return pl.pallas_call(
        functools.partial(backward_kernel, n_dp, cap, seq_len, kv),
        out_shape=tuple(jax.ShapeDtypeStruct((CAPB, w), BF16) for w in (qw, kw, kw)),
        in_specs=[SMEM, SMEM] + [VMEM] * (6 + n_dp),
        out_specs=(VMEM,) * 3,
        scratch_shapes=[pltpu.VMEM((tall, w), F32) for w in (qw, qw, kw, kw)],
        compiler_params=params(60),
        name="attention_backward",
    )(start, size, a, b, wgw, acc, *probs, *blocks)


def select(index, options):
    out = options[0]
    for k in range(1, len(options)):
        out = jnp.where(index == k, options[k], out)
    return out


def row_round(first, mid, col, weights, sent, got, gains, before, acc, sq, vd, own, pays):
    tile = CAPB // 3
    for t in range(CAPB // tile):
        rows = slice(t * tile, (t + 1) * tile)
        pieces = [jnp.where(mid, s[rows, :], g[rows, :]) for s, g in zip(sent, got)]
        own[rows, :] = select(col, pieces)
        squares = 0.0 if first else before[1][rows, :]
        dots = 0.0 if first else before[2][rows, :]
        total = None if first else before[0][rows, :]
        for j, piece in enumerate(pieces):
            pays[j, rows, :] = piece
            wide = piece.astype(F32)
            squares = squares + jnp.sum(wide * wide, axis=1, keepdims=True)
            dots = dots + jnp.sum(wide * gains[j][...], axis=1, keepdims=True)
            term = mm(piece, weights[j], ((1,), (1,)))
            total = term if total is None else total + term
        acc[rows, :] = total
        sq[rows, :] = squares
        vd[rows, :] = dots


def row_of(column):
    return jnp.transpose(jnp.broadcast_to(column, (column.shape[0], 128)))[0:1, :]


def column_of(row):
    return jnp.transpose(jnp.broadcast_to(row, (128, row.shape[1])))[:, 0:1]


def finish_kernel(n_piece, model_width, sq_ref, vd_ref, target_ref, gw_ref, ctx_ref, *refs):
    pieces = refs[:n_piece]
    out, sums, b_row, critic_row, a_col, b_col = refs[n_piece:]
    inv_rms = lax.rsqrt(sq_ref[...] / model_width + EPS)
    critic = inv_rms * vd_ref[...]
    err = critic - target_ref[:CAPB, :]
    a = inv_rms * err
    b = inv_rms * inv_rms * inv_rms * err * vd_ref[...] / model_width
    a_col[...] = a
    b_col[...] = b
    b_row[...] = row_of(b)
    critic_row[...] = row_of(critic)
    width = pieces[0].shape[1]
    for k in range(n_piece):
        cols = slice(k * width, (k + 1) * width)
        hidden = pieces[k][...].astype(F32)
        out[:, cols] = (a * gw_ref[:, cols] - b * hidden).astype(BF16)
        sums[0:1, cols] = jnp.sum(a * hidden, axis=0, keepdims=True)
    sums[1:2, :] = jnp.sum(a * ctx_ref[...].astype(F32), axis=0, keepdims=True)


def finish(sq, vd, target, gw_own, context, pieces, model_width):
    width = context.shape[1]
    return pl.pallas_call(
        functools.partial(finish_kernel, len(pieces), model_width),
        out_shape=(
            jax.ShapeDtypeStruct((CAPB, width), BF16),
            jax.ShapeDtypeStruct((2, width), F32),
            jax.ShapeDtypeStruct((1, CAPB), F32),
            jax.ShapeDtypeStruct((1, CAPB), F32),
            jax.ShapeDtypeStruct((CAPB, 1), F32),
            jax.ShapeDtypeStruct((CAPB, 1), F32),
        ),
        in_specs=[VMEM] * (5 + len(pieces)),
        out_specs=(VMEM,) * 6,
        compiler_params=params(32),
        name="finish",
    )(sq, vd, target, gw_own, context, *pieces)


def weight_kernel(n_dp, n_piece, pos_ref, gw_ref, va_ref, *refs):
    bs, (ctx_hbm,), pieces = refs[:n_dp], refs[n_dp : n_dp + 1], refs[n_dp + 1 : n_dp + 1 + n_piece]
    out, ctx, held, made, ctx_sems, in_sems, out_sems = refs[n_dp + 1 + n_piece :]
    me = pos_ref[0]
    rows_of = lambda d: pl.ds(pl.multiple_of(jnp.bitwise_xor(me, d) * CAPB, CAPB), CAPB)
    width = pieces[0].shape[1]
    ctx_in = [
        pltpu.make_async_copy(ctx_hbm.at[rows_of(d)], ctx.at[rows_of(d)], ctx_sems.at[d])
        for d in range(n_dp)
    ]
    piece_in = [pltpu.make_async_copy(pieces[r], held.at[r], in_sems.at[r]) for r in range(n_piece)]
    out_rows = lambda r: pl.ds(r * width, width)
    store = [
        pltpu.make_async_copy(made.at[r % 2], out.at[out_rows(r)], out_sems.at[r % 2])
        for r in range(n_piece)
    ]
    for copy in ctx_in + piece_in:
        copy.start()
    for d in range(n_dp):
        ctx_in[d].wait()
        factor = column_of(bs[d][...])
        rows = rows_of(d)
        ctx[rows, :] = (factor * ctx[rows, :].astype(F32)).astype(BF16)
    for r in range(n_piece):
        piece_in[r].wait()
        if r >= 2:
            store[r - 2].wait()
        rank_one = gw_ref[r * width : (r + 1) * width, :] * va_ref[...]
        made[r % 2] = rank_one - mm(held[r], ctx[...], ((0,), (0,)))
        store[r].start()
    for r in range(max(0, n_piece - 2), n_piece):
        store[r].wait()


def weight_grad(pos, gw_col, va, bs, contexts, pieces):
    n_dp, n_piece = len(bs), len(pieces)
    width = contexts.shape[1]
    rows, cols = pieces[0].shape
    return pl.pallas_call(
        functools.partial(weight_kernel, n_dp, n_piece),
        out_shape=jax.ShapeDtypeStruct((n_piece * cols, width), F32),
        in_specs=[SMEM] + [VMEM] * (2 + n_dp) + [ANY] * (1 + n_piece),
        out_specs=ANY,
        scratch_shapes=[
            pltpu.VMEM(contexts.shape, BF16),
            pltpu.VMEM((n_piece, rows, cols), BF16),
            pltpu.VMEM((2, cols, width), F32),
            pltpu.SemaphoreType.DMA((n_dp,)),
            pltpu.SemaphoreType.DMA((n_piece,)),
            pltpu.SemaphoreType.DMA((2,)),
        ],
        compiler_params=params(60),
        name="weight_grad",
    )(pos, gw_col, va, *bs, contexts, *pieces)


def step_kernel(cfg, pos_ref, *refs):
    refs = list(refs)
    take = lambda n=1: [refs.pop(0) for _ in range(n)]
    sems, columns = refs.pop(), refs.pop()
    col, mid = pos_ref[1], pos_ref[2] == 1
    begins, rounds, n_blk = cfg["begins"], cfg["rounds"], cfg["n_blk"]
    if begins is not None or rounds is not None:
        (weight,) = take()
    starts = ([] if rounds is None else rounds["starts"]) + ([] if begins is None else [begins[1]])
    fetch = [
        pltpu.make_async_copy(weight.at[:, pl.ds(at, CW)], columns.at[k], sems.at[k])
        for k, at in enumerate(starts)
    ]
    for copy in fetch:
        copy.start()
    if begins is not None:
        context, resid = take(2)
    parts = take(2) if cfg["joins"] else None
    halves = take(2) if cfg["totals"] else None
    if rounds is not None:
        sent, got, gains = take(n_blk), take(n_blk), take(n_blk)
        before = None if rounds["first"] else take(3)
    take(cfg["ties"])
    part_new = total = None
    if begins is not None:
        fetch[-1].wait()
        part_new = jnp.dot(context[...], columns[len(starts) - 1], preferred_element_type=F32)
        own = jnp.where(col == begins[0], resid[:, cfg["resid"]].astype(F32), 0.0)
        part_new = (part_new + own).astype(BF16)
        take()[0][...] = part_new
    if parts is not None:
        a, b = parts
        take()[0][...] = (a[...].astype(F32) + b[...].astype(F32)).astype(BF16)
    if halves is not None:
        a, b = halves
        total = (a[...].astype(F32) + b[...].astype(F32)).astype(BF16)
        take()[0][...] = total if part_new is None else jnp.where(mid, total, part_new)
    if rounds is not None:
        for copy in fetch[:n_blk]:
            copy.wait()
        weights = [columns[j] for j in range(n_blk)]
        row_round(rounds["first"], mid, col, weights, sent, got, gains, before, *take(5))


def line_sum(context, resid_of, out_weight, gw_row, pos, after_first, round_done):
    edge = [(0, 1), (1, 0), (2, 3), (3, 2)]
    middle = [(1, 2), (2, 1)]
    width = context.shape[1]
    depth = out_weight.shape[0]
    per_block = width // CW
    blocks = (1, 2, 0, 3)
    n_blk = len(blocks)
    order = [(j, r) for r in range(per_block) for j in blocks]
    n = len(order)
    shape = jax.ShapeDtypeStruct
    piece, column = shape((CAPB, CW), BF16), shape((CAPB, 1), F32)
    parts, joined, from_edge, from_mid, payloads = {}, {}, {}, {}, {}
    state = None
    for s in range(-2, n + 4):
        begins, joins, totals = s + 2 < n, 0 <= s < n, 2 <= s < n + 2
        ends_round = s >= 4 and (s - 4) % n_blk == n_blk - 1
        if not (begins or joins or totals or ends_round):
            continue
        cfg = {"begins": None, "joins": joins, "totals": totals, "rounds": None}
        cfg |= {"n_blk": n_blk, "ties": 0, "resid": None}
        ins, args, outs = [SMEM], [pos], {}
        if begins or ends_round:
            ins.append(ANY)
            args.append(out_weight)
        if begins:
            j, r = order[s + 2]
            resid, at = resid_of(r)
            cfg["begins"] = (j, j * width + r * CW)
            cfg["resid"] = slice(at * CW, (at + 1) * CW)
            args += [context, resid]
            outs["part"] = piece
        if joins:
            args += [parts[s], from_edge[s]]
            outs["joined"] = piece
        if totals:
            args += [joined[s - 2], from_mid[s - 2]]
            outs["payload"] = piece
        if ends_round:
            r = order[s - 4][1]
            at = [s - n_blk + 1 + blocks.index(j) for j in range(n_blk)]
            starts = [j * width + r * CW for j in range(n_blk)]
            cfg["rounds"] = {"starts": starts, "first": state is None}
            args += [payloads[k] for k in at] + [from_edge[k] for k in at]
            args += [gw_row[:, lo : lo + CW] for lo in starts]
            args += [] if state is None else state
            outs |= {"acc": shape((CAPB, depth), F32), "sq": column, "vd": column}
            outs |= {"own": piece, "pays": shape((n_blk, CAPB, CW), BF16)}
        ins += [VMEM] * (len(args) - len(ins))
        flops = 2 * CAPB * CW * depth * (begins + n_blk * ends_round)
        made = pl.pallas_call(
            functools.partial(step_kernel, cfg),
            out_shape=tuple(outs.values()),
            in_specs=ins,
            out_specs=(VMEM,) * len(outs),
            scratch_shapes=[
                pltpu.VMEM((n_blk + 1, depth, CW), BF16),
                pltpu.SemaphoreType.DMA((n_blk + 1,)),
            ],
            compiler_params=params(24),
            cost_estimate=pl.CostEstimate(
                flops=flops, bytes_accessed=4_000_000, transcendentals=0
            ),
            name="row_step" if ends_round else "line_step",
        )(*args)
        made = dict(zip(outs, made))
        if begins:
            parts[s + 2] = made["part"]
        if begins or totals:
            payloads[s + 2] = made.get("payload", made.get("part"))
            from_edge[s + 2] = lax.ppermute(payloads[s + 2], "tensor", edge)
        if joins:
            joined[s] = made["joined"]
            from_mid[s] = lax.ppermute(joined[s], "tensor", middle)
        if s == 0:
            after_first(joined[s])
        if ends_round:
            state = [made["acc"], made["sq"], made["vd"]]
            round_done(made["own"], made["pays"])
    return state


def butterfly(value, n_dp):
    step = 1
    while step < n_dp:
        value = value + xor_move(value, step, n_dp)
        step *= 2
    return value


def on_device(
    query_states,
    key_states,
    value_states,
    residual,
    returns,
    lengths,
    balance_list,
    out_weight,
    norm_gain,
    value_weight,
):
    n_dp, n_tensor = lax.axis_size("dp"), lax.axis_size("tensor")
    me, col = lax.axis_index("dp"), lax.axis_index("tensor")
    per_dev = query_states.shape[0]
    width = query_states.shape[2]
    model_width = out_weight.shape[1]
    kv = key_states.shape[2] // HD

    seq_len = query_states.shape[1]
    cap = per_dev // n_dp
    qkv = width + 2 * kv * HD
    first = CW if width > CW else width
    pick, start, size = route(me.reshape(1), lengths, balance_list, n_dp, per_dev)
    sent = gather_rollouts(
        pick,
        (query_states, key_states, value_states, residual),
        ((0, width), (0, kv * HD), (0, kv * HD), (0, first)),
        returns,
        n_dp,
    )
    blocks = exchange(sent, n_dp)
    rest = exchange(
        gather_rollouts(pick, (residual,), ((first, width),), None, n_dp), n_dp
    )
    gw_own = norm_gain * value_weight
    gw = lax.all_gather(gw_own, "tensor", axis=0, tiled=True)
    gw_high = gw.astype(BF16)
    gw_low = (gw - gw_high.astype(F32)).astype(BF16)
    pair = jnp.stack([gw_high, gw_low])
    wgw = jnp.sum(mm(pair, out_weight, ((1,), (1,))), axis=0, keepdims=True)
    context, probs = attention_forward(start, size, blocks, kv, seq_len, cap, (wgw,))
    resid_first, target = pack(start, size, blocks, seq_len, cap, (qkv, qkv + first), None)
    block = model_width // n_dp
    gw_col = lax.dynamic_slice_in_dim(gw, me * block, block).reshape(block, 1)

    is_mid = (col == 1) | (col == 2)
    pos = jnp.stack([me, col, is_mid.astype(jnp.int32)]).astype(jnp.int32)
    if n_tensor == 4 and n_dp == 4:
        later = {}

        def after_first(tie):
            later["resid"], later["context"] = pack(
                start, size, rest, seq_len, cap, (0, width - first), context, (tie,)
            )

        own, pieces = [], []

        def round_done(mine, pays):
            own.append(mine)
            moved = lax.all_to_all(pays, "dp", split_axis=0, concat_axis=0, tiled=True)
            pieces.append(moved.reshape(n_dp * CAPB, CW))

        acc, sq, vd = line_sum(
            context,
            lambda r: (resid_first, 0) if r == 0 else (later["resid"], r - 1),
            out_weight,
            gw.reshape(1, model_width),
            pos,
            after_first,
            round_done,
        )
        contexts = lax.all_gather(later["context"], "dp", axis=0, tiled=True)
    else:
        resid_rest, _ = pack(start, size, rest, seq_len, cap, (0, width - first), context)
        contexts = lax.all_gather(context, "dp", axis=0, tiled=True)
        resid = jnp.concatenate([resid_first, resid_rest], axis=1)
        part = jnp.dot(context, out_weight, preferred_element_type=F32)
        mine = lax.dynamic_slice_in_dim(part, col * width, width, axis=1) + resid.astype(F32)
        part = lax.dynamic_update_slice_in_dim(part, mine, col * width, axis=1)
        hidden = lax.psum(part.astype(BF16), "tensor")
        wide = hidden.astype(F32)
        sq = jnp.sum(wide * wide, axis=1, keepdims=True)
        vd = jnp.sum(wide * gw[None, :], axis=1, keepdims=True)
        acc = mm(hidden, out_weight, ((1,), (1,)))
        own = [lax.dynamic_slice_in_dim(hidden, col * width, width, axis=1)]
        pieces = [lax.all_to_all(hidden, "dp", split_axis=1, concat_axis=0, tiled=True)]

    resid_out, sums, b_row, critic_row, a, b = finish(
        sq, vd, target, gw_own.reshape(1, width), context, own, model_width
    )
    bs = [b_row] + [xor_move(b_row, d, n_dp) for d in range(1, n_dp)]
    sums = butterfly(sums, n_dp)
    query_out, key_out, value_out = attention_backward(
        start, size, a, b, wgw, acc, probs, blocks, kv, seq_len, cap
    )
    weight_out = weight_grad(pos, gw_col, sums[1:2], bs, contexts, pieces)
    gain_sum = sums[0]
    return (
        critic_row.reshape(CAPB).astype(BF16),
        query_out,
        key_out,
        value_out,
        resid_out,
        weight_out,
        value_weight * gain_sum,
        norm_gain * gain_sum,
    )


def solution(mesh):
    rows = P(("groups", "dp"), None, "tensor")
    packed = P(("groups", "dp"), "tensor")
    placed = (rows, rows, rows, rows, P(("groups", "dp"), None), P("groups"), P("groups"))
    placed += (P("tensor", None), P("tensor"), P("tensor"))
    return jax.shard_map(
        on_device,
        mesh=mesh,
        in_specs=placed,
        out_specs=(
            P(("groups", "dp")),
            packed,
            packed,
            packed,
            packed,
            packed,
            P(("groups", "tensor")),
            P(("groups", "tensor")),
        ),
        check_vma=False,
    )
```

```python
import functools
import math

import jax
import jax.numpy as jnp
from jax import lax
from jax.experimental import pallas as pl
from jax.experimental.pallas import tpu as pltpu
from jax.sharding import PartitionSpec as P

H = 40
KVH = 8
HD = 128
RATIO = H // KVH
CAPB = 576
EPS = 1e-06
NEG = -1e30
CW = 256
TAIL = 16
F32 = jnp.float32
BF16 = jnp.bfloat16
VMEM = pl.BlockSpec(memory_space=pltpu.VMEM)
SMEM = pl.BlockSpec(memory_space=pltpu.SMEM)
ANY = pl.BlockSpec(memory_space=pl.ANY)
HBM = pl.BlockSpec(memory_space=pltpu.HBM)


def params(mib):
    return pltpu.CompilerParams(vmem_limit_bytes=mib * 1024 * 1024)


def mm(a, b, dims):
    return lax.dot_general(a, b, (dims, ((), ())), preferred_element_type=F32)


def route_kernel(n_dp, per_dev, me_ref, len_ref, bal_ref, pick_ref, start_ref, size_ref, cnt_ref):
    cap = per_dev // n_dp
    me = me_ref[0]
    for d in range(n_dp):
        target = jnp.bitwise_xor(me, d)

        def outgoing(s, count):
            b = bal_ref[target * per_dev + s]
            home = lax.div(b, per_dev)

            @pl.when(home == me)
            def _():
                pick_ref[d * cap + count] = lax.rem(b, per_dev)

            return count + (home == me).astype(jnp.int32)

        lax.fori_loop(0, per_dev, outgoing, jnp.int32(0))
        cnt_ref[d] = jnp.int32(0)

    def incoming(s, run):
        b = bal_ref[me * per_dev + s]
        d = jnp.bitwise_xor(lax.div(b, per_dev), me)
        count = cnt_ref[d]
        size = len_ref[b]
        start_ref[d * cap + count] = run
        size_ref[d * cap + count] = size
        cnt_ref[d] = count + 1
        return run + size

    lax.fori_loop(0, per_dev, incoming, jnp.int32(0))


def route(me, lengths, balance_list, n_dp, per_dev):
    table = jax.ShapeDtypeStruct((per_dev,), jnp.int32)
    return pl.pallas_call(
        functools.partial(route_kernel, n_dp, per_dev),
        out_shape=(table, table, table),
        in_specs=[SMEM] * 3,
        out_specs=(SMEM, SMEM, SMEM),
        scratch_shapes=[pltpu.SMEM((n_dp,), jnp.int32)],
        name="route",
    )(me, lengths, balance_list)


def gather_kernel(n_dp, cap, seq_len, spans, pick_ref, *refs):
    parts = refs[: len(spans)]
    returns = refs[len(spans)] if len(refs) > len(spans) + n_dp + 1 else None
    outs, sems = refs[-n_dp - 1 : -1], refs[-1]
    copies = []
    for d in range(n_dp):
        for i in range(cap):
            row = pick_ref[d * cap + i]
            col = 0
            for p, (part, (lo, hi)) in enumerate(zip(parts, spans)):
                rows = pl.ds(i * seq_len, seq_len)
                copies.append(
                    pltpu.make_async_copy(
                        part.at[row, :, pl.ds(lo, hi - lo)],
                        outs[d].at[rows, pl.ds(col, hi - lo)],
                        sems.at[d * cap + i, p],
                    )
                )
                copies[-1].start()
                col += hi - lo
    for d in range(n_dp):
        if returns is not None:
            rows = returns[...].astype(F32)
            at = lax.broadcasted_iota(jnp.int32, rows.shape, 0)
            picked = [
                jnp.sum(jnp.where(at == pick_ref[d * cap + i], rows, 0.0), axis=0, keepdims=True)
                for i in range(cap)
            ]
            picked += [jnp.zeros((TAIL - cap, seq_len), F32)]
            outs[d][cap * seq_len :, :seq_len] = jnp.concatenate(picked, axis=0).astype(BF16)
            outs[d][cap * seq_len :, seq_len:] = jnp.zeros(
                (TAIL, outs[d].shape[1] - seq_len), BF16
            )
    for copy in copies:
        copy.wait()


def gather_rollouts(pick, parts, spans, returns, n_dp):
    per_dev, seq_len = parts[0].shape[:2]
    cap = per_dev // n_dp
    rows = cap * seq_len + (TAIL if returns is not None else 0)
    out = jax.ShapeDtypeStruct((rows, sum(hi - lo for lo, hi in spans)), BF16)
    extra = [] if returns is None else [returns]
    return pl.pallas_call(
        functools.partial(gather_kernel, n_dp, cap, seq_len, spans),
        out_shape=(out,) * n_dp,
        in_specs=[SMEM] + [ANY] * len(parts) + [VMEM] * len(extra),
        out_specs=(VMEM,) * n_dp,
        scratch_shapes=[pltpu.SemaphoreType.DMA((n_dp * cap, len(parts)))],
        compiler_params=params(60),
        name="gather_rollouts",
    )(pick, *parts, *extra)


def xor_move(value, d, n_dp):
    return lax.ppermute(value, "dp", [(i, i ^ d) for i in range(n_dp)])


def exchange(blocks, n_dp):
    order = sorted(range(1, n_dp), key=lambda d: d < 2)
    moved = {d: xor_move(blocks[d], d, n_dp) for d in order}
    return [blocks[0]] + [moved[d] for d in range(1, n_dp)]


def window(start, size, seq_len):
    tall = seq_len + 8
    base = pl.multiple_of(lax.div(start, 8) * 8, 8)
    shift = start - base
    fill = lambda shape, axis: lax.broadcasted_iota(jnp.int32, shape, axis)
    place = (fill((tall, seq_len), 0) - shift == fill((tall, seq_len), 1)) & (
        fill((tall, seq_len), 1) < size
    )
    fetch = (fill((seq_len, tall), 1) - shift == fill((seq_len, tall), 0)) & (
        fill((seq_len, tall), 0) < size
    )
    return pl.ds(base, tall), place.astype(BF16), fetch.astype(BF16)


def pack_kernel(n_dp, cap, seq_len, lo, hi, with_target, start_ref, size_ref, *refs):
    blocks = refs[:n_dp]
    out, other, room = refs[-3:]
    room[...] = jnp.zeros_like(room)
    if with_target:
        other[...] = jnp.zeros_like(other)
    else:
        other[...] = refs[n_dp][...]
    for d in range(n_dp):
        for i in range(cap):
            spot, place, _ = window(start_ref[d * cap + i], size_ref[d * cap + i], seq_len)
            room[spot, :] += mm(place, blocks[d][i * seq_len : (i + 1) * seq_len, lo:hi], ((1,), (0,)))
            if with_target:
                at = cap * seq_len
                row = blocks[d][at : at + TAIL, :seq_len].astype(F32)[i : i + 1, :]
                other[spot, :] += jnp.sum(place.astype(F32) * row, axis=1, keepdims=True)
    out[...] = room[:CAPB, :].astype(BF16)


def pack(start, size, blocks, seq_len, cap, span, context, tie=()):
    n_dp = len(blocks)
    lo, hi = span
    with_target = context is None
    tall = CAPB + seq_len
    second = ((tall, 1), F32) if with_target else (context.shape, BF16)
    extra = [] if with_target else [context]
    return pl.pallas_call(
        functools.partial(pack_kernel, n_dp, cap, seq_len, lo, hi, with_target),
        out_shape=(
            jax.ShapeDtypeStruct((CAPB, hi - lo), BF16),
            jax.ShapeDtypeStruct(*second),
        ),
        in_specs=[SMEM, SMEM] + [VMEM] * (n_dp + len(extra)) + [ANY] * len(tie),
        out_specs=(VMEM, VMEM),
        scratch_shapes=[pltpu.VMEM((tall, hi - lo), F32)],
        compiler_params=params(20),
        name="pack",
    )(start, size, *blocks, *extra, *tie)


def heads_of(rows, first):
    return jnp.concatenate(
        [rows[:, (first + r) * HD : (first + r + 1) * HD] for r in range(RATIO)], axis=0
    )


def forward_kernel(first, count, cap, seq_len, kv, start_ref, size_ref, *refs):
    blocks = refs[:count]
    if first == 0:
        probs_ref, room = refs[-2:]
    else:
        out, probs_ref, room = refs[-3:]
    qw = kv * RATIO * HD
    scale = 1.0 / math.sqrt(HD)
    span = RATIO * seq_len
    room[...] = jnp.zeros_like(room) if first == 0 else refs[count][...]
    at_u = lax.broadcasted_iota(jnp.int32, (seq_len, span), 0)
    at_t = lax.rem(lax.broadcasted_iota(jnp.int32, (seq_len, span), 1), seq_len)
    at_t1 = lax.rem(lax.broadcasted_iota(jnp.int32, (1, span), 1), seq_len)
    causal = at_u <= at_t
    for d in range(count):

        def step(i, _):
            size = size_ref[(first + d) * cap + i]
            spot, place, _ = window(start_ref[(first + d) * cap + i], size, seq_len)
            rows_i = pl.ds(pl.multiple_of(i * seq_len, seq_len), seq_len)
            keep = causal & (at_u < size)
            parts = []
            for g in range(kv):
                queries = heads_of(blocks[d][rows_i, g * RATIO * HD : (g + 1) * RATIO * HD], 0)
                keys = blocks[d][rows_i, qw + g * HD : qw + (g + 1) * HD]
                values = blocks[d][rows_i, qw + (kv + g) * HD : qw + (kv + g + 1) * HD]
                scores = jnp.where(keep, mm(keys, queries, ((1,), (1,))) * scale, NEG)
                top = jnp.max(scores, axis=0, keepdims=True)
                weights = jnp.exp(scores - top)
                total = jnp.sum(weights, axis=0, keepdims=True)
                probs = (weights * jnp.where(at_t1 < size, 1.0 / total, 0.0)).astype(BF16)
                probs_ref[d * cap + i, g] = probs
                mixed = mm(probs, values, ((0,), (0,)))
                parts += [mixed[r * seq_len : (r + 1) * seq_len] for r in range(RATIO)]
            mixed = jnp.concatenate(parts, axis=1).astype(BF16)
            room[spot, :] += mm(place, mixed, ((1,), (0,)))
            return 0

        lax.fori_loop(0, cap, step, 0)
    if first:
        out[...] = room[:CAPB, :].astype(BF16)


def attention_forward(start, size, blocks, kv, seq_len, cap, ahead):
    n_dp = len(blocks)
    half = n_dp // 2
    width = kv * RATIO * HD
    tall = CAPB + seq_len
    probs = jax.ShapeDtypeStruct((half * cap, kv, seq_len, RATIO * seq_len), BF16)
    call = lambda first, outs, scratch, before: pl.pallas_call(
        functools.partial(forward_kernel, first, half, cap, seq_len, kv),
        out_shape=outs,
        in_specs=[SMEM, SMEM] + [VMEM] * (half + (first > 0)) + [ANY] * (len(before) - (first > 0)),
        out_specs=(VMEM, VMEM),
        scratch_shapes=scratch,
        compiler_params=params(20),
        name="attention_forward",
    )(start, size, *blocks[first : first + half], *before)
    probs_low, room = call(0, (probs, jax.ShapeDtypeStruct((tall, width), F32)), [], ahead)
    context, probs_high = call(
        half,
        (jax.ShapeDtypeStruct((CAPB, width), BF16), probs),
        [pltpu.VMEM((tall, width), F32)],
        (room,),
    )
    return context, (probs_low, probs_high)


def backward_kernel(
    n_dp, cap, seq_len, kv, start_ref, size_ref, a_ref, b_ref, wgw_ref, acc_ref, *refs
):
    all_probs, refs = refs[:2], refs[2:]
    blocks = refs[:n_dp]
    dq_out, dk_out, dv_out = refs[n_dp : n_dp + 3]
    grads, dq_room, dk_room, dv_room = refs[n_dp + 3 :]
    qw = kv * RATIO * HD
    scale = 1.0 / math.sqrt(HD)
    half = n_dp // 2
    for room in (dq_room, dk_room, dv_room):
        room[...] = jnp.zeros_like(room)
    grads[:CAPB, :] = a_ref[...] * wgw_ref[...] - b_ref[...] * acc_ref[...]
    grads[CAPB:, :] = jnp.zeros((seq_len, qw), F32)
    lanes = 2 if cap % 2 == 0 else 1

    def rollout(d, i):
        spot, place, fetch = window(start_ref[d * cap + i], size_ref[d * cap + i], seq_len)
        mine = mm(fetch, grads[spot, :].astype(BF16), ((1,), (0,))).astype(BF16)
        rows_i = pl.ds(pl.multiple_of(i * seq_len, seq_len), seq_len)
        dq_parts, dk_parts, dv_parts = [], [], []
        for g in range(kv):
            cols = slice(g * RATIO * HD, (g + 1) * RATIO * HD)
            queries = heads_of(blocks[d][rows_i, cols], 0)
            keys = blocks[d][rows_i, qw + g * HD : qw + (g + 1) * HD]
            values = blocks[d][rows_i, qw + (kv + g) * HD : qw + (kv + g + 1) * HD]
            out_grad = heads_of(mine[:, cols], 0)
            probs_low = all_probs[d // half][d % half * cap + i, g]
            probs = probs_low.astype(F32)
            prob_grad = mm(values, out_grad, ((1,), (1,)))
            row_dot = jnp.sum(probs * prob_grad, axis=0, keepdims=True)
            score_grad = (probs * (prob_grad - row_dot) * scale).astype(BF16)
            dq = mm(score_grad, keys, ((0,), (0,)))
            dq_parts += [dq[r * seq_len : (r + 1) * seq_len] for r in range(RATIO)]
            dk_parts.append(mm(score_grad, queries, ((1,), (0,))))
            dv_parts.append(mm(probs_low, out_grad, ((1,), (0,))))
        wide = [jnp.concatenate(parts, axis=1).astype(BF16) for parts in (dq_parts, dk_parts, dv_parts)]
        return spot, [mm(place, rows, ((1,), (0,))) for rows in wide]

    for d in range(n_dp):

        def step(i, _):
            for spot, moved in [rollout(d, i * lanes + k) for k in range(lanes)]:
                for room, rows in zip((dq_room, dk_room, dv_room), moved):
                    room[spot, :] += rows
            return 0

        lax.fori_loop(0, cap // lanes, step, 0)
    dq_out[...] = dq_room[:CAPB, :].astype(BF16)
    dk_out[...] = dk_room[:CAPB, :].astype(BF16)
    dv_out[...] = dv_room[:CAPB, :].astype(BF16)


def attention_backward(start, size, a, b, wgw, acc, probs, blocks, kv, seq_len, cap):
    n_dp = len(blocks)
    qw, kw = kv * RATIO * HD, kv * HD
    tall = CAPB + seq_len
    return pl.pallas_call(
        functools.partial(backward_kernel, n_dp, cap, seq_len, kv),
        out_shape=tuple(jax.ShapeDtypeStruct((CAPB, w), BF16) for w in (qw, kw, kw)),
        in_specs=[SMEM, SMEM] + [VMEM] * (6 + n_dp),
        out_specs=(VMEM,) * 3,
        scratch_shapes=[pltpu.VMEM((tall, w), F32) for w in (qw, qw, kw, kw)],
        compiler_params=params(60),
        name="attention_backward",
    )(start, size, a, b, wgw, acc, *probs, *blocks)


def select(index, options):
    out = options[0]
    for k in range(1, len(options)):
        out = jnp.where(index == k, options[k], out)
    return out


def row_round(first, mid, col, weights, sent, got, gains, before, acc, sq, vd, own, pays):
    tile = CAPB // 3
    for t in range(CAPB // tile):
        rows = slice(t * tile, (t + 1) * tile)
        pieces = [jnp.where(mid, s[rows, :], g[rows, :]) for s, g in zip(sent, got)]
        own[rows, :] = select(col, pieces)
        squares = 0.0 if first else before[1][rows, :]
        dots = 0.0 if first else before[2][rows, :]
        total = None if first else before[0][rows, :]
        for j, piece in enumerate(pieces):
            pays[j, rows, :] = piece
            wide = piece.astype(F32)
            squares = squares + jnp.sum(wide * wide, axis=1, keepdims=True)
            dots = dots + jnp.sum(wide * gains[j][...], axis=1, keepdims=True)
            term = mm(piece, weights[j], ((1,), (1,)))
            total = term if total is None else total + term
        acc[rows, :] = total
        sq[rows, :] = squares
        vd[rows, :] = dots


def row_of(column):
    return jnp.transpose(jnp.broadcast_to(column, (column.shape[0], 128)))[0:1, :]


def column_of(row):
    return jnp.transpose(jnp.broadcast_to(row, (128, row.shape[1])))[:, 0:1]


def finish_kernel(n_piece, model_width, sq_ref, vd_ref, target_ref, gw_ref, ctx_ref, *refs):
    pieces = refs[:n_piece]
    out, sums, b_row, critic_row, a_col, b_col = refs[n_piece:]
    inv_rms = lax.rsqrt(sq_ref[...] / model_width + EPS)
    critic = inv_rms * vd_ref[...]
    err = critic - target_ref[:CAPB, :]
    a = inv_rms * err
    b = inv_rms * inv_rms * inv_rms * err * vd_ref[...] / model_width
    a_col[...] = a
    b_col[...] = b
    b_row[...] = row_of(b)
    critic_row[...] = row_of(critic)
    width = pieces[0].shape[1]
    for k in range(n_piece):
        cols = slice(k * width, (k + 1) * width)
        hidden = pieces[k][...].astype(F32)
        out[:, cols] = (a * gw_ref[:, cols] - b * hidden).astype(BF16)
        sums[0:1, cols] = jnp.sum(a * hidden, axis=0, keepdims=True)
    sums[1:2, :] = jnp.sum(a * ctx_ref[...].astype(F32), axis=0, keepdims=True)


def finish(sq, vd, target, gw_own, context, pieces, model_width):
    width = context.shape[1]
    return pl.pallas_call(
        functools.partial(finish_kernel, len(pieces), model_width),
        out_shape=(
            jax.ShapeDtypeStruct((CAPB, width), BF16),
            jax.ShapeDtypeStruct((2, width), F32),
            jax.ShapeDtypeStruct((1, CAPB), F32),
            jax.ShapeDtypeStruct((1, CAPB), F32),
            jax.ShapeDtypeStruct((CAPB, 1), F32),
            jax.ShapeDtypeStruct((CAPB, 1), F32),
        ),
        in_specs=[VMEM] * (5 + len(pieces)),
        out_specs=(VMEM,) * 6,
        compiler_params=params(32),
        name="finish",
    )(sq, vd, target, gw_own, context, *pieces)


def weight_kernel(n_dp, n_piece, pos_ref, gw_ref, va_ref, *refs):
    bs, (ctx_hbm,), pieces = refs[:n_dp], refs[n_dp : n_dp + 1], refs[n_dp + 1 : n_dp + 1 + n_piece]
    out, ctx, held, made, ctx_sems, in_sems, out_sems = refs[n_dp + 1 + n_piece :]
    me = pos_ref[0]
    rows_of = lambda d: pl.ds(pl.multiple_of(jnp.bitwise_xor(me, d) * CAPB, CAPB), CAPB)
    width = pieces[0].shape[1]
    ctx_in = [
        pltpu.make_async_copy(ctx_hbm.at[rows_of(d)], ctx.at[rows_of(d)], ctx_sems.at[d])
        for d in range(n_dp)
    ]
    piece_in = [pltpu.make_async_copy(pieces[r], held.at[r], in_sems.at[r]) for r in range(n_piece)]
    out_rows = lambda r: pl.ds(r * width, width)
    store = [
        pltpu.make_async_copy(made.at[r % 2], out.at[out_rows(r)], out_sems.at[r % 2])
        for r in range(n_piece)
    ]
    for copy in ctx_in + piece_in:
        copy.start()
    for d in range(n_dp):
        ctx_in[d].wait()
        factor = column_of(bs[d][...])
        rows = rows_of(d)
        ctx[rows, :] = (factor * ctx[rows, :].astype(F32)).astype(BF16)
    for r in range(n_piece):
        piece_in[r].wait()
        if r >= 2:
            store[r - 2].wait()
        rank_one = gw_ref[r * width : (r + 1) * width, :] * va_ref[...]
        made[r % 2] = rank_one - mm(held[r], ctx[...], ((0,), (0,)))
        store[r].start()
    for r in range(max(0, n_piece - 2), n_piece):
        store[r].wait()


def weight_grad(pos, gw_col, va, bs, contexts, pieces):
    n_dp, n_piece = len(bs), len(pieces)
    width = contexts.shape[1]
    rows, cols = pieces[0].shape
    return pl.pallas_call(
        functools.partial(weight_kernel, n_dp, n_piece),
        out_shape=jax.ShapeDtypeStruct((n_piece * cols, width), F32),
        in_specs=[SMEM] + [VMEM] * (2 + n_dp) + [ANY] * (1 + n_piece),
        out_specs=ANY,
        scratch_shapes=[
            pltpu.VMEM(contexts.shape, BF16),
            pltpu.VMEM((n_piece, rows, cols), BF16),
            pltpu.VMEM((2, cols, width), F32),
            pltpu.SemaphoreType.DMA((n_dp,)),
            pltpu.SemaphoreType.DMA((n_piece,)),
            pltpu.SemaphoreType.DMA((2,)),
        ],
        compiler_params=params(60),
        name="weight_grad",
    )(pos, gw_col, va, *bs, contexts, *pieces)


def step_kernel(cfg, pos_ref, *refs):
    refs = list(refs)
    take = lambda n=1: [refs.pop(0) for _ in range(n)]
    sems, columns = refs.pop(), refs.pop()
    col, mid = pos_ref[1], pos_ref[2] == 1
    begins, rounds, n_blk = cfg["begins"], cfg["rounds"], cfg["n_blk"]
    if begins is not None or rounds is not None:
        (weight,) = take()
    starts = ([] if rounds is None else rounds["starts"]) + ([] if begins is None else [begins[1]])
    fetch = [
        pltpu.make_async_copy(weight.at[:, pl.ds(at, CW)], columns.at[k], sems.at[k])
        for k, at in enumerate(starts)
    ]
    for copy in fetch:
        copy.start()
    if begins is not None:
        context, resid = take(2)
    parts = take(2) if cfg["joins"] else None
    halves = take(2) if cfg["totals"] else None
    if rounds is not None:
        sent, got, gains = take(n_blk), take(n_blk), take(n_blk)
        before = None if rounds["first"] else take(3)
    take(cfg["ties"])
    part_new = total = None
    if begins is not None:
        fetch[-1].wait()
        part_new = jnp.dot(context[...], columns[len(starts) - 1], preferred_element_type=F32)
        own = jnp.where(col == begins[0], resid[:, cfg["resid"]].astype(F32), 0.0)
        part_new = (part_new + own).astype(BF16)
        take()[0][...] = part_new
    if parts is not None:
        a, b = parts
        take()[0][...] = (a[...].astype(F32) + b[...].astype(F32)).astype(BF16)
    if halves is not None:
        a, b = halves
        total = (a[...].astype(F32) + b[...].astype(F32)).astype(BF16)
        take()[0][...] = total if part_new is None else jnp.where(mid, total, part_new)
    if rounds is not None:
        for copy in fetch[:n_blk]:
            copy.wait()
        weights = [columns[j] for j in range(n_blk)]
        row_round(rounds["first"], mid, col, weights, sent, got, gains, before, *take(5))


def line_sum(context, resid_of, out_weight, gw_row, pos, after_first, round_done):
    edge = [(0, 1), (1, 0), (2, 3), (3, 2)]
    middle = [(1, 2), (2, 1)]
    width = context.shape[1]
    depth = out_weight.shape[0]
    per_block = width // CW
    blocks = (1, 2, 0, 3)
    n_blk = len(blocks)
    order = [(j, r) for r in range(per_block) for j in blocks]
    n = len(order)
    shape = jax.ShapeDtypeStruct
    piece, column = shape((CAPB, CW), BF16), shape((CAPB, 1), F32)
    parts, joined, from_edge, from_mid, payloads = {}, {}, {}, {}, {}
    state = tie = None
    for s in range(-2, n + 4):
        begins, joins, totals = s + 2 < n, 0 <= s < n, 2 <= s < n + 2
        ends_round = s >= 4 and (s - 4) % n_blk == n_blk - 1
        if not (begins or joins or totals or ends_round):
            continue
        cfg = {"begins": None, "joins": joins, "totals": totals, "rounds": None}
        cfg |= {"n_blk": n_blk, "ties": 0, "resid": None}
        ins, args, outs = [SMEM], [pos], {}
        if begins or ends_round:
            ins.append(ANY)
            args.append(out_weight)
        if begins:
            j, r = order[s + 2]
            resid, at = resid_of(r)
            cfg["begins"] = (j, j * width + r * CW)
            cfg["resid"] = slice(at * CW, (at + 1) * CW)
            args += [context, resid]
            outs["part"] = piece
        if joins:
            args += [parts[s], from_edge[s]]
            outs["joined"] = piece
        if totals:
            args += [joined[s - 2], from_mid[s - 2]]
            outs["payload"] = piece
        if ends_round:
            r = order[s - 4][1]
            at = [s - n_blk + 1 + blocks.index(j) for j in range(n_blk)]
            starts = [j * width + r * CW for j in range(n_blk)]
            cfg["rounds"] = {"starts": starts, "first": state is None}
            args += [payloads[k] for k in at] + [from_edge[k] for k in at]
            args += [gw_row[:, lo : lo + CW] for lo in starts]
            args += [] if state is None else state
            outs |= {"acc": shape((CAPB, depth), F32), "sq": column, "vd": column}
            outs |= {"own": piece, "pays": shape((n_blk, CAPB, CW), BF16)}
        ins += [VMEM] * (len(args) - len(ins))
        if tie is not None:
            cfg["ties"] = 1
            ins.append(ANY)
            args.append(tie)
        made = pl.pallas_call(
            functools.partial(step_kernel, cfg),
            out_shape=tuple(outs.values()),
            in_specs=ins,
            out_specs=(VMEM,) * len(outs),
            scratch_shapes=[
                pltpu.VMEM((n_blk + 1, depth, CW), BF16),
                pltpu.SemaphoreType.DMA((n_blk + 1,)),
            ],
            compiler_params=params(52),
            cost_estimate=pl.CostEstimate(flops=0, bytes_accessed=0, transcendentals=0),
            name="row_step" if ends_round else "line_step",
        )(*args)
        made = dict(zip(outs, made))
        tie = next(iter(made.values()))
        if begins:
            parts[s + 2] = made["part"]
        if begins or totals:
            payloads[s + 2] = made.get("payload", made.get("part"))
            from_edge[s + 2] = lax.ppermute(payloads[s + 2], "tensor", edge)
        if joins:
            joined[s] = made["joined"]
            from_mid[s] = lax.ppermute(joined[s], "tensor", middle)
        if s == 0:
            after_first(joined[s])
        if ends_round:
            state = [made["acc"], made["sq"], made["vd"]]
            round_done(made["own"], made["pays"])
    return state


def butterfly(value, n_dp):
    step = 1
    while step < n_dp:
        value = value + xor_move(value, step, n_dp)
        step *= 2
    return value


def on_device(
    query_states,
    key_states,
    value_states,
    residual,
    returns,
    lengths,
    balance_list,
    out_weight,
    norm_gain,
    value_weight,
):
    n_dp, n_tensor = lax.axis_size("dp"), lax.axis_size("tensor")
    me, col = lax.axis_index("dp"), lax.axis_index("tensor")
    per_dev = query_states.shape[0]
    width = query_states.shape[2]
    model_width = out_weight.shape[1]
    kv = key_states.shape[2] // HD

    seq_len = query_states.shape[1]
    cap = per_dev // n_dp
    qkv = width + 2 * kv * HD
    first = CW if width > CW else width
    pick, start, size = route(me.reshape(1), lengths, balance_list, n_dp, per_dev)
    sent = gather_rollouts(
        pick,
        (query_states, key_states, value_states, residual),
        ((0, width), (0, kv * HD), (0, kv * HD), (0, first)),
        returns,
        n_dp,
    )
    blocks = exchange(sent, n_dp)
    rest = exchange(
        gather_rollouts(pick, (residual,), ((first, width),), None, n_dp), n_dp
    )
    gw_own = norm_gain * value_weight
    gw = lax.all_gather(gw_own, "tensor", axis=0, tiled=True)
    gw_high = gw.astype(BF16)
    gw_low = (gw - gw_high.astype(F32)).astype(BF16)
    pair = jnp.stack([gw_high, gw_low])
    wgw = jnp.sum(mm(pair, out_weight, ((1,), (1,))), axis=0, keepdims=True)
    context, probs = attention_forward(start, size, blocks, kv, seq_len, cap, (wgw,))
    resid_first, target = pack(start, size, blocks, seq_len, cap, (qkv, qkv + first), None)
    block = model_width // n_dp
    gw_col = lax.dynamic_slice_in_dim(gw, me * block, block).reshape(block, 1)

    is_mid = (col == 1) | (col == 2)
    pos = jnp.stack([me, col, is_mid.astype(jnp.int32)]).astype(jnp.int32)
    if n_tensor == 4 and n_dp == 4:
        later = {}

        def after_first(tie):
            later["resid"], later["context"] = pack(
                start, size, rest, seq_len, cap, (0, width - first), context, (tie,)
            )

        own, pieces = [], []

        def round_done(mine, pays):
            own.append(mine)
            moved = lax.all_to_all(pays, "dp", split_axis=0, concat_axis=0, tiled=True)
            pieces.append(moved.reshape(n_dp * CAPB, CW))

        acc, sq, vd = line_sum(
            context,
            lambda r: (resid_first, 0) if r == 0 else (later["resid"], r - 1),
            out_weight,
            gw.reshape(1, model_width),
            pos,
            after_first,
            round_done,
        )
        contexts = lax.all_gather(later["context"], "dp", axis=0, tiled=True)
    else:
        resid_rest, _ = pack(start, size, rest, seq_len, cap, (0, width - first), context)
        contexts = lax.all_gather(context, "dp", axis=0, tiled=True)
        resid = jnp.concatenate([resid_first, resid_rest], axis=1)
        part = jnp.dot(context, out_weight, preferred_element_type=F32)
        mine = lax.dynamic_slice_in_dim(part, col * width, width, axis=1) + resid.astype(F32)
        part = lax.dynamic_update_slice_in_dim(part, mine, col * width, axis=1)
        hidden = lax.psum(part.astype(BF16), "tensor")
        wide = hidden.astype(F32)
        sq = jnp.sum(wide * wide, axis=1, keepdims=True)
        vd = jnp.sum(wide * gw[None, :], axis=1, keepdims=True)
        acc = mm(hidden, out_weight, ((1,), (1,)))
        own = [lax.dynamic_slice_in_dim(hidden, col * width, width, axis=1)]
        pieces = [lax.all_to_all(hidden, "dp", split_axis=1, concat_axis=0, tiled=True)]

    resid_out, sums, b_row, critic_row, a, b = finish(
        sq, vd, target, gw_own.reshape(1, width), context, own, model_width
    )
    bs = [b_row] + [xor_move(b_row, d, n_dp) for d in range(1, n_dp)]
    sums = butterfly(sums, n_dp)
    query_out, key_out, value_out = attention_backward(
        start, size, a, b, wgw, acc, probs, blocks, kv, seq_len, cap
    )
    weight_out = weight_grad(pos, gw_col, sums[1:2], bs, contexts, pieces)
    gain_sum = sums[0]
    return (
        critic_row.reshape(CAPB).astype(BF16),
        query_out,
        key_out,
        value_out,
        resid_out,
        weight_out,
        value_weight * gain_sum,
        norm_gain * gain_sum,
    )


def solution(mesh):
    rows = P(("groups", "dp"), None, "tensor")
    packed = P(("groups", "dp"), "tensor")
    placed = (rows, rows, rows, rows, P(("groups", "dp"), None), P("groups"), P("groups"))
    placed += (P("tensor", None), P("tensor"), P("tensor"))
    return jax.shard_map(
        on_device,
        mesh=mesh,
        in_specs=placed,
        out_specs=(
            P(("groups", "dp")),
            packed,
            packed,
            packed,
            packed,
            packed,
            P(("groups", "tensor")),
            P(("groups", "tensor")),
        ),
        check_vma=False,
    )
```

```python
import functools
import math

import jax
import jax.numpy as jnp
from jax import lax
from jax.experimental import pallas as pl
from jax.experimental.pallas import tpu as pltpu
from jax.sharding import PartitionSpec as P

H = 40
KVH = 8
HD = 128
RATIO = H // KVH
CAPB = 576
EPS = 1e-06
NEG = -1e30
CW = 256
TAIL = 16
F32 = jnp.float32
BF16 = jnp.bfloat16
VMEM = pl.BlockSpec(memory_space=pltpu.VMEM)
SMEM = pl.BlockSpec(memory_space=pltpu.SMEM)
ANY = pl.BlockSpec(memory_space=pl.ANY)
HBM = pl.BlockSpec(memory_space=pltpu.HBM)


def params(mib):
    return pltpu.CompilerParams(vmem_limit_bytes=mib * 1024 * 1024)


def mm(a, b, dims):
    return lax.dot_general(a, b, (dims, ((), ())), preferred_element_type=F32)


def route_kernel(n_dp, per_dev, me_ref, len_ref, bal_ref, pick_ref, start_ref, size_ref, cnt_ref):
    cap = per_dev // n_dp
    me = me_ref[0]
    for d in range(n_dp):
        target = jnp.bitwise_xor(me, d)

        def outgoing(s, count):
            b = bal_ref[target * per_dev + s]
            home = lax.div(b, per_dev)

            @pl.when(home == me)
            def _():
                pick_ref[d * cap + count] = lax.rem(b, per_dev)

            return count + (home == me).astype(jnp.int32)

        lax.fori_loop(0, per_dev, outgoing, jnp.int32(0))
        cnt_ref[d] = jnp.int32(0)

    def incoming(s, run):
        b = bal_ref[me * per_dev + s]
        d = jnp.bitwise_xor(lax.div(b, per_dev), me)
        count = cnt_ref[d]
        size = len_ref[b]
        start_ref[d * cap + count] = run
        size_ref[d * cap + count] = size
        cnt_ref[d] = count + 1
        return run + size

    lax.fori_loop(0, per_dev, incoming, jnp.int32(0))


def route(me, lengths, balance_list, n_dp, per_dev):
    table = jax.ShapeDtypeStruct((per_dev,), jnp.int32)
    return pl.pallas_call(
        functools.partial(route_kernel, n_dp, per_dev),
        out_shape=(table, table, table),
        in_specs=[SMEM] * 3,
        out_specs=(SMEM, SMEM, SMEM),
        scratch_shapes=[pltpu.SMEM((n_dp,), jnp.int32)],
        name="route",
    )(me, lengths, balance_list)


def gather_kernel(n_dp, cap, seq_len, spans, pick_ref, *refs):
    parts = refs[: len(spans)]
    returns = refs[len(spans)] if len(refs) > len(spans) + n_dp + 1 else None
    outs, sems = refs[-n_dp - 1 : -1], refs[-1]
    copies = []
    for d in range(n_dp):
        for i in range(cap):
            row = pick_ref[d * cap + i]
            col = 0
            for p, (part, (lo, hi)) in enumerate(zip(parts, spans)):
                rows = pl.ds(i * seq_len, seq_len)
                copies.append(
                    pltpu.make_async_copy(
                        part.at[row, :, pl.ds(lo, hi - lo)],
                        outs[d].at[rows, pl.ds(col, hi - lo)],
                        sems.at[d * cap + i, p],
                    )
                )
                copies[-1].start()
                col += hi - lo
    for d in range(n_dp):
        if returns is not None:
            rows = returns[...].astype(F32)
            at = lax.broadcasted_iota(jnp.int32, rows.shape, 0)
            picked = [
                jnp.sum(jnp.where(at == pick_ref[d * cap + i], rows, 0.0), axis=0, keepdims=True)
                for i in range(cap)
            ]
            picked += [jnp.zeros((TAIL - cap, seq_len), F32)]
            outs[d][cap * seq_len :, :seq_len] = jnp.concatenate(picked, axis=0).astype(BF16)
            outs[d][cap * seq_len :, seq_len:] = jnp.zeros(
                (TAIL, outs[d].shape[1] - seq_len), BF16
            )
    for copy in copies:
        copy.wait()


def gather_rollouts(pick, parts, spans, returns, n_dp):
    per_dev, seq_len = parts[0].shape[:2]
    cap = per_dev // n_dp
    rows = cap * seq_len + (TAIL if returns is not None else 0)
    out = jax.ShapeDtypeStruct((rows, sum(hi - lo for lo, hi in spans)), BF16)
    extra = [] if returns is None else [returns]
    return pl.pallas_call(
        functools.partial(gather_kernel, n_dp, cap, seq_len, spans),
        out_shape=(out,) * n_dp,
        in_specs=[SMEM] + [ANY] * len(parts) + [VMEM] * len(extra),
        out_specs=(VMEM,) * n_dp,
        scratch_shapes=[pltpu.SemaphoreType.DMA((n_dp * cap, len(parts)))],
        compiler_params=params(60),
        name="gather_rollouts",
    )(pick, *parts, *extra)


def xor_move(value, d, n_dp):
    return lax.ppermute(value, "dp", [(i, i ^ d) for i in range(n_dp)])


def exchange(blocks, n_dp):
    order = sorted(range(1, n_dp), key=lambda d: d < 2)
    moved = {d: xor_move(blocks[d], d, n_dp) for d in order}
    return [blocks[0]] + [moved[d] for d in range(1, n_dp)]


def window(start, size, seq_len):
    tall = seq_len + 8
    base = pl.multiple_of(lax.div(start, 8) * 8, 8)
    shift = start - base
    fill = lambda shape, axis: lax.broadcasted_iota(jnp.int32, shape, axis)
    place = (fill((tall, seq_len), 0) - shift == fill((tall, seq_len), 1)) & (
        fill((tall, seq_len), 1) < size
    )
    fetch = (fill((seq_len, tall), 1) - shift == fill((seq_len, tall), 0)) & (
        fill((seq_len, tall), 0) < size
    )
    return pl.ds(base, tall), place.astype(BF16), fetch.astype(BF16)


def pack_kernel(n_dp, cap, seq_len, start_ref, size_ref, ctx_ref, *refs):
    blocks = refs[:n_dp]
    out, target, ctx_copy, room = refs[-4:]
    room[...] = jnp.zeros_like(room)
    target[...] = jnp.zeros_like(target)
    ctx_copy[...] = ctx_ref[...]
    for d in range(n_dp):
        for i in range(cap):
            spot, place, _ = window(start_ref[d * cap + i], size_ref[d * cap + i], seq_len)
            room[spot, :] += mm(place, blocks[d][i * seq_len : (i + 1) * seq_len, :], ((1,), (0,)))
            at = cap * seq_len
            row = blocks[d][at : at + TAIL, :seq_len].astype(F32)[i : i + 1, :]
            target[spot, :] += jnp.sum(place.astype(F32) * row, axis=1, keepdims=True)
    out[...] = room[:CAPB, :].astype(BF16)


def pack(start, size, blocks, seq_len, cap, context, tie=()):
    n_dp = len(blocks)
    width = blocks[0].shape[1]
    tall = CAPB + seq_len
    return pl.pallas_call(
        functools.partial(pack_kernel, n_dp, cap, seq_len),
        out_shape=(
            jax.ShapeDtypeStruct((CAPB, width), BF16),
            jax.ShapeDtypeStruct((tall, 1), F32),
            jax.ShapeDtypeStruct(context.shape, BF16),
        ),
        in_specs=[SMEM, SMEM] + [VMEM] * (n_dp + 1) + [ANY] * len(tie),
        out_specs=(VMEM,) * 3,
        scratch_shapes=[pltpu.VMEM((tall, width), F32)],
        compiler_params=params(20),
        name="pack",
    )(start, size, context, *blocks, *tie)


def heads_of(rows, first):
    return jnp.concatenate(
        [rows[:, (first + r) * HD : (first + r + 1) * HD] for r in range(RATIO)], axis=0
    )


def forward_kernel(first, count, cap, seq_len, kv, start_ref, size_ref, *refs):
    blocks = refs[:count]
    if first == 0:
        probs_ref, room = refs[-2:]
    else:
        out, extra, probs_ref, room = refs[-4:]
    qw = kv * RATIO * HD
    scale = 1.0 / math.sqrt(HD)
    span = RATIO * seq_len
    room[...] = jnp.zeros_like(room) if first == 0 else refs[count][...]
    at_u = lax.broadcasted_iota(jnp.int32, (seq_len, span), 0)
    at_t = lax.rem(lax.broadcasted_iota(jnp.int32, (seq_len, span), 1), seq_len)
    at_t1 = lax.rem(lax.broadcasted_iota(jnp.int32, (1, span), 1), seq_len)
    causal = at_u <= at_t
    for d in range(count):

        def step(i, _):
            size = size_ref[(first + d) * cap + i]
            spot, place, _ = window(start_ref[(first + d) * cap + i], size, seq_len)
            rows_i = pl.ds(pl.multiple_of(i * seq_len, seq_len), seq_len)
            keep = causal & (at_u < size)
            parts = []
            for g in range(kv):
                queries = heads_of(blocks[d][rows_i, g * RATIO * HD : (g + 1) * RATIO * HD], 0)
                keys = blocks[d][rows_i, qw + g * HD : qw + (g + 1) * HD]
                values = blocks[d][rows_i, qw + (kv + g) * HD : qw + (kv + g + 1) * HD]
                scores = jnp.where(keep, mm(keys, queries, ((1,), (1,))) * scale, NEG)
                top = jnp.max(scores, axis=0, keepdims=True)
                weights = jnp.exp(scores - top)
                total = jnp.sum(weights, axis=0, keepdims=True)
                probs = (weights * jnp.where(at_t1 < size, 1.0 / total, 0.0)).astype(BF16)
                probs_ref[d * cap + i, g] = probs
                mixed = mm(probs, values, ((0,), (0,)))
                parts += [mixed[r * seq_len : (r + 1) * seq_len] for r in range(RATIO)]
            beside = blocks[d][rows_i, qw + 2 * kv * HD :]
            mixed = jnp.concatenate([jnp.concatenate(parts, axis=1).astype(BF16), beside], axis=1)
            room[spot, :] += mm(place, mixed, ((1,), (0,)))
            return 0

        lax.fori_loop(0, cap, step, 0)
    if first:
        out[...] = room[:CAPB, :qw].astype(BF16)
        extra[...] = room[:CAPB, qw:].astype(BF16)


def attention_forward(start, size, blocks, kv, seq_len, cap, ahead):
    n_dp = len(blocks)
    half = n_dp // 2
    width = kv * RATIO * HD
    extra = blocks[0].shape[1] - width - 2 * kv * HD
    tall = CAPB + seq_len
    shape = jax.ShapeDtypeStruct
    probs = shape((half * cap, kv, seq_len, RATIO * seq_len), BF16)
    call = lambda first, outs, scratch, before: pl.pallas_call(
        functools.partial(forward_kernel, first, half, cap, seq_len, kv),
        out_shape=outs,
        in_specs=[SMEM, SMEM] + [VMEM] * (half + (first > 0)) + [ANY] * (len(before) - (first > 0)),
        out_specs=(VMEM,) * len(outs),
        scratch_shapes=scratch,
        compiler_params=params(20),
        name="attention_forward",
    )(start, size, *blocks[first : first + half], *before)
    probs_low, room = call(0, (probs, shape((tall, width + extra), F32)), [], ahead)
    context, beside, probs_high = call(
        half,
        (shape((CAPB, width), BF16), shape((CAPB, extra), BF16), probs),
        [pltpu.VMEM((tall, width + extra), F32)],
        (room,),
    )
    return context, beside, (probs_low, probs_high)


def backward_kernel(
    n_dp, cap, seq_len, kv, start_ref, size_ref, a_ref, b_ref, wgw_ref, acc_ref, *refs
):
    all_probs, refs = refs[:2], refs[2:]
    blocks = refs[:n_dp]
    dq_out, dk_out, dv_out = refs[n_dp : n_dp + 3]
    grads, dq_room, dk_room, dv_room = refs[n_dp + 3 :]
    qw = kv * RATIO * HD
    scale = 1.0 / math.sqrt(HD)
    half = n_dp // 2
    for room in (dq_room, dk_room, dv_room):
        room[...] = jnp.zeros_like(room)
    grads[:CAPB, :] = a_ref[...] * wgw_ref[...] - b_ref[...] * acc_ref[...]
    grads[CAPB:, :] = jnp.zeros((seq_len, qw), F32)
    lanes = 2 if cap % 2 == 0 else 1

    def rollout(d, i):
        spot, place, fetch = window(start_ref[d * cap + i], size_ref[d * cap + i], seq_len)
        mine = mm(fetch, grads[spot, :].astype(BF16), ((1,), (0,))).astype(BF16)
        rows_i = pl.ds(pl.multiple_of(i * seq_len, seq_len), seq_len)
        dq_parts, dk_parts, dv_parts = [], [], []
        for g in range(kv):
            cols = slice(g * RATIO * HD, (g + 1) * RATIO * HD)
            queries = heads_of(blocks[d][rows_i, cols], 0)
            keys = blocks[d][rows_i, qw + g * HD : qw + (g + 1) * HD]
            values = blocks[d][rows_i, qw + (kv + g) * HD : qw + (kv + g + 1) * HD]
            out_grad = heads_of(mine[:, cols], 0)
            probs_low = all_probs[d // half][d % half * cap + i, g]
            probs = probs_low.astype(F32)
            prob_grad = mm(values, out_grad, ((1,), (1,)))
            row_dot = jnp.sum(probs * prob_grad, axis=0, keepdims=True)
            score_grad = (probs * (prob_grad - row_dot) * scale).astype(BF16)
            dq = mm(score_grad, keys, ((0,), (0,)))
            dq_parts += [dq[r * seq_len : (r + 1) * seq_len] for r in range(RATIO)]
            dk_parts.append(mm(score_grad, queries, ((1,), (0,))))
            dv_parts.append(mm(probs_low, out_grad, ((1,), (0,))))
        wide = [jnp.concatenate(parts, axis=1).astype(BF16) for parts in (dq_parts, dk_parts, dv_parts)]
        return spot, [mm(place, rows, ((1,), (0,))) for rows in wide]

    for d in range(n_dp):

        def step(i, _):
            for spot, moved in [rollout(d, i * lanes + k) for k in range(lanes)]:
                for room, rows in zip((dq_room, dk_room, dv_room), moved):
                    room[spot, :] += rows
            return 0

        lax.fori_loop(0, cap // lanes, step, 0)
    dq_out[...] = dq_room[:CAPB, :].astype(BF16)
    dk_out[...] = dk_room[:CAPB, :].astype(BF16)
    dv_out[...] = dv_room[:CAPB, :].astype(BF16)


def attention_backward(start, size, a, b, wgw, acc, probs, blocks, kv, seq_len, cap):
    n_dp = len(blocks)
    qw, kw = kv * RATIO * HD, kv * HD
    tall = CAPB + seq_len
    return pl.pallas_call(
        functools.partial(backward_kernel, n_dp, cap, seq_len, kv),
        out_shape=tuple(jax.ShapeDtypeStruct((CAPB, w), BF16) for w in (qw, kw, kw)),
        in_specs=[SMEM, SMEM] + [VMEM] * (6 + n_dp),
        out_specs=(VMEM,) * 3,
        scratch_shapes=[pltpu.VMEM((tall, w), F32) for w in (qw, qw, kw, kw)],
        compiler_params=params(60),
        name="attention_backward",
    )(start, size, a, b, wgw, acc, *probs, *blocks)


def select(index, options):
    out = options[0]
    for k in range(1, len(options)):
        out = jnp.where(index == k, options[k], out)
    return out


def rows_kernel(blocks, starts, spans, first, pos_ref, weight, gw_ref, *refs):
    n_blk, n_bundle = len(blocks), len(spans)
    bundles, refs = refs[:n_bundle], refs[n_bundle:]
    before, refs = (None, refs) if first else (refs[:3], refs[3:])
    acc, sq, vd, own, columns, sems = refs[-6:]
    col = pos_ref[1]
    fetch = [
        pltpu.make_async_copy(
            weight.at[:, pl.ds(at, hi - lo)], columns.at[j, :, pl.ds(lo, hi - lo)], sems.at[j, k]
        )
        for k, (lo, hi) in enumerate(spans)
        for j, at in enumerate(starts[k])
    ]
    for copy in fetch:
        copy.start()
    tile = CAPB // 3
    for k, (lo, hi) in enumerate(spans):
        for t in range(CAPB // tile):
            rows = slice(t * tile, (t + 1) * tile)
            pieces = [bundles[k][j, rows, :] for j in range(n_blk)]
            own[rows, lo:hi] = select(col, pieces)
            fresh = first and k == 0
            squares = 0.0 if fresh else (before[1] if k == 0 else sq)[rows, :]
            dots = 0.0 if fresh else (before[2] if k == 0 else vd)[rows, :]
            for j, piece in enumerate(pieces):
                wide = piece.astype(F32)
                at = starts[k][j]
                squares = squares + jnp.sum(wide * wide, axis=1, keepdims=True)
                dots = dots + jnp.sum(wide * gw_ref[:, at : at + hi - lo], axis=1, keepdims=True)
            sq[rows, :] = squares
            vd[rows, :] = dots
    for k, (lo, hi) in enumerate(spans):
        for copy in fetch[k * n_blk : (k + 1) * n_blk]:
            copy.wait()
        for t in range(CAPB // tile):
            rows = slice(t * tile, (t + 1) * tile)
            total = None if first and k == 0 else (before[0] if k == 0 else acc)[rows, :]
            for j in range(n_blk):
                term = mm(bundles[k][j, rows, :], columns[j, :, lo:hi], ((1,), (1,)))
                total = term if total is None else total + term
            acc[rows, :] = total


def row_products(pos, out_weight, gw_row, bundles, first_col, width, state, tie):
    n_blk = bundles[0].shape[0]
    depth = out_weight.shape[0]
    spans, starts, at = [], [], 0
    for bundle in bundles:
        spans.append((at, at + bundle.shape[2]))
        starts.append([j * width + first_col + at for j in range(n_blk)])
        at += bundle.shape[2]
    shape = jax.ShapeDtypeStruct
    column = shape((CAPB, 1), F32)
    before = [] if state is None else list(state)
    return pl.pallas_call(
        functools.partial(rows_kernel, tuple(range(n_blk)), starts, spans, state is None),
        out_shape=(shape((CAPB, depth), F32), column, column, shape((CAPB, at), BF16)),
        in_specs=[SMEM, ANY] + [VMEM] * (1 + len(bundles) + len(before)) + [ANY] * len(tie),
        out_specs=(VMEM,) * 4,
        scratch_shapes=[
            pltpu.VMEM((n_blk, depth, at), BF16),
            pltpu.SemaphoreType.DMA((n_blk, len(bundles))),
        ],
        compiler_params=params(56),
        cost_estimate=pl.CostEstimate(flops=0, bytes_accessed=0, transcendentals=0),
        name="row_products",
    )(pos, out_weight, gw_row, *bundles, *before, *tie)


def row_of(column):
    return jnp.transpose(jnp.broadcast_to(column, (column.shape[0], 128)))[0:1, :]


def column_of(row):
    return jnp.transpose(jnp.broadcast_to(row, (128, row.shape[1])))[:, 0:1]


def finish_kernel(n_piece, model_width, sq_ref, vd_ref, target_ref, gw_ref, ctx_ref, *refs):
    pieces = refs[:n_piece]
    out, sums, b_row, critic_row, a_col, b_col = refs[n_piece:]
    inv_rms = lax.rsqrt(sq_ref[...] / model_width + EPS)
    critic = inv_rms * vd_ref[...]
    err = critic - target_ref[:CAPB, :]
    a = inv_rms * err
    b = inv_rms * inv_rms * inv_rms * err * vd_ref[...] / model_width
    a_col[...] = a
    b_col[...] = b
    b_row[...] = row_of(b)
    critic_row[...] = row_of(critic)
    at = 0
    for k in range(n_piece):
        cols = slice(at, at + pieces[k].shape[1])
        at += pieces[k].shape[1]
        hidden = pieces[k][...].astype(F32)
        out[:, cols] = (a * gw_ref[:, cols] - b * hidden).astype(BF16)
        sums[0:1, cols] = jnp.sum(a * hidden, axis=0, keepdims=True)
    sums[1:2, :] = jnp.sum(a * ctx_ref[...].astype(F32), axis=0, keepdims=True)


def finish(sq, vd, target, gw_own, context, pieces, model_width):
    width = context.shape[1]
    return pl.pallas_call(
        functools.partial(finish_kernel, len(pieces), model_width),
        out_shape=(
            jax.ShapeDtypeStruct((CAPB, width), BF16),
            jax.ShapeDtypeStruct((2, width), F32),
            jax.ShapeDtypeStruct((1, CAPB), F32),
            jax.ShapeDtypeStruct((1, CAPB), F32),
            jax.ShapeDtypeStruct((CAPB, 1), F32),
            jax.ShapeDtypeStruct((CAPB, 1), F32),
        ),
        in_specs=[VMEM] * (5 + len(pieces)),
        out_specs=(VMEM,) * 6,
        compiler_params=params(32),
        name="finish",
    )(sq, vd, target, gw_own, context, *pieces)


def weight_kernel(n_dp, spans, pos_ref, gw_ref, va_ref, *refs):
    n_piece = len(spans)
    bs, (ctx_hbm,), pieces = refs[:n_dp], refs[n_dp : n_dp + 1], refs[n_dp + 1 : n_dp + 1 + n_piece]
    out, ctx, held, made, ctx_sems, in_sems, out_sems = refs[n_dp + 1 + n_piece :]
    me = pos_ref[0]
    rows_of = lambda d: pl.ds(pl.multiple_of(jnp.bitwise_xor(me, d) * CAPB, CAPB), CAPB)
    ctx_in = [
        pltpu.make_async_copy(ctx_hbm.at[rows_of(d)], ctx.at[rows_of(d)], ctx_sems.at[d])
        for d in range(n_dp)
    ]
    piece_in = [
        pltpu.make_async_copy(pieces[r], held.at[:, pl.ds(lo, hi - lo)], in_sems.at[r])
        for r, (lo, hi) in enumerate(spans)
    ]
    for copy in ctx_in + piece_in:
        copy.start()
    for d in range(n_dp):
        ctx_in[d].wait()
        factor = column_of(bs[d][...])
        rows = rows_of(d)
        ctx[rows, :] = (factor * ctx[rows, :].astype(F32)).astype(BF16)
    store, arrived = [], 0
    step = made.shape[1]
    for t in range(spans[-1][1] // step):
        lo, hi = t * step, (t + 1) * step
        while arrived < n_piece and spans[arrived][0] < hi:
            piece_in[arrived].wait()
            arrived += 1
        if t >= 2:
            store[t - 2].wait()
        rank_one = gw_ref[lo:hi, :] * va_ref[...]
        made[t % 2] = rank_one - mm(held[:, lo:hi], ctx[...], ((0,), (0,)))
        store.append(
            pltpu.make_async_copy(made.at[t % 2], out.at[pl.ds(lo, step)], out_sems.at[t % 2])
        )
        store[t].start()
    for copy in store[-2:]:
        copy.wait()


def weight_grad(pos, gw_col, va, bs, contexts, pieces):
    n_dp = len(bs)
    width = contexts.shape[1]
    rows = pieces[0].shape[0]
    spans, at = [], 0
    for piece in pieces:
        spans.append((at, at + piece.shape[1]))
        at += piece.shape[1]
    step = CW if at % CW == 0 else at
    return pl.pallas_call(
        functools.partial(weight_kernel, n_dp, spans),
        out_shape=jax.ShapeDtypeStruct((at, width), F32),
        in_specs=[SMEM] + [VMEM] * (2 + n_dp) + [ANY] * (1 + len(pieces)),
        out_specs=ANY,
        scratch_shapes=[
            pltpu.VMEM(contexts.shape, BF16),
            pltpu.VMEM((rows, at), BF16),
            pltpu.VMEM((2, step, width), F32),
            pltpu.SemaphoreType.DMA((n_dp,)),
            pltpu.SemaphoreType.DMA((len(pieces),)),
            pltpu.SemaphoreType.DMA((2,)),
        ],
        compiler_params=params(60),
        name="weight_grad",
    )(pos, gw_col, va, *bs, contexts, *pieces)


def parts_kernel(chunks, resid_cols, pos_ref, context, weight, resid, *refs):
    outs, columns, sems = refs[-len(chunks) - 2 : -2], refs[-2], refs[-1]
    fetch = [
        pltpu.make_async_copy(weight.at[:, pl.ds(at, CW)], columns.at[k], sems.at[k])
        for k, (_, at) in enumerate(chunks)
    ]
    for copy in fetch:
        copy.start()
    for k, (j, _) in enumerate(chunks):
        fetch[k].wait()
        part = jnp.dot(context[...], columns[k], preferred_element_type=F32)
        own = jnp.where(pos_ref[1] == j, resid[:, resid_cols].astype(F32), 0.0)
        outs[k][...] = (part + own).astype(BF16)


def partial_sums(pos, context, out_weight, resid, at, chunks, tie):
    piece = jax.ShapeDtypeStruct((CAPB, CW), BF16)
    n = len(chunks)
    return pl.pallas_call(
        functools.partial(parts_kernel, chunks, slice(at * CW, (at + 1) * CW)),
        out_shape=(piece,) * n,
        in_specs=[SMEM, VMEM, ANY, VMEM] + [ANY] * len(tie),
        out_specs=(VMEM,) * n,
        scratch_shapes=[
            pltpu.VMEM((n, out_weight.shape[0], CW), BF16),
            pltpu.SemaphoreType.DMA((n,)),
        ],
        compiler_params=params(52),
        cost_estimate=pl.CostEstimate(flops=0, bytes_accessed=0, transcendentals=0),
        name="partial_sums",
    )(pos, context, out_weight, resid, *tie)


def step_kernel(part, joins, totals, ends, n_tie, pos_ref, *refs):
    refs = list(refs)
    take = lambda n=1: [refs.pop(0) for _ in range(n)]
    mid = pos_ref[2] == 1
    add = lambda a, b: (a[...].astype(F32) + b[...].astype(F32)).astype(BF16)
    (new,) = take() if part else (None,)
    pair = take(2) if joins else None
    halves = take(2) if totals else None
    last = take(2) if ends else None
    take(n_tie)
    if joins:
        take()[0][...] = add(*pair)
    if totals:
        total = add(*halves)
        take()[0][...] = total if new is None else jnp.where(mid, total, new[...])
    if ends:
        take()[0][...] = jnp.where(mid, last[0][...], last[1][...])


def line_sum(context, resid_of, out_weight, pos, after_first, chunk_done):
    edge = [(0, 1), (1, 0), (2, 3), (3, 2)]
    middle = [(1, 2), (2, 1)]
    width = context.shape[1]
    per_block = width // CW
    blocks = (1, 2, 0, 3)
    n_blk = len(blocks)
    order = [(j, r) for r in range(per_block) for j in blocks]
    n = len(order)
    piece = jax.ShapeDtypeStruct((CAPB, CW), BF16)
    parts, joined, from_edge, from_mid, payloads = {}, {}, {}, {}, {}

    def make_parts(first, count, tie):
        r = order[first][1]
        resid, at = resid_of(r)
        chunks = [(j, j * width + r * CW) for j, _ in order[first : first + count]]
        made = partial_sums(pos, context, out_weight, resid, at, chunks, tie)
        parts.update(zip(range(first, first + count), made))

    make_parts(0, 2, ())
    for s in (0, 1):
        payloads[s] = parts[s]
        from_edge[s] = lax.ppermute(parts[s], "tensor", edge)
    make_parts(2, 2, (parts[1],))
    tie = (parts[3],)
    for s in range(n + 4):
        joins, totals, ends = s < n, 2 <= s < n + 2, s >= 4
        part = totals and s + 2 < n
        outs, args = {}, [pos]
        if part:
            args.append(parts[s + 2])
        if joins:
            args += [parts[s], from_edge[s]]
            outs["joined"] = piece
        if totals:
            args += [joined[s - 2], from_mid[s - 2]]
            outs["payload"] = piece
        if ends:
            args += [payloads[s], from_edge[s]]
            outs["hidden"] = piece
        made = pl.pallas_call(
            functools.partial(step_kernel, part, joins, totals, ends, len(tie)),
            out_shape=tuple(outs.values()),
            in_specs=[SMEM] + [VMEM] * (len(args) - 1) + [ANY] * len(tie),
            out_specs=(VMEM,) * len(outs),
            compiler_params=params(16),
            cost_estimate=pl.CostEstimate(flops=0, bytes_accessed=0, transcendentals=0),
            name="line_step",
        )(*args, *tie)
        made = dict(zip(outs, made))
        tie = (next(iter(made.values())),)
        if joins:
            joined[s] = made["joined"]
            from_mid[s] = lax.ppermute(joined[s], "tensor", middle)
        if s + 2 < n + 4:
            payloads[s + 2] = made["payload"] if totals else parts[s + 2]
            from_edge[s + 2] = lax.ppermute(payloads[s + 2], "tensor", edge)
        if s == 0:
            after_first(tie)
        if s % n_blk == 0 and s + n_blk < n:
            make_parts(s + n_blk, n_blk, tie)
        if ends:
            chunk_done(order[s - 4], made["hidden"], s == n + 1, tie)


def butterfly(value, n_dp):
    step = 1
    while step < n_dp:
        value = value + xor_move(value, step, n_dp)
        step *= 2
    return value


def on_device(
    query_states,
    key_states,
    value_states,
    residual,
    returns,
    lengths,
    balance_list,
    out_weight,
    norm_gain,
    value_weight,
):
    n_dp, n_tensor = lax.axis_size("dp"), lax.axis_size("tensor")
    me, col = lax.axis_index("dp"), lax.axis_index("tensor")
    per_dev = query_states.shape[0]
    width = query_states.shape[2]
    model_width = out_weight.shape[1]
    kv = key_states.shape[2] // HD

    seq_len = query_states.shape[1]
    cap = per_dev // n_dp
    first = CW if width > CW else width
    pick, start, size = route(me.reshape(1), lengths, balance_list, n_dp, per_dev)
    sent = gather_rollouts(
        pick,
        (query_states, key_states, value_states, residual),
        ((0, width), (0, kv * HD), (0, kv * HD), (0, first)),
        None,
        n_dp,
    )
    blocks = exchange(sent, n_dp)
    rest = exchange(
        gather_rollouts(pick, (residual,), ((first, width),), returns, n_dp), n_dp
    )
    gw_own = norm_gain * value_weight
    gw = lax.all_gather(gw_own, "tensor", axis=0, tiled=True)
    gw_high = gw.astype(BF16)
    gw_low = (gw - gw_high.astype(F32)).astype(BF16)
    pair = jnp.stack([gw_high, gw_low])
    wgw = jnp.sum(mm(pair, out_weight, ((1,), (1,))), axis=0, keepdims=True)
    context, resid_first, probs = attention_forward(
        start, size, blocks, kv, seq_len, cap, (wgw,)
    )
    block = model_width // n_dp
    gw_col = lax.dynamic_slice_in_dim(gw, me * block, block).reshape(block, 1)

    is_mid = (col == 1) | (col == 2)
    pos = jnp.stack([me, col, is_mid.astype(jnp.int32)]).astype(jnp.int32)
    if n_tensor == 4 and n_dp == 4:
        per_block = width // CW
        later, hidden = {}, {}
        own, pieces, state = [], [], None
        gw_row = gw.reshape(1, model_width)

        def after_first(tie):
            later["resid"], later["target"], later["context"] = pack(
                start, size, rest, seq_len, cap, context, tie
            )

        def move(bundle):
            moved = lax.all_to_all(bundle, "dp", split_axis=0, concat_axis=0, tiled=True)
            pieces.append(moved.reshape(n_dp * CAPB, bundle.shape[2]))

        def bundle_of(rounds):
            return jnp.stack(
                [
                    jnp.concatenate([hidden[j, r] for r in rounds], axis=1)
                    for j in range(n_tensor)
                ]
            )

        groups = [(0, 1), (2, 3)] + [(r,) for r in range(4, per_block)]
        bundles = []

        def chunk_done(key, piece, draining, tie):
            nonlocal state
            hidden[key] = piece
            if len(bundles) < len(groups):
                rounds = groups[len(bundles)]
                if all((j, r) in hidden for j in range(n_tensor) for r in rounds):
                    bundles.append(bundle_of(rounds))
                    move(bundles[-1])
            if draining:
                *state, mine = row_products(
                    pos, out_weight, gw_row, bundles[:2], 0, width, None, tie
                )
                own.append(mine)

        line_sum(
            context,
            lambda r: (resid_first, 0) if r == 0 else (later["resid"], r - 1),
            out_weight,
            pos,
            after_first,
            chunk_done,
        )
        acc, sq, vd, mine = row_products(
            pos, out_weight, gw_row, bundles[2:], 4 * CW, width, state, ()
        )
        own.append(mine)
        target = later["target"]
        contexts = lax.all_gather(later["context"], "dp", axis=0, tiled=True)
    else:
        resid_rest, target, _ = pack(start, size, rest, seq_len, cap, context)
        contexts = lax.all_gather(context, "dp", axis=0, tiled=True)
        resid = jnp.concatenate([resid_first, resid_rest], axis=1)
        part = jnp.dot(context, out_weight, preferred_element_type=F32)
        mine = lax.dynamic_slice_in_dim(part, col * width, width, axis=1) + resid.astype(F32)
        part = lax.dynamic_update_slice_in_dim(part, mine, col * width, axis=1)
        hidden = lax.psum(part.astype(BF16), "tensor")
        wide = hidden.astype(F32)
        sq = jnp.sum(wide * wide, axis=1, keepdims=True)
        vd = jnp.sum(wide * gw[None, :], axis=1, keepdims=True)
        acc = mm(hidden, out_weight, ((1,), (1,)))
        own = [lax.dynamic_slice_in_dim(hidden, col * width, width, axis=1)]
        pieces = [lax.all_to_all(hidden, "dp", split_axis=1, concat_axis=0, tiled=True)]

    resid_out, sums, b_row, critic_row, a, b = finish(
        sq, vd, target, gw_own.reshape(1, width), context, own, model_width
    )
    bs = [b_row] + [xor_move(b_row, d, n_dp) for d in range(1, n_dp)]
    sums = butterfly(sums, n_dp)
    query_out, key_out, value_out = attention_backward(
        start, size, a, b, wgw, acc, probs, blocks, kv, seq_len, cap
    )
    weight_out = weight_grad(pos, gw_col, sums[1:2], bs, contexts, pieces)
    gain_sum = sums[0]
    return (
        critic_row.reshape(CAPB).astype(BF16),
        query_out,
        key_out,
        value_out,
        resid_out,
        weight_out,
        value_weight * gain_sum,
        norm_gain * gain_sum,
    )


def solution(mesh):
    rows = P(("groups", "dp"), None, "tensor")
    packed = P(("groups", "dp"), "tensor")
    placed = (rows, rows, rows, rows, P(("groups", "dp"), None), P("groups"), P("groups"))
    placed += (P("tensor", None), P("tensor"), P("tensor"))
    return jax.shard_map(
        on_device,
        mesh=mesh,
        in_specs=placed,
        out_specs=(
            P(("groups", "dp")),
            packed,
            packed,
            packed,
            packed,
            packed,
            P(("groups", "tensor")),
            P(("groups", "tensor")),
        ),
        check_vma=False,
    )
```

```python
import functools
import math

import jax
import jax.numpy as jnp
from jax import lax
from jax.experimental import pallas as pl
from jax.experimental.pallas import tpu as pltpu
from jax.sharding import PartitionSpec as P

H = 40
KVH = 8
HD = 128
RATIO = H // KVH
CAPB = 576
EPS = 1e-06
NEG = -1e30
CW = 256
TAIL = 16
F32 = jnp.float32
BF16 = jnp.bfloat16
VMEM = pl.BlockSpec(memory_space=pltpu.VMEM)
SMEM = pl.BlockSpec(memory_space=pltpu.SMEM)
ANY = pl.BlockSpec(memory_space=pl.ANY)
HBM = pl.BlockSpec(memory_space=pltpu.HBM)


def params(mib):
    return pltpu.CompilerParams(vmem_limit_bytes=mib * 1024 * 1024)


def mm(a, b, dims):
    return lax.dot_general(a, b, (dims, ((), ())), preferred_element_type=F32)


def route_kernel(n_dp, per_dev, me_ref, len_ref, bal_ref, pick_ref, start_ref, size_ref, cnt_ref):
    cap = per_dev // n_dp
    me = me_ref[0]
    for d in range(n_dp):
        target = jnp.bitwise_xor(me, d)

        def outgoing(s, count):
            b = bal_ref[target * per_dev + s]
            home = lax.div(b, per_dev)

            @pl.when(home == me)
            def _():
                pick_ref[d * cap + count] = lax.rem(b, per_dev)

            return count + (home == me).astype(jnp.int32)

        lax.fori_loop(0, per_dev, outgoing, jnp.int32(0))
        cnt_ref[d] = jnp.int32(0)

    def incoming(s, run):
        b = bal_ref[me * per_dev + s]
        d = jnp.bitwise_xor(lax.div(b, per_dev), me)
        count = cnt_ref[d]
        size = len_ref[b]
        start_ref[d * cap + count] = run
        size_ref[d * cap + count] = size
        cnt_ref[d] = count + 1
        return run + size

    lax.fori_loop(0, per_dev, incoming, jnp.int32(0))


def route(me, lengths, balance_list, n_dp, per_dev):
    table = jax.ShapeDtypeStruct((per_dev,), jnp.int32)
    return pl.pallas_call(
        functools.partial(route_kernel, n_dp, per_dev),
        out_shape=(table, table, table),
        in_specs=[SMEM] * 3,
        out_specs=(SMEM, SMEM, SMEM),
        scratch_shapes=[pltpu.SMEM((n_dp,), jnp.int32)],
        name="route",
    )(me, lengths, balance_list)


def gather_kernel(n_dp, cap, seq_len, spans, pick_ref, *refs):
    parts, outs, sems = refs[: len(spans)], refs[len(spans) : -1], refs[-1]
    copies = []
    for d in range(n_dp):
        for i in range(cap):
            row = pick_ref[d * cap + i]
            col = 0
            for p, (part, (lo, hi)) in enumerate(zip(parts, spans)):
                copies.append(
                    pltpu.make_async_copy(
                        part.at[row, :, pl.ds(lo, hi - lo)],
                        outs[d].at[pl.ds(i * seq_len, seq_len), pl.ds(col, hi - lo)],
                        sems.at[d * cap + i, p],
                    )
                )
                copies[-1].start()
                col += hi - lo
    for copy in copies:
        copy.wait()


def gather_rollouts(pick, parts, spans, n_dp):
    per_dev, seq_len = parts[0].shape[:2]
    cap = per_dev // n_dp
    out = jax.ShapeDtypeStruct((cap * seq_len, sum(hi - lo for lo, hi in spans)), BF16)
    return pl.pallas_call(
        functools.partial(gather_kernel, n_dp, cap, seq_len, spans),
        out_shape=(out,) * n_dp,
        in_specs=[SMEM] + [ANY] * len(parts),
        out_specs=(VMEM,) * n_dp,
        scratch_shapes=[pltpu.SemaphoreType.DMA((n_dp * cap, len(parts)))],
        compiler_params=params(60),
        name="gather_rollouts",
    )(pick, *parts)


def stack_kernel(n_dp, cap, seq_len, lo, hi, me_ref, pick_ref, part, returns, out, sems):
    copies = []
    for d in range(n_dp):
        to = jnp.bitwise_xor(me_ref[0], d)
        for i in range(cap):
            copies.append(
                pltpu.make_async_copy(
                    part.at[pick_ref[d * cap + i], :, pl.ds(lo, hi - lo)],
                    out.at[to, pl.ds(i * seq_len, seq_len)],
                    sems.at[d * cap + i],
                )
            )
            copies[-1].start()
    rows = returns[...].astype(F32)
    at = lax.broadcasted_iota(jnp.int32, rows.shape, 0)
    for d in range(n_dp):
        to = jnp.bitwise_xor(me_ref[0], d)
        picked = [
            jnp.sum(jnp.where(at == pick_ref[d * cap + i], rows, 0.0), axis=0, keepdims=True)
            for i in range(cap)
        ]
        picked.append(jnp.zeros((TAIL - cap, seq_len), F32))
        tail = jnp.concatenate(picked, axis=0).astype(BF16)
        out[to, cap * seq_len :, :] = jnp.concatenate(
            [tail, jnp.zeros((TAIL, hi - lo - seq_len), BF16)], axis=1
        )
    for copy in copies:
        copy.wait()


def stack_rollouts(me, pick, part, span, returns, n_dp):
    per_dev, seq_len = part.shape[:2]
    cap = per_dev // n_dp
    lo, hi = span
    return pl.pallas_call(
        functools.partial(stack_kernel, n_dp, cap, seq_len, lo, hi),
        out_shape=jax.ShapeDtypeStruct((n_dp, cap * seq_len + TAIL, hi - lo), BF16),
        in_specs=[SMEM, SMEM, ANY, VMEM],
        out_specs=VMEM,
        scratch_shapes=[pltpu.SemaphoreType.DMA((n_dp * cap,))],
        compiler_params=params(60),
        name="stack_rollouts",
    )(me, pick, part, returns)


def xor_move(value, d, n_dp):
    return lax.ppermute(value, "dp", [(i, i ^ d) for i in range(n_dp)])


def exchange(blocks, n_dp):
    order = sorted(range(1, n_dp), key=lambda d: d < 2)
    moved = {d: xor_move(blocks[d], d, n_dp) for d in order}
    return [blocks[0]] + [moved[d] for d in range(1, n_dp)]


def window(start, size, seq_len):
    tall = seq_len + 8
    base = pl.multiple_of(lax.div(start, 8) * 8, 8)
    shift = start - base
    fill = lambda shape, axis: lax.broadcasted_iota(jnp.int32, shape, axis)
    place = (fill((tall, seq_len), 0) - shift == fill((tall, seq_len), 1)) & (
        fill((tall, seq_len), 1) < size
    )
    fetch = (fill((seq_len, tall), 1) - shift == fill((seq_len, tall), 0)) & (
        fill((seq_len, tall), 0) < size
    )
    return pl.ds(base, tall), place.astype(BF16), fetch.astype(BF16)


def pack_kernel(n_dp, cap, seq_len, me_ref, start_ref, size_ref, ctx_ref, blocks, *refs):
    out, target, ctx_copy, room = refs[-4:]
    room[...] = jnp.zeros_like(room)
    target[...] = jnp.zeros_like(target)
    ctx_copy[...] = ctx_ref[...]
    for d in range(n_dp):
        source = jnp.bitwise_xor(me_ref[0], d)
        tail = blocks[source, cap * seq_len :, :seq_len].astype(F32)
        for i in range(cap):
            spot, place, _ = window(start_ref[d * cap + i], size_ref[d * cap + i], seq_len)
            rows = blocks[source, i * seq_len : (i + 1) * seq_len, :]
            room[spot, :] += mm(place, rows, ((1,), (0,)))
            target[spot, :] += jnp.sum(
                place.astype(F32) * tail[i : i + 1, :], axis=1, keepdims=True
            )
    out[...] = room[:CAPB, :].astype(BF16)


def pack(me, start, size, blocks, seq_len, cap, context, tie=()):
    n_dp, _, width = blocks.shape
    tall = CAPB + seq_len
    return pl.pallas_call(
        functools.partial(pack_kernel, n_dp, cap, seq_len),
        out_shape=(
            jax.ShapeDtypeStruct((CAPB, width), BF16),
            jax.ShapeDtypeStruct((tall, 1), F32),
            jax.ShapeDtypeStruct(context.shape, BF16),
        ),
        in_specs=[SMEM] * 3 + [VMEM] * 2 + [ANY] * len(tie),
        out_specs=(VMEM,) * 3,
        scratch_shapes=[pltpu.VMEM((tall, width), F32)],
        compiler_params=params(20),
        name="pack",
    )(me, start, size, context, blocks, *tie)


def heads_of(rows, first):
    return jnp.concatenate(
        [rows[:, (first + r) * HD : (first + r + 1) * HD] for r in range(RATIO)], axis=0
    )


def forward_kernel(first, count, cap, seq_len, kv, chunks, start_ref, size_ref, *refs):
    blocks = refs[:count]
    if first == 0:
        probs_ref, room = refs[-2:]
    else:
        pos_ref, weight = refs[count + 1 : count + 3]
        out, extra, probs_ref, *part_refs = refs[count + 3 : -3]
        room, columns, sems = refs[-3:]
        fetch = [
            pltpu.make_async_copy(weight.at[:, pl.ds(at, CW)], columns.at[k], sems.at[k])
            for k, (_, at) in enumerate(chunks)
        ]
        for copy in fetch:
            copy.start()
    qw = kv * RATIO * HD
    scale = 1.0 / math.sqrt(HD)
    span = RATIO * seq_len
    room[...] = jnp.zeros_like(room) if first == 0 else refs[count][...]
    at_u = lax.broadcasted_iota(jnp.int32, (seq_len, span), 0)
    at_t = lax.rem(lax.broadcasted_iota(jnp.int32, (seq_len, span), 1), seq_len)
    at_t1 = lax.rem(lax.broadcasted_iota(jnp.int32, (1, span), 1), seq_len)
    causal = at_u <= at_t
    for d in range(count):

        def step(i, _):
            size = size_ref[(first + d) * cap + i]
            spot, place, _ = window(start_ref[(first + d) * cap + i], size, seq_len)
            rows_i = pl.ds(pl.multiple_of(i * seq_len, seq_len), seq_len)
            keep = causal & (at_u < size)
            parts = []
            for g in range(kv):
                queries = heads_of(blocks[d][rows_i, g * RATIO * HD : (g + 1) * RATIO * HD], 0)
                keys = blocks[d][rows_i, qw + g * HD : qw + (g + 1) * HD]
                values = blocks[d][rows_i, qw + (kv + g) * HD : qw + (kv + g + 1) * HD]
                scores = jnp.where(keep, mm(keys, queries, ((1,), (1,))) * scale, NEG)
                top = jnp.max(scores, axis=0, keepdims=True)
                weights = jnp.exp(scores - top)
                total = jnp.sum(weights, axis=0, keepdims=True)
                probs = (weights * jnp.where(at_t1 < size, 1.0 / total, 0.0)).astype(BF16)
                probs_ref[d * cap + i, g] = probs
                mixed = mm(probs, values, ((0,), (0,)))
                parts += [mixed[r * seq_len : (r + 1) * seq_len] for r in range(RATIO)]
            beside = blocks[d][rows_i, qw + 2 * kv * HD :]
            mixed = jnp.concatenate([jnp.concatenate(parts, axis=1).astype(BF16), beside], axis=1)
            room[spot, :] += mm(place, mixed, ((1,), (0,)))
            return 0

        lax.fori_loop(0, cap, step, 0)
    if first:
        mixed = room[:CAPB, :qw].astype(BF16)
        beside = room[:CAPB, qw:]
        out[...] = mixed
        extra[...] = beside.astype(BF16)
        for k, (j, _) in enumerate(chunks):
            fetch[k].wait()
            own = jnp.where(pos_ref[1] == j, beside, 0.0)
            part = jnp.dot(mixed, columns[k], preferred_element_type=F32)
            part_refs[k][...] = (part + own).astype(BF16)


def attention_forward(start, size, blocks, kv, seq_len, cap, ahead, pos, out_weight, chunks):
    n_dp = len(blocks)
    half = n_dp // 2
    width = kv * RATIO * HD
    extra = blocks[0].shape[1] - width - 2 * kv * HD
    tall = CAPB + seq_len
    shape = jax.ShapeDtypeStruct
    probs = shape((half * cap, kv, seq_len, RATIO * seq_len), BF16)
    call = lambda first, outs, scratch, specs, more: pl.pallas_call(
        functools.partial(forward_kernel, first, half, cap, seq_len, kv, chunks),
        out_shape=outs,
        in_specs=[SMEM, SMEM] + [VMEM] * half + specs,
        out_specs=(VMEM,) * len(outs),
        scratch_shapes=scratch,
        compiler_params=params(24),
        name="attention_forward",
    )(start, size, *blocks[first : first + half], *more)
    probs_low, room = call(
        0, (probs, shape((tall, width + extra), F32)), [], [ANY] * len(ahead), ahead
    )
    context, beside, probs_high, *parts = call(
        half,
        (shape((CAPB, width), BF16), shape((CAPB, extra), BF16), probs)
        + (shape((CAPB, CW), BF16),) * len(chunks),
        [
            pltpu.VMEM((tall, width + extra), F32),
            pltpu.VMEM((max(1, len(chunks)), width, CW), BF16),
            pltpu.SemaphoreType.DMA((max(1, len(chunks)),)),
        ],
        [VMEM, SMEM, ANY],
        (room, pos, out_weight),
    )
    return context, beside, (probs_low, probs_high), parts


def backward_kernel(
    n_dp, cap, seq_len, kv, start_ref, size_ref, a_ref, b_ref, wgw_ref, acc_ref, *refs
):
    all_probs, refs = refs[:2], refs[2:]
    blocks = refs[:n_dp]
    dq_out, dk_out, dv_out = refs[n_dp : n_dp + 3]
    grads, dq_room, dk_room, dv_room = refs[n_dp + 3 :]
    qw = kv * RATIO * HD
    scale = 1.0 / math.sqrt(HD)
    half = n_dp // 2
    for room in (dq_room, dk_room, dv_room):
        room[...] = jnp.zeros_like(room)
    grads[:CAPB, :] = a_ref[...] * wgw_ref[...] - b_ref[...] * acc_ref[...]
    grads[CAPB:, :] = jnp.zeros((seq_len, qw), F32)
    lanes = 2 if cap % 2 == 0 else 1

    def rollout(d, i):
        spot, place, fetch = window(start_ref[d * cap + i], size_ref[d * cap + i], seq_len)
        mine = mm(fetch, grads[spot, :].astype(BF16), ((1,), (0,))).astype(BF16)
        rows_i = pl.ds(pl.multiple_of(i * seq_len, seq_len), seq_len)
        dq_parts, dk_parts, dv_parts = [], [], []
        for g in range(kv):
            cols = slice(g * RATIO * HD, (g + 1) * RATIO * HD)
            queries = heads_of(blocks[d][rows_i, cols], 0)
            keys = blocks[d][rows_i, qw + g * HD : qw + (g + 1) * HD]
            values = blocks[d][rows_i, qw + (kv + g) * HD : qw + (kv + g + 1) * HD]
            out_grad = heads_of(mine[:, cols], 0)
            probs_low = all_probs[d // half][d % half * cap + i, g]
            probs = probs_low.astype(F32)
            prob_grad = mm(values, out_grad, ((1,), (1,)))
            row_dot = jnp.sum(probs * prob_grad, axis=0, keepdims=True)
            score_grad = (probs * (prob_grad - row_dot) * scale).astype(BF16)
            dq = mm(score_grad, keys, ((0,), (0,)))
            dq_parts += [dq[r * seq_len : (r + 1) * seq_len] for r in range(RATIO)]
            dk_parts.append(mm(score_grad, queries, ((1,), (0,))))
            dv_parts.append(mm(probs_low, out_grad, ((1,), (0,))))
        wide = [jnp.concatenate(parts, axis=1).astype(BF16) for parts in (dq_parts, dk_parts, dv_parts)]
        return spot, [mm(place, rows, ((1,), (0,))) for rows in wide]

    for d in range(n_dp):

        def step(i, _):
            for spot, moved in [rollout(d, i * lanes + k) for k in range(lanes)]:
                for room, rows in zip((dq_room, dk_room, dv_room), moved):
                    room[spot, :] += rows
            return 0

        lax.fori_loop(0, cap // lanes, step, 0)
    dq_out[...] = dq_room[:CAPB, :].astype(BF16)
    dk_out[...] = dk_room[:CAPB, :].astype(BF16)
    dv_out[...] = dv_room[:CAPB, :].astype(BF16)


def attention_backward(start, size, a, b, wgw, acc, probs, blocks, kv, seq_len, cap):
    n_dp = len(blocks)
    qw, kw = kv * RATIO * HD, kv * HD
    tall = CAPB + seq_len
    return pl.pallas_call(
        functools.partial(backward_kernel, n_dp, cap, seq_len, kv),
        out_shape=tuple(jax.ShapeDtypeStruct((CAPB, w), BF16) for w in (qw, kw, kw)),
        in_specs=[SMEM, SMEM] + [VMEM] * (6 + n_dp),
        out_specs=(VMEM,) * 3,
        scratch_shapes=[pltpu.VMEM((tall, w), F32) for w in (qw, qw, kw, kw)],
        compiler_params=params(60),
        name="attention_backward",
    )(start, size, a, b, wgw, acc, *probs, *blocks)


def select(index, options):
    out = options[0]
    for k in range(1, len(options)):
        out = jnp.where(index == k, options[k], out)
    return out


def bundle_kernel(n_blk, *refs):
    pieces, out = refs[: n_blk * 2], refs[-1]
    for j in range(n_blk):
        for k in range(2):
            out[j, :, k * CW : (k + 1) * CW] = pieces[j * 2 + k][...]


def bundle_pieces(pieces, tie):
    n_blk = len(pieces) // 2
    return pl.pallas_call(
        functools.partial(bundle_kernel, n_blk),
        out_shape=jax.ShapeDtypeStruct((n_blk, CAPB, 2 * CW), BF16),
        in_specs=[VMEM] * len(pieces) + [ANY] * len(tie),
        out_specs=VMEM,
        compiler_params=params(16),
        cost_estimate=pl.CostEstimate(flops=0, bytes_accessed=0, transcendentals=0),
        name="bundle_pieces",
    )(*pieces, *tie)


def products(starts, n_cols, col, weight, gw_ref, piece, before, acc, sq, vd, own, columns, sems):
    n_blk = len(starts)
    cut = lambda j: slice(j * n_cols, (j + 1) * n_cols)
    fetch = [
        pltpu.make_async_copy(
            weight.at[:, pl.ds(at, n_cols)], columns.at[:, pl.ds(j * n_cols, n_cols)], sems.at[j]
        )
        for j, at in enumerate(starts)
    ]
    for copy in fetch:
        copy.start()
    tile = CAPB // 9
    for t in range(CAPB // tile):
        rows = slice(t * tile, (t + 1) * tile)
        pieces = [piece(j, rows) for j in range(n_blk)]
        own[rows, :] = select(col, pieces)
        squares = 0.0 if before is None else before[1][rows, :]
        dots = 0.0 if before is None else before[2][rows, :]
        for j, part in enumerate(pieces):
            wide = part.astype(F32)
            gain = gw_ref[:, starts[j] : starts[j] + n_cols]
            squares = squares + jnp.sum(wide * wide, axis=1, keepdims=True)
            dots = dots + jnp.sum(wide * gain, axis=1, keepdims=True)
        sq[rows, :] = squares
        vd[rows, :] = dots
    for copy in fetch:
        copy.wait()
    left = jnp.concatenate([piece(j, slice(0, CAPB)) for j in range(n_blk)], axis=1)
    total = mm(left, columns[...], ((1,), (1,)))
    acc[...] = total if before is None else total + before[0][...]


def rows_kernel(starts, n_cols, first, n_tie, pos_ref, weight, gw_ref, bundle, *refs):
    before, refs = (None, refs) if first else (refs[:3], refs[3:])
    piece = lambda j, rows: bundle[j, rows, :]
    products(starts, n_cols, pos_ref[1], weight, gw_ref, piece, before, *refs[n_tie:])


def row_products(pos, out_weight, gw_row, bundle, first_col, width, state, tie):
    n_blk, _, n_cols = bundle.shape
    depth = out_weight.shape[0]
    starts = [j * width + first_col for j in range(n_blk)]
    shape = jax.ShapeDtypeStruct
    column = shape((CAPB, 1), F32)
    before = [] if state is None else list(state)
    return pl.pallas_call(
        functools.partial(rows_kernel, starts, n_cols, state is None, len(tie)),
        out_shape=(shape((CAPB, depth), F32), column, column, shape((CAPB, n_cols), BF16)),
        in_specs=[SMEM, ANY] + [VMEM] * (2 + len(before)) + [ANY] * len(tie),
        out_specs=(VMEM,) * 4,
        scratch_shapes=[
            pltpu.VMEM((depth, n_blk * n_cols), BF16),
            pltpu.SemaphoreType.DMA((n_blk,)),
        ],
        compiler_params=params(52),
        cost_estimate=pl.CostEstimate(flops=0, bytes_accessed=0, transcendentals=0),
        name="row_products",
    )(pos, out_weight, gw_row, bundle, *before, *tie)


def row_of(column):
    return jnp.transpose(jnp.broadcast_to(column, (column.shape[0], 128)))[0:1, :]


def column_of(row):
    return jnp.transpose(jnp.broadcast_to(row, (128, row.shape[1])))[:, 0:1]


def norm_grads(model_width, sq, vd, target, gw_ref, ctx_ref, owns, outs):
    resid_out, sums, critic_row, a_col, b_col = outs
    inv_rms = lax.rsqrt(sq / model_width + EPS)
    critic = inv_rms * vd
    err = critic - target
    a = inv_rms * err
    b = inv_rms * inv_rms * inv_rms * err * vd / model_width
    a_col[...] = a
    b_col[...] = b
    critic_row[...] = row_of(critic)
    sums[...] = jnp.zeros_like(sums)
    sums[2:3, :CAPB] = row_of(b)
    at = 0
    for own in owns:
        cols = slice(at, at + own.shape[1])
        at += own.shape[1]
        hidden = own[...].astype(F32)
        resid_out[:, cols] = (a * gw_ref[:, cols] - b * hidden).astype(BF16)
        sums[0:1, cols] = jnp.sum(a * hidden, axis=0, keepdims=True)
    sums[1:2, :] = jnp.sum(a * ctx_ref[...].astype(F32), axis=0, keepdims=True)


def norm_shapes(width):
    shape = jax.ShapeDtypeStruct
    column = shape((CAPB, 1), F32)
    return (shape((CAPB, width), BF16), shape((8, width), F32), shape((1, CAPB), F32), column, column)


def last_kernel(starts, model_width, n_own, pos_ref, weight, gw_ref, gw_own, ctx, target, *refs):
    n_blk = len(starts)
    pieces, refs = refs[:n_blk], refs[n_blk:]
    before, owns, refs = refs[:3], refs[3 : 3 + n_own], refs[3 + n_own :]
    acc, pays, outs, refs = refs[0], refs[1], refs[2:7], refs[7:]
    sq, vd, own, columns, sems = refs
    for j in range(n_blk):
        pays[j] = pieces[j][...]
    piece = lambda j, rows: pieces[j][rows, :]
    products(
        starts, CW, pos_ref[1], weight, gw_ref, piece, before, acc, sq, vd, own, columns, sems
    )
    norm_grads(model_width, sq[...], vd[...], target[:CAPB, :], gw_own, ctx, (*owns, own), outs)


def last_products(pos, out_weight, gw_row, gw_own, context, target, pieces, first_col, state, owns):
    n_blk = len(pieces)
    depth, model_width = out_weight.shape
    width = context.shape[1]
    starts = [j * width + first_col for j in range(n_blk)]
    shape = jax.ShapeDtypeStruct
    return pl.pallas_call(
        functools.partial(last_kernel, starts, model_width, len(owns)),
        out_shape=(shape((CAPB, depth), F32), shape((n_blk, CAPB, CW), BF16)) + norm_shapes(width),
        in_specs=[SMEM, ANY] + [VMEM] * (4 + n_blk + 3 + len(owns)),
        out_specs=(VMEM,) * 7,
        scratch_shapes=[
            pltpu.VMEM((CAPB, 1), F32),
            pltpu.VMEM((CAPB, 1), F32),
            pltpu.VMEM((CAPB, CW), BF16),
            pltpu.VMEM((depth, n_blk * CW), BF16),
            pltpu.SemaphoreType.DMA((n_blk,)),
        ],
        compiler_params=params(52),
        name="last_products",
    )(pos, out_weight, gw_row, gw_own, context, target, *pieces, *state, *owns)


def finish_kernel(model_width, sq, vd, target, gw_ref, ctx_ref, own, *outs):
    norm_grads(model_width, sq[...], vd[...], target[:CAPB, :], gw_ref, ctx_ref, (own,), outs)


def finish(sq, vd, target, gw_own, context, own, model_width):
    return pl.pallas_call(
        functools.partial(finish_kernel, model_width),
        out_shape=norm_shapes(context.shape[1]),
        in_specs=[VMEM] * 6,
        out_specs=(VMEM,) * 5,
        compiler_params=params(32),
        name="finish",
    )(sq, vd, target, gw_own, context, own)


def paired_sum(terms):
    while len(terms) > 1:
        terms = [terms[k] + terms[k + 1] for k in range(0, len(terms), 2)]
    return terms[0]


def weight_kernel(n_dp, spans, pos_ref, gw_ref, norm_gain, value_weight, *refs):
    n_piece = len(spans)
    sums, (ctx_hbm,) = refs[:n_dp], refs[n_dp : n_dp + 1]
    pieces = refs[n_dp + 1 : n_dp + 1 + n_piece]
    out, gain_out, value_out, *refs = refs[n_dp + 1 + n_piece :]
    ctx, held, made, ctx_sems, in_sems, out_sems = refs
    me = pos_ref[0]
    gain_sum = paired_sum([s[0:1, :] for s in sums])
    context_sum = paired_sum([s[1:2, :] for s in sums])
    gain_out[...] = value_weight[...] * gain_sum
    value_out[...] = norm_gain[...] * gain_sum
    rows_of = lambda d: pl.ds(pl.multiple_of(jnp.bitwise_xor(me, d) * CAPB, CAPB), CAPB)
    ctx_in = [
        pltpu.make_async_copy(ctx_hbm.at[rows_of(d)], ctx.at[rows_of(d)], ctx_sems.at[d])
        for d in range(n_dp)
    ]
    piece_in = [
        pltpu.make_async_copy(pieces[r], held.at[:, pl.ds(lo, hi - lo)], in_sems.at[r])
        for r, (lo, hi) in enumerate(spans)
    ]
    for copy in ctx_in + piece_in:
        copy.start()
    for d in range(n_dp):
        ctx_in[d].wait()
        factor = column_of(sums[d][2:3, :CAPB])
        rows = rows_of(d)
        ctx[rows, :] = (factor * ctx[rows, :].astype(F32)).astype(BF16)
    store, arrived = [], 0
    step = made.shape[1]
    for t in range(spans[-1][1] // step):
        lo, hi = t * step, (t + 1) * step
        while arrived < n_piece and spans[arrived][0] < hi:
            piece_in[arrived].wait()
            arrived += 1
        if t >= 2:
            store[t - 2].wait()
        rank_one = gw_ref[lo:hi, :] * context_sum
        made[t % 2] = rank_one - mm(held[:, lo:hi], ctx[...], ((0,), (0,)))
        store.append(
            pltpu.make_async_copy(made.at[t % 2], out.at[pl.ds(lo, step)], out_sems.at[t % 2])
        )
        store[t].start()
    for copy in store[-2:]:
        copy.wait()


def weight_grad(pos, gw_col, norm_gain, value_weight, sums, contexts, pieces):
    n_dp = len(sums)
    width = contexts.shape[1]
    rows = pieces[0].shape[0]
    spans, at = [], 0
    for piece in pieces:
        spans.append((at, at + piece.shape[1]))
        at += piece.shape[1]
    step = CW if at % CW == 0 else at
    return pl.pallas_call(
        functools.partial(weight_kernel, n_dp, spans),
        out_shape=(
            jax.ShapeDtypeStruct((at, width), F32),
            jax.ShapeDtypeStruct((1, width), F32),
            jax.ShapeDtypeStruct((1, width), F32),
        ),
        in_specs=[SMEM] + [VMEM] * (3 + n_dp) + [ANY] * (1 + len(pieces)),
        out_specs=(ANY, VMEM, VMEM),
        scratch_shapes=[
            pltpu.VMEM(contexts.shape, BF16),
            pltpu.VMEM((rows, at), BF16),
            pltpu.VMEM((2, step, width), F32),
            pltpu.SemaphoreType.DMA((n_dp,)),
            pltpu.SemaphoreType.DMA((len(pieces),)),
            pltpu.SemaphoreType.DMA((2,)),
        ],
        compiler_params=params(60),
        name="weight_grad",
    )(pos, gw_col, norm_gain, value_weight, *sums, contexts, *pieces)


def parts_kernel(chunks, resid_cols, pos_ref, context, weight, resid, *refs):
    outs, columns, sems = refs[-len(chunks) - 2 : -2], refs[-2], refs[-1]
    fetch = [
        pltpu.make_async_copy(weight.at[:, pl.ds(at, CW)], columns.at[k], sems.at[k])
        for k, (_, at) in enumerate(chunks)
    ]
    for copy in fetch:
        copy.start()
    for k, (j, _) in enumerate(chunks):
        fetch[k].wait()
        part = jnp.dot(context[...], columns[k], preferred_element_type=F32)
        own = jnp.where(pos_ref[1] == j, resid[:, resid_cols].astype(F32), 0.0)
        outs[k][...] = (part + own).astype(BF16)


def partial_sums(pos, context, out_weight, resid, at, chunks, tie):
    piece = jax.ShapeDtypeStruct((CAPB, CW), BF16)
    n = len(chunks)
    return pl.pallas_call(
        functools.partial(parts_kernel, chunks, slice(at * CW, (at + 1) * CW)),
        out_shape=(piece,) * n,
        in_specs=[SMEM, VMEM, ANY, VMEM] + [ANY] * len(tie),
        out_specs=(VMEM,) * n,
        scratch_shapes=[
            pltpu.VMEM((n, out_weight.shape[0], CW), BF16),
            pltpu.SemaphoreType.DMA((n,)),
        ],
        compiler_params=params(52),
        cost_estimate=pl.CostEstimate(flops=0, bytes_accessed=0, transcendentals=0),
        name="partial_sums",
    )(pos, context, out_weight, resid, *tie)


def step_kernel(part, joins, totals, ends, n_tie, pos_ref, *refs):
    refs = list(refs)
    take = lambda n=1: [refs.pop(0) for _ in range(n)]
    mid = pos_ref[2] == 1
    add = lambda a, b: (a[...].astype(F32) + b[...].astype(F32)).astype(BF16)
    (new,) = take() if part else (None,)
    pair = take(2) if joins else None
    halves = take(2) if totals else None
    last = take(2) if ends else None
    take(n_tie)
    if joins:
        take()[0][...] = add(*pair)
    if totals:
        total = add(*halves)
        take()[0][...] = total if new is None else jnp.where(mid, total, new[...])
    if ends:
        take()[0][...] = jnp.where(mid, last[0][...], last[1][...])


def line_sum(context, resid_of, out_weight, pos, order, first_parts, after_step):
    edge = [(0, 1), (1, 0), (2, 3), (3, 2)]
    middle = [(1, 2), (2, 1)]
    width = context.shape[1]
    n, n_blk = len(order), 4
    piece = jax.ShapeDtypeStruct((CAPB, CW), BF16)
    parts, joined, from_edge, from_mid, payloads = dict(enumerate(first_parts)), {}, {}, {}, {}
    hidden = {}

    def make_parts(first, count, tie):
        r = order[first][1]
        resid, at = resid_of(r)
        chunks = [(j, j * width + r * CW) for j, _ in order[first : first + count]]
        made = partial_sums(pos, context, out_weight, resid, at, chunks, tie)
        parts.update(zip(range(first, first + count), made))

    for s in (0, 1):
        payloads[s] = parts[s]
        from_edge[s] = lax.ppermute(parts[s], "tensor", edge)
    make_parts(2, 2, (parts[1],))
    tie = (parts[3],)
    for s in range(n + 4):
        joins, totals, ends = s < n, 2 <= s < n + 2, s >= 4
        part = totals and s + 2 < n
        outs, args = {}, [pos]
        if part:
            args.append(parts[s + 2])
        if joins:
            args += [parts[s], from_edge[s]]
            outs["joined"] = piece
        if totals:
            args += [joined[s - 2], from_mid[s - 2]]
            outs["payload"] = piece
        if ends:
            args += [payloads[s], from_edge[s]]
            outs["hidden"] = piece
        made = pl.pallas_call(
            functools.partial(step_kernel, part, joins, totals, ends, len(tie)),
            out_shape=tuple(outs.values()),
            in_specs=[SMEM] + [VMEM] * (len(args) - 1) + [ANY] * len(tie),
            out_specs=(VMEM,) * len(outs),
            compiler_params=params(16),
            cost_estimate=pl.CostEstimate(flops=0, bytes_accessed=0, transcendentals=0),
            name="line_step",
        )(*args, *tie)
        made = dict(zip(outs, made))
        tie = (next(iter(made.values())),)
        if joins:
            joined[s] = made["joined"]
            from_mid[s] = lax.ppermute(joined[s], "tensor", middle)
        if s + 2 < n + 4:
            payloads[s + 2] = made["payload"] if totals else parts[s + 2]
            from_edge[s + 2] = lax.ppermute(payloads[s + 2], "tensor", edge)
        if ends:
            hidden[order[s - 4]] = made["hidden"]
        tie = after_step(s, hidden, tie)
        if s % n_blk == 0 and s + n_blk < n:
            make_parts(s + n_blk, n_blk, tie)


def on_device(
    query_states,
    key_states,
    value_states,
    residual,
    returns,
    lengths,
    balance_list,
    out_weight,
    norm_gain,
    value_weight,
):
    n_dp, n_tensor = lax.axis_size("dp"), lax.axis_size("tensor")
    me, col = lax.axis_index("dp"), lax.axis_index("tensor")
    per_dev = query_states.shape[0]
    width = query_states.shape[2]
    model_width = out_weight.shape[1]
    kv = key_states.shape[2] // HD

    seq_len = query_states.shape[1]
    cap = per_dev // n_dp
    first = CW if width > CW else width
    pick, start, size = route(me.reshape(1), lengths, balance_list, n_dp, per_dev)
    sent = gather_rollouts(
        pick,
        (query_states, key_states, value_states, residual),
        ((0, width), (0, kv * HD), (0, kv * HD), (0, first)),
        n_dp,
    )
    blocks = exchange(sent, n_dp)
    rest = stack_rollouts(me.reshape(1), pick, residual, (first, width), returns, n_dp)
    rest = lax.all_to_all(rest, "dp", split_axis=0, concat_axis=0, tiled=True)
    gw_own = norm_gain * value_weight
    gw = lax.all_gather(gw_own, "tensor", axis=0, tiled=True)
    gw_high = gw.astype(BF16)
    gw_low = (gw - gw_high.astype(F32)).astype(BF16)
    pair = jnp.stack([gw_high, gw_low])
    wgw = jnp.sum(mm(pair, out_weight, ((1,), (1,))), axis=0, keepdims=True)
    block = model_width // n_dp
    gw_col = lax.dynamic_slice_in_dim(gw, me * block, block).reshape(block, 1)
    is_mid = (col == 1) | (col == 2)
    pos = jnp.stack([me, col, is_mid.astype(jnp.int32)]).astype(jnp.int32)
    on_line = n_tensor == 4 and n_dp == 4
    per_block = width // CW
    order = [(j, r) for r in range(per_block) for j in (1, 2, 0, 3)]
    chunks = tuple((j, j * width + r * CW) for j, r in order[:2]) if on_line else ()
    context, resid_first, probs, parts = attention_forward(
        start, size, blocks, kv, seq_len, cap, (wgw, gw_col), pos, out_weight, chunks
    )
    gw_row, gw_mine = gw.reshape(1, model_width), gw_own.reshape(1, width)

    if on_line:
        later, bundles, owns, pieces = {}, [], [], []

        def move(bundle):
            moved = lax.all_to_all(bundle, "dp", split_axis=0, concat_axis=0, tiled=True)
            pieces.append(moved.reshape(n_dp * CAPB, bundle.shape[2]))

        def after_step(s, hidden, tie):
            if s == 0:
                later["resid"], later["target"], later["context"] = pack(
                    me.reshape(1), start, size, rest, seq_len, cap, context, tie
                )
            if s in (11, 19):
                r = 2 * len(bundles)
                pair = [hidden[j, k] for j in range(n_tensor) for k in (r, r + 1)]
                bundles.append(bundle_pieces(pair, tie))
                move(bundles[-1])
                return (bundles[-1],)
            if s in (14, 21):
                k = len(owns)
                *later["state"], own = row_products(
                    pos, out_weight, gw_row, bundles[k], 2 * CW * k, width, later.get("state"), tie
                )
                owns.append(own)
                return (own,)
            if s == len(order) + 3:
                later["last"] = [hidden[j, per_block - 1] for j in range(n_tensor)]
            return tie

        line_sum(
            context,
            lambda r: (resid_first, 0) if r == 0 else (later["resid"], r - 1),
            out_weight,
            pos,
            order,
            parts,
            after_step,
        )
        acc, pays, resid_out, sums, critic_row, a, b = last_products(
            pos,
            out_weight,
            gw_row,
            gw_mine,
            context,
            later["target"],
            later["last"],
            4 * CW,
            later["state"],
            owns,
        )
        move(pays)
        contexts = lax.all_gather(later["context"], "dp", axis=0, tiled=True)
    else:
        resid_rest, target, _ = pack(me.reshape(1), start, size, rest, seq_len, cap, context)
        contexts = lax.all_gather(context, "dp", axis=0, tiled=True)
        resid = jnp.concatenate([resid_first, resid_rest], axis=1)
        part = jnp.dot(context, out_weight, preferred_element_type=F32)
        mine = lax.dynamic_slice_in_dim(part, col * width, width, axis=1) + resid.astype(F32)
        part = lax.dynamic_update_slice_in_dim(part, mine, col * width, axis=1)
        hidden = lax.psum(part.astype(BF16), "tensor")
        wide = hidden.astype(F32)
        sq = jnp.sum(wide * wide, axis=1, keepdims=True)
        vd = jnp.sum(wide * gw[None, :], axis=1, keepdims=True)
        acc = mm(hidden, out_weight, ((1,), (1,)))
        own = lax.dynamic_slice_in_dim(hidden, col * width, width, axis=1)
        pieces = [lax.all_to_all(hidden, "dp", split_axis=1, concat_axis=0, tiled=True)]
        resid_out, sums, critic_row, a, b = finish(
            sq, vd, target, gw_mine, context, own, model_width
        )

    all_sums = [sums] + [xor_move(sums, d, n_dp) for d in range(1, n_dp)]
    query_out, key_out, value_out = attention_backward(
        start, size, a, b, wgw, acc, probs, blocks, kv, seq_len, cap
    )
    weight_out, gain_out, value_weight_out = weight_grad(
        pos,
        gw_col,
        norm_gain.reshape(1, width),
        value_weight.reshape(1, width),
        all_sums,
        contexts,
        pieces,
    )
    return (
        critic_row.reshape(CAPB).astype(BF16),
        query_out,
        key_out,
        value_out,
        resid_out,
        weight_out,
        gain_out.reshape(width),
        value_weight_out.reshape(width),
    )


def solution(mesh):
    rows = P(("groups", "dp"), None, "tensor")
    packed = P(("groups", "dp"), "tensor")
    placed = (rows, rows, rows, rows, P(("groups", "dp"), None), P("groups"), P("groups"))
    placed += (P("tensor", None), P("tensor"), P("tensor"))
    return jax.shard_map(
        on_device,
        mesh=mesh,
        in_specs=placed,
        out_specs=(
            P(("groups", "dp")),
            packed,
            packed,
            packed,
            packed,
            packed,
            P(("groups", "tensor")),
            P(("groups", "tensor")),
        ),
        check_vma=False,
    )
```

```python
import functools
import math

import jax
import jax.numpy as jnp
from jax import lax
from jax.experimental import pallas as pl
from jax.experimental.pallas import tpu as pltpu
from jax.sharding import PartitionSpec as P

H = 40
KVH = 8
HD = 128
RATIO = H // KVH
CAPB = 576
EPS = 1e-06
NEG = -1e30
CW = 256
TAIL = 16
F32 = jnp.float32
BF16 = jnp.bfloat16
VMEM = pl.BlockSpec(memory_space=pltpu.VMEM)
SMEM = pl.BlockSpec(memory_space=pltpu.SMEM)
ANY = pl.BlockSpec(memory_space=pl.ANY)
HBM = pl.BlockSpec(memory_space=pltpu.HBM)


def params(mib):
    return pltpu.CompilerParams(vmem_limit_bytes=mib * 1024 * 1024)


def mm(a, b, dims):
    return lax.dot_general(a, b, (dims, ((), ())), preferred_element_type=F32)


def route_kernel(n_dp, per_dev, me_ref, len_ref, bal_ref, pick_ref, start_ref, size_ref, cnt_ref):
    cap = per_dev // n_dp
    me = me_ref[0]
    for d in range(n_dp):
        target = jnp.bitwise_xor(me, d)

        def outgoing(s, count):
            b = bal_ref[target * per_dev + s]
            home = lax.div(b, per_dev)

            @pl.when(home == me)
            def _():
                pick_ref[d * cap + count] = lax.rem(b, per_dev)

            return count + (home == me).astype(jnp.int32)

        lax.fori_loop(0, per_dev, outgoing, jnp.int32(0))
        cnt_ref[d] = jnp.int32(0)

    def incoming(s, run):
        b = bal_ref[me * per_dev + s]
        d = jnp.bitwise_xor(lax.div(b, per_dev), me)
        count = cnt_ref[d]
        size = len_ref[b]
        start_ref[d * cap + count] = run
        size_ref[d * cap + count] = size
        cnt_ref[d] = count + 1
        return run + size

    lax.fori_loop(0, per_dev, incoming, jnp.int32(0))


def route(me, lengths, balance_list, n_dp, per_dev):
    table = jax.ShapeDtypeStruct((per_dev,), jnp.int32)
    return pl.pallas_call(
        functools.partial(route_kernel, n_dp, per_dev),
        out_shape=(table, table, table),
        in_specs=[SMEM] * 3,
        out_specs=(SMEM, SMEM, SMEM),
        scratch_shapes=[pltpu.SMEM((n_dp,), jnp.int32)],
        name="route",
    )(me, lengths, balance_list)


def gather_kernel(n_dp, cap, seq_len, spans, pick_ref, *refs):
    parts, outs, sems = refs[: len(spans)], refs[len(spans) : -1], refs[-1]
    copies = []
    for d in range(n_dp):
        for i in range(cap):
            row = pick_ref[d * cap + i]
            col = 0
            for p, (part, (lo, hi)) in enumerate(zip(parts, spans)):
                copies.append(
                    pltpu.make_async_copy(
                        part.at[row, :, pl.ds(lo, hi - lo)],
                        outs[d].at[pl.ds(i * seq_len, seq_len), pl.ds(col, hi - lo)],
                        sems.at[d * cap + i, p],
                    )
                )
                copies[-1].start()
                col += hi - lo
    for copy in copies:
        copy.wait()


def gather_rollouts(pick, parts, spans, n_dp):
    per_dev, seq_len = parts[0].shape[:2]
    cap = per_dev // n_dp
    out = jax.ShapeDtypeStruct((cap * seq_len, sum(hi - lo for lo, hi in spans)), BF16)
    return pl.pallas_call(
        functools.partial(gather_kernel, n_dp, cap, seq_len, spans),
        out_shape=(out,) * n_dp,
        in_specs=[SMEM] + [ANY] * len(parts),
        out_specs=(VMEM,) * n_dp,
        scratch_shapes=[pltpu.SemaphoreType.DMA((n_dp * cap, len(parts)))],
        compiler_params=params(60),
        name="gather_rollouts",
    )(pick, *parts)


def stack_kernel(n_dp, cap, seq_len, lo, hi, me_ref, pick_ref, part, returns, tie, out, order, sems):
    copies = []
    for d in range(n_dp):
        to = jnp.bitwise_xor(me_ref[0], d)
        for i in range(cap):
            copies.append(
                pltpu.make_async_copy(
                    part.at[pick_ref[d * cap + i], :, pl.ds(lo, hi - lo)],
                    out.at[to, pl.ds(i * seq_len, seq_len)],
                    sems.at[d * cap + i],
                )
            )
            copies[-1].start()
    order[0] = jnp.int32(0)
    rows = returns[...].astype(F32)
    at = lax.broadcasted_iota(jnp.int32, rows.shape, 0)
    for d in range(n_dp):
        to = jnp.bitwise_xor(me_ref[0], d)
        picked = [
            jnp.sum(jnp.where(at == pick_ref[d * cap + i], rows, 0.0), axis=0, keepdims=True)
            for i in range(cap)
        ]
        picked.append(jnp.zeros((TAIL - cap, seq_len), F32))
        tail = jnp.concatenate(picked, axis=0).astype(BF16)
        out[to, cap * seq_len :, :] = jnp.concatenate(
            [tail, jnp.zeros((TAIL, hi - lo - seq_len), BF16)], axis=1
        )
    for copy in copies:
        copy.wait()


def stack_rollouts(me, pick, part, span, returns, n_dp, tie):
    per_dev, seq_len = part.shape[:2]
    cap = per_dev // n_dp
    lo, hi = span
    return pl.pallas_call(
        functools.partial(stack_kernel, n_dp, cap, seq_len, lo, hi),
        out_shape=(
            jax.ShapeDtypeStruct((n_dp, cap * seq_len + TAIL, hi - lo), BF16),
            jax.ShapeDtypeStruct((1,), jnp.int32),
        ),
        in_specs=[SMEM, SMEM, ANY, VMEM, ANY],
        out_specs=(VMEM, SMEM),
        scratch_shapes=[pltpu.SemaphoreType.DMA((n_dp * cap,))],
        compiler_params=params(60),
        name="stack_rollouts",
    )(me, pick, part, returns, tie)


def xor_move(value, d, n_dp):
    return lax.ppermute(value, "dp", [(i, i ^ d) for i in range(n_dp)])


def exchange(blocks, n_dp):
    order = sorted(range(1, n_dp), key=lambda d: d < 2)
    moved = {d: xor_move(blocks[d], d, n_dp) for d in order}
    return [blocks[0]] + [moved[d] for d in range(1, n_dp)]


def pack_kernel(n_dp, cap, seq_len, me_ref, place, ctx_ref, blocks, *refs):
    out, target, ctx_copy, rolled = refs[-4:]
    ctx_copy[...] = ctx_ref[...]
    returned = 0.0
    width = cap * seq_len
    for d in range(n_dp):
        source = jnp.bitwise_xor(me_ref[0], d)
        rolled[d * width : (d + 1) * width, :] = blocks[source, :width, :]
        tail = blocks[source, width:, :seq_len].astype(F32)
        line = jnp.concatenate([tail[i : i + 1, :] for i in range(cap)], axis=1)
        spots = place[:, d * width : (d + 1) * width].astype(F32)
        returned = returned + jnp.sum(spots * line, axis=1, keepdims=True)
    target[...] = returned
    out[...] = mm(place[...], rolled[...], ((1,), (0,))).astype(BF16)


def pack(me, place, blocks, seq_len, cap, context, tie=()):
    n_dp, _, width = blocks.shape
    return pl.pallas_call(
        functools.partial(pack_kernel, n_dp, cap, seq_len),
        out_shape=(
            jax.ShapeDtypeStruct((CAPB, width), BF16),
            jax.ShapeDtypeStruct((CAPB, 1), F32),
            jax.ShapeDtypeStruct(context.shape, BF16),
        ),
        in_specs=[SMEM] + [VMEM] * 3 + [ANY] * len(tie),
        out_specs=(VMEM,) * 3,
        scratch_shapes=[pltpu.VMEM((n_dp * cap * seq_len, width), BF16)],
        compiler_params=params(20),
        name="pack",
    )(me, place, context, blocks, *tie)


def heads_of(rows, first):
    return jnp.concatenate(
        [rows[:, (first + r) * HD : (first + r + 1) * HD] for r in range(RATIO)], axis=0
    )


def spread_kernel(n_rollout, seq_len, start_ref, size_ref, place, fetch):
    iota = lambda shape, axis: lax.broadcasted_iota(jnp.int32, shape, axis)
    pair = (CAPB, 2 * seq_len)
    lane = iota(pair, 1)
    second = lane >= seq_len
    within = jnp.where(second, lane - seq_len, lane)
    offset = iota(pair, 0) - within
    turned = iota((seq_len, CAPB), 1) - iota((seq_len, CAPB), 0)
    row = iota((seq_len, CAPB), 0)
    for k in range(0, n_rollout, 2):
        first = (offset == start_ref[k]) & (within < size_ref[k]) & ~second
        other = (offset == start_ref[k + 1]) & (within < size_ref[k + 1]) & second
        place[:, k * seq_len : (k + 2) * seq_len] = (first | other).astype(BF16)
        for i in (k, k + 1):
            hit = (turned == start_ref[i]) & (row < size_ref[i])
            fetch[i * seq_len : (i + 1) * seq_len, :] = hit.astype(BF16)


def spread(start, size, seq_len):
    n_rollout = start.shape[0]
    rows = n_rollout * seq_len
    return pl.pallas_call(
        functools.partial(spread_kernel, n_rollout, seq_len),
        out_shape=(
            jax.ShapeDtypeStruct((CAPB, rows), BF16),
            jax.ShapeDtypeStruct((rows, CAPB), BF16),
        ),
        in_specs=[SMEM, SMEM],
        out_specs=(VMEM, VMEM),
        compiler_params=params(16),
        name="spread",
    )(start, size)


def forward_kernel(first, count, cap, seq_len, kv, chunks, size_ref, place, *refs):
    blocks, refs = refs[:count], refs[count:]
    if first == 0:
        probs_ref, room, rolled = refs[-3:]
    else:
        before, pos_ref, weight, out, extra, probs_ref, *part_refs = refs[:-3]
        rolled, columns, sems = refs[-3:]
        fetch = [
            pltpu.make_async_copy(weight.at[:, pl.ds(at, CW)], columns.at[k], sems.at[k])
            for k, (_, at) in enumerate(chunks)
        ]
        for copy in fetch:
            copy.start()
    qw = kv * RATIO * HD
    scale = 1.0 / math.sqrt(HD)
    span = RATIO * seq_len
    at_u = lax.broadcasted_iota(jnp.int32, (seq_len, span), 0)
    at_t = lax.rem(lax.broadcasted_iota(jnp.int32, (seq_len, span), 1), seq_len)
    at_t1 = lax.rem(lax.broadcasted_iota(jnp.int32, (1, span), 1), seq_len)
    causal = at_u <= at_t
    for d in range(count):
        for i in range(cap):
            size = size_ref[(first + d) * cap + i]
            rows = slice(i * seq_len, (i + 1) * seq_len)
            to = slice((d * cap + i) * seq_len, (d * cap + i + 1) * seq_len)
            keep = causal & (at_u < size)
            parts = []
            for g in range(kv):
                queries = heads_of(blocks[d][rows, g * RATIO * HD : (g + 1) * RATIO * HD], 0)
                keys = blocks[d][rows, qw + g * HD : qw + (g + 1) * HD]
                values = blocks[d][rows, qw + (kv + g) * HD : qw + (kv + g + 1) * HD]
                scores = jnp.where(keep, mm(keys, queries, ((1,), (1,))) * scale, NEG)
                top = jnp.max(scores, axis=0, keepdims=True)
                weights = jnp.exp(scores - top)
                total = jnp.sum(weights, axis=0, keepdims=True)
                probs = (weights * jnp.where(at_t1 < size, 1.0 / total, 0.0)).astype(BF16)
                probs_ref[d * cap + i, g] = probs
                mixed = mm(probs, values, ((0,), (0,)))
                parts += [mixed[r * seq_len : (r + 1) * seq_len] for r in range(RATIO)]
            rolled[to, :qw] = jnp.concatenate(parts, axis=1).astype(BF16)
            rolled[to, qw:] = blocks[d][rows, qw + 2 * kv * HD :]
    packed = mm(place[:, first * cap * seq_len : (first + count) * cap * seq_len], rolled[...], ((1,), (0,)))
    if first == 0:
        room[...] = packed
    else:
        packed = packed + before[...]
        mixed = packed[:, :qw].astype(BF16)
        beside = packed[:, qw:]
        out[...] = mixed
        extra[...] = beside.astype(BF16)
        for k, (j, _) in enumerate(chunks):
            fetch[k].wait()
            own = jnp.where(pos_ref[1] == j, beside, 0.0)
            part = jnp.dot(mixed, columns[k], preferred_element_type=F32)
            part_refs[k][...] = (part + own).astype(BF16)


def attention_forward(size, place, blocks, kv, seq_len, cap, ahead, pos, out_weight, chunks, between):
    n_dp = len(blocks)
    half = n_dp // 2
    width = kv * RATIO * HD
    extra = blocks[0].shape[1] - width - 2 * kv * HD
    shape = jax.ShapeDtypeStruct
    probs = shape((half * cap, kv, seq_len, RATIO * seq_len), BF16)
    rolled = pltpu.VMEM((half * cap * seq_len, width + extra), BF16)
    call = lambda first, outs, scratch, specs, more: pl.pallas_call(
        functools.partial(forward_kernel, first, half, cap, seq_len, kv, chunks),
        out_shape=outs,
        in_specs=[SMEM] + [VMEM] * (1 + half) + specs,
        out_specs=(VMEM,) * len(outs),
        scratch_shapes=scratch,
        compiler_params=params(52),
        name="attention_forward",
    )(size, place, *blocks[first : first + half], *more)
    probs_low, room = call(
        0, (probs, shape((CAPB, width + extra), F32)), [rolled], [ANY] * len(ahead), ahead
    )
    tie = between(room)
    context, beside, probs_high, *parts = call(
        half,
        (shape((CAPB, width), BF16), shape((CAPB, extra), BF16), probs)
        + (shape((CAPB, CW), BF16),) * len(chunks),
        [
            rolled,
            pltpu.VMEM((max(1, len(chunks)), width, CW), BF16),
            pltpu.SemaphoreType.DMA((max(1, len(chunks)),)),
        ],
        [VMEM, SMEM, ANY],
        (room, pos if tie is None else pos + tie, out_weight),
    )
    return context, beside, (probs_low, probs_high), parts


def backward_kernel(n_dp, cap, seq_len, kv, place, fetch, a_ref, b_ref, wgw_ref, acc_ref, *refs):
    all_probs, refs = refs[:2], refs[2:]
    blocks = refs[:n_dp]
    dq_out, dk_out, dv_out, grads, dq_all, dk_all, dv_all = refs[n_dp:]
    half = n_dp // 2
    qw = kv * RATIO * HD
    scale = 1.0 / math.sqrt(HD)
    packed = (a_ref[...] * wgw_ref[...] - b_ref[...] * acc_ref[...]).astype(BF16)
    grads[...] = mm(fetch[...], packed, ((1,), (0,))).astype(BF16)
    for d in range(n_dp):
        for i in range(cap):
            rows = slice(i * seq_len, (i + 1) * seq_len)
            to = slice((d * cap + i) * seq_len, (d * cap + i + 1) * seq_len)
            dq_parts, dk_parts, dv_parts = [], [], []
            for g in range(kv):
                cols = slice(g * RATIO * HD, (g + 1) * RATIO * HD)
                queries = heads_of(blocks[d][rows, cols], 0)
                keys = blocks[d][rows, qw + g * HD : qw + (g + 1) * HD]
                values = blocks[d][rows, qw + (kv + g) * HD : qw + (kv + g + 1) * HD]
                out_grad = heads_of(grads[to, cols], 0)
                probs_low = all_probs[d // half][d % half * cap + i, g]
                probs = probs_low.astype(F32)
                prob_grad = mm(values, out_grad, ((1,), (1,)))
                row_dot = jnp.sum(probs * prob_grad, axis=0, keepdims=True)
                score_grad = (probs * (prob_grad - row_dot) * scale).astype(BF16)
                dq = mm(score_grad, keys, ((0,), (0,)))
                dq_parts += [dq[r * seq_len : (r + 1) * seq_len] for r in range(RATIO)]
                dk_parts.append(mm(score_grad, queries, ((1,), (0,))))
                dv_parts.append(mm(probs_low, out_grad, ((1,), (0,))))
            for kept, parts in ((dq_all, dq_parts), (dk_all, dk_parts), (dv_all, dv_parts)):
                kept[to, :] = jnp.concatenate(parts, axis=1).astype(BF16)
    for out, kept in ((dq_out, dq_all), (dk_out, dk_all), (dv_out, dv_all)):
        out[...] = mm(place[...], kept[...], ((1,), (0,))).astype(BF16)


def attention_backward(place, fetch, a, b, wgw, acc, probs, blocks, kv, seq_len, cap):
    n_dp = len(blocks)
    qw, kw = kv * RATIO * HD, kv * HD
    rows = n_dp * cap * seq_len
    return pl.pallas_call(
        functools.partial(backward_kernel, n_dp, cap, seq_len, kv),
        out_shape=tuple(jax.ShapeDtypeStruct((CAPB, w), BF16) for w in (qw, kw, kw)),
        in_specs=[VMEM] * (8 + n_dp),
        out_specs=(VMEM,) * 3,
        scratch_shapes=[pltpu.VMEM((rows, w), BF16) for w in (qw, qw, kw, kw)],
        compiler_params=params(60),
        name="attention_backward",
    )(place, fetch, a, b, wgw, acc, *probs, *blocks)


def select(index, options):
    out = options[0]
    for k in range(1, len(options)):
        out = jnp.where(index == k, options[k], out)
    return out


def bundle_kernel(n_blk, *refs):
    pieces, out = refs[: n_blk * 2], refs[-1]
    for j in range(n_blk):
        for k in range(2):
            out[j, :, k * CW : (k + 1) * CW] = pieces[j * 2 + k][...]


def bundle_pieces(pieces, tie):
    n_blk = len(pieces) // 2
    return pl.pallas_call(
        functools.partial(bundle_kernel, n_blk),
        out_shape=jax.ShapeDtypeStruct((n_blk, CAPB, 2 * CW), BF16),
        in_specs=[VMEM] * len(pieces) + [ANY] * len(tie),
        out_specs=VMEM,
        compiler_params=params(16),
        cost_estimate=pl.CostEstimate(flops=0, bytes_accessed=0, transcendentals=0),
        name="bundle_pieces",
    )(*pieces, *tie)


def products(starts, n_cols, col, weight, gw_ref, piece, before, acc, sq, vd, own, columns, sems):
    n_blk = len(starts)
    cut = lambda j: slice(j * n_cols, (j + 1) * n_cols)
    fetch = [
        pltpu.make_async_copy(
            weight.at[:, pl.ds(at, n_cols)], columns.at[:, pl.ds(j * n_cols, n_cols)], sems.at[j]
        )
        for j, at in enumerate(starts)
    ]
    for copy in fetch:
        copy.start()
    tile = CAPB // 9
    for t in range(CAPB // tile):
        rows = slice(t * tile, (t + 1) * tile)
        pieces = [piece(j, rows) for j in range(n_blk)]
        own[rows, :] = select(col, pieces)
        squares = 0.0 if before is None else before[1][rows, :]
        dots = 0.0 if before is None else before[2][rows, :]
        for j, part in enumerate(pieces):
            wide = part.astype(F32)
            gain = gw_ref[:, starts[j] : starts[j] + n_cols]
            squares = squares + jnp.sum(wide * wide, axis=1, keepdims=True)
            dots = dots + jnp.sum(wide * gain, axis=1, keepdims=True)
        sq[rows, :] = squares
        vd[rows, :] = dots
    for copy in fetch:
        copy.wait()
    left = jnp.concatenate([piece(j, slice(0, CAPB)) for j in range(n_blk)], axis=1)
    total = mm(left, columns[...], ((1,), (1,)))
    acc[...] = total if before is None else total + before[0][...]


def rows_kernel(starts, n_cols, first, n_tie, pos_ref, weight, gw_ref, bundle, *refs):
    before, refs = (None, refs) if first else (refs[:3], refs[3:])
    piece = lambda j, rows: bundle[j, rows, :]
    products(starts, n_cols, pos_ref[1], weight, gw_ref, piece, before, *refs[n_tie:])


def row_products(pos, out_weight, gw_row, bundle, first_col, width, state, tie):
    n_blk, _, n_cols = bundle.shape
    depth = out_weight.shape[0]
    starts = [j * width + first_col for j in range(n_blk)]
    shape = jax.ShapeDtypeStruct
    column = shape((CAPB, 1), F32)
    before = [] if state is None else list(state)
    return pl.pallas_call(
        functools.partial(rows_kernel, starts, n_cols, state is None, len(tie)),
        out_shape=(shape((CAPB, depth), F32), column, column, shape((CAPB, n_cols), BF16)),
        in_specs=[SMEM, ANY] + [VMEM] * (2 + len(before)) + [ANY] * len(tie),
        out_specs=(VMEM,) * 4,
        scratch_shapes=[
            pltpu.VMEM((depth, n_blk * n_cols), BF16),
            pltpu.SemaphoreType.DMA((n_blk,)),
        ],
        compiler_params=params(52),
        cost_estimate=pl.CostEstimate(flops=0, bytes_accessed=0, transcendentals=0),
        name="row_products",
    )(pos, out_weight, gw_row, bundle, *before, *tie)


def row_of(column):
    return jnp.transpose(jnp.broadcast_to(column, (column.shape[0], 128)))[0:1, :]


def column_of(row):
    return jnp.transpose(jnp.broadcast_to(row, (128, row.shape[1])))[:, 0:1]


def norm_grads(model_width, sq, vd, target, gw_ref, ctx_ref, owns, outs):
    resid_out, sums, critic_row, a_col, b_col = outs
    inv_rms = lax.rsqrt(sq / model_width + EPS)
    critic = inv_rms * vd
    err = critic - target
    a = inv_rms * err
    b = inv_rms * inv_rms * inv_rms * err * vd / model_width
    a_col[...] = a
    b_col[...] = b
    critic_row[...] = row_of(critic)
    sums[...] = jnp.zeros_like(sums)
    sums[2:3, :CAPB] = row_of(b)
    at = 0
    for own in owns:
        cols = slice(at, at + own.shape[1])
        at += own.shape[1]
        hidden = own[...].astype(F32)
        resid_out[:, cols] = (a * gw_ref[:, cols] - b * hidden).astype(BF16)
        sums[0:1, cols] = jnp.sum(a * hidden, axis=0, keepdims=True)
    sums[1:2, :] = jnp.sum(a * ctx_ref[...].astype(F32), axis=0, keepdims=True)


def norm_shapes(width):
    shape = jax.ShapeDtypeStruct
    column = shape((CAPB, 1), F32)
    return (shape((CAPB, width), BF16), shape((8, width), F32), shape((1, CAPB), F32), column, column)


def last_kernel(starts, model_width, n_own, n_tie, pos_ref, weight, gw_ref, gw_own, ctx, target, *refs):
    n_blk = len(starts)
    pieces, refs = refs[:n_blk], refs[n_blk:]
    before, owns, refs = refs[:3], refs[3 : 3 + n_own], refs[3 + n_own + n_tie :]
    acc, pays, outs, refs = refs[0], refs[1], refs[2:7], refs[7:]
    sq, vd, own, columns, sems = refs
    for j in range(n_blk):
        pays[j] = pieces[j][...]
    piece = lambda j, rows: pieces[j][rows, :]
    products(
        starts, CW, pos_ref[1], weight, gw_ref, piece, before, acc, sq, vd, own, columns, sems
    )
    norm_grads(model_width, sq[...], vd[...], target[...], gw_own, ctx, (*owns, own), outs)


def last_products(
    pos, out_weight, gw_row, gw_own, context, target, pieces, first_col, state, owns, tie
):
    n_blk = len(pieces)
    depth, model_width = out_weight.shape
    width = context.shape[1]
    starts = [j * width + first_col for j in range(n_blk)]
    shape = jax.ShapeDtypeStruct
    return pl.pallas_call(
        functools.partial(last_kernel, starts, model_width, len(owns), len(tie)),
        out_shape=(shape((CAPB, depth), F32), shape((n_blk, CAPB, CW), BF16)) + norm_shapes(width),
        in_specs=[SMEM, ANY] + [VMEM] * (4 + n_blk + 3 + len(owns)) + [ANY] * len(tie),
        out_specs=(VMEM,) * 7,
        scratch_shapes=[
            pltpu.VMEM((CAPB, 1), F32),
            pltpu.VMEM((CAPB, 1), F32),
            pltpu.VMEM((CAPB, CW), BF16),
            pltpu.VMEM((depth, n_blk * CW), BF16),
            pltpu.SemaphoreType.DMA((n_blk,)),
        ],
        compiler_params=params(52),
        name="last_products",
    )(pos, out_weight, gw_row, gw_own, context, target, *pieces, *state, *owns, *tie)


def finish_kernel(model_width, sq, vd, target, gw_ref, ctx_ref, own, *outs):
    norm_grads(model_width, sq[...], vd[...], target[...], gw_ref, ctx_ref, (own,), outs)


def finish(sq, vd, target, gw_own, context, own, model_width):
    return pl.pallas_call(
        functools.partial(finish_kernel, model_width),
        out_shape=norm_shapes(context.shape[1]),
        in_specs=[VMEM] * 6,
        out_specs=(VMEM,) * 5,
        compiler_params=params(32),
        name="finish",
    )(sq, vd, target, gw_own, context, own)


def paired_sum(terms):
    while len(terms) > 1:
        terms = [terms[k] + terms[k + 1] for k in range(0, len(terms), 2)]
    return terms[0]


def weight_kernel(n_dp, spans, pos_ref, gw_ref, norm_gain, value_weight, *refs):
    n_piece = len(spans)
    sums, (ctx_hbm,) = refs[:n_dp], refs[n_dp : n_dp + 1]
    pieces = refs[n_dp + 1 : n_dp + 1 + n_piece]
    out, gain_out, value_out, *refs = refs[n_dp + 1 + n_piece :]
    ctx, held, made, ctx_sems, in_sems, out_sems = refs
    me = pos_ref[0]
    gain_sum = paired_sum([s[0:1, :] for s in sums])
    context_sum = paired_sum([s[1:2, :] for s in sums])
    for ref, row in ((gain_out, value_weight[...] * gain_sum), (value_out, norm_gain[...] * gain_sum)):
        ref[...] = jnp.concatenate([row[:, k * 128 : (k + 1) * 128] for k in range(ref.shape[0])], axis=0)
    rows_of = lambda d: pl.ds(pl.multiple_of(jnp.bitwise_xor(me, d) * CAPB, CAPB), CAPB)
    ctx_in = [
        pltpu.make_async_copy(ctx_hbm.at[rows_of(d)], ctx.at[rows_of(d)], ctx_sems.at[d])
        for d in range(n_dp)
    ]
    piece_in = [
        pltpu.make_async_copy(pieces[r], held.at[:, pl.ds(lo, hi - lo)], in_sems.at[r])
        for r, (lo, hi) in enumerate(spans)
    ]
    for copy in ctx_in + piece_in:
        copy.start()
    for d in range(n_dp):
        ctx_in[d].wait()
        factor = column_of(sums[d][2:3, :CAPB])
        rows = rows_of(d)
        ctx[rows, :] = (factor * ctx[rows, :].astype(F32)).astype(BF16)
    store, arrived = [], 0
    step = made.shape[1]
    for t in range(spans[-1][1] // step):
        lo, hi = t * step, (t + 1) * step
        while arrived < n_piece and spans[arrived][0] < hi:
            piece_in[arrived].wait()
            arrived += 1
        if t >= 2:
            store[t - 2].wait()
        rank_one = gw_ref[lo:hi, :] * context_sum
        made[t % 2] = rank_one - mm(held[:, lo:hi], ctx[...], ((0,), (0,)))
        store.append(
            pltpu.make_async_copy(made.at[t % 2], out.at[pl.ds(lo, step)], out_sems.at[t % 2])
        )
        store[t].start()
    for copy in store[-2:]:
        copy.wait()


def weight_grad(pos, gw_col, norm_gain, value_weight, sums, contexts, pieces):
    n_dp = len(sums)
    width = contexts.shape[1]
    rows = pieces[0].shape[0]
    spans, at = [], 0
    for piece in pieces:
        spans.append((at, at + piece.shape[1]))
        at += piece.shape[1]
    step = CW if at % CW == 0 else at
    return pl.pallas_call(
        functools.partial(weight_kernel, n_dp, spans),
        out_shape=(
            jax.ShapeDtypeStruct((at, width), F32),
            jax.ShapeDtypeStruct((width // 128, 128), F32),
            jax.ShapeDtypeStruct((width // 128, 128), F32),
        ),
        in_specs=[SMEM] + [VMEM] * (3 + n_dp) + [ANY] * (1 + len(pieces)),
        out_specs=(ANY, VMEM, VMEM),
        scratch_shapes=[
            pltpu.VMEM(contexts.shape, BF16),
            pltpu.VMEM((rows, at), BF16),
            pltpu.VMEM((2, step, width), F32),
            pltpu.SemaphoreType.DMA((n_dp,)),
            pltpu.SemaphoreType.DMA((len(pieces),)),
            pltpu.SemaphoreType.DMA((2,)),
        ],
        compiler_params=params(60),
        name="weight_grad",
    )(pos, gw_col, norm_gain, value_weight, *sums, contexts, *pieces)


def parts_kernel(chunks, resid_cols, pos_ref, context, weight, resid, *refs):
    outs, columns, sems = refs[-len(chunks) - 2 : -2], refs[-2], refs[-1]
    fetch = [
        pltpu.make_async_copy(weight.at[:, pl.ds(at, CW)], columns.at[k], sems.at[k])
        for k, (_, at) in enumerate(chunks)
    ]
    for copy in fetch:
        copy.start()
    for k, (j, _) in enumerate(chunks):
        fetch[k].wait()
        part = jnp.dot(context[...], columns[k], preferred_element_type=F32)
        own = jnp.where(pos_ref[1] == j, resid[:, resid_cols].astype(F32), 0.0)
        outs[k][...] = (part + own).astype(BF16)


def partial_sums(pos, context, out_weight, resid, at, chunks, tie):
    piece = jax.ShapeDtypeStruct((CAPB, CW), BF16)
    n = len(chunks)
    return pl.pallas_call(
        functools.partial(parts_kernel, chunks, slice(at * CW, (at + 1) * CW)),
        out_shape=(piece,) * n,
        in_specs=[SMEM, VMEM, ANY, VMEM] + [ANY] * len(tie),
        out_specs=(VMEM,) * n,
        scratch_shapes=[
            pltpu.VMEM((n, out_weight.shape[0], CW), BF16),
            pltpu.SemaphoreType.DMA((n,)),
        ],
        compiler_params=params(52),
        cost_estimate=pl.CostEstimate(flops=0, bytes_accessed=0, transcendentals=0),
        name="partial_sums",
    )(pos, context, out_weight, resid, *tie)


def step_kernel(part, joins, totals, ends, n_tie, pos_ref, *refs):
    refs = list(refs)
    take = lambda n=1: [refs.pop(0) for _ in range(n)]
    mid = pos_ref[2] == 1
    add = lambda a, b: (a[...].astype(F32) + b[...].astype(F32)).astype(BF16)
    (new,) = take() if part else (None,)
    pair = take(2) if joins else None
    halves = take(2) if totals else None
    last = take(2) if ends else None
    take(n_tie)
    if joins:
        take()[0][...] = add(*pair)
    if totals:
        total = add(*halves)
        take()[0][...] = total if new is None else jnp.where(mid, total, new[...])
    if ends:
        take()[0][...] = jnp.where(mid, last[0][...], last[1][...])


def line_sum(context, resid_of, out_weight, pos, order, first_parts, after_step):
    edge = [(0, 1), (1, 0), (2, 3), (3, 2)]
    middle = [(1, 2), (2, 1)]
    width = context.shape[1]
    n, n_blk = len(order), 4
    piece = jax.ShapeDtypeStruct((CAPB, CW), BF16)
    parts, joined, from_edge, from_mid, payloads = dict(enumerate(first_parts)), {}, {}, {}, {}
    hidden = {}

    def make_parts(first, count, tie):
        r = order[first][1]
        resid, at = resid_of(r)
        chunks = [(j, j * width + r * CW) for j, _ in order[first : first + count]]
        made = partial_sums(pos, context, out_weight, resid, at, chunks, tie)
        parts.update(zip(range(first, first + count), made))

    for s in (0, 1):
        payloads[s] = parts[s]
        from_edge[s] = lax.ppermute(parts[s], "tensor", edge)
    make_parts(2, 2, (parts[1],))
    tie = (parts[3],)
    for s in range(n + 4):
        joins, totals, ends = s < n, 2 <= s < n + 2, s >= 4
        part = totals and s + 2 < n
        outs, args = {}, [pos]
        if part:
            args.append(parts[s + 2])
        if joins:
            args += [parts[s], from_edge[s]]
            outs["joined"] = piece
        if totals:
            args += [joined[s - 2], from_mid[s - 2]]
            outs["payload"] = piece
        if ends:
            args += [payloads[s], from_edge[s]]
            outs["hidden"] = piece
        made = pl.pallas_call(
            functools.partial(step_kernel, part, joins, totals, ends, len(tie)),
            out_shape=tuple(outs.values()),
            in_specs=[SMEM] + [VMEM] * (len(args) - 1) + [ANY] * len(tie),
            out_specs=(VMEM,) * len(outs),
            compiler_params=params(16),
            cost_estimate=pl.CostEstimate(flops=0, bytes_accessed=0, transcendentals=0),
            name="line_step",
        )(*args, *tie)
        made = dict(zip(outs, made))
        tie = (next(iter(made.values())),)
        if joins:
            joined[s] = made["joined"]
            from_mid[s] = lax.ppermute(joined[s], "tensor", middle)
        if s + 2 < n + 4:
            payloads[s + 2] = made["payload"] if totals else parts[s + 2]
            from_edge[s + 2] = lax.ppermute(payloads[s + 2], "tensor", edge)
        if ends:
            hidden[order[s - 4]] = made["hidden"]
        tie = after_step(s, hidden, tie)
        if s % 2 == 0 and s + n_blk < n:
            make_parts(s + n_blk, 2, tie)


def on_device(
    query_states,
    key_states,
    value_states,
    residual,
    returns,
    lengths,
    balance_list,
    out_weight,
    norm_gain,
    value_weight,
):
    n_dp, n_tensor = lax.axis_size("dp"), lax.axis_size("tensor")
    me, col = lax.axis_index("dp"), lax.axis_index("tensor")
    per_dev = query_states.shape[0]
    width = query_states.shape[2]
    model_width = out_weight.shape[1]
    kv = key_states.shape[2] // HD

    seq_len = query_states.shape[1]
    cap = per_dev // n_dp
    first = CW if width > CW else width
    pick, start, size = route(me.reshape(1), lengths, balance_list, n_dp, per_dev)
    sent = gather_rollouts(
        pick,
        (query_states, key_states, value_states, residual),
        ((0, width), (0, kv * HD), (0, kv * HD), (0, first)),
        n_dp,
    )
    blocks = exchange(sent, n_dp)
    place, fetch = spread(start, size, seq_len)
    gw_own = norm_gain * value_weight
    gw = lax.all_gather(gw_own, "tensor", axis=0, tiled=True)
    gw_high = gw.astype(BF16)
    gw_low = (gw - gw_high.astype(F32)).astype(BF16)
    pair = jnp.stack([gw_high, gw_low])
    wgw = jnp.sum(mm(pair, out_weight, ((1,), (1,))), axis=0, keepdims=True)
    block = model_width // n_dp
    gw_col = lax.dynamic_slice_in_dim(gw, me * block, block).reshape(block, 1)
    is_mid = (col == 1) | (col == 2)
    pos = jnp.stack([me, col, is_mid.astype(jnp.int32)]).astype(jnp.int32)
    on_line = n_tensor == 4 and n_dp == 4
    per_block = width // CW
    order = [(j, r) for r in range(per_block) for j in (1, 2, 0, 3)]
    chunks = tuple((j, j * width + r * CW) for j, r in order[:2]) if on_line else ()
    later = {}

    def between(tie):
        later["rest"], order_after = stack_rollouts(
            me.reshape(1), pick, residual, (first, width), returns, n_dp, tie
        )
        return order_after

    context, resid_first, probs, parts = attention_forward(
        size, place, blocks, kv, seq_len, cap, (wgw, gw_col), pos, out_weight, chunks, between
    )
    rest = lax.all_to_all(later["rest"], "dp", split_axis=0, concat_axis=0, tiled=True)
    gw_row, gw_mine = gw.reshape(1, model_width), gw_own.reshape(1, width)

    if on_line:
        bundles, owns, pieces = [], [], []

        def move(bundle):
            moved = lax.all_to_all(bundle, "dp", split_axis=0, concat_axis=0, tiled=True)
            pieces.append(moved.reshape(n_dp * CAPB, bundle.shape[2]))

        def after_step(s, hidden, tie):
            if s == 0:
                later["resid"], later["target"], later["context"] = pack(
                    me.reshape(1), place, rest, seq_len, cap, context, tie
                )
            if s in (11, 19):
                r = 2 * len(bundles)
                pair = [hidden[j, k] for j in range(n_tensor) for k in (r, r + 1)]
                bundles.append(bundle_pieces(pair, tie))
                move(bundles[-1])
                return (bundles[-1],)
            if s in (14, 21):
                k = len(owns)
                *later["state"], own = row_products(
                    pos, out_weight, gw_row, bundles[k], 2 * CW * k, width, later.get("state"), tie
                )
                owns.append(own)
                return (own,)
            if s == len(order) + 3:
                later["last"] = [hidden[j, per_block - 1] for j in range(n_tensor)]
            return tie

        line_sum(
            context,
            lambda r: (resid_first, 0) if r == 0 else (later["resid"], r - 1),
            out_weight,
            pos,
            order,
            parts,
            after_step,
        )
        acc, pays, resid_out, sums, critic_row, a, b = last_products(
            pos,
            out_weight,
            gw_row,
            gw_mine,
            context,
            later["target"],
            later["last"],
            4 * CW,
            later["state"],
            owns,
            (pieces[1],),
        )
        move(pays)
        contexts = lax.all_gather(later["context"], "dp", axis=0, tiled=True)
    else:
        resid_rest, target, _ = pack(me.reshape(1), place, rest, seq_len, cap, context)
        contexts = lax.all_gather(context, "dp", axis=0, tiled=True)
        resid = jnp.concatenate([resid_first, resid_rest], axis=1)
        part = jnp.dot(context, out_weight, preferred_element_type=F32)
        mine = lax.dynamic_slice_in_dim(part, col * width, width, axis=1) + resid.astype(F32)
        part = lax.dynamic_update_slice_in_dim(part, mine, col * width, axis=1)
        hidden = lax.psum(part.astype(BF16), "tensor")
        wide = hidden.astype(F32)
        sq = jnp.sum(wide * wide, axis=1, keepdims=True)
        vd = jnp.sum(wide * gw[None, :], axis=1, keepdims=True)
        acc = mm(hidden, out_weight, ((1,), (1,)))
        own = lax.dynamic_slice_in_dim(hidden, col * width, width, axis=1)
        pieces = [lax.all_to_all(hidden, "dp", split_axis=1, concat_axis=0, tiled=True)]
        resid_out, sums, critic_row, a, b = finish(
            sq, vd, target, gw_mine, context, own, model_width
        )

    all_sums = [sums] + [xor_move(sums, d, n_dp) for d in range(1, n_dp)]
    query_out, key_out, value_out = attention_backward(
        place, fetch, a, b, wgw, acc, probs, blocks, kv, seq_len, cap
    )
    weight_out, gain_out, value_weight_out = weight_grad(
        pos,
        gw_col,
        norm_gain.reshape(1, width),
        value_weight.reshape(1, width),
        all_sums,
        contexts,
        pieces,
    )
    return (
        critic_row.reshape(CAPB).astype(BF16),
        query_out,
        key_out,
        value_out,
        resid_out,
        weight_out,
        gain_out.reshape(width),
        value_weight_out.reshape(width),
    )


def solution(mesh):
    rows = P(("groups", "dp"), None, "tensor")
    packed = P(("groups", "dp"), "tensor")
    placed = (rows, rows, rows, rows, P(("groups", "dp"), None), P("groups"), P("groups"))
    placed += (P("tensor", None), P("tensor"), P("tensor"))
    return jax.shard_map(
        on_device,
        mesh=mesh,
        in_specs=placed,
        out_specs=(
            P(("groups", "dp")),
            packed,
            packed,
            packed,
            packed,
            packed,
            P(("groups", "tensor")),
            P(("groups", "tensor")),
        ),
        check_vma=False,
    )
```

```python
import functools
import math

import jax
import jax.numpy as jnp
from jax import lax
from jax.experimental import pallas as pl
from jax.experimental.pallas import tpu as pltpu
from jax.sharding import PartitionSpec as P

H = 40
KVH = 8
HD = 128
RATIO = H // KVH
CAPB = 576
EPS = 1e-06
NEG = -1e30
CW = 256
TAIL = 16
F32 = jnp.float32
BF16 = jnp.bfloat16
VMEM = pl.BlockSpec(memory_space=pltpu.VMEM)
SMEM = pl.BlockSpec(memory_space=pltpu.SMEM)
ANY = pl.BlockSpec(memory_space=pl.ANY)
HBM = pl.BlockSpec(memory_space=pltpu.HBM)


FREE = pl.CostEstimate(flops=0, bytes_accessed=0, transcendentals=0)


def params(mib):
    return pltpu.CompilerParams(vmem_limit_bytes=mib * 1024 * 1024)


def mm(a, b, dims):
    return lax.dot_general(a, b, (dims, ((), ())), preferred_element_type=F32)


def route_kernel(n_dp, per_dev, me_ref, len_ref, bal_ref, pick_ref, start_ref, size_ref, cnt_ref):
    cap = per_dev // n_dp
    me = me_ref[0]
    for d in range(n_dp):
        target = jnp.bitwise_xor(me, d)

        def outgoing(s, count):
            b = bal_ref[target * per_dev + s]
            home = lax.div(b, per_dev)

            @pl.when(home == me)
            def _():
                pick_ref[d * cap + count] = lax.rem(b, per_dev)

            return count + (home == me).astype(jnp.int32)

        lax.fori_loop(0, per_dev, outgoing, jnp.int32(0))
        cnt_ref[d] = jnp.int32(0)

    def incoming(s, run):
        b = bal_ref[me * per_dev + s]
        d = jnp.bitwise_xor(lax.div(b, per_dev), me)
        count = cnt_ref[d]
        size = len_ref[b]
        start_ref[d * cap + count] = run
        size_ref[d * cap + count] = size
        cnt_ref[d] = count + 1
        return run + size

    lax.fori_loop(0, per_dev, incoming, jnp.int32(0))


def route(me, lengths, balance_list, n_dp, per_dev):
    table = jax.ShapeDtypeStruct((per_dev,), jnp.int32)
    return pl.pallas_call(
        functools.partial(route_kernel, n_dp, per_dev),
        out_shape=(table, table, table),
        in_specs=[SMEM] * 3,
        out_specs=(SMEM, SMEM, SMEM),
        scratch_shapes=[pltpu.SMEM((n_dp,), jnp.int32)],
        cost_estimate=FREE,
        name="route",
    )(me, lengths, balance_list)


def gather_kernel(n_dp, cap, seq_len, spans, pick_ref, *refs):
    parts, outs, sems = refs[: len(spans)], refs[len(spans) : -1], refs[-1]
    copies = []
    for d in range(n_dp):
        for i in range(cap):
            row = pick_ref[d * cap + i]
            col = 0
            for p, (part, (lo, hi)) in enumerate(zip(parts, spans)):
                copies.append(
                    pltpu.make_async_copy(
                        part.at[row, :, pl.ds(lo, hi - lo)],
                        outs[d].at[pl.ds(i * seq_len, seq_len), pl.ds(col, hi - lo)],
                        sems.at[d * cap + i, p],
                    )
                )
                copies[-1].start()
                col += hi - lo
    for copy in copies:
        copy.wait()


def gather_rollouts(pick, parts, spans, n_dp):
    per_dev, seq_len = parts[0].shape[:2]
    cap = per_dev // n_dp
    out = jax.ShapeDtypeStruct((cap * seq_len, sum(hi - lo for lo, hi in spans)), BF16)
    return pl.pallas_call(
        functools.partial(gather_kernel, n_dp, cap, seq_len, spans),
        out_shape=(out,) * n_dp,
        in_specs=[SMEM] + [ANY] * len(parts),
        out_specs=(VMEM,) * n_dp,
        scratch_shapes=[pltpu.SemaphoreType.DMA((n_dp * cap, len(parts)))],
        compiler_params=params(60),
        cost_estimate=FREE,
        name="gather_rollouts",
    )(pick, *parts)


def stack_kernel(n_dp, cap, seq_len, lo, hi, me_ref, pick_ref, part, returns, tie, out, order, sems):
    copies = []
    for d in range(n_dp):
        to = jnp.bitwise_xor(me_ref[0], d)
        for i in range(cap):
            copies.append(
                pltpu.make_async_copy(
                    part.at[pick_ref[d * cap + i], :, pl.ds(lo, hi - lo)],
                    out.at[to, pl.ds(i * seq_len, seq_len)],
                    sems.at[d * cap + i],
                )
            )
            copies[-1].start()
    order[0] = jnp.int32(0)
    rows = returns[...].astype(F32)
    at = lax.broadcasted_iota(jnp.int32, rows.shape, 0)
    for d in range(n_dp):
        to = jnp.bitwise_xor(me_ref[0], d)
        picked = [
            jnp.sum(jnp.where(at == pick_ref[d * cap + i], rows, 0.0), axis=0, keepdims=True)
            for i in range(cap)
        ]
        picked.append(jnp.zeros((TAIL - cap, seq_len), F32))
        tail = jnp.concatenate(picked, axis=0).astype(BF16)
        out[to, cap * seq_len :, :] = jnp.concatenate(
            [tail, jnp.zeros((TAIL, hi - lo - seq_len), BF16)], axis=1
        )
    for copy in copies:
        copy.wait()


def stack_rollouts(me, pick, part, span, returns, n_dp, tie):
    per_dev, seq_len = part.shape[:2]
    cap = per_dev // n_dp
    lo, hi = span
    return pl.pallas_call(
        functools.partial(stack_kernel, n_dp, cap, seq_len, lo, hi),
        out_shape=(
            jax.ShapeDtypeStruct((n_dp, cap * seq_len + TAIL, hi - lo), BF16),
            jax.ShapeDtypeStruct((1,), jnp.int32),
        ),
        in_specs=[SMEM, SMEM, ANY, VMEM, ANY],
        out_specs=(VMEM, SMEM),
        scratch_shapes=[pltpu.SemaphoreType.DMA((n_dp * cap,))],
        compiler_params=params(60),
        cost_estimate=FREE,
        name="stack_rollouts",
    )(me, pick, part, returns, tie)


def xor_move(value, d, n_dp):
    return lax.ppermute(value, "dp", [(i, i ^ d) for i in range(n_dp)])


def exchange(blocks, n_dp):
    order = sorted(range(1, n_dp), key=lambda d: d < 2)
    moved = {d: xor_move(blocks[d], d, n_dp) for d in order}
    return [blocks[0]] + [moved[d] for d in range(1, n_dp)]


def pack_kernel(n_dp, cap, seq_len, me_ref, place, ctx_ref, blocks, *refs):
    out, target, ctx_copy, rolled = refs[-4:]
    ctx_copy[...] = ctx_ref[...]
    returned = 0.0
    width = cap * seq_len
    for d in range(n_dp):
        source = jnp.bitwise_xor(me_ref[0], d)
        rolled[d * width : (d + 1) * width, :] = blocks[source, :width, :]
        tail = blocks[source, width:, :seq_len].astype(F32)
        line = jnp.concatenate([tail[i : i + 1, :] for i in range(cap)], axis=1)
        spots = place[:, d * width : (d + 1) * width].astype(F32)
        returned = returned + jnp.sum(spots * line, axis=1, keepdims=True)
    target[...] = returned
    out[...] = mm(place[...], rolled[...], ((1,), (0,))).astype(BF16)


def pack(me, place, blocks, seq_len, cap, context, tie=()):
    n_dp, _, width = blocks.shape
    return pl.pallas_call(
        functools.partial(pack_kernel, n_dp, cap, seq_len),
        out_shape=(
            jax.ShapeDtypeStruct((CAPB, width), BF16),
            jax.ShapeDtypeStruct((CAPB, 1), F32),
            jax.ShapeDtypeStruct(context.shape, BF16),
        ),
        in_specs=[SMEM] + [VMEM] * 3 + [ANY] * len(tie),
        out_specs=(VMEM,) * 3,
        scratch_shapes=[pltpu.VMEM((n_dp * cap * seq_len, width), BF16)],
        compiler_params=params(20),
        cost_estimate=FREE,
        name="pack",
    )(me, place, context, blocks, *tie)


def heads_of(rows, first):
    return jnp.concatenate(
        [rows[:, (first + r) * HD : (first + r + 1) * HD] for r in range(RATIO)], axis=0
    )


def spread_kernel(n_rollout, seq_len, start_ref, size_ref, place, fetch):
    iota = lambda shape, axis: lax.broadcasted_iota(jnp.int32, shape, axis)
    pair = (CAPB, 2 * seq_len)
    lane = iota(pair, 1)
    second = lane >= seq_len
    within = jnp.where(second, lane - seq_len, lane)
    offset = iota(pair, 0) - within
    turned = iota((seq_len, CAPB), 1) - iota((seq_len, CAPB), 0)
    row = iota((seq_len, CAPB), 0)
    for k in range(0, n_rollout, 2):
        first = (offset == start_ref[k]) & (within < size_ref[k]) & ~second
        other = (offset == start_ref[k + 1]) & (within < size_ref[k + 1]) & second
        place[:, k * seq_len : (k + 2) * seq_len] = (first | other).astype(BF16)
        for i in (k, k + 1):
            hit = (turned == start_ref[i]) & (row < size_ref[i])
            fetch[i * seq_len : (i + 1) * seq_len, :] = hit.astype(BF16)


def spread(start, size, seq_len):
    n_rollout = start.shape[0]
    rows = n_rollout * seq_len
    return pl.pallas_call(
        functools.partial(spread_kernel, n_rollout, seq_len),
        out_shape=(
            jax.ShapeDtypeStruct((CAPB, rows), BF16),
            jax.ShapeDtypeStruct((rows, CAPB), BF16),
        ),
        in_specs=[SMEM, SMEM],
        out_specs=(VMEM, VMEM),
        compiler_params=params(16),
        cost_estimate=FREE,
        name="spread",
    )(start, size)


def forward_kernel(first, count, cap, seq_len, kv, chunks, size_ref, place, *refs):
    blocks, refs = refs[:count], refs[count:]
    if first == 0:
        probs_ref, room, rolled = refs[-3:]
    else:
        before, pos_ref, weight, _, out, extra, probs_ref, *part_refs = refs[:-3]
        rolled, columns, sems = refs[-3:]
        fetch = [
            pltpu.make_async_copy(weight.at[:, pl.ds(at, CW)], columns.at[k], sems.at[k])
            for k, (_, at) in enumerate(chunks)
        ]
        for copy in fetch:
            copy.start()
    qw = kv * RATIO * HD
    scale = 1.0 / math.sqrt(HD)
    span = RATIO * seq_len
    at_u = lax.broadcasted_iota(jnp.int32, (seq_len, span), 0)
    at_t = lax.rem(lax.broadcasted_iota(jnp.int32, (seq_len, span), 1), seq_len)
    at_t1 = lax.rem(lax.broadcasted_iota(jnp.int32, (1, span), 1), seq_len)
    causal = at_u <= at_t
    for d in range(count):
        for i in range(cap):
            size = size_ref[(first + d) * cap + i]
            rows = slice(i * seq_len, (i + 1) * seq_len)
            to = slice((d * cap + i) * seq_len, (d * cap + i + 1) * seq_len)
            keep = causal & (at_u < size)
            parts = []
            for g in range(kv):
                queries = heads_of(blocks[d][rows, g * RATIO * HD : (g + 1) * RATIO * HD], 0)
                keys = blocks[d][rows, qw + g * HD : qw + (g + 1) * HD]
                values = blocks[d][rows, qw + (kv + g) * HD : qw + (kv + g + 1) * HD]
                scores = jnp.where(keep, mm(keys, queries, ((1,), (1,))) * scale, NEG)
                top = jnp.max(scores, axis=0, keepdims=True)
                weights = jnp.exp(scores - top)
                total = jnp.sum(weights, axis=0, keepdims=True)
                probs = (weights * jnp.where(at_t1 < size, 1.0 / total, 0.0)).astype(BF16)
                probs_ref[d * cap + i, g] = probs
                mixed = mm(probs, values, ((0,), (0,)))
                parts += [mixed[r * seq_len : (r + 1) * seq_len] for r in range(RATIO)]
            rolled[to, :qw] = jnp.concatenate(parts, axis=1).astype(BF16)
            rolled[to, qw:] = blocks[d][rows, qw + 2 * kv * HD :]
    packed = mm(place[:, first * cap * seq_len : (first + count) * cap * seq_len], rolled[...], ((1,), (0,)))
    if first == 0:
        room[...] = packed
    else:
        packed = packed + before[...]
        mixed = packed[:, :qw].astype(BF16)
        beside = packed[:, qw:]
        out[...] = mixed
        extra[...] = beside.astype(BF16)
        for k, (j, _) in enumerate(chunks):
            fetch[k].wait()
            own = jnp.where(pos_ref[1] == j, beside, 0.0)
            part = jnp.dot(mixed, columns[k], preferred_element_type=F32)
            part_refs[k][...] = (part + own).astype(BF16)


def attention_forward(size, place, blocks, kv, seq_len, cap, ahead, pos, out_weight, chunks, between):
    n_dp = len(blocks)
    half = n_dp // 2
    width = kv * RATIO * HD
    extra = blocks[0].shape[1] - width - 2 * kv * HD
    shape = jax.ShapeDtypeStruct
    probs = shape((half * cap, kv, seq_len, RATIO * seq_len), BF16)
    rolled = pltpu.VMEM((half * cap * seq_len, width + extra), BF16)
    call = lambda first, outs, scratch, specs, more: pl.pallas_call(
        functools.partial(forward_kernel, first, half, cap, seq_len, kv, chunks),
        out_shape=outs,
        in_specs=[SMEM] + [VMEM] * (1 + half) + specs,
        out_specs=(VMEM,) * len(outs),
        scratch_shapes=scratch,
        compiler_params=params(52),
        cost_estimate=FREE,
        name="attention_forward",
    )(size, place, *blocks[first : first + half], *more)
    probs_low, room = call(
        0, (probs, shape((CAPB, width + extra), F32)), [rolled], [ANY] * len(ahead), ahead
    )
    tie = between(blocks[half])
    context, beside, probs_high, *parts = call(
        half,
        (shape((CAPB, width), BF16), shape((CAPB, extra), BF16), probs)
        + (shape((CAPB, CW), BF16),) * len(chunks),
        [
            rolled,
            pltpu.VMEM((max(1, len(chunks)), width, CW), BF16),
            pltpu.SemaphoreType.DMA((max(1, len(chunks)),)),
        ],
        [VMEM, SMEM, ANY, SMEM],
        (room, pos, out_weight, tie),
    )
    return context, beside, (probs_low, probs_high), parts


def backward_kernel(n_dp, cap, seq_len, kv, place, fetch, a_ref, b_ref, wgw_ref, acc_ref, *refs):
    all_probs, refs = refs[:2], refs[2:]
    blocks = refs[:n_dp]
    dq_out, dk_out, dv_out, grads, dq_all, dk_all, dv_all = refs[n_dp:]
    half = n_dp // 2
    qw = kv * RATIO * HD
    scale = 1.0 / math.sqrt(HD)
    packed = (a_ref[...] * wgw_ref[...] - b_ref[...] * acc_ref[...]).astype(BF16)
    grads[...] = mm(fetch[...], packed, ((1,), (0,))).astype(BF16)
    for d in range(n_dp):
        for i in range(cap):
            rows = slice(i * seq_len, (i + 1) * seq_len)
            to = slice((d * cap + i) * seq_len, (d * cap + i + 1) * seq_len)
            dq_parts, dk_parts, dv_parts = [], [], []
            for g in range(kv):
                cols = slice(g * RATIO * HD, (g + 1) * RATIO * HD)
                queries = heads_of(blocks[d][rows, cols], 0)
                keys = blocks[d][rows, qw + g * HD : qw + (g + 1) * HD]
                values = blocks[d][rows, qw + (kv + g) * HD : qw + (kv + g + 1) * HD]
                out_grad = heads_of(grads[to, cols], 0)
                probs_low = all_probs[d // half][d % half * cap + i, g]
                probs = probs_low.astype(F32)
                prob_grad = mm(values, out_grad, ((1,), (1,)))
                row_dot = jnp.sum(probs * prob_grad, axis=0, keepdims=True)
                score_grad = (probs * (prob_grad - row_dot) * scale).astype(BF16)
                dq = mm(score_grad, keys, ((0,), (0,)))
                dq_parts += [dq[r * seq_len : (r + 1) * seq_len] for r in range(RATIO)]
                dk_parts.append(mm(score_grad, queries, ((1,), (0,))))
                dv_parts.append(mm(probs_low, out_grad, ((1,), (0,))))
            for kept, parts in ((dq_all, dq_parts), (dk_all, dk_parts), (dv_all, dv_parts)):
                kept[to, :] = jnp.concatenate(parts, axis=1).astype(BF16)
    for out, kept in ((dq_out, dq_all), (dk_out, dk_all), (dv_out, dv_all)):
        out[...] = mm(place[...], kept[...], ((1,), (0,))).astype(BF16)


def attention_backward(place, fetch, a, b, wgw, acc, probs, blocks, kv, seq_len, cap):
    n_dp = len(blocks)
    qw, kw = kv * RATIO * HD, kv * HD
    rows = n_dp * cap * seq_len
    return pl.pallas_call(
        functools.partial(backward_kernel, n_dp, cap, seq_len, kv),
        out_shape=tuple(jax.ShapeDtypeStruct((CAPB, w), BF16) for w in (qw, kw, kw)),
        in_specs=[VMEM] * (8 + n_dp),
        out_specs=(VMEM,) * 3,
        scratch_shapes=[pltpu.VMEM((rows, w), BF16) for w in (qw, qw, kw, kw)],
        compiler_params=params(60),
        cost_estimate=FREE,
        name="attention_backward",
    )(place, fetch, a, b, wgw, acc, *probs, *blocks)


def select(index, options):
    out = options[0]
    for k in range(1, len(options)):
        out = jnp.where(index == k, options[k], out)
    return out


def bundle_kernel(n_blk, *refs):
    pieces, out = refs[: n_blk * 2], refs[-1]
    for j in range(n_blk):
        for k in range(2):
            out[j, :, k * CW : (k + 1) * CW] = pieces[j * 2 + k][...]


def bundle_pieces(pieces, tie):
    n_blk = len(pieces) // 2
    return pl.pallas_call(
        functools.partial(bundle_kernel, n_blk),
        out_shape=jax.ShapeDtypeStruct((n_blk, CAPB, 2 * CW), BF16),
        in_specs=[VMEM] * len(pieces) + [ANY] * len(tie),
        out_specs=VMEM,
        compiler_params=params(16),
        cost_estimate=FREE,
        name="bundle_pieces",
    )(*pieces, *tie)


def products(starts, n_cols, col, weight, gw_ref, piece, before, acc, sq, vd, own, columns, sems):
    n_blk = len(starts)
    cut = lambda j: slice(j * n_cols, (j + 1) * n_cols)
    fetch = [
        pltpu.make_async_copy(
            weight.at[:, pl.ds(at, n_cols)], columns.at[:, pl.ds(j * n_cols, n_cols)], sems.at[j]
        )
        for j, at in enumerate(starts)
    ]
    for copy in fetch:
        copy.start()
    tile = CAPB // 9
    for t in range(CAPB // tile):
        rows = slice(t * tile, (t + 1) * tile)
        pieces = [piece(j, rows) for j in range(n_blk)]
        own[rows, :] = select(col, pieces)
        squares = 0.0 if before is None else before[1][rows, :]
        dots = 0.0 if before is None else before[2][rows, :]
        for j, part in enumerate(pieces):
            wide = part.astype(F32)
            gain = gw_ref[:, starts[j] : starts[j] + n_cols]
            squares = squares + jnp.sum(wide * wide, axis=1, keepdims=True)
            dots = dots + jnp.sum(wide * gain, axis=1, keepdims=True)
        sq[rows, :] = squares
        vd[rows, :] = dots
    for copy in fetch:
        copy.wait()
    left = jnp.concatenate([piece(j, slice(0, CAPB)) for j in range(n_blk)], axis=1)
    total = mm(left, columns[...], ((1,), (1,)))
    acc[...] = total if before is None else total + before[0][...]


def rows_kernel(starts, n_cols, first, n_tie, pos_ref, weight, gw_ref, bundle, *refs):
    before, refs = (None, refs) if first else (refs[:3], refs[3:])
    piece = lambda j, rows: bundle[j, rows, :]
    products(starts, n_cols, pos_ref[1], weight, gw_ref, piece, before, *refs[n_tie:])


def row_products(pos, out_weight, gw_row, bundle, first_col, width, state, tie):
    n_blk, _, n_cols = bundle.shape
    depth = out_weight.shape[0]
    starts = [j * width + first_col for j in range(n_blk)]
    shape = jax.ShapeDtypeStruct
    column = shape((CAPB, 1), F32)
    before = [] if state is None else list(state)
    return pl.pallas_call(
        functools.partial(rows_kernel, starts, n_cols, state is None, len(tie)),
        out_shape=(shape((CAPB, depth), F32), column, column, shape((CAPB, n_cols), BF16)),
        in_specs=[SMEM, ANY] + [VMEM] * (2 + len(before)) + [ANY] * len(tie),
        out_specs=(VMEM,) * 4,
        scratch_shapes=[
            pltpu.VMEM((depth, n_blk * n_cols), BF16),
            pltpu.SemaphoreType.DMA((n_blk,)),
        ],
        compiler_params=params(52),
        cost_estimate=FREE,
        name="row_products",
    )(pos, out_weight, gw_row, bundle, *before, *tie)


def row_of(column):
    return jnp.transpose(jnp.broadcast_to(column, (column.shape[0], 128)))[0:1, :]


def column_of(row):
    return jnp.transpose(jnp.broadcast_to(row, (128, row.shape[1])))[:, 0:1]


def norm_grads(model_width, sq, vd, target, gw_ref, ctx_ref, owns, outs):
    resid_out, sums, critic_row, a_col, b_col = outs
    inv_rms = lax.rsqrt(sq / model_width + EPS)
    critic = inv_rms * vd
    err = critic - target
    a = inv_rms * err
    b = inv_rms * inv_rms * inv_rms * err * vd / model_width
    a_col[...] = a
    b_col[...] = b
    critic_row[...] = row_of(critic)
    sums[...] = jnp.zeros_like(sums)
    sums[2:3, :CAPB] = row_of(b)
    at = 0
    for own in owns:
        cols = slice(at, at + own.shape[1])
        at += own.shape[1]
        hidden = own[...].astype(F32)
        resid_out[:, cols] = (a * gw_ref[:, cols] - b * hidden).astype(BF16)
        sums[0:1, cols] = jnp.sum(a * hidden, axis=0, keepdims=True)
    sums[1:2, :] = jnp.sum(a * ctx_ref[...].astype(F32), axis=0, keepdims=True)


def norm_shapes(width):
    shape = jax.ShapeDtypeStruct
    column = shape((CAPB, 1), F32)
    return (shape((CAPB, width), BF16), shape((8, width), F32), shape((1, CAPB), F32), column, column)


def last_kernel(starts, model_width, n_own, n_tie, pos_ref, weight, gw_ref, gw_own, ctx, target, *refs):
    n_blk = len(starts)
    pieces, refs = refs[:n_blk], refs[n_blk:]
    before, owns, refs = refs[:3], refs[3 : 3 + n_own], refs[3 + n_own + n_tie :]
    acc, pays, outs, refs = refs[0], refs[1], refs[2:7], refs[7:]
    sq, vd, own, columns, sems = refs
    for j in range(n_blk):
        pays[j] = pieces[j][...]
    piece = lambda j, rows: pieces[j][rows, :]
    products(
        starts, CW, pos_ref[1], weight, gw_ref, piece, before, acc, sq, vd, own, columns, sems
    )
    norm_grads(model_width, sq[...], vd[...], target[...], gw_own, ctx, (*owns, own), outs)


def last_products(
    pos, out_weight, gw_row, gw_own, context, target, pieces, first_col, state, owns, tie
):
    n_blk = len(pieces)
    depth, model_width = out_weight.shape
    width = context.shape[1]
    starts = [j * width + first_col for j in range(n_blk)]
    shape = jax.ShapeDtypeStruct
    return pl.pallas_call(
        functools.partial(last_kernel, starts, model_width, len(owns), len(tie)),
        out_shape=(shape((CAPB, depth), F32), shape((n_blk, CAPB, CW), BF16)) + norm_shapes(width),
        in_specs=[SMEM, ANY] + [VMEM] * (4 + n_blk + 3 + len(owns)) + [ANY] * len(tie),
        out_specs=(VMEM,) * 7,
        scratch_shapes=[
            pltpu.VMEM((CAPB, 1), F32),
            pltpu.VMEM((CAPB, 1), F32),
            pltpu.VMEM((CAPB, CW), BF16),
            pltpu.VMEM((depth, n_blk * CW), BF16),
            pltpu.SemaphoreType.DMA((n_blk,)),
        ],
        compiler_params=params(52),
        cost_estimate=FREE,
        name="last_products",
    )(pos, out_weight, gw_row, gw_own, context, target, *pieces, *state, *owns, *tie)


def finish_kernel(model_width, sq, vd, target, gw_ref, ctx_ref, own, *outs):
    norm_grads(model_width, sq[...], vd[...], target[...], gw_ref, ctx_ref, (own,), outs)


def finish(sq, vd, target, gw_own, context, own, model_width):
    return pl.pallas_call(
        functools.partial(finish_kernel, model_width),
        out_shape=norm_shapes(context.shape[1]),
        in_specs=[VMEM] * 6,
        out_specs=(VMEM,) * 5,
        compiler_params=params(32),
        cost_estimate=FREE,
        name="finish",
    )(sq, vd, target, gw_own, context, own)


def paired_sum(terms):
    while len(terms) > 1:
        terms = [terms[k] + terms[k + 1] for k in range(0, len(terms), 2)]
    return terms[0]


def weight_kernel(n_dp, spans, pos_ref, gw_ref, norm_gain, value_weight, *refs):
    n_piece = len(spans)
    sums, (ctx_hbm,) = refs[:n_dp], refs[n_dp : n_dp + 1]
    pieces = refs[n_dp + 1 : n_dp + 1 + n_piece]
    out, gain_out, value_out, *refs = refs[n_dp + 1 + n_piece :]
    ctx, held, made, ctx_sems, in_sems, out_sems = refs
    me = pos_ref[0]
    gain_sum = paired_sum([s[0:1, :] for s in sums])
    context_sum = paired_sum([s[1:2, :] for s in sums])
    for ref, row in ((gain_out, value_weight[...] * gain_sum), (value_out, norm_gain[...] * gain_sum)):
        ref[...] = jnp.concatenate([row[:, k * 128 : (k + 1) * 128] for k in range(ref.shape[0])], axis=0)
    rows_of = lambda d: pl.ds(pl.multiple_of(jnp.bitwise_xor(me, d) * CAPB, CAPB), CAPB)
    ctx_in = [
        pltpu.make_async_copy(ctx_hbm.at[rows_of(d)], ctx.at[rows_of(d)], ctx_sems.at[d])
        for d in range(n_dp)
    ]
    piece_in = [
        pltpu.make_async_copy(pieces[r], held.at[:, pl.ds(lo, hi - lo)], in_sems.at[r])
        for r, (lo, hi) in enumerate(spans)
    ]
    for copy in ctx_in + piece_in:
        copy.start()
    for d in range(n_dp):
        ctx_in[d].wait()
        factor = column_of(sums[d][2:3, :CAPB])
        rows = rows_of(d)
        ctx[rows, :] = (factor * ctx[rows, :].astype(F32)).astype(BF16)
    store, arrived = [], 0
    step = made.shape[1]
    for t in range(spans[-1][1] // step):
        lo, hi = t * step, (t + 1) * step
        while arrived < n_piece and spans[arrived][0] < hi:
            piece_in[arrived].wait()
            arrived += 1
        if t >= 2:
            store[t - 2].wait()
        rank_one = gw_ref[lo:hi, :] * context_sum
        made[t % 2] = rank_one - mm(held[:, lo:hi], ctx[...], ((0,), (0,)))
        store.append(
            pltpu.make_async_copy(made.at[t % 2], out.at[pl.ds(lo, step)], out_sems.at[t % 2])
        )
        store[t].start()
    for copy in store[-2:]:
        copy.wait()


def weight_grad(pos, gw_col, norm_gain, value_weight, sums, contexts, pieces):
    n_dp = len(sums)
    width = contexts.shape[1]
    rows = pieces[0].shape[0]
    spans, at = [], 0
    for piece in pieces:
        spans.append((at, at + piece.shape[1]))
        at += piece.shape[1]
    step = CW if at % CW == 0 else at
    return pl.pallas_call(
        functools.partial(weight_kernel, n_dp, spans),
        out_shape=(
            jax.ShapeDtypeStruct((at, width), F32),
            jax.ShapeDtypeStruct((width // 128, 128), F32),
            jax.ShapeDtypeStruct((width // 128, 128), F32),
        ),
        in_specs=[SMEM] + [VMEM] * (3 + n_dp) + [ANY] * (1 + len(pieces)),
        out_specs=(ANY, VMEM, VMEM),
        scratch_shapes=[
            pltpu.VMEM(contexts.shape, BF16),
            pltpu.VMEM((rows, at), BF16),
            pltpu.VMEM((2, step, width), F32),
            pltpu.SemaphoreType.DMA((n_dp,)),
            pltpu.SemaphoreType.DMA((len(pieces),)),
            pltpu.SemaphoreType.DMA((2,)),
        ],
        compiler_params=params(60),
        cost_estimate=FREE,
        name="weight_grad",
    )(pos, gw_col, norm_gain, value_weight, *sums, contexts, *pieces)


def parts_kernel(chunks, resid_cols, pos_ref, context, weight, resid, *refs):
    outs, columns, sems = refs[-len(chunks) - 2 : -2], refs[-2], refs[-1]
    fetch = [
        pltpu.make_async_copy(weight.at[:, pl.ds(at, CW)], columns.at[k], sems.at[k])
        for k, (_, at) in enumerate(chunks)
    ]
    for copy in fetch:
        copy.start()
    for k, (j, _) in enumerate(chunks):
        fetch[k].wait()
        part = jnp.dot(context[...], columns[k], preferred_element_type=F32)
        own = jnp.where(pos_ref[1] == j, resid[:, resid_cols].astype(F32), 0.0)
        outs[k][...] = (part + own).astype(BF16)


def partial_sums(pos, context, out_weight, resid, at, chunks, tie):
    piece = jax.ShapeDtypeStruct((CAPB, CW), BF16)
    n = len(chunks)
    return pl.pallas_call(
        functools.partial(parts_kernel, chunks, slice(at * CW, (at + 1) * CW)),
        out_shape=(piece,) * n,
        in_specs=[SMEM, VMEM, ANY, VMEM] + [ANY] * len(tie),
        out_specs=(VMEM,) * n,
        scratch_shapes=[
            pltpu.VMEM((n, out_weight.shape[0], CW), BF16),
            pltpu.SemaphoreType.DMA((n,)),
        ],
        compiler_params=params(52),
        cost_estimate=FREE,
        name="partial_sums",
    )(pos, context, out_weight, resid, *tie)


def step_kernel(part, joins, totals, ends, n_tie, pos_ref, *refs):
    refs = list(refs)
    take = lambda n=1: [refs.pop(0) for _ in range(n)]
    mid = pos_ref[2] == 1
    add = lambda a, b: (a[...].astype(F32) + b[...].astype(F32)).astype(BF16)
    (new,) = take() if part else (None,)
    pair = take(2) if joins else None
    halves = take(2) if totals else None
    last = take(2) if ends else None
    take(n_tie)
    if joins:
        take()[0][...] = add(*pair)
    if totals:
        total = add(*halves)
        take()[0][...] = total if new is None else jnp.where(mid, total, new[...])
    if ends:
        take()[0][...] = jnp.where(mid, last[0][...], last[1][...])


def line_sum(context, resid_of, out_weight, pos, order, first_parts, after_step):
    edge = [(0, 1), (1, 0), (2, 3), (3, 2)]
    middle = [(1, 2), (2, 1)]
    width = context.shape[1]
    n, n_blk = len(order), 4
    piece = jax.ShapeDtypeStruct((CAPB, CW), BF16)
    parts, joined, from_edge, from_mid, payloads = dict(enumerate(first_parts)), {}, {}, {}, {}
    hidden = {}

    def make_parts(first, count, tie):
        r = order[first][1]
        resid, at = resid_of(r)
        chunks = [(j, j * width + r * CW) for j, _ in order[first : first + count]]
        made = partial_sums(pos, context, out_weight, resid, at, chunks, tie)
        parts.update(zip(range(first, first + count), made))

    for s in (0, 1):
        payloads[s] = parts[s]
        from_edge[s] = lax.ppermute(parts[s], "tensor", edge)
    make_parts(2, 2, (parts[1],))
    tie = (parts[3],)
    for s in range(n + 4):
        joins, totals, ends = s < n, 2 <= s < n + 2, s >= 4
        part = totals and s + 2 < n
        outs, args = {}, [pos]
        if part:
            args.append(parts[s + 2])
        if joins:
            args += [parts[s], from_edge[s]]
            outs["joined"] = piece
        if totals:
            args += [joined[s - 2], from_mid[s - 2]]
            outs["payload"] = piece
        if ends:
            args += [payloads[s], from_edge[s]]
            outs["hidden"] = piece
        made = pl.pallas_call(
            functools.partial(step_kernel, part, joins, totals, ends, len(tie)),
            out_shape=tuple(outs.values()),
            in_specs=[SMEM] + [VMEM] * (len(args) - 1) + [ANY] * len(tie),
            out_specs=(VMEM,) * len(outs),
            compiler_params=params(16),
            cost_estimate=FREE,
            name="line_step",
        )(*args, *tie)
        made = dict(zip(outs, made))
        tie = (next(iter(made.values())),)
        if joins:
            joined[s] = made["joined"]
            from_mid[s] = lax.ppermute(joined[s], "tensor", middle)
        if s + 2 < n + 4:
            payloads[s + 2] = made["payload"] if totals else parts[s + 2]
            from_edge[s + 2] = lax.ppermute(payloads[s + 2], "tensor", edge)
        if ends:
            hidden[order[s - 4]] = made["hidden"]
        tie = after_step(s, hidden, tie)
        if s % 2 == 0 and s + n_blk < n:
            make_parts(s + n_blk, 2, tie)


def on_device(
    query_states,
    key_states,
    value_states,
    residual,
    returns,
    lengths,
    balance_list,
    out_weight,
    norm_gain,
    value_weight,
):
    n_dp, n_tensor = lax.axis_size("dp"), lax.axis_size("tensor")
    me, col = lax.axis_index("dp"), lax.axis_index("tensor")
    per_dev = query_states.shape[0]
    width = query_states.shape[2]
    model_width = out_weight.shape[1]
    kv = key_states.shape[2] // HD

    seq_len = query_states.shape[1]
    cap = per_dev // n_dp
    first = CW if width > CW else width
    pick, start, size = route(me.reshape(1), lengths, balance_list, n_dp, per_dev)
    sent = gather_rollouts(
        pick,
        (query_states, key_states, value_states, residual),
        ((0, width), (0, kv * HD), (0, kv * HD), (0, first)),
        n_dp,
    )
    blocks = exchange(sent, n_dp)
    place, fetch = spread(start, size, seq_len)
    gw_own = norm_gain * value_weight
    gw = lax.all_gather(gw_own, "tensor", axis=0, tiled=True)
    gw_high = gw.astype(BF16)
    gw_low = (gw - gw_high.astype(F32)).astype(BF16)
    pair = jnp.stack([gw_high, gw_low])
    wgw = jnp.sum(mm(pair, out_weight, ((1,), (1,))), axis=0, keepdims=True)
    block = model_width // n_dp
    gw_col = lax.dynamic_slice_in_dim(gw, me * block, block).reshape(block, 1)
    is_mid = (col == 1) | (col == 2)
    pos = jnp.stack([me, col, is_mid.astype(jnp.int32)]).astype(jnp.int32)
    on_line = n_tensor == 4 and n_dp == 4
    per_block = width // CW
    order = [(j, r) for r in range(per_block) for j in (1, 2, 0, 3)]
    chunks = tuple((j, j * width + r * CW) for j, r in order[:2]) if on_line else ()
    later = {}

    def between(tie):
        later["rest"], order_after = stack_rollouts(
            me.reshape(1), pick, residual, (first, width), returns, n_dp, tie
        )
        return order_after

    context, resid_first, probs, parts = attention_forward(
        size, place, blocks, kv, seq_len, cap, (wgw, gw_col), pos, out_weight, chunks, between
    )
    rest = lax.all_to_all(later["rest"], "dp", split_axis=0, concat_axis=0, tiled=True)
    gw_row, gw_mine = gw.reshape(1, model_width), gw_own.reshape(1, width)

    if on_line:
        bundles, owns, pieces = [], [], []

        def move(bundle):
            moved = lax.all_to_all(bundle, "dp", split_axis=0, concat_axis=0, tiled=True)
            pieces.append(moved.reshape(n_dp * CAPB, bundle.shape[2]))

        def after_step(s, hidden, tie):
            if s == 0:
                later["resid"], later["target"], later["context"] = pack(
                    me.reshape(1), place, rest, seq_len, cap, context, tie
                )
            if s in (11, 19):
                r = 2 * len(bundles)
                pair = [hidden[j, k] for j in range(n_tensor) for k in (r, r + 1)]
                bundles.append(bundle_pieces(pair, tie))
                move(bundles[-1])
                return (bundles[-1],)
            if s in (14, 21):
                k = len(owns)
                *later["state"], own = row_products(
                    pos, out_weight, gw_row, bundles[k], 2 * CW * k, width, later.get("state"), tie
                )
                owns.append(own)
                return (own,)
            if s == 17:
                return tie + (pieces[0],)
            if s == len(order) + 3:
                later["last"] = [hidden[j, per_block - 1] for j in range(n_tensor)]
            return tie

        line_sum(
            context,
            lambda r: (resid_first, 0) if r == 0 else (later["resid"], r - 1),
            out_weight,
            pos,
            order,
            parts,
            after_step,
        )
        acc, pays, resid_out, sums, critic_row, a, b = last_products(
            pos,
            out_weight,
            gw_row,
            gw_mine,
            context,
            later["target"],
            later["last"],
            4 * CW,
            later["state"],
            owns,
            (pieces[1],),
        )
        move(pays)
        contexts = lax.all_gather(later["context"], "dp", axis=0, tiled=True)
    else:
        resid_rest, target, _ = pack(me.reshape(1), place, rest, seq_len, cap, context)
        contexts = lax.all_gather(context, "dp", axis=0, tiled=True)
        resid = jnp.concatenate([resid_first, resid_rest], axis=1)
        part = jnp.dot(context, out_weight, preferred_element_type=F32)
        mine = lax.dynamic_slice_in_dim(part, col * width, width, axis=1) + resid.astype(F32)
        part = lax.dynamic_update_slice_in_dim(part, mine, col * width, axis=1)
        hidden = lax.psum(part.astype(BF16), "tensor")
        wide = hidden.astype(F32)
        sq = jnp.sum(wide * wide, axis=1, keepdims=True)
        vd = jnp.sum(wide * gw[None, :], axis=1, keepdims=True)
        acc = mm(hidden, out_weight, ((1,), (1,)))
        own = lax.dynamic_slice_in_dim(hidden, col * width, width, axis=1)
        pieces = [lax.all_to_all(hidden, "dp", split_axis=1, concat_axis=0, tiled=True)]
        resid_out, sums, critic_row, a, b = finish(
            sq, vd, target, gw_mine, context, own, model_width
        )

    all_sums = [sums] + [xor_move(sums, d, n_dp) for d in range(1, n_dp)]
    query_out, key_out, value_out = attention_backward(
        place, fetch, a, b, wgw, acc, probs, blocks, kv, seq_len, cap
    )
    weight_out, gain_out, value_weight_out = weight_grad(
        pos,
        gw_col,
        norm_gain.reshape(1, width),
        value_weight.reshape(1, width),
        all_sums,
        contexts,
        pieces,
    )
    return (
        critic_row.reshape(CAPB).astype(BF16),
        query_out,
        key_out,
        value_out,
        resid_out,
        weight_out,
        gain_out.reshape(width),
        value_weight_out.reshape(width),
    )


def solution(mesh):
    rows = P(("groups", "dp"), None, "tensor")
    packed = P(("groups", "dp"), "tensor")
    placed = (rows, rows, rows, rows, P(("groups", "dp"), None), P("groups"), P("groups"))
    placed += (P("tensor", None), P("tensor"), P("tensor"))
    return jax.shard_map(
        on_device,
        mesh=mesh,
        in_specs=placed,
        out_specs=(
            P(("groups", "dp")),
            packed,
            packed,
            packed,
            packed,
            packed,
            P(("groups", "tensor")),
            P(("groups", "tensor")),
        ),
        check_vma=False,
    )
```

```python
import functools
import math

import jax
import jax.numpy as jnp
from jax import lax
from jax.experimental import pallas as pl
from jax.experimental.pallas import tpu as pltpu
from jax.sharding import PartitionSpec as P

H = 40
KVH = 8
HD = 128
RATIO = H // KVH
CAPB = 576
EPS = 1e-06
NEG = -1e30
CW = 256
TAIL = 16
F32 = jnp.float32
BF16 = jnp.bfloat16
VMEM = pl.BlockSpec(memory_space=pltpu.VMEM)
SMEM = pl.BlockSpec(memory_space=pltpu.SMEM)
ANY = pl.BlockSpec(memory_space=pl.ANY)
HBM = pl.BlockSpec(memory_space=pltpu.HBM)


def params(mib):
    return pltpu.CompilerParams(vmem_limit_bytes=mib * 1024 * 1024)


def mm(a, b, dims):
    return lax.dot_general(a, b, (dims, ((), ())), preferred_element_type=F32)


def route_kernel(n_dp, per_dev, me_ref, len_ref, bal_ref, pick_ref, start_ref, size_ref, cnt_ref):
    cap = per_dev // n_dp
    me = me_ref[0]
    for d in range(n_dp):
        target = jnp.bitwise_xor(me, d)

        def outgoing(s, count):
            b = bal_ref[target * per_dev + s]
            home = lax.div(b, per_dev)

            @pl.when(home == me)
            def _():
                pick_ref[d * cap + count] = lax.rem(b, per_dev)

            return count + (home == me).astype(jnp.int32)

        lax.fori_loop(0, per_dev, outgoing, jnp.int32(0))
        cnt_ref[d] = jnp.int32(0)

    def incoming(s, run):
        b = bal_ref[me * per_dev + s]
        d = jnp.bitwise_xor(lax.div(b, per_dev), me)
        count = cnt_ref[d]
        size = len_ref[b]
        start_ref[d * cap + count] = run
        size_ref[d * cap + count] = size
        cnt_ref[d] = count + 1
        return run + size

    lax.fori_loop(0, per_dev, incoming, jnp.int32(0))


def route(me, lengths, balance_list, n_dp, per_dev):
    table = jax.ShapeDtypeStruct((per_dev,), jnp.int32)
    return pl.pallas_call(
        functools.partial(route_kernel, n_dp, per_dev),
        out_shape=(table, table, table),
        in_specs=[SMEM] * 3,
        out_specs=(SMEM, SMEM, SMEM),
        scratch_shapes=[pltpu.SMEM((n_dp,), jnp.int32)],
        name="route",
    )(me, lengths, balance_list)


def gather_kernel(cap, seq_len, outputs, n_part, pick_ref, *refs):
    parts, returns, outs, sems = refs[:n_part], refs[n_part], refs[-1 - len(outputs) : -1], refs[-1]
    copies = []
    for (d, spans, _), out in zip(outputs, outs):
        for i in range(cap):
            row = pick_ref[d * cap + i]
            col = 0
            for p, lo, hi in spans:
                copies.append(
                    pltpu.make_async_copy(
                        parts[p].at[row, :, pl.ds(lo, hi - lo)],
                        out.at[pl.ds(i * seq_len, seq_len), pl.ds(col, hi - lo)],
                        sems.at[len(copies)],
                    )
                )
                copies[-1].start()
                col += hi - lo
    for (d, _, at), out in zip(outputs, outs):
        if at is not None:
            rows = returns[...].astype(F32)
            home = lax.broadcasted_iota(jnp.int32, rows.shape, 0)
            picked = [
                jnp.sum(jnp.where(home == pick_ref[d * cap + i], rows, 0.0), axis=0, keepdims=True)
                for i in range(cap)
            ]
            picked.append(jnp.zeros((TAIL - cap, seq_len), F32))
            tail = jnp.concatenate(picked, axis=0).astype(BF16)
            out[cap * seq_len :, :] = jnp.zeros((TAIL, out.shape[1]), BF16)
            out[cap * seq_len :, at : at + seq_len] = tail
    for copy in copies:
        copy.wait()


def gather_rollouts(pick, parts, returns, outputs, n_dp, tie=()):
    per_dev, seq_len = parts[0].shape[:2]
    cap = per_dev // n_dp
    shapes = [
        (cap * seq_len + (0 if at is None else TAIL), sum(hi - lo for _, lo, hi in spans))
        for _, spans, at in outputs
    ]
    n_copy = sum(cap * len(spans) for _, spans, _ in outputs)
    return pl.pallas_call(
        functools.partial(gather_kernel, cap, seq_len, outputs, len(parts)),
        out_shape=tuple(jax.ShapeDtypeStruct(shape, BF16) for shape in shapes),
        in_specs=[SMEM] + [ANY] * len(parts) + [VMEM] + [ANY] * len(tie),
        out_specs=(VMEM,) * len(outputs),
        scratch_shapes=[pltpu.SemaphoreType.DMA((n_copy,))],
        compiler_params=params(60),
        name="gather_rollouts",
    )(pick, *parts, returns, *tie)


def xor_move(value, d, n_dp):
    return lax.ppermute(value, "dp", [(i, i ^ d) for i in range(n_dp)])


def pack_kernel(n_dp, cap, seq_len, cols, place, ctx_ref, *refs):
    blocks = refs[:n_dp]
    out, target, ctx_copy, rolled = refs[-4:]
    ctx_copy[...] = ctx_ref[...]
    returned = 0.0
    width = cap * seq_len
    for d in range(n_dp):
        lo = cols[d]
        rolled[d * width : (d + 1) * width, :] = blocks[d][:width, lo:]
        tail = blocks[d][width:, lo : lo + seq_len].astype(F32)
        line = jnp.concatenate([tail[i : i + 1, :] for i in range(cap)], axis=1)
        spots = place[:, d * width : (d + 1) * width].astype(F32)
        returned = returned + jnp.sum(spots * line, axis=1, keepdims=True)
    target[...] = returned
    out[...] = mm(place[...], rolled[...], ((1,), (0,))).astype(BF16)


def pack(place, blocks, cols, seq_len, cap, context, tie=()):
    n_dp = len(blocks)
    width = blocks[-1].shape[1] - cols[-1]
    return pl.pallas_call(
        functools.partial(pack_kernel, n_dp, cap, seq_len, cols),
        out_shape=(
            jax.ShapeDtypeStruct((CAPB, width), BF16),
            jax.ShapeDtypeStruct((CAPB, 1), F32),
            jax.ShapeDtypeStruct(context.shape, BF16),
        ),
        in_specs=[VMEM] * (2 + n_dp) + [ANY] * len(tie),
        out_specs=(VMEM,) * 3,
        scratch_shapes=[pltpu.VMEM((n_dp * cap * seq_len, width), BF16)],
        compiler_params=params(24),
        name="pack",
    )(place, context, *blocks, *tie)


def heads_of(rows, first):
    return jnp.concatenate(
        [rows[:, (first + r) * HD : (first + r + 1) * HD] for r in range(RATIO)], axis=0
    )


def spread_kernel(n_rollout, seq_len, start_ref, size_ref, place, fetch):
    iota = lambda shape, axis: lax.broadcasted_iota(jnp.int32, shape, axis)
    pair = (CAPB, 2 * seq_len)
    lane = iota(pair, 1)
    second = lane >= seq_len
    within = jnp.where(second, lane - seq_len, lane)
    offset = iota(pair, 0) - within
    turned = iota((seq_len, CAPB), 1) - iota((seq_len, CAPB), 0)
    row = iota((seq_len, CAPB), 0)
    for k in range(0, n_rollout, 2):
        first = (offset == start_ref[k]) & (within < size_ref[k]) & ~second
        other = (offset == start_ref[k + 1]) & (within < size_ref[k + 1]) & second
        place[:, k * seq_len : (k + 2) * seq_len] = (first | other).astype(BF16)
        for i in (k, k + 1):
            hit = (turned == start_ref[i]) & (row < size_ref[i])
            fetch[i * seq_len : (i + 1) * seq_len, :] = hit.astype(BF16)


def spread(start, size, seq_len):
    n_rollout = start.shape[0]
    rows = n_rollout * seq_len
    return pl.pallas_call(
        functools.partial(spread_kernel, n_rollout, seq_len),
        out_shape=(
            jax.ShapeDtypeStruct((CAPB, rows), BF16),
            jax.ShapeDtypeStruct((rows, CAPB), BF16),
        ),
        in_specs=[SMEM, SMEM],
        out_specs=(VMEM, VMEM),
        compiler_params=params(16),
        name="spread",
    )(start, size)


def forward_kernel(first, count, cap, seq_len, kv, chunks, size_ref, place, *refs):
    blocks, refs = refs[:count], refs[count:]
    if first == 0:
        probs_ref, room, rolled = refs[-3:]
    else:
        before, pos_ref, weight, out, extra, probs_ref, *part_refs = refs[:-3]
        rolled, columns, sems = refs[-3:]
        fetch = [
            pltpu.make_async_copy(weight.at[:, pl.ds(at, CW)], columns.at[k], sems.at[k])
            for k, (_, at) in enumerate(chunks)
        ]
        for copy in fetch:
            copy.start()
    qw = kv * RATIO * HD
    scale = 1.0 / math.sqrt(HD)
    span = RATIO * seq_len
    at_u = lax.broadcasted_iota(jnp.int32, (seq_len, span), 0)
    at_t = lax.rem(lax.broadcasted_iota(jnp.int32, (seq_len, span), 1), seq_len)
    at_t1 = lax.rem(lax.broadcasted_iota(jnp.int32, (1, span), 1), seq_len)
    causal = at_u <= at_t
    for d in range(count):
        for i in range(cap):
            size = size_ref[(first + d) * cap + i]
            rows = slice(i * seq_len, (i + 1) * seq_len)
            to = slice((d * cap + i) * seq_len, (d * cap + i + 1) * seq_len)
            keep = causal & (at_u < size)
            parts = []
            for g in range(kv):
                queries = heads_of(blocks[d][rows, g * RATIO * HD : (g + 1) * RATIO * HD], 0)
                keys = blocks[d][rows, qw + g * HD : qw + (g + 1) * HD]
                values = blocks[d][rows, qw + (kv + g) * HD : qw + (kv + g + 1) * HD]
                scores = jnp.where(keep, mm(keys, queries, ((1,), (1,))) * scale, NEG)
                top = jnp.max(scores, axis=0, keepdims=True)
                weights = jnp.exp(scores - top)
                total = jnp.sum(weights, axis=0, keepdims=True)
                probs = (weights * jnp.where(at_t1 < size, 1.0 / total, 0.0)).astype(BF16)
                probs_ref[d * cap + i, g] = probs
                mixed = mm(probs, values, ((0,), (0,)))
                parts += [mixed[r * seq_len : (r + 1) * seq_len] for r in range(RATIO)]
            rolled[to, :qw] = jnp.concatenate(parts, axis=1).astype(BF16)
            beside_from = qw + 2 * kv * HD
            beside_to = beside_from + rolled.shape[1] - qw
            rolled[to, qw:] = blocks[d][rows, beside_from:beside_to]
    packed = mm(place[:, first * cap * seq_len : (first + count) * cap * seq_len], rolled[...], ((1,), (0,)))
    if first == 0:
        room[...] = packed
    else:
        packed = packed + before[...]
        mixed = packed[:, :qw].astype(BF16)
        beside = packed[:, qw:]
        out[...] = mixed
        extra[...] = beside.astype(BF16)
        for k, (j, _) in enumerate(chunks):
            fetch[k].wait()
            own = jnp.where(pos_ref[1] == j, beside, 0.0)
            part = jnp.dot(mixed, columns[k], preferred_element_type=F32)
            part_refs[k][...] = (part + own).astype(BF16)


def attention_forward(size, place, blocks, extra, kv, seq_len, cap, ahead, pos, out_weight, chunks):
    n_dp = len(blocks)
    half = n_dp // 2
    width = kv * RATIO * HD
    shape = jax.ShapeDtypeStruct
    probs = shape((half * cap, kv, seq_len, RATIO * seq_len), BF16)
    rolled = pltpu.VMEM((half * cap * seq_len, width + extra), BF16)
    call = lambda first, outs, scratch, specs, more: pl.pallas_call(
        functools.partial(forward_kernel, first, half, cap, seq_len, kv, chunks),
        out_shape=outs,
        in_specs=[SMEM] + [VMEM] * (1 + half) + specs,
        out_specs=(VMEM,) * len(outs),
        scratch_shapes=scratch,
        compiler_params=params(52),
        name="attention_forward",
    )(size, place, *blocks[first : first + half], *more)
    probs_low, room = call(
        0, (probs, shape((CAPB, width + extra), F32)), [rolled], [ANY] * len(ahead), ahead
    )
    context, beside, probs_high, *parts = call(
        half,
        (shape((CAPB, width), BF16), shape((CAPB, extra), BF16), probs)
        + (shape((CAPB, CW), BF16),) * len(chunks),
        [
            rolled,
            pltpu.VMEM((max(1, len(chunks)), width, CW), BF16),
            pltpu.SemaphoreType.DMA((max(1, len(chunks)),)),
        ],
        [VMEM, SMEM, ANY],
        (room, pos, out_weight),
    )
    return context, beside, (probs_low, probs_high), parts


def backward_kernel(n_dp, cap, seq_len, kv, place, fetch, a_ref, b_ref, wgw_ref, acc_ref, *refs):
    all_probs, refs = refs[:2], refs[2:]
    blocks = refs[:n_dp]
    dq_out, dk_out, dv_out, grads, dq_all, dk_all, dv_all = refs[n_dp:]
    half = n_dp // 2
    qw = kv * RATIO * HD
    scale = 1.0 / math.sqrt(HD)
    packed = (a_ref[...] * wgw_ref[...] - b_ref[...] * acc_ref[...]).astype(BF16)
    grads[...] = mm(fetch[...], packed, ((1,), (0,))).astype(BF16)
    for d in range(n_dp):
        for i in range(cap):
            rows = slice(i * seq_len, (i + 1) * seq_len)
            to = slice((d * cap + i) * seq_len, (d * cap + i + 1) * seq_len)
            dq_parts, dk_parts, dv_parts = [], [], []
            for g in range(kv):
                cols = slice(g * RATIO * HD, (g + 1) * RATIO * HD)
                queries = heads_of(blocks[d][rows, cols], 0)
                keys = blocks[d][rows, qw + g * HD : qw + (g + 1) * HD]
                values = blocks[d][rows, qw + (kv + g) * HD : qw + (kv + g + 1) * HD]
                out_grad = heads_of(grads[to, cols], 0)
                probs_low = all_probs[d // half][d % half * cap + i, g]
                probs = probs_low.astype(F32)
                prob_grad = mm(values, out_grad, ((1,), (1,)))
                row_dot = jnp.sum(probs * prob_grad, axis=0, keepdims=True)
                score_grad = (probs * (prob_grad - row_dot) * scale).astype(BF16)
                dq = mm(score_grad, keys, ((0,), (0,)))
                dq_parts += [dq[r * seq_len : (r + 1) * seq_len] for r in range(RATIO)]
                dk_parts.append(mm(score_grad, queries, ((1,), (0,))))
                dv_parts.append(mm(probs_low, out_grad, ((1,), (0,))))
            for kept, parts in ((dq_all, dq_parts), (dk_all, dk_parts), (dv_all, dv_parts)):
                kept[to, :] = jnp.concatenate(parts, axis=1).astype(BF16)
    for out, kept in ((dq_out, dq_all), (dk_out, dk_all), (dv_out, dv_all)):
        out[...] = mm(place[...], kept[...], ((1,), (0,))).astype(BF16)


def attention_backward(place, fetch, a, b, wgw, acc, probs, blocks, kv, seq_len, cap):
    n_dp = len(blocks)
    qw, kw = kv * RATIO * HD, kv * HD
    rows = n_dp * cap * seq_len
    return pl.pallas_call(
        functools.partial(backward_kernel, n_dp, cap, seq_len, kv),
        out_shape=tuple(jax.ShapeDtypeStruct((CAPB, w), BF16) for w in (qw, kw, kw)),
        in_specs=[VMEM] * (8 + n_dp),
        out_specs=(VMEM,) * 3,
        scratch_shapes=[pltpu.VMEM((rows, w), BF16) for w in (qw, qw, kw, kw)],
        compiler_params=params(60),
        name="attention_backward",
    )(place, fetch, a, b, wgw, acc, *probs, *blocks)


def select(index, options):
    out = options[0]
    for k in range(1, len(options)):
        out = jnp.where(index == k, options[k], out)
    return out


def bundle_kernel(n_blk, n_round, *refs):
    pieces, out = refs[: n_blk * n_round], refs[-1]
    for j in range(n_blk):
        for k in range(n_round):
            out[j, :, k * CW : (k + 1) * CW] = pieces[j * n_round + k][...]


def bundle_pieces(pieces, n_round, tie):
    n_blk = len(pieces) // n_round
    return pl.pallas_call(
        functools.partial(bundle_kernel, n_blk, n_round),
        out_shape=jax.ShapeDtypeStruct((n_blk, CAPB, n_round * CW), BF16),
        in_specs=[VMEM] * len(pieces) + [ANY] * len(tie),
        out_specs=VMEM,
        compiler_params=params(16),
        cost_estimate=pl.CostEstimate(flops=0, bytes_accessed=0, transcendentals=0),
        name="bundle_pieces",
    )(*pieces, *tie)


def products(starts, n_cols, col, weight, gw_ref, piece, before, acc, sq, vd, own, columns, sems):
    n_blk = len(starts)
    cut = lambda j: slice(j * n_cols, (j + 1) * n_cols)
    fetch = [
        pltpu.make_async_copy(
            weight.at[:, pl.ds(at, n_cols)], columns.at[:, pl.ds(j * n_cols, n_cols)], sems.at[j]
        )
        for j, at in enumerate(starts)
    ]
    for copy in fetch:
        copy.start()
    tile = CAPB // 9
    for t in range(CAPB // tile):
        rows = slice(t * tile, (t + 1) * tile)
        pieces = [piece(j, rows) for j in range(n_blk)]
        own[rows, :] = select(col, pieces)
        squares = 0.0 if before is None else before[1][rows, :]
        dots = 0.0 if before is None else before[2][rows, :]
        for j, part in enumerate(pieces):
            wide = part.astype(F32)
            gain = gw_ref[:, starts[j] : starts[j] + n_cols]
            squares = squares + jnp.sum(wide * wide, axis=1, keepdims=True)
            dots = dots + jnp.sum(wide * gain, axis=1, keepdims=True)
        sq[rows, :] = squares
        vd[rows, :] = dots
    for copy in fetch:
        copy.wait()
    left = jnp.concatenate([piece(j, slice(0, CAPB)) for j in range(n_blk)], axis=1)
    total = mm(left, columns[...], ((1,), (1,)))
    acc[...] = total if before is None else total + before[0][...]


def rows_kernel(starts, n_cols, first, n_tie, pos_ref, weight, gw_ref, *refs):
    n_round = n_cols // CW
    held, refs = refs[: len(starts) * n_round], refs[len(starts) * n_round :]
    before, refs = (None, refs) if first else (refs[:3], refs[3:])
    piece = lambda j, rows: jnp.concatenate(
        [held[j * n_round + k][rows, :] for k in range(n_round)], axis=1
    )
    products(starts, n_cols, pos_ref[1], weight, gw_ref, piece, before, *refs[n_tie:])


def row_products(pos, out_weight, gw_row, pieces, n_round, first_col, width, state, tie):
    n_blk, n_cols = len(pieces) // n_round, n_round * CW
    depth = out_weight.shape[0]
    starts = [j * width + first_col for j in range(n_blk)]
    shape = jax.ShapeDtypeStruct
    column = shape((CAPB, 1), F32)
    before = [] if state is None else list(state)
    return pl.pallas_call(
        functools.partial(rows_kernel, starts, n_cols, state is None, len(tie)),
        out_shape=(shape((CAPB, depth), F32), column, column, shape((CAPB, n_cols), BF16)),
        in_specs=[SMEM, ANY] + [VMEM] * (1 + len(pieces) + len(before)) + [ANY] * len(tie),
        out_specs=(VMEM,) * 4,
        scratch_shapes=[
            pltpu.VMEM((depth, n_blk * n_cols), BF16),
            pltpu.SemaphoreType.DMA((n_blk,)),
        ],
        compiler_params=params(52),
        cost_estimate=pl.CostEstimate(flops=0, bytes_accessed=0, transcendentals=0),
        name="row_products",
    )(pos, out_weight, gw_row, *pieces, *before, *tie)


def row_of(column):
    return jnp.transpose(jnp.broadcast_to(column, (column.shape[0], 128)))[0:1, :]


def column_of(row):
    return jnp.transpose(jnp.broadcast_to(row, (128, row.shape[1])))[:, 0:1]


def norm_grads(model_width, sq, vd, target, gw_ref, ctx_ref, owns, outs):
    resid_out, sums, critic_row, a_col, b_col = outs
    inv_rms = lax.rsqrt(sq / model_width + EPS)
    critic = inv_rms * vd
    err = critic - target
    a = inv_rms * err
    b = inv_rms * inv_rms * inv_rms * err * vd / model_width
    a_col[...] = a
    b_col[...] = b
    critic_row[...] = row_of(critic)
    sums[...] = jnp.zeros_like(sums)
    sums[2:3, :CAPB] = row_of(b)
    at = 0
    for own in owns:
        cols = slice(at, at + own.shape[1])
        at += own.shape[1]
        hidden = own[...].astype(F32)
        resid_out[:, cols] = (a * gw_ref[:, cols] - b * hidden).astype(BF16)
        sums[0:1, cols] = jnp.sum(a * hidden, axis=0, keepdims=True)
    sums[1:2, :] = jnp.sum(a * ctx_ref[...].astype(F32), axis=0, keepdims=True)


def norm_shapes(width):
    shape = jax.ShapeDtypeStruct
    column = shape((CAPB, 1), F32)
    return (shape((CAPB, width), BF16), shape((8, width), F32), shape((1, CAPB), F32), column, column)


def last_kernel(starts, model_width, n_own, n_tie, pos_ref, weight, gw_ref, gw_own, ctx, target, *refs):
    n_blk = len(starts)
    pieces, refs = refs[:n_blk], refs[n_blk:]
    before, owns, refs = refs[:3], refs[3 : 3 + n_own], refs[3 + n_own + n_tie :]
    acc, outs, refs = refs[0], refs[1:6], refs[6:]
    sq, vd, own, columns, sems = refs
    piece = lambda j, rows: pieces[j][rows, :]
    products(
        starts, CW, pos_ref[1], weight, gw_ref, piece, before, acc, sq, vd, own, columns, sems
    )
    norm_grads(model_width, sq[...], vd[...], target[...], gw_own, ctx, (*owns, own), outs)


def last_products(
    pos, out_weight, gw_row, gw_own, context, target, pieces, first_col, state, owns, tie
):
    n_blk = len(pieces)
    depth, model_width = out_weight.shape
    width = context.shape[1]
    starts = [j * width + first_col for j in range(n_blk)]
    shape = jax.ShapeDtypeStruct
    return pl.pallas_call(
        functools.partial(last_kernel, starts, model_width, len(owns), len(tie)),
        out_shape=(shape((CAPB, depth), F32),) + norm_shapes(width),
        in_specs=[SMEM, ANY] + [VMEM] * (4 + n_blk + 3 + len(owns)) + [ANY] * len(tie),
        out_specs=(VMEM,) * 6,
        scratch_shapes=[
            pltpu.VMEM((CAPB, 1), F32),
            pltpu.VMEM((CAPB, 1), F32),
            pltpu.VMEM((CAPB, CW), BF16),
            pltpu.VMEM((depth, n_blk * CW), BF16),
            pltpu.SemaphoreType.DMA((n_blk,)),
        ],
        compiler_params=params(52),
        name="last_products",
    )(pos, out_weight, gw_row, gw_own, context, target, *pieces, *state, *owns, *tie)


def finish_kernel(model_width, sq, vd, target, gw_ref, ctx_ref, own, *outs):
    norm_grads(model_width, sq[...], vd[...], target[...], gw_ref, ctx_ref, (own,), outs)


def finish(sq, vd, target, gw_own, context, own, model_width):
    return pl.pallas_call(
        functools.partial(finish_kernel, model_width),
        out_shape=norm_shapes(context.shape[1]),
        in_specs=[VMEM] * 6,
        out_specs=(VMEM,) * 5,
        compiler_params=params(32),
        name="finish",
    )(sq, vd, target, gw_own, context, own)


def paired_sum(terms):
    while len(terms) > 1:
        terms = [terms[k] + terms[k + 1] for k in range(0, len(terms), 2)]
    return terms[0]


def weight_kernel(n_dp, spans, pos_ref, gw_ref, norm_gain, value_weight, *refs):
    n_piece = len(spans)
    sums, (ctx_hbm,) = refs[:n_dp], refs[n_dp : n_dp + 1]
    pieces = refs[n_dp + 1 : n_dp + 1 + n_piece]
    out, gain_out, value_out, *refs = refs[n_dp + 1 + n_piece :]
    ctx, held, made, ctx_sems, in_sems, out_sems = refs
    me = pos_ref[0]
    gain_sum = paired_sum([s[0:1, :] for s in sums])
    context_sum = paired_sum([s[1:2, :] for s in sums])
    for ref, row in ((gain_out, value_weight[...] * gain_sum), (value_out, norm_gain[...] * gain_sum)):
        ref[...] = jnp.concatenate([row[:, k * 128 : (k + 1) * 128] for k in range(ref.shape[0])], axis=0)
    rows_of = lambda d: pl.ds(pl.multiple_of(jnp.bitwise_xor(me, d) * CAPB, CAPB), CAPB)
    ctx_in = [
        pltpu.make_async_copy(ctx_hbm.at[rows_of(d)], ctx.at[rows_of(d)], ctx_sems.at[d])
        for d in range(n_dp)
    ]
    piece_in = [
        pltpu.make_async_copy(pieces[r], held.at[:, pl.ds(lo, hi - lo)], in_sems.at[r])
        for r, (lo, hi) in enumerate(spans)
    ]
    for copy in ctx_in + piece_in:
        copy.start()
    for d in range(n_dp):
        ctx_in[d].wait()
        factor = column_of(sums[d][2:3, :CAPB])
        rows = rows_of(d)
        ctx[rows, :] = (factor * ctx[rows, :].astype(F32)).astype(BF16)
    store, arrived = [], 0
    step = made.shape[1]
    for t in range(spans[-1][1] // step):
        lo, hi = t * step, (t + 1) * step
        while arrived < n_piece and spans[arrived][0] < hi:
            piece_in[arrived].wait()
            arrived += 1
        if t >= 2:
            store[t - 2].wait()
        rank_one = gw_ref[lo:hi, :] * context_sum
        made[t % 2] = rank_one - mm(held[:, lo:hi], ctx[...], ((0,), (0,)))
        store.append(
            pltpu.make_async_copy(made.at[t % 2], out.at[pl.ds(lo, step)], out_sems.at[t % 2])
        )
        store[t].start()
    for copy in store[-2:]:
        copy.wait()


def weight_grad(pos, gw_col, norm_gain, value_weight, sums, contexts, pieces):
    n_dp = len(sums)
    width = contexts.shape[1]
    rows = pieces[0].shape[0]
    spans, at = [], 0
    for piece in pieces:
        spans.append((at, at + piece.shape[1]))
        at += piece.shape[1]
    step = CW if at % CW == 0 else at
    return pl.pallas_call(
        functools.partial(weight_kernel, n_dp, spans),
        out_shape=(
            jax.ShapeDtypeStruct((at, width), F32),
            jax.ShapeDtypeStruct((width // 128, 128), F32),
            jax.ShapeDtypeStruct((width // 128, 128), F32),
        ),
        in_specs=[SMEM] + [VMEM] * (3 + n_dp) + [ANY] * (1 + len(pieces)),
        out_specs=(ANY, VMEM, VMEM),
        scratch_shapes=[
            pltpu.VMEM(contexts.shape, BF16),
            pltpu.VMEM((rows, at), BF16),
            pltpu.VMEM((2, step, width), F32),
            pltpu.SemaphoreType.DMA((n_dp,)),
            pltpu.SemaphoreType.DMA((len(pieces),)),
            pltpu.SemaphoreType.DMA((2,)),
        ],
        compiler_params=params(60),
        name="weight_grad",
    )(pos, gw_col, norm_gain, value_weight, *sums, contexts, *pieces)


def parts_kernel(chunks, resid_cols, pos_ref, context, weight, resid, *refs):
    outs, columns, sems = refs[-len(chunks) - 2 : -2], refs[-2], refs[-1]
    fetch = [
        pltpu.make_async_copy(weight.at[:, pl.ds(at, CW)], columns.at[k], sems.at[k])
        for k, (_, at) in enumerate(chunks)
    ]
    for copy in fetch:
        copy.start()
    for k, (j, _) in enumerate(chunks):
        fetch[k].wait()
        part = jnp.dot(context[...], columns[k], preferred_element_type=F32)
        own = jnp.where(pos_ref[1] == j, resid[:, resid_cols].astype(F32), 0.0)
        outs[k][...] = (part + own).astype(BF16)


def partial_sums(pos, context, out_weight, resid, at, chunks, tie):
    piece = jax.ShapeDtypeStruct((CAPB, CW), BF16)
    n = len(chunks)
    return pl.pallas_call(
        functools.partial(parts_kernel, chunks, slice(at * CW, (at + 1) * CW)),
        out_shape=(piece,) * n,
        in_specs=[SMEM, VMEM, ANY, VMEM] + [ANY] * len(tie),
        out_specs=(VMEM,) * n,
        scratch_shapes=[
            pltpu.VMEM((n, out_weight.shape[0], CW), BF16),
            pltpu.SemaphoreType.DMA((n,)),
        ],
        compiler_params=params(52),
        cost_estimate=pl.CostEstimate(flops=0, bytes_accessed=0, transcendentals=0),
        name="partial_sums",
    )(pos, context, out_weight, resid, *tie)


def step_kernel(part, joins, totals, ends, n_tie, pos_ref, *refs):
    refs = list(refs)
    take = lambda n=1: [refs.pop(0) for _ in range(n)]
    mid = pos_ref[2] == 1
    add = lambda a, b: (a[...].astype(F32) + b[...].astype(F32)).astype(BF16)
    (new,) = take() if part else (None,)
    pair = take(2) if joins else None
    halves = take(2) if totals else None
    last = take(2) if ends else None
    take(n_tie)
    if joins:
        take()[0][...] = add(*pair)
    if totals:
        total = add(*halves)
        take()[0][...] = total if new is None else jnp.where(mid, total, new[...])
    if ends:
        take()[0][...] = jnp.where(mid, last[0][...], last[1][...])


def line_sum(context, resid_of, out_weight, pos, order, first_parts, after_step):
    edge = [(0, 1), (1, 0), (2, 3), (3, 2)]
    middle = [(1, 2), (2, 1)]
    width = context.shape[1]
    n, n_blk = len(order), 4
    piece = jax.ShapeDtypeStruct((CAPB, CW), BF16)
    parts, joined, from_edge, from_mid, payloads = dict(enumerate(first_parts)), {}, {}, {}, {}
    hidden = {}

    def make_parts(first, count, tie):
        r = order[first][1]
        resid, at = resid_of(r)
        chunks = [(j, j * width + r * CW) for j, _ in order[first : first + count]]
        made = partial_sums(pos, context, out_weight, resid, at, chunks, tie)
        parts.update(zip(range(first, first + count), made))

    for s in (0, 1):
        payloads[s] = parts[s]
        from_edge[s] = lax.ppermute(parts[s], "tensor", edge)
    make_parts(2, 2, (parts[1],))
    tie = (parts[3],)
    for s in range(n + 4):
        joins, totals, ends = s < n, 2 <= s < n + 2, s >= 4
        part = totals and s + 2 < n
        outs, args = {}, [pos]
        if part:
            args.append(parts[s + 2])
        if joins:
            args += [parts[s], from_edge[s]]
            outs["joined"] = piece
        if totals:
            args += [joined[s - 2], from_mid[s - 2]]
            outs["payload"] = piece
        if ends:
            args += [payloads[s], from_edge[s]]
            outs["hidden"] = piece
        made = pl.pallas_call(
            functools.partial(step_kernel, part, joins, totals, ends, len(tie)),
            out_shape=tuple(outs.values()),
            in_specs=[SMEM] + [VMEM] * (len(args) - 1) + [ANY] * len(tie),
            out_specs=(VMEM,) * len(outs),
            compiler_params=params(16),
            cost_estimate=pl.CostEstimate(flops=0, bytes_accessed=0, transcendentals=0),
            name="line_step",
        )(*args, *tie)
        made = dict(zip(outs, made))
        tie = (next(iter(made.values())),)
        if joins:
            joined[s] = made["joined"]
            from_mid[s] = lax.ppermute(joined[s], "tensor", middle)
        if s + 2 < n + 4:
            payloads[s + 2] = made["payload"] if totals else parts[s + 2]
            from_edge[s + 2] = lax.ppermute(payloads[s + 2], "tensor", edge)
        if ends:
            hidden[order[s - 4]] = made["hidden"]
        tie = after_step(s, hidden, tie)
        if s % 2 == 0 and s + n_blk < n:
            make_parts(s + n_blk, 2, tie)


def on_device(
    query_states,
    key_states,
    value_states,
    residual,
    returns,
    lengths,
    balance_list,
    out_weight,
    norm_gain,
    value_weight,
):
    n_dp, n_tensor = lax.axis_size("dp"), lax.axis_size("tensor")
    me, col = lax.axis_index("dp"), lax.axis_index("tensor")
    per_dev = query_states.shape[0]
    width = query_states.shape[2]
    model_width = out_weight.shape[1]
    kv = key_states.shape[2] // HD

    seq_len = query_states.shape[1]
    cap = per_dev // n_dp
    first = CW if width > CW else width
    pick, start, size = route(me.reshape(1), lengths, balance_list, n_dp, per_dev)
    parts_in = (query_states, key_states, value_states, residual)
    used = width + 2 * kv * HD + first
    start_spans = ((0, 0, width), (1, 0, kv * HD), (2, 0, kv * HD), (3, 0, first))
    rest_span = (3, first, width)
    far = range(2, n_dp)
    blocks, rest = [None] * n_dp, [None] * n_dp
    sent = gather_rollouts(
        pick, parts_in, returns, tuple((d, start_spans, None) for d in far), n_dp
    )
    for d, payload in zip(far, sent):
        blocks[d] = xor_move(payload, d, n_dp)
    near = tuple((d, start_spans + (rest_span,), used) for d in (0, 1))
    sent = gather_rollouts(
        pick, parts_in, returns, near + tuple((d, (rest_span,), 0) for d in far), n_dp, sent[:1]
    )
    blocks[0], blocks[1] = sent[0], xor_move(sent[1], 1, n_dp)
    rest[:2] = blocks[:2]
    for d, payload in zip(far, sent[2:]):
        rest[d] = xor_move(payload, d, n_dp)
    rest_cols = (used, used) + (0,) * len(far)
    place, fetch = spread(start, size, seq_len)
    gw_own = norm_gain * value_weight
    gw = lax.all_gather(gw_own, "tensor", axis=0, tiled=True)
    gw_high = gw.astype(BF16)
    gw_low = (gw - gw_high.astype(F32)).astype(BF16)
    pair = jnp.stack([gw_high, gw_low])
    wgw = jnp.sum(mm(pair, out_weight, ((1,), (1,))), axis=0, keepdims=True)
    block = model_width // n_dp
    gw_col = lax.dynamic_slice_in_dim(gw, me * block, block).reshape(block, 1)
    is_mid = (col == 1) | (col == 2)
    pos = jnp.stack([me, col, is_mid.astype(jnp.int32)]).astype(jnp.int32)
    on_line = n_tensor == 4 and n_dp == 4
    per_block = width // CW
    order = [(j, r) for r in range(per_block) for j in (1, 2, 0, 3)]
    chunks = tuple((j, j * width + r * CW) for j, r in order[:2]) if on_line else ()
    context, resid_first, probs, parts = attention_forward(
        size, place, blocks, first, kv, seq_len, cap, (wgw, gw_col), pos, out_weight, chunks
    )
    gw_row, gw_mine = gw.reshape(1, model_width), gw_own.reshape(1, width)

    if on_line:
        later, owns, pieces = {}, [], []

        def move(held, tie):
            rounds = later["rounds"]
            bundle = bundle_pieces(
                [held[j, r] for j in range(n_tensor) for r in rounds], len(rounds), tie
            )
            moved = lax.all_to_all(bundle, "dp", split_axis=0, concat_axis=0, tiled=True)
            pieces.append(moved.reshape(n_dp * CAPB, bundle.shape[2]))
            return (bundle,)

        def after_step(s, hidden, tie):
            if s == 0:
                later["resid"], later["target"], later["context"] = pack(
                    place, rest, rest_cols, seq_len, cap, context, tie
                )
            if s in (14, 21):
                r = 2 * len(owns)
                *later["state"], own = row_products(
                    pos,
                    out_weight,
                    gw_row,
                    [hidden[j, k] for j in range(n_tensor) for k in (r, r + 1)],
                    2,
                    r * CW,
                    width,
                    later.get("state"),
                    tie,
                )
                owns.append(own)
                return (own,)
            if s in (15, len(order) + 3):
                later["rounds"] = (0, 1, 2) if s == 15 else tuple(range(3, per_block))
                later["last"] = [hidden.get((j, per_block - 1)) for j in range(n_tensor)]
                return move(hidden, tie)
            return tie

        line_sum(
            context,
            lambda r: (resid_first, 0) if r == 0 else (later["resid"], r - 1),
            out_weight,
            pos,
            order,
            parts,
            after_step,
        )
        acc, resid_out, sums, critic_row, a, b = last_products(
            pos,
            out_weight,
            gw_row,
            gw_mine,
            context,
            later["target"],
            later["last"],
            4 * CW,
            later["state"],
            owns,
            (),
        )
        contexts = lax.all_gather(later["context"], "dp", axis=0, tiled=True)
    else:
        resid_rest, target, _ = pack(place, rest, rest_cols, seq_len, cap, context)
        contexts = lax.all_gather(context, "dp", axis=0, tiled=True)
        resid = jnp.concatenate([resid_first, resid_rest], axis=1)
        part = jnp.dot(context, out_weight, preferred_element_type=F32)
        mine = lax.dynamic_slice_in_dim(part, col * width, width, axis=1) + resid.astype(F32)
        part = lax.dynamic_update_slice_in_dim(part, mine, col * width, axis=1)
        hidden = lax.psum(part.astype(BF16), "tensor")
        wide = hidden.astype(F32)
        sq = jnp.sum(wide * wide, axis=1, keepdims=True)
        vd = jnp.sum(wide * gw[None, :], axis=1, keepdims=True)
        acc = mm(hidden, out_weight, ((1,), (1,)))
        own = lax.dynamic_slice_in_dim(hidden, col * width, width, axis=1)
        pieces = [lax.all_to_all(hidden, "dp", split_axis=1, concat_axis=0, tiled=True)]
        resid_out, sums, critic_row, a, b = finish(
            sq, vd, target, gw_mine, context, own, model_width
        )

    all_sums = [sums] + [xor_move(sums, d, n_dp) for d in range(1, n_dp)]
    query_out, key_out, value_out = attention_backward(
        place, fetch, a, b, wgw, acc, probs, blocks, kv, seq_len, cap
    )
    weight_out, gain_out, value_weight_out = weight_grad(
        pos,
        gw_col,
        norm_gain.reshape(1, width),
        value_weight.reshape(1, width),
        all_sums,
        contexts,
        pieces,
    )
    return (
        critic_row.reshape(CAPB).astype(BF16),
        query_out,
        key_out,
        value_out,
        resid_out,
        weight_out,
        gain_out.reshape(width),
        value_weight_out.reshape(width),
    )


def solution(mesh):
    rows = P(("groups", "dp"), None, "tensor")
    packed = P(("groups", "dp"), "tensor")
    placed = (rows, rows, rows, rows, P(("groups", "dp"), None), P("groups"), P("groups"))
    placed += (P("tensor", None), P("tensor"), P("tensor"))
    return jax.shard_map(
        on_device,
        mesh=mesh,
        in_specs=placed,
        out_specs=(
            P(("groups", "dp")),
            packed,
            packed,
            packed,
            packed,
            packed,
            P(("groups", "tensor")),
            P(("groups", "tensor")),
        ),
        check_vma=False,
    )
```

```python
import functools
import math

import jax
import jax.numpy as jnp
from jax import lax
from jax.experimental import pallas as pl
from jax.experimental.pallas import tpu as pltpu
from jax.sharding import PartitionSpec as P

H = 40
KVH = 8
HD = 128
RATIO = H // KVH
CAPB = 576
EPS = 1e-06
NEG = -1e30
CW = 256
TAIL = 16
F32 = jnp.float32
BF16 = jnp.bfloat16
VMEM = pl.BlockSpec(memory_space=pltpu.VMEM)
SMEM = pl.BlockSpec(memory_space=pltpu.SMEM)
ANY = pl.BlockSpec(memory_space=pl.ANY)
HBM = pl.BlockSpec(memory_space=pltpu.HBM)


def params(mib):
    return pltpu.CompilerParams(vmem_limit_bytes=mib * 1024 * 1024)


def mm(a, b, dims):
    return lax.dot_general(a, b, (dims, ((), ())), preferred_element_type=F32)


def route_kernel(n_dp, per_dev, me_ref, len_ref, bal_ref, pick_ref, start_ref, size_ref, cnt_ref):
    cap = per_dev // n_dp
    me = me_ref[0]
    for d in range(n_dp):
        target = jnp.bitwise_xor(me, d)

        def outgoing(s, count):
            b = bal_ref[target * per_dev + s]
            home = lax.div(b, per_dev)

            @pl.when(home == me)
            def _():
                pick_ref[d * cap + count] = lax.rem(b, per_dev)

            return count + (home == me).astype(jnp.int32)

        lax.fori_loop(0, per_dev, outgoing, jnp.int32(0))
        cnt_ref[d] = jnp.int32(0)

    def incoming(s, run):
        b = bal_ref[me * per_dev + s]
        d = jnp.bitwise_xor(lax.div(b, per_dev), me)
        count = cnt_ref[d]
        size = len_ref[b]
        start_ref[d * cap + count] = run
        size_ref[d * cap + count] = size
        cnt_ref[d] = count + 1
        return run + size

    lax.fori_loop(0, per_dev, incoming, jnp.int32(0))


def route(me, lengths, balance_list, n_dp, per_dev):
    table = jax.ShapeDtypeStruct((per_dev,), jnp.int32)
    return pl.pallas_call(
        functools.partial(route_kernel, n_dp, per_dev),
        out_shape=(table, table, table),
        in_specs=[SMEM] * 3,
        out_specs=(SMEM, SMEM, SMEM),
        scratch_shapes=[pltpu.SMEM((n_dp,), jnp.int32)],
        name="route",
    )(me, lengths, balance_list)


def gather_kernel(cap, seq_len, outputs, n_part, pick_ref, *refs):
    parts, returns, outs, sems = refs[:n_part], refs[n_part], refs[-1 - len(outputs) : -1], refs[-1]
    copies = []
    for (d, spans, _), out in zip(outputs, outs):
        for i in range(cap):
            row = pick_ref[d * cap + i]
            col = 0
            for p, lo, hi in spans:
                copies.append(
                    pltpu.make_async_copy(
                        parts[p].at[row, :, pl.ds(lo, hi - lo)],
                        out.at[pl.ds(i * seq_len, seq_len), pl.ds(col, hi - lo)],
                        sems.at[len(copies)],
                    )
                )
                copies[-1].start()
                col += hi - lo
    for (d, _, at), out in zip(outputs, outs):
        if at is not None:
            rows = returns[...].astype(F32)
            home = lax.broadcasted_iota(jnp.int32, rows.shape, 0)
            picked = [
                jnp.sum(jnp.where(home == pick_ref[d * cap + i], rows, 0.0), axis=0, keepdims=True)
                for i in range(cap)
            ]
            picked.append(jnp.zeros((TAIL - cap, seq_len), F32))
            tail = jnp.concatenate(picked, axis=0).astype(BF16)
            out[cap * seq_len :, :] = jnp.zeros((TAIL, out.shape[1]), BF16)
            out[cap * seq_len :, at : at + seq_len] = tail
    for copy in copies:
        copy.wait()


def gather_rollouts(pick, parts, returns, outputs, n_dp, tie=()):
    per_dev, seq_len = parts[0].shape[:2]
    cap = per_dev // n_dp
    shapes = [
        (cap * seq_len + (0 if at is None else TAIL), sum(hi - lo for _, lo, hi in spans))
        for _, spans, at in outputs
    ]
    n_copy = sum(cap * len(spans) for _, spans, _ in outputs)
    return pl.pallas_call(
        functools.partial(gather_kernel, cap, seq_len, outputs, len(parts)),
        out_shape=tuple(jax.ShapeDtypeStruct(shape, BF16) for shape in shapes),
        in_specs=[SMEM] + [ANY] * len(parts) + [VMEM] + [ANY] * len(tie),
        out_specs=(VMEM,) * len(outputs),
        scratch_shapes=[pltpu.SemaphoreType.DMA((n_copy,))],
        compiler_params=params(60),
        name="gather_rollouts",
    )(pick, *parts, returns, *tie)


def xor_move(value, d, n_dp):
    return lax.ppermute(value, "dp", [(i, i ^ d) for i in range(n_dp)])


def pack_kernel(n_dp, cap, seq_len, cols, place, ctx_ref, *refs):
    blocks = refs[:n_dp]
    out, target, ctx_copy, rolled = refs[-4:]
    ctx_copy[...] = ctx_ref[...]
    returned = 0.0
    width = cap * seq_len
    for d in range(n_dp):
        lo = cols[d]
        rolled[d * width : (d + 1) * width, :] = blocks[d][:width, lo:]
        tail = blocks[d][width:, lo : lo + seq_len].astype(F32)
        line = jnp.concatenate([tail[i : i + 1, :] for i in range(cap)], axis=1)
        spots = place[:, d * width : (d + 1) * width].astype(F32)
        returned = returned + jnp.sum(spots * line, axis=1, keepdims=True)
    target[...] = returned
    out[...] = mm(place[...], rolled[...], ((1,), (0,))).astype(BF16)


def pack(place, blocks, cols, seq_len, cap, context, tie=()):
    n_dp = len(blocks)
    width = blocks[-1].shape[1] - cols[-1]
    return pl.pallas_call(
        functools.partial(pack_kernel, n_dp, cap, seq_len, cols),
        out_shape=(
            jax.ShapeDtypeStruct((CAPB, width), BF16),
            jax.ShapeDtypeStruct((CAPB, 1), F32),
            jax.ShapeDtypeStruct(context.shape, BF16),
        ),
        in_specs=[VMEM] * (2 + n_dp) + [ANY] * len(tie),
        out_specs=(VMEM,) * 3,
        scratch_shapes=[pltpu.VMEM((n_dp * cap * seq_len, width), BF16)],
        compiler_params=params(24),
        name="pack",
    )(place, context, *blocks, *tie)


def heads_of(rows, first):
    return jnp.concatenate(
        [rows[:, (first + r) * HD : (first + r + 1) * HD] for r in range(RATIO)], axis=0
    )


def spread_kernel(n_rollout, seq_len, start_ref, size_ref, place, fetch):
    iota = lambda shape, axis: lax.broadcasted_iota(jnp.int32, shape, axis)
    pair = (CAPB, 2 * seq_len)
    lane = iota(pair, 1)
    second = lane >= seq_len
    within = jnp.where(second, lane - seq_len, lane)
    offset = iota(pair, 0) - within
    turned = iota((seq_len, CAPB), 1) - iota((seq_len, CAPB), 0)
    row = iota((seq_len, CAPB), 0)
    for k in range(0, n_rollout, 2):
        first = (offset == start_ref[k]) & (within < size_ref[k]) & ~second
        other = (offset == start_ref[k + 1]) & (within < size_ref[k + 1]) & second
        place[:, k * seq_len : (k + 2) * seq_len] = (first | other).astype(BF16)
        for i in (k, k + 1):
            hit = (turned == start_ref[i]) & (row < size_ref[i])
            fetch[i * seq_len : (i + 1) * seq_len, :] = hit.astype(BF16)


def spread(start, size, seq_len):
    n_rollout = start.shape[0]
    rows = n_rollout * seq_len
    return pl.pallas_call(
        functools.partial(spread_kernel, n_rollout, seq_len),
        out_shape=(
            jax.ShapeDtypeStruct((CAPB, rows), BF16),
            jax.ShapeDtypeStruct((rows, CAPB), BF16),
        ),
        in_specs=[SMEM, SMEM],
        out_specs=(VMEM, VMEM),
        compiler_params=params(16),
        name="spread",
    )(start, size)


def forward_kernel(first, count, cap, seq_len, kv, chunks, size_ref, place, *refs):
    blocks, refs = refs[:count], refs[count:]
    if first == 0:
        probs_ref, room, rolled = refs[-3:]
    else:
        before, pos_ref, weight, out, extra, probs_ref, parts_ref = refs[:-3]
        rolled, columns, sems = refs[-3:]
        fetch = [
            pltpu.make_async_copy(weight.at[:, pl.ds(at, CW)], columns.at[k], sems.at[k])
            for k, (_, at) in enumerate(chunks)
        ]
        for copy in fetch:
            copy.start()
    qw = kv * RATIO * HD
    scale = 1.0 / math.sqrt(HD)
    span = RATIO * seq_len
    at_u = lax.broadcasted_iota(jnp.int32, (seq_len, span), 0)
    at_t = lax.rem(lax.broadcasted_iota(jnp.int32, (seq_len, span), 1), seq_len)
    at_t1 = lax.rem(lax.broadcasted_iota(jnp.int32, (1, span), 1), seq_len)
    causal = at_u <= at_t
    for d in range(count):
        for i in range(cap):
            size = size_ref[(first + d) * cap + i]
            rows = slice(i * seq_len, (i + 1) * seq_len)
            to = slice((d * cap + i) * seq_len, (d * cap + i + 1) * seq_len)
            keep = causal & (at_u < size)
            parts = []
            for g in range(kv):
                queries = heads_of(blocks[d][rows, g * RATIO * HD : (g + 1) * RATIO * HD], 0)
                keys = blocks[d][rows, qw + g * HD : qw + (g + 1) * HD]
                values = blocks[d][rows, qw + (kv + g) * HD : qw + (kv + g + 1) * HD]
                scores = jnp.where(keep, mm(keys, queries, ((1,), (1,))) * scale, NEG)
                top = jnp.max(scores, axis=0, keepdims=True)
                weights = jnp.exp(scores - top)
                total = jnp.sum(weights, axis=0, keepdims=True)
                probs = (weights * jnp.where(at_t1 < size, 1.0 / total, 0.0)).astype(BF16)
                probs_ref[d * cap + i, g] = probs
                mixed = mm(probs, values, ((0,), (0,)))
                parts += [mixed[r * seq_len : (r + 1) * seq_len] for r in range(RATIO)]
            rolled[to, :qw] = jnp.concatenate(parts, axis=1).astype(BF16)
            beside_from = qw + 2 * kv * HD
            beside_to = beside_from + rolled.shape[1] - qw
            rolled[to, qw:] = blocks[d][rows, beside_from:beside_to]
    packed = mm(place[:, first * cap * seq_len : (first + count) * cap * seq_len], rolled[...], ((1,), (0,)))
    if first == 0:
        room[...] = packed
    else:
        packed = packed + before[...]
        mixed = packed[:, :qw].astype(BF16)
        beside = packed[:, qw:]
        out[...] = mixed
        extra[...] = beside.astype(BF16)
        for k, (j, _) in enumerate(chunks):
            fetch[k].wait()
            own = jnp.where(pos_ref[1] == j, beside, 0.0)
            part = jnp.dot(mixed, columns[k], preferred_element_type=F32)
            parts_ref[:, k * CW : (k + 1) * CW] = (part + own).astype(BF16)


def attention_forward(size, place, blocks, extra, kv, seq_len, cap, ahead, pos, out_weight, chunks):
    n_dp = len(blocks)
    half = n_dp // 2
    width = kv * RATIO * HD
    shape = jax.ShapeDtypeStruct
    probs = shape((half * cap, kv, seq_len, RATIO * seq_len), BF16)
    rolled = pltpu.VMEM((half * cap * seq_len, width + extra), BF16)
    call = lambda first, outs, scratch, specs, more: pl.pallas_call(
        functools.partial(forward_kernel, first, half, cap, seq_len, kv, chunks),
        out_shape=outs,
        in_specs=[SMEM] + [VMEM] * (1 + half) + specs,
        out_specs=(VMEM,) * len(outs),
        scratch_shapes=scratch,
        compiler_params=params(52),
        name="attention_forward",
    )(size, place, *blocks[first : first + half], *more)
    probs_low, room = call(
        0, (probs, shape((CAPB, width + extra), F32)), [rolled], [ANY] * len(ahead), ahead
    )
    context, beside, probs_high, parts = call(
        half,
        (shape((CAPB, width), BF16), shape((CAPB, extra), BF16), probs)
        + (shape((CAPB, max(1, len(chunks)) * CW), BF16),),
        [
            rolled,
            pltpu.VMEM((max(1, len(chunks)), width, CW), BF16),
            pltpu.SemaphoreType.DMA((max(1, len(chunks)),)),
        ],
        [VMEM, SMEM, ANY],
        (room, pos, out_weight),
    )
    return context, beside, (probs_low, probs_high), parts


def backward_kernel(n_dp, cap, seq_len, kv, place, fetch, a_ref, b_ref, wgw_ref, acc_ref, *refs):
    all_probs, refs = refs[:2], refs[2:]
    blocks = refs[:n_dp]
    dq_out, dk_out, dv_out, grads, dq_all, dk_all, dv_all = refs[n_dp:]
    half = n_dp // 2
    qw = kv * RATIO * HD
    scale = 1.0 / math.sqrt(HD)
    packed = (a_ref[...] * wgw_ref[...] - b_ref[...] * acc_ref[...]).astype(BF16)
    grads[...] = mm(fetch[...], packed, ((1,), (0,))).astype(BF16)
    for d in range(n_dp):
        for i in range(cap):
            rows = slice(i * seq_len, (i + 1) * seq_len)
            to = slice((d * cap + i) * seq_len, (d * cap + i + 1) * seq_len)
            dq_parts, dk_parts, dv_parts = [], [], []
            for g in range(kv):
                cols = slice(g * RATIO * HD, (g + 1) * RATIO * HD)
                queries = heads_of(blocks[d][rows, cols], 0)
                keys = blocks[d][rows, qw + g * HD : qw + (g + 1) * HD]
                values = blocks[d][rows, qw + (kv + g) * HD : qw + (kv + g + 1) * HD]
                out_grad = heads_of(grads[to, cols], 0)
                probs_low = all_probs[d // half][d % half * cap + i, g]
                probs = probs_low.astype(F32)
                prob_grad = mm(values, out_grad, ((1,), (1,)))
                row_dot = jnp.sum(probs * prob_grad, axis=0, keepdims=True)
                score_grad = (probs * (prob_grad - row_dot) * scale).astype(BF16)
                dq = mm(score_grad, keys, ((0,), (0,)))
                dq_parts += [dq[r * seq_len : (r + 1) * seq_len] for r in range(RATIO)]
                dk_parts.append(mm(score_grad, queries, ((1,), (0,))))
                dv_parts.append(mm(probs_low, out_grad, ((1,), (0,))))
            for kept, parts in ((dq_all, dq_parts), (dk_all, dk_parts), (dv_all, dv_parts)):
                kept[to, :] = jnp.concatenate(parts, axis=1).astype(BF16)
    for out, kept in ((dq_out, dq_all), (dk_out, dk_all), (dv_out, dv_all)):
        out[...] = mm(place[...], kept[...], ((1,), (0,))).astype(BF16)


def attention_backward(place, fetch, a, b, wgw, acc, probs, blocks, kv, seq_len, cap):
    n_dp = len(blocks)
    qw, kw = kv * RATIO * HD, kv * HD
    rows = n_dp * cap * seq_len
    return pl.pallas_call(
        functools.partial(backward_kernel, n_dp, cap, seq_len, kv),
        out_shape=tuple(jax.ShapeDtypeStruct((CAPB, w), BF16) for w in (qw, kw, kw)),
        in_specs=[VMEM] * (8 + n_dp),
        out_specs=(VMEM,) * 3,
        scratch_shapes=[pltpu.VMEM((rows, w), BF16) for w in (qw, qw, kw, kw)],
        compiler_params=params(60),
        name="attention_backward",
    )(place, fetch, a, b, wgw, acc, *probs, *blocks)


def select(index, options):
    out = options[0]
    for k in range(1, len(options)):
        out = jnp.where(index == k, options[k], out)
    return out


def bundle_kernel(n_blk, n_round, *refs):
    pieces, out = refs[: n_blk * n_round], refs[-1]
    for j in range(n_blk):
        for k in range(n_round):
            out[j, :, k * CW : (k + 1) * CW] = pieces[j * n_round + k][...]


def bundle_pieces(pieces, n_round, tie):
    n_blk = len(pieces) // n_round
    return pl.pallas_call(
        functools.partial(bundle_kernel, n_blk, n_round),
        out_shape=jax.ShapeDtypeStruct((n_blk, CAPB, n_round * CW), BF16),
        in_specs=[VMEM] * len(pieces) + [ANY] * len(tie),
        out_specs=VMEM,
        compiler_params=params(16),
        cost_estimate=pl.CostEstimate(flops=0, bytes_accessed=0, transcendentals=0),
        name="bundle_pieces",
    )(*pieces, *tie)


def products(starts, n_cols, col, weight, gw_ref, piece, before, acc, sq, vd, own, columns, sems):
    n_blk = len(starts)
    cut = lambda j: slice(j * n_cols, (j + 1) * n_cols)
    fetch = [
        pltpu.make_async_copy(
            weight.at[:, pl.ds(at, n_cols)], columns.at[:, pl.ds(j * n_cols, n_cols)], sems.at[j]
        )
        for j, at in enumerate(starts)
    ]
    for copy in fetch:
        copy.start()
    tile = CAPB // 9
    for t in range(CAPB // tile):
        rows = slice(t * tile, (t + 1) * tile)
        pieces = [piece(j, rows) for j in range(n_blk)]
        own[rows, :] = select(col, pieces)
        squares = 0.0 if before is None else before[1][rows, :]
        dots = 0.0 if before is None else before[2][rows, :]
        for j, part in enumerate(pieces):
            wide = part.astype(F32)
            gain = gw_ref[:, starts[j] : starts[j] + n_cols]
            squares = squares + jnp.sum(wide * wide, axis=1, keepdims=True)
            dots = dots + jnp.sum(wide * gain, axis=1, keepdims=True)
        sq[rows, :] = squares
        vd[rows, :] = dots
    for copy in fetch:
        copy.wait()
    left = jnp.concatenate([piece(j, slice(0, CAPB)) for j in range(n_blk)], axis=1)
    total = mm(left, columns[...], ((1,), (1,)))
    acc[...] = total if before is None else total + before[0][...]


def rows_kernel(starts, n_cols, first, n_tie, pos_ref, weight, gw_ref, *refs):
    n_round = n_cols // CW
    held, refs = refs[: len(starts) * n_round], refs[len(starts) * n_round :]
    before, refs = (None, refs) if first else (refs[:3], refs[3:])
    piece = lambda j, rows: jnp.concatenate(
        [held[j * n_round + k][rows, :] for k in range(n_round)], axis=1
    )
    products(starts, n_cols, pos_ref[1], weight, gw_ref, piece, before, *refs[n_tie:])


def row_products(pos, out_weight, gw_row, pieces, n_round, first_col, width, state, tie):
    n_blk, n_cols = len(pieces) // n_round, n_round * CW
    depth = out_weight.shape[0]
    starts = [j * width + first_col for j in range(n_blk)]
    shape = jax.ShapeDtypeStruct
    column = shape((CAPB, 1), F32)
    before = [] if state is None else list(state)
    return pl.pallas_call(
        functools.partial(rows_kernel, starts, n_cols, state is None, len(tie)),
        out_shape=(shape((CAPB, depth), F32), column, column, shape((CAPB, n_cols), BF16)),
        in_specs=[SMEM, ANY] + [VMEM] * (1 + len(pieces) + len(before)) + [ANY] * len(tie),
        out_specs=(VMEM,) * 4,
        scratch_shapes=[
            pltpu.VMEM((depth, n_blk * n_cols), BF16),
            pltpu.SemaphoreType.DMA((n_blk,)),
        ],
        compiler_params=params(52),
        cost_estimate=pl.CostEstimate(flops=0, bytes_accessed=0, transcendentals=0),
        name="row_products",
    )(pos, out_weight, gw_row, *pieces, *before, *tie)


def row_of(column):
    return jnp.transpose(jnp.broadcast_to(column, (column.shape[0], 128)))[0:1, :]


def column_of(row):
    return jnp.transpose(jnp.broadcast_to(row, (128, row.shape[1])))[:, 0:1]


def norm_grads(model_width, sq, vd, target, gw_ref, ctx_ref, owns, outs):
    resid_out, sums, critic_row, a_col, b_col = outs
    inv_rms = lax.rsqrt(sq / model_width + EPS)
    critic = inv_rms * vd
    err = critic - target
    a = inv_rms * err
    b = inv_rms * inv_rms * inv_rms * err * vd / model_width
    a_col[...] = a
    b_col[...] = b
    critic_row[...] = row_of(critic)
    sums[...] = jnp.zeros_like(sums)
    sums[2:3, :CAPB] = row_of(b)
    at = 0
    for own in owns:
        cols = slice(at, at + own.shape[1])
        at += own.shape[1]
        hidden = own[...].astype(F32)
        resid_out[:, cols] = (a * gw_ref[:, cols] - b * hidden).astype(BF16)
        sums[0:1, cols] = jnp.sum(a * hidden, axis=0, keepdims=True)
    sums[1:2, :] = jnp.sum(a * ctx_ref[...].astype(F32), axis=0, keepdims=True)


def norm_shapes(width):
    shape = jax.ShapeDtypeStruct
    column = shape((CAPB, 1), F32)
    return (shape((CAPB, width), BF16), shape((8, width), F32), shape((1, CAPB), F32), column, column)


def last_kernel(starts, model_width, n_own, n_tie, pos_ref, weight, gw_ref, gw_own, ctx, target, *refs):
    n_blk = len(starts)
    pieces, refs = refs[:n_blk], refs[n_blk:]
    before, owns, refs = refs[:3], refs[3 : 3 + n_own], refs[3 + n_own + n_tie :]
    acc, outs, refs = refs[0], refs[1:6], refs[6:]
    sq, vd, own, columns, sems = refs
    piece = lambda j, rows: pieces[j][rows, :]
    products(
        starts, CW, pos_ref[1], weight, gw_ref, piece, before, acc, sq, vd, own, columns, sems
    )
    norm_grads(model_width, sq[...], vd[...], target[...], gw_own, ctx, (*owns, own), outs)


def last_products(
    pos, out_weight, gw_row, gw_own, context, target, pieces, first_col, state, owns, tie
):
    n_blk = len(pieces)
    depth, model_width = out_weight.shape
    width = context.shape[1]
    starts = [j * width + first_col for j in range(n_blk)]
    shape = jax.ShapeDtypeStruct
    return pl.pallas_call(
        functools.partial(last_kernel, starts, model_width, len(owns), len(tie)),
        out_shape=(shape((CAPB, depth), F32),) + norm_shapes(width),
        in_specs=[SMEM, ANY] + [VMEM] * (4 + n_blk + 3 + len(owns)) + [ANY] * len(tie),
        out_specs=(VMEM,) * 6,
        scratch_shapes=[
            pltpu.VMEM((CAPB, 1), F32),
            pltpu.VMEM((CAPB, 1), F32),
            pltpu.VMEM((CAPB, CW), BF16),
            pltpu.VMEM((depth, n_blk * CW), BF16),
            pltpu.SemaphoreType.DMA((n_blk,)),
        ],
        compiler_params=params(52),
        name="last_products",
    )(pos, out_weight, gw_row, gw_own, context, target, *pieces, *state, *owns, *tie)


def finish_kernel(model_width, sq, vd, target, gw_ref, ctx_ref, own, *outs):
    norm_grads(model_width, sq[...], vd[...], target[...], gw_ref, ctx_ref, (own,), outs)


def finish(sq, vd, target, gw_own, context, own, model_width):
    return pl.pallas_call(
        functools.partial(finish_kernel, model_width),
        out_shape=norm_shapes(context.shape[1]),
        in_specs=[VMEM] * 6,
        out_specs=(VMEM,) * 5,
        compiler_params=params(32),
        name="finish",
    )(sq, vd, target, gw_own, context, own)


def paired_sum(terms):
    while len(terms) > 1:
        terms = [terms[k] + terms[k + 1] for k in range(0, len(terms), 2)]
    return terms[0]


def weight_kernel(n_dp, spans, pos_ref, gw_ref, norm_gain, value_weight, *refs):
    n_piece = len(spans)
    sums, (ctx_hbm,) = refs[:n_dp], refs[n_dp : n_dp + 1]
    pieces = refs[n_dp + 1 : n_dp + 1 + n_piece]
    out, gain_out, value_out, *refs = refs[n_dp + 1 + n_piece :]
    ctx, held, made, ctx_sems, in_sems, out_sems = refs
    me = pos_ref[0]
    gain_sum = paired_sum([s[0:1, :] for s in sums])
    context_sum = paired_sum([s[1:2, :] for s in sums])
    for ref, row in ((gain_out, value_weight[...] * gain_sum), (value_out, norm_gain[...] * gain_sum)):
        ref[...] = jnp.concatenate([row[:, k * 128 : (k + 1) * 128] for k in range(ref.shape[0])], axis=0)
    rows_of = lambda d: pl.ds(pl.multiple_of(jnp.bitwise_xor(me, d) * CAPB, CAPB), CAPB)
    ctx_in = [
        pltpu.make_async_copy(ctx_hbm.at[rows_of(d)], ctx.at[rows_of(d)], ctx_sems.at[d])
        for d in range(n_dp)
    ]
    piece_in = [
        pltpu.make_async_copy(pieces[r], held.at[:, pl.ds(lo, hi - lo)], in_sems.at[r])
        for r, (lo, hi) in enumerate(spans)
    ]
    for copy in ctx_in + piece_in:
        copy.start()
    for d in range(n_dp):
        ctx_in[d].wait()
        factor = column_of(sums[d][2:3, :CAPB])
        rows = rows_of(d)
        ctx[rows, :] = (factor * ctx[rows, :].astype(F32)).astype(BF16)
    store, arrived = [], 0
    step = made.shape[1]
    for t in range(spans[-1][1] // step):
        lo, hi = t * step, (t + 1) * step
        while arrived < n_piece and spans[arrived][0] < hi:
            piece_in[arrived].wait()
            arrived += 1
        if t >= 2:
            store[t - 2].wait()
        rank_one = gw_ref[lo:hi, :] * context_sum
        made[t % 2] = rank_one - mm(held[:, lo:hi], ctx[...], ((0,), (0,)))
        store.append(
            pltpu.make_async_copy(made.at[t % 2], out.at[pl.ds(lo, step)], out_sems.at[t % 2])
        )
        store[t].start()
    for copy in store[-2:]:
        copy.wait()


def weight_grad(pos, gw_col, norm_gain, value_weight, sums, contexts, pieces):
    n_dp = len(sums)
    width = contexts.shape[1]
    rows = pieces[0].shape[0]
    spans, at = [], 0
    for piece in pieces:
        spans.append((at, at + piece.shape[1]))
        at += piece.shape[1]
    step = CW if at % CW == 0 else at
    return pl.pallas_call(
        functools.partial(weight_kernel, n_dp, spans),
        out_shape=(
            jax.ShapeDtypeStruct((at, width), F32),
            jax.ShapeDtypeStruct((width // 128, 128), F32),
            jax.ShapeDtypeStruct((width // 128, 128), F32),
        ),
        in_specs=[SMEM] + [VMEM] * (3 + n_dp) + [ANY] * (1 + len(pieces)),
        out_specs=(ANY, VMEM, VMEM),
        scratch_shapes=[
            pltpu.VMEM(contexts.shape, BF16),
            pltpu.VMEM((rows, at), BF16),
            pltpu.VMEM((2, step, width), F32),
            pltpu.SemaphoreType.DMA((n_dp,)),
            pltpu.SemaphoreType.DMA((len(pieces),)),
            pltpu.SemaphoreType.DMA((2,)),
        ],
        compiler_params=params(60),
        name="weight_grad",
    )(pos, gw_col, norm_gain, value_weight, *sums, contexts, *pieces)


def parts_kernel(chunks, resid_cols, pos_ref, context, weight, resid, *refs):
    outs, columns, sems = refs[-len(chunks) - 2 : -2], refs[-2], refs[-1]
    fetch = [
        pltpu.make_async_copy(weight.at[:, pl.ds(at, CW)], columns.at[k], sems.at[k])
        for k, (_, at) in enumerate(chunks)
    ]
    for copy in fetch:
        copy.start()
    for k, (j, _) in enumerate(chunks):
        fetch[k].wait()
        part = jnp.dot(context[...], columns[k], preferred_element_type=F32)
        own = jnp.where(pos_ref[1] == j, resid[:, resid_cols].astype(F32), 0.0)
        outs[k][...] = (part + own).astype(BF16)


def partial_sums(pos, context, out_weight, resid, at, chunks, tie):
    piece = jax.ShapeDtypeStruct((CAPB, CW), BF16)
    n = len(chunks)
    return pl.pallas_call(
        functools.partial(parts_kernel, chunks, slice(at * CW, (at + 1) * CW)),
        out_shape=(piece,) * n,
        in_specs=[SMEM, VMEM, ANY, VMEM] + [ANY] * len(tie),
        out_specs=(VMEM,) * n,
        scratch_shapes=[
            pltpu.VMEM((n, out_weight.shape[0], CW), BF16),
            pltpu.SemaphoreType.DMA((n,)),
        ],
        compiler_params=params(52),
        cost_estimate=pl.CostEstimate(flops=0, bytes_accessed=0, transcendentals=0),
        name="partial_sums",
    )(pos, context, out_weight, resid, *tie)


def step_kernel(part, joins, totals, ends, n_tie, pos_ref, *refs):
    refs = list(refs)
    take = lambda n=1: [refs.pop(0) for _ in range(n)]
    mid = pos_ref[2] == 1
    add = lambda a, b: (a[...].astype(F32) + b[...].astype(F32)).astype(BF16)
    (new,) = take() if part else (None,)
    pair = take(2) if joins else None
    halves = take(2) if totals else None
    last = take(2) if ends else None
    take(n_tie)
    if joins:
        take()[0][...] = add(*pair)
    if totals:
        total = add(*halves)
        take()[0][...] = total if new is None else jnp.where(mid, total, new[...])
    if ends:
        take()[0][...] = jnp.where(mid, last[0][...], last[1][...])


def pair_kernel(parts, arrived, *refs):
    for k, out in enumerate(refs[-2:]):
        cols = slice(k * CW, (k + 1) * CW)
        out[...] = (parts[:, cols].astype(F32) + arrived[:, cols].astype(F32)).astype(BF16)


def join_pair(parts, arrived, tie):
    piece = jax.ShapeDtypeStruct((CAPB, CW), BF16)
    return pl.pallas_call(
        pair_kernel,
        out_shape=(piece, piece),
        in_specs=[VMEM, VMEM] + [ANY] * len(tie),
        out_specs=(VMEM, VMEM),
        compiler_params=params(16),
        cost_estimate=pl.CostEstimate(flops=0, bytes_accessed=0, transcendentals=0),
        name="join_pair",
    )(parts, arrived, *tie)


def line_sum(context, resid_of, out_weight, pos, order, first_pair, after_step):
    edge = [(0, 1), (1, 0), (2, 3), (3, 2)]
    middle = [(1, 2), (2, 1)]
    width = context.shape[1]
    n, n_blk = len(order), 4
    piece = jax.ShapeDtypeStruct((CAPB, CW), BF16)
    parts, joined, from_edge, from_mid, payloads, hidden = {}, {}, {}, {}, {}, {}

    def make_parts(first, count, tie):
        r = order[first][1]
        resid, at = resid_of(r)
        chunks = [(j, j * width + r * CW) for j, _ in order[first : first + count]]
        made = partial_sums(pos, context, out_weight, resid, at, chunks, tie)
        parts.update(zip(range(first, first + count), made))

    arrived = lax.ppermute(first_pair, "tensor", edge)
    make_parts(2, 2, (first_pair,))
    for s in (2, 3):
        payloads[s] = parts[s]
        from_edge[s] = lax.ppermute(parts[s], "tensor", edge)
    joined[0], joined[1] = join_pair(first_pair, arrived, (parts[3],))
    for s in (0, 1):
        from_mid[s] = lax.ppermute(joined[s], "tensor", middle)
    tie = after_step(1, hidden, (joined[1],))
    make_parts(4, 2, tie)
    for s in range(2, n + 4):
        joins, totals, ends = s < n, s < n + 2, s >= 4
        part = totals and s + 2 < n
        outs, args = {}, [pos]
        if part:
            args.append(parts[s + 2])
        if joins:
            args += [parts[s], from_edge[s]]
            outs["joined"] = piece
        if totals:
            args += [joined[s - 2], from_mid[s - 2]]
            outs["payload"] = piece
        if ends:
            args += [payloads[s], from_edge[s]]
            outs["hidden"] = piece
        made = pl.pallas_call(
            functools.partial(step_kernel, part, joins, totals, ends, len(tie)),
            out_shape=tuple(outs.values()),
            in_specs=[SMEM] + [VMEM] * (len(args) - 1) + [ANY] * len(tie),
            out_specs=(VMEM,) * len(outs),
            compiler_params=params(16),
            cost_estimate=pl.CostEstimate(flops=0, bytes_accessed=0, transcendentals=0),
            name="line_step",
        )(*args, *tie)
        made = dict(zip(outs, made))
        tie = (next(iter(made.values())),)
        if joins:
            joined[s] = made["joined"]
            from_mid[s] = lax.ppermute(joined[s], "tensor", middle)
        if s + 2 < n + 4:
            payloads[s + 2] = made["payload"]
            from_edge[s + 2] = lax.ppermute(payloads[s + 2], "tensor", edge)
        if ends:
            hidden[order[s - 4]] = made["hidden"]
        tie = after_step(s, hidden, tie)
        if s % 2 == 0 and s + n_blk < n:
            make_parts(s + n_blk, 2, tie)


def on_device(
    query_states,
    key_states,
    value_states,
    residual,
    returns,
    lengths,
    balance_list,
    out_weight,
    norm_gain,
    value_weight,
):
    n_dp, n_tensor = lax.axis_size("dp"), lax.axis_size("tensor")
    me, col = lax.axis_index("dp"), lax.axis_index("tensor")
    per_dev = query_states.shape[0]
    width = query_states.shape[2]
    model_width = out_weight.shape[1]
    kv = key_states.shape[2] // HD

    seq_len = query_states.shape[1]
    cap = per_dev // n_dp
    first = CW if width > CW else width
    pick, start, size = route(me.reshape(1), lengths, balance_list, n_dp, per_dev)
    parts_in = (query_states, key_states, value_states, residual)
    used = width + 2 * kv * HD + first
    start_spans = ((0, 0, width), (1, 0, kv * HD), (2, 0, kv * HD), (3, 0, first))
    rest_span = (3, first, width)
    far = range(2, n_dp)
    blocks, rest = [None] * n_dp, [None] * n_dp
    sent = gather_rollouts(
        pick, parts_in, returns, tuple((d, start_spans, None) for d in far), n_dp
    )
    for d, payload in zip(far, sent):
        blocks[d] = xor_move(payload, d, n_dp)
    near = tuple((d, start_spans + (rest_span,), used) for d in (0, 1))
    sent = gather_rollouts(
        pick, parts_in, returns, near + tuple((d, (rest_span,), 0) for d in far), n_dp, sent[:1]
    )
    blocks[0], blocks[1] = sent[0], xor_move(sent[1], 1, n_dp)
    rest[:2] = blocks[:2]
    for d, payload in zip(far, sent[2:]):
        rest[d] = xor_move(payload, d, n_dp)
    rest_cols = (used, used) + (0,) * len(far)
    place, fetch = spread(start, size, seq_len)
    gw_own = norm_gain * value_weight
    gw = lax.all_gather(gw_own, "tensor", axis=0, tiled=True)
    gw_high = gw.astype(BF16)
    gw_low = (gw - gw_high.astype(F32)).astype(BF16)
    pair = jnp.stack([gw_high, gw_low])
    wgw = jnp.sum(mm(pair, out_weight, ((1,), (1,))), axis=0, keepdims=True)
    block = model_width // n_dp
    gw_col = lax.dynamic_slice_in_dim(gw, me * block, block).reshape(block, 1)
    is_mid = (col == 1) | (col == 2)
    pos = jnp.stack([me, col, is_mid.astype(jnp.int32)]).astype(jnp.int32)
    on_line = n_tensor == 4 and n_dp == 4
    per_block = width // CW
    order = [(j, r) for r in range(per_block) for j in (1, 2, 0, 3)]
    chunks = tuple((j, j * width + r * CW) for j, r in order[:2]) if on_line else ()
    context, resid_first, probs, parts = attention_forward(
        size, place, blocks, first, kv, seq_len, cap, (wgw, gw_col), pos, out_weight, chunks
    )
    gw_row, gw_mine = gw.reshape(1, model_width), gw_own.reshape(1, width)

    if on_line:
        later, owns, pieces = {}, [], []

        def move(held, tie):
            rounds = later["rounds"]
            bundle = bundle_pieces(
                [held[j, r] for j in range(n_tensor) for r in rounds], len(rounds), tie
            )
            moved = lax.all_to_all(bundle, "dp", split_axis=0, concat_axis=0, tiled=True)
            pieces.append(moved.reshape(n_dp * CAPB, bundle.shape[2]))
            return (bundle,)

        def after_step(s, hidden, tie):
            if s == 1:
                later["resid"], later["target"], later["context"] = pack(
                    place, rest, rest_cols, seq_len, cap, context, tie
                )
            if s in (13, 20, 21):
                r, count = {13: (0, 2), 20: (2, 1), 21: (3, 1)}[s]
                *later["state"], own = row_products(
                    pos,
                    out_weight,
                    gw_row,
                    [hidden[j, r + k] for j in range(n_tensor) for k in range(count)],
                    count,
                    r * CW,
                    width,
                    later.get("state"),
                    tie,
                )
                owns.append(own)
                return (own,)
            if s in (17, len(order) + 3):
                later["rounds"] = (0, 1, 2) if s == 17 else tuple(range(3, per_block))
                later["last"] = [hidden.get((j, per_block - 1)) for j in range(n_tensor)]
                later["tie"] = move(hidden, tie)
                return later["tie"]
            return tie

        line_sum(
            context,
            lambda r: (resid_first, 0) if r == 0 else (later["resid"], r - 1),
            out_weight,
            pos,
            order,
            parts,
            after_step,
        )
        acc, resid_out, sums, critic_row, a, b = last_products(
            pos,
            out_weight,
            gw_row,
            gw_mine,
            context,
            later["target"],
            later["last"],
            4 * CW,
            later["state"],
            owns,
            later["tie"],
        )
        contexts = lax.all_gather(later["context"], "dp", axis=0, tiled=True)
    else:
        resid_rest, target, _ = pack(place, rest, rest_cols, seq_len, cap, context)
        contexts = lax.all_gather(context, "dp", axis=0, tiled=True)
        resid = jnp.concatenate([resid_first, resid_rest], axis=1)
        part = jnp.dot(context, out_weight, preferred_element_type=F32)
        mine = lax.dynamic_slice_in_dim(part, col * width, width, axis=1) + resid.astype(F32)
        part = lax.dynamic_update_slice_in_dim(part, mine, col * width, axis=1)
        hidden = lax.psum(part.astype(BF16), "tensor")
        wide = hidden.astype(F32)
        sq = jnp.sum(wide * wide, axis=1, keepdims=True)
        vd = jnp.sum(wide * gw[None, :], axis=1, keepdims=True)
        acc = mm(hidden, out_weight, ((1,), (1,)))
        own = lax.dynamic_slice_in_dim(hidden, col * width, width, axis=1)
        pieces = [lax.all_to_all(hidden, "dp", split_axis=1, concat_axis=0, tiled=True)]
        resid_out, sums, critic_row, a, b = finish(
            sq, vd, target, gw_mine, context, own, model_width
        )

    all_sums = [sums] + [xor_move(sums, d, n_dp) for d in range(1, n_dp)]
    query_out, key_out, value_out = attention_backward(
        place, fetch, a, b, wgw, acc, probs, blocks, kv, seq_len, cap
    )
    weight_out, gain_out, value_weight_out = weight_grad(
        pos,
        gw_col,
        norm_gain.reshape(1, width),
        value_weight.reshape(1, width),
        all_sums,
        contexts,
        pieces,
    )
    return (
        critic_row.reshape(CAPB).astype(BF16),
        query_out,
        key_out,
        value_out,
        resid_out,
        weight_out,
        gain_out.reshape(width),
        value_weight_out.reshape(width),
    )


def solution(mesh):
    rows = P(("groups", "dp"), None, "tensor")
    packed = P(("groups", "dp"), "tensor")
    placed = (rows, rows, rows, rows, P(("groups", "dp"), None), P("groups"), P("groups"))
    placed += (P("tensor", None), P("tensor"), P("tensor"))
    return jax.shard_map(
        on_device,
        mesh=mesh,
        in_specs=placed,
        out_specs=(
            P(("groups", "dp")),
            packed,
            packed,
            packed,
            packed,
            packed,
            P(("groups", "tensor")),
            P(("groups", "tensor")),
        ),
        check_vma=False,
    )
```

```python
import functools
import math

import jax
import jax.numpy as jnp
from jax import lax
from jax.experimental import pallas as pl
from jax.experimental.pallas import tpu as pltpu
from jax.sharding import PartitionSpec as P

H = 40
KVH = 8
HD = 128
RATIO = H // KVH
CAPB = 576
EPS = 1e-06
NEG = -1e30
CW = 256
TAIL = 16
F32 = jnp.float32
BF16 = jnp.bfloat16
VMEM = pl.BlockSpec(memory_space=pltpu.VMEM)
SMEM = pl.BlockSpec(memory_space=pltpu.SMEM)
ANY = pl.BlockSpec(memory_space=pl.ANY)
HBM = pl.BlockSpec(memory_space=pltpu.HBM)


def params(mib):
    return pltpu.CompilerParams(vmem_limit_bytes=mib * 1024 * 1024)


def mm(a, b, dims):
    return lax.dot_general(a, b, (dims, ((), ())), preferred_element_type=F32)


def route_kernel(n_dp, per_dev, me_ref, len_ref, bal_ref, pick_ref, start_ref, size_ref, cnt_ref):
    cap = per_dev // n_dp
    me = me_ref[0]
    for d in range(n_dp):
        target = jnp.bitwise_xor(me, d)

        def outgoing(s, count):
            b = bal_ref[target * per_dev + s]
            home = lax.div(b, per_dev)

            @pl.when(home == me)
            def _():
                pick_ref[d * cap + count] = lax.rem(b, per_dev)

            return count + (home == me).astype(jnp.int32)

        lax.fori_loop(0, per_dev, outgoing, jnp.int32(0))
        cnt_ref[d] = jnp.int32(0)

    def incoming(s, run):
        b = bal_ref[me * per_dev + s]
        d = jnp.bitwise_xor(lax.div(b, per_dev), me)
        count = cnt_ref[d]
        size = len_ref[b]
        start_ref[d * cap + count] = run
        size_ref[d * cap + count] = size
        cnt_ref[d] = count + 1
        return run + size

    lax.fori_loop(0, per_dev, incoming, jnp.int32(0))


def route(me, lengths, balance_list, n_dp, per_dev):
    table = jax.ShapeDtypeStruct((per_dev,), jnp.int32)
    return pl.pallas_call(
        functools.partial(route_kernel, n_dp, per_dev),
        out_shape=(table, table, table),
        in_specs=[SMEM] * 3,
        out_specs=(SMEM, SMEM, SMEM),
        scratch_shapes=[pltpu.SMEM((n_dp,), jnp.int32)],
        name="route",
    )(me, lengths, balance_list)


def gather_kernel(cap, seq_len, outputs, n_part, pick_ref, *refs):
    parts, returns, outs, sems = refs[:n_part], refs[n_part], refs[-1 - len(outputs) : -1], refs[-1]
    copies = []
    for (d, spans, _), out in zip(outputs, outs):
        for i in range(cap):
            row = pick_ref[d * cap + i]
            col = 0
            for p, lo, hi in spans:
                copies.append(
                    pltpu.make_async_copy(
                        parts[p].at[row, :, pl.ds(lo, hi - lo)],
                        out.at[pl.ds(i * seq_len, seq_len), pl.ds(col, hi - lo)],
                        sems.at[len(copies)],
                    )
                )
                copies[-1].start()
                col += hi - lo
    for (d, _, at), out in zip(outputs, outs):
        if at is not None:
            rows = returns[...].astype(F32)
            home = lax.broadcasted_iota(jnp.int32, rows.shape, 0)
            picked = [
                jnp.sum(jnp.where(home == pick_ref[d * cap + i], rows, 0.0), axis=0, keepdims=True)
                for i in range(cap)
            ]
            picked.append(jnp.zeros((TAIL - cap, seq_len), F32))
            tail = jnp.concatenate(picked, axis=0).astype(BF16)
            out[cap * seq_len :, :] = jnp.zeros((TAIL, out.shape[1]), BF16)
            out[cap * seq_len :, at : at + seq_len] = tail
    for copy in copies:
        copy.wait()


def gather_rollouts(pick, parts, returns, outputs, n_dp, tie=()):
    per_dev, seq_len = parts[0].shape[:2]
    cap = per_dev // n_dp
    shapes = [
        (cap * seq_len + (0 if at is None else TAIL), sum(hi - lo for _, lo, hi in spans))
        for _, spans, at in outputs
    ]
    n_copy = sum(cap * len(spans) for _, spans, _ in outputs)
    return pl.pallas_call(
        functools.partial(gather_kernel, cap, seq_len, outputs, len(parts)),
        out_shape=tuple(jax.ShapeDtypeStruct(shape, BF16) for shape in shapes),
        in_specs=[SMEM] + [ANY] * len(parts) + [VMEM] + [ANY] * len(tie),
        out_specs=(VMEM,) * len(outputs),
        scratch_shapes=[pltpu.SemaphoreType.DMA((n_copy,))],
        compiler_params=params(60),
        name="gather_rollouts",
    )(pick, *parts, returns, *tie)


def xor_move(value, d, n_dp):
    return lax.ppermute(value, "dp", [(i, i ^ d) for i in range(n_dp)])


def pack_kernel(n_dp, cap, seq_len, cols, place, ctx_ref, *refs):
    blocks = refs[:n_dp]
    out, target, ctx_copy, rolled = refs[-4:]
    ctx_copy[...] = ctx_ref[...]
    returned = 0.0
    width = cap * seq_len
    for d in range(n_dp):
        lo = cols[d]
        rolled[d * width : (d + 1) * width, :] = blocks[d][:width, lo:]
        tail = blocks[d][width:, lo : lo + seq_len].astype(F32)
        line = jnp.concatenate([tail[i : i + 1, :] for i in range(cap)], axis=1)
        spots = place[:, d * width : (d + 1) * width].astype(F32)
        returned = returned + jnp.sum(spots * line, axis=1, keepdims=True)
    target[...] = returned
    out[...] = mm(place[...], rolled[...], ((1,), (0,))).astype(BF16)


def pack(place, blocks, cols, seq_len, cap, context, tie=()):
    n_dp = len(blocks)
    width = blocks[-1].shape[1] - cols[-1]
    return pl.pallas_call(
        functools.partial(pack_kernel, n_dp, cap, seq_len, cols),
        out_shape=(
            jax.ShapeDtypeStruct((CAPB, width), BF16),
            jax.ShapeDtypeStruct((CAPB, 1), F32),
            jax.ShapeDtypeStruct(context.shape, BF16),
        ),
        in_specs=[VMEM] * (2 + n_dp) + [ANY] * len(tie),
        out_specs=(VMEM,) * 3,
        scratch_shapes=[pltpu.VMEM((n_dp * cap * seq_len, width), BF16)],
        compiler_params=params(24),
        cost_estimate=pl.CostEstimate(flops=0, bytes_accessed=0, transcendentals=0),
        name="pack",
    )(place, context, *blocks, *tie)


def heads_of(rows, first):
    return jnp.concatenate(
        [rows[:, (first + r) * HD : (first + r + 1) * HD] for r in range(RATIO)], axis=0
    )


def spread_kernel(n_rollout, seq_len, start_ref, size_ref, place, fetch):
    iota = lambda shape, axis: lax.broadcasted_iota(jnp.int32, shape, axis)
    pair = (CAPB, 2 * seq_len)
    lane = iota(pair, 1)
    second = lane >= seq_len
    within = jnp.where(second, lane - seq_len, lane)
    offset = iota(pair, 0) - within
    turned = iota((seq_len, CAPB), 1) - iota((seq_len, CAPB), 0)
    row = iota((seq_len, CAPB), 0)
    for k in range(0, n_rollout, 2):
        first = (offset == start_ref[k]) & (within < size_ref[k]) & ~second
        other = (offset == start_ref[k + 1]) & (within < size_ref[k + 1]) & second
        place[:, k * seq_len : (k + 2) * seq_len] = (first | other).astype(BF16)
        for i in (k, k + 1):
            hit = (turned == start_ref[i]) & (row < size_ref[i])
            fetch[i * seq_len : (i + 1) * seq_len, :] = hit.astype(BF16)


def spread(start, size, seq_len):
    n_rollout = start.shape[0]
    rows = n_rollout * seq_len
    return pl.pallas_call(
        functools.partial(spread_kernel, n_rollout, seq_len),
        out_shape=(
            jax.ShapeDtypeStruct((CAPB, rows), BF16),
            jax.ShapeDtypeStruct((rows, CAPB), BF16),
        ),
        in_specs=[SMEM, SMEM],
        out_specs=(VMEM, VMEM),
        compiler_params=params(16),
        name="spread",
    )(start, size)


def forward_kernel(first, count, cap, seq_len, kv, chunks, size_ref, place, *refs):
    blocks, refs = refs[:count], refs[count:]
    if first == 0:
        probs_ref, room, rolled = refs[-3:]
    else:
        before, pos_ref, weight, out, extra, probs_ref, *part_refs = refs[:-3]
        rolled, columns, sems = refs[-3:]
        fetch = [
            pltpu.make_async_copy(weight.at[:, pl.ds(at, CW)], columns.at[k], sems.at[k])
            for k, (_, at) in enumerate(chunks)
        ]
        for copy in fetch:
            copy.start()
    qw = kv * RATIO * HD
    scale = 1.0 / math.sqrt(HD)
    span = RATIO * seq_len
    at_u = lax.broadcasted_iota(jnp.int32, (seq_len, span), 0)
    at_t = lax.rem(lax.broadcasted_iota(jnp.int32, (seq_len, span), 1), seq_len)
    at_t1 = lax.rem(lax.broadcasted_iota(jnp.int32, (1, span), 1), seq_len)
    causal = at_u <= at_t
    for d in range(count):
        for i in range(cap):
            size = size_ref[(first + d) * cap + i]
            rows = slice(i * seq_len, (i + 1) * seq_len)
            to = slice((d * cap + i) * seq_len, (d * cap + i + 1) * seq_len)
            keep = causal & (at_u < size)
            parts = []
            for g in range(kv):
                queries = heads_of(blocks[d][rows, g * RATIO * HD : (g + 1) * RATIO * HD], 0)
                keys = blocks[d][rows, qw + g * HD : qw + (g + 1) * HD]
                values = blocks[d][rows, qw + (kv + g) * HD : qw + (kv + g + 1) * HD]
                scores = jnp.where(keep, mm(keys, queries, ((1,), (1,))) * scale, NEG)
                top = jnp.max(scores, axis=0, keepdims=True)
                weights = jnp.exp(scores - top)
                total = jnp.sum(weights, axis=0, keepdims=True)
                probs = (weights * jnp.where(at_t1 < size, 1.0 / total, 0.0)).astype(BF16)
                probs_ref[d * cap + i, g] = probs
                mixed = mm(probs, values, ((0,), (0,)))
                parts += [mixed[r * seq_len : (r + 1) * seq_len] for r in range(RATIO)]
            rolled[to, :qw] = jnp.concatenate(parts, axis=1).astype(BF16)
            beside_from = qw + 2 * kv * HD
            beside_to = beside_from + rolled.shape[1] - qw
            rolled[to, qw:] = blocks[d][rows, beside_from:beside_to]
    packed = mm(place[:, first * cap * seq_len : (first + count) * cap * seq_len], rolled[...], ((1,), (0,)))
    if first == 0:
        room[...] = packed
    else:
        packed = packed + before[...]
        mixed = packed[:, :qw].astype(BF16)
        beside = packed[:, qw:]
        out[...] = mixed
        extra[...] = beside.astype(BF16)
        for k, (j, _) in enumerate(chunks):
            fetch[k].wait()
            own = jnp.where(pos_ref[1] == j, beside, 0.0)
            part = jnp.dot(mixed, columns[k], preferred_element_type=F32)
            part_refs[k][...] = (part + own).astype(BF16)


def attention_forward(size, place, blocks, extra, kv, seq_len, cap, ahead, pos, out_weight, chunks):
    n_dp = len(blocks)
    half = n_dp // 2
    width = kv * RATIO * HD
    shape = jax.ShapeDtypeStruct
    probs = shape((half * cap, kv, seq_len, RATIO * seq_len), BF16)
    rolled = pltpu.VMEM((half * cap * seq_len, width + extra), BF16)
    call = lambda first, outs, scratch, specs, more: pl.pallas_call(
        functools.partial(forward_kernel, first, half, cap, seq_len, kv, chunks),
        out_shape=outs,
        in_specs=[SMEM] + [VMEM] * (1 + half) + specs,
        out_specs=(VMEM,) * len(outs),
        scratch_shapes=scratch,
        compiler_params=params(52),
        name="attention_forward",
    )(size, place, *blocks[first : first + half], *more)
    probs_low, room = call(
        0, (probs, shape((CAPB, width + extra), F32)), [rolled], [ANY] * len(ahead), ahead
    )
    context, beside, probs_high, *parts = call(
        half,
        (shape((CAPB, width), BF16), shape((CAPB, extra), BF16), probs)
        + (shape((CAPB, CW), BF16),) * len(chunks),
        [
            rolled,
            pltpu.VMEM((max(1, len(chunks)), width, CW), BF16),
            pltpu.SemaphoreType.DMA((max(1, len(chunks)),)),
        ],
        [VMEM, SMEM, ANY],
        (room, pos, out_weight),
    )
    return context, beside, (probs_low, probs_high), parts


def backward_kernel(n_dp, cap, seq_len, kv, place, fetch, a_ref, b_ref, wgw_ref, acc_ref, *refs):
    all_probs, refs = refs[:2], refs[2:]
    blocks = refs[:n_dp]
    dq_out, dk_out, dv_out, grads, dq_all, dk_all, dv_all = refs[n_dp:]
    half = n_dp // 2
    qw = kv * RATIO * HD
    scale = 1.0 / math.sqrt(HD)
    packed = (a_ref[...] * wgw_ref[...] - b_ref[...] * acc_ref[...]).astype(BF16)
    grads[...] = mm(fetch[...], packed, ((1,), (0,))).astype(BF16)
    for d in range(n_dp):
        for i in range(cap):
            rows = slice(i * seq_len, (i + 1) * seq_len)
            to = slice((d * cap + i) * seq_len, (d * cap + i + 1) * seq_len)
            dq_parts, dk_parts, dv_parts = [], [], []
            for g in range(kv):
                cols = slice(g * RATIO * HD, (g + 1) * RATIO * HD)
                queries = heads_of(blocks[d][rows, cols], 0)
                keys = blocks[d][rows, qw + g * HD : qw + (g + 1) * HD]
                values = blocks[d][rows, qw + (kv + g) * HD : qw + (kv + g + 1) * HD]
                out_grad = heads_of(grads[to, cols], 0)
                probs_low = all_probs[d // half][d % half * cap + i, g]
                probs = probs_low.astype(F32)
                prob_grad = mm(values, out_grad, ((1,), (1,)))
                row_dot = jnp.sum(probs * prob_grad, axis=0, keepdims=True)
                score_grad = (probs * (prob_grad - row_dot) * scale).astype(BF16)
                dq = mm(score_grad, keys, ((0,), (0,)))
                dq_parts += [dq[r * seq_len : (r + 1) * seq_len] for r in range(RATIO)]
                dk_parts.append(mm(score_grad, queries, ((1,), (0,))))
                dv_parts.append(mm(probs_low, out_grad, ((1,), (0,))))
            for kept, parts in ((dq_all, dq_parts), (dk_all, dk_parts), (dv_all, dv_parts)):
                kept[to, :] = jnp.concatenate(parts, axis=1).astype(BF16)
    for out, kept in ((dq_out, dq_all), (dk_out, dk_all), (dv_out, dv_all)):
        out[...] = mm(place[...], kept[...], ((1,), (0,))).astype(BF16)


def attention_backward(place, fetch, a, b, wgw, acc, probs, blocks, kv, seq_len, cap):
    n_dp = len(blocks)
    qw, kw = kv * RATIO * HD, kv * HD
    rows = n_dp * cap * seq_len
    return pl.pallas_call(
        functools.partial(backward_kernel, n_dp, cap, seq_len, kv),
        out_shape=tuple(jax.ShapeDtypeStruct((CAPB, w), BF16) for w in (qw, kw, kw)),
        in_specs=[VMEM] * (8 + n_dp),
        out_specs=(VMEM,) * 3,
        scratch_shapes=[pltpu.VMEM((rows, w), BF16) for w in (qw, qw, kw, kw)],
        compiler_params=params(60),
        name="attention_backward",
    )(place, fetch, a, b, wgw, acc, *probs, *blocks)


def select(index, options):
    out = options[0]
    for k in range(1, len(options)):
        out = jnp.where(index == k, options[k], out)
    return out


def bundle_kernel(n_blk, n_round, *refs):
    pieces, out = refs[: n_blk * n_round], refs[-1]
    for j in range(n_blk):
        for k in range(n_round):
            out[j, :, k * CW : (k + 1) * CW] = pieces[j * n_round + k][...]


def bundle_pieces(pieces, n_round, tie):
    n_blk = len(pieces) // n_round
    return pl.pallas_call(
        functools.partial(bundle_kernel, n_blk, n_round),
        out_shape=jax.ShapeDtypeStruct((n_blk, CAPB, n_round * CW), BF16),
        in_specs=[VMEM] * len(pieces) + [ANY] * len(tie),
        out_specs=VMEM,
        compiler_params=params(16),
        cost_estimate=pl.CostEstimate(flops=0, bytes_accessed=0, transcendentals=0),
        name="bundle_pieces",
    )(*pieces, *tie)


def products(starts, n_cols, col, weight, gw_ref, piece, before, acc, sq, vd, own, columns, sems):
    n_blk = len(starts)
    cut = lambda j: slice(j * n_cols, (j + 1) * n_cols)
    fetch = [
        pltpu.make_async_copy(
            weight.at[:, pl.ds(at, n_cols)], columns.at[:, pl.ds(j * n_cols, n_cols)], sems.at[j]
        )
        for j, at in enumerate(starts)
    ]
    for copy in fetch:
        copy.start()
    tile = CAPB // 9
    for t in range(CAPB // tile):
        rows = slice(t * tile, (t + 1) * tile)
        pieces = [piece(j, rows) for j in range(n_blk)]
        own[rows, :] = select(col, pieces)
        squares = 0.0 if before is None else before[1][rows, :]
        dots = 0.0 if before is None else before[2][rows, :]
        for j, part in enumerate(pieces):
            wide = part.astype(F32)
            gain = gw_ref[:, starts[j] : starts[j] + n_cols]
            squares = squares + jnp.sum(wide * wide, axis=1, keepdims=True)
            dots = dots + jnp.sum(wide * gain, axis=1, keepdims=True)
        sq[rows, :] = squares
        vd[rows, :] = dots
    for copy in fetch:
        copy.wait()
    left = jnp.concatenate([piece(j, slice(0, CAPB)) for j in range(n_blk)], axis=1)
    total = mm(left, columns[...], ((1,), (1,)))
    acc[...] = total if before is None else total + before[0][...]


def rows_kernel(starts, n_cols, first, n_tie, pos_ref, weight, gw_ref, *refs):
    n_round = n_cols // CW
    held, refs = refs[: len(starts) * n_round], refs[len(starts) * n_round :]
    before, refs = (None, refs) if first else (refs[:3], refs[3:])
    piece = lambda j, rows: jnp.concatenate(
        [held[j * n_round + k][rows, :] for k in range(n_round)], axis=1
    )
    products(starts, n_cols, pos_ref[1], weight, gw_ref, piece, before, *refs[n_tie:])


def row_products(pos, out_weight, gw_row, pieces, n_round, first_col, width, state, tie):
    n_blk, n_cols = len(pieces) // n_round, n_round * CW
    depth = out_weight.shape[0]
    starts = [j * width + first_col for j in range(n_blk)]
    shape = jax.ShapeDtypeStruct
    column = shape((CAPB, 1), F32)
    before = [] if state is None else list(state)
    return pl.pallas_call(
        functools.partial(rows_kernel, starts, n_cols, state is None, len(tie)),
        out_shape=(shape((CAPB, depth), F32), column, column, shape((CAPB, n_cols), BF16)),
        in_specs=[SMEM, ANY] + [VMEM] * (1 + len(pieces) + len(before)) + [ANY] * len(tie),
        out_specs=(VMEM,) * 4,
        scratch_shapes=[
            pltpu.VMEM((depth, n_blk * n_cols), BF16),
            pltpu.SemaphoreType.DMA((n_blk,)),
        ],
        compiler_params=params(52),
        cost_estimate=pl.CostEstimate(flops=0, bytes_accessed=0, transcendentals=0),
        name="row_products",
    )(pos, out_weight, gw_row, *pieces, *before, *tie)


def row_of(column):
    return jnp.transpose(jnp.broadcast_to(column, (column.shape[0], 128)))[0:1, :]


def column_of(row):
    return jnp.transpose(jnp.broadcast_to(row, (128, row.shape[1])))[:, 0:1]


def norm_grads(model_width, sq, vd, target, gw_ref, ctx_ref, owns, outs):
    resid_out, sums, critic_row, a_col, b_col = outs
    inv_rms = lax.rsqrt(sq / model_width + EPS)
    critic = inv_rms * vd
    err = critic - target
    a = inv_rms * err
    b = inv_rms * inv_rms * inv_rms * err * vd / model_width
    a_col[...] = a
    b_col[...] = b
    critic_row[...] = row_of(critic)
    sums[...] = jnp.zeros_like(sums)
    sums[2:3, :CAPB] = row_of(b)
    at = 0
    for own in owns:
        cols = slice(at, at + own.shape[1])
        at += own.shape[1]
        hidden = own[...].astype(F32)
        resid_out[:, cols] = (a * gw_ref[:, cols] - b * hidden).astype(BF16)
        sums[0:1, cols] = jnp.sum(a * hidden, axis=0, keepdims=True)
    sums[1:2, :] = jnp.sum(a * ctx_ref[...].astype(F32), axis=0, keepdims=True)


def norm_shapes(width):
    shape = jax.ShapeDtypeStruct
    column = shape((CAPB, 1), F32)
    return (shape((CAPB, width), BF16), shape((8, width), F32), shape((1, CAPB), F32), column, column)


def last_kernel(starts, model_width, n_own, n_tie, pos_ref, weight, gw_ref, gw_own, ctx, target, *refs):
    n_blk = len(starts)
    pieces, refs = refs[:n_blk], refs[n_blk:]
    before, owns, refs = refs[:3], refs[3 : 3 + n_own], refs[3 + n_own + n_tie :]
    acc, outs, refs = refs[0], refs[1:6], refs[6:]
    sq, vd, own, columns, sems = refs
    piece = lambda j, rows: pieces[j][rows, :]
    products(
        starts, CW, pos_ref[1], weight, gw_ref, piece, before, acc, sq, vd, own, columns, sems
    )
    norm_grads(model_width, sq[...], vd[...], target[...], gw_own, ctx, (*owns, own), outs)


def last_products(
    pos, out_weight, gw_row, gw_own, context, target, pieces, first_col, state, owns, tie
):
    n_blk = len(pieces)
    depth, model_width = out_weight.shape
    width = context.shape[1]
    starts = [j * width + first_col for j in range(n_blk)]
    shape = jax.ShapeDtypeStruct
    return pl.pallas_call(
        functools.partial(last_kernel, starts, model_width, len(owns), len(tie)),
        out_shape=(shape((CAPB, depth), F32),) + norm_shapes(width),
        in_specs=[SMEM, ANY] + [VMEM] * (4 + n_blk + 3 + len(owns)) + [ANY] * len(tie),
        out_specs=(VMEM,) * 6,
        scratch_shapes=[
            pltpu.VMEM((CAPB, 1), F32),
            pltpu.VMEM((CAPB, 1), F32),
            pltpu.VMEM((CAPB, CW), BF16),
            pltpu.VMEM((depth, n_blk * CW), BF16),
            pltpu.SemaphoreType.DMA((n_blk,)),
        ],
        compiler_params=params(52),
        name="last_products",
    )(pos, out_weight, gw_row, gw_own, context, target, *pieces, *state, *owns, *tie)


def finish_kernel(model_width, sq, vd, target, gw_ref, ctx_ref, own, *outs):
    norm_grads(model_width, sq[...], vd[...], target[...], gw_ref, ctx_ref, (own,), outs)


def finish(sq, vd, target, gw_own, context, own, model_width):
    return pl.pallas_call(
        functools.partial(finish_kernel, model_width),
        out_shape=norm_shapes(context.shape[1]),
        in_specs=[VMEM] * 6,
        out_specs=(VMEM,) * 5,
        compiler_params=params(32),
        name="finish",
    )(sq, vd, target, gw_own, context, own)


def paired_sum(terms):
    while len(terms) > 1:
        terms = [terms[k] + terms[k + 1] for k in range(0, len(terms), 2)]
    return terms[0]


def weight_kernel(n_dp, spans, pos_ref, gw_ref, norm_gain, value_weight, *refs):
    n_piece = len(spans)
    sums, (ctx_hbm,) = refs[:n_dp], refs[n_dp : n_dp + 1]
    pieces = refs[n_dp + 1 : n_dp + 1 + n_piece]
    out, gain_out, value_out, *refs = refs[n_dp + 1 + n_piece :]
    ctx, held, made, ctx_sems, in_sems, out_sems = refs
    me = pos_ref[0]
    gain_sum = paired_sum([s[0:1, :] for s in sums])
    context_sum = paired_sum([s[1:2, :] for s in sums])
    for ref, row in ((gain_out, value_weight[...] * gain_sum), (value_out, norm_gain[...] * gain_sum)):
        ref[...] = jnp.concatenate([row[:, k * 128 : (k + 1) * 128] for k in range(ref.shape[0])], axis=0)
    rows_of = lambda d: pl.ds(pl.multiple_of(jnp.bitwise_xor(me, d) * CAPB, CAPB), CAPB)
    ctx_in = [
        pltpu.make_async_copy(ctx_hbm.at[rows_of(d)], ctx.at[rows_of(d)], ctx_sems.at[d])
        for d in range(n_dp)
    ]
    piece_in = [
        pltpu.make_async_copy(pieces[r], held.at[:, pl.ds(lo, hi - lo)], in_sems.at[r])
        for r, (lo, hi) in enumerate(spans)
    ]
    for copy in ctx_in + piece_in:
        copy.start()
    for d in range(n_dp):
        ctx_in[d].wait()
        factor = column_of(sums[d][2:3, :CAPB])
        rows = rows_of(d)
        ctx[rows, :] = (factor * ctx[rows, :].astype(F32)).astype(BF16)
    store, arrived = [], 0
    step = made.shape[1]
    for t in range(spans[-1][1] // step):
        lo, hi = t * step, (t + 1) * step
        while arrived < n_piece and spans[arrived][0] < hi:
            piece_in[arrived].wait()
            arrived += 1
        if t >= 2:
            store[t - 2].wait()
        rank_one = gw_ref[lo:hi, :] * context_sum
        made[t % 2] = rank_one - mm(held[:, lo:hi], ctx[...], ((0,), (0,)))
        store.append(
            pltpu.make_async_copy(made.at[t % 2], out.at[pl.ds(lo, step)], out_sems.at[t % 2])
        )
        store[t].start()
    for copy in store[-2:]:
        copy.wait()


def weight_grad(pos, gw_col, norm_gain, value_weight, sums, contexts, pieces):
    n_dp = len(sums)
    width = contexts.shape[1]
    rows = pieces[0].shape[0]
    spans, at = [], 0
    for piece in pieces:
        spans.append((at, at + piece.shape[1]))
        at += piece.shape[1]
    step = CW if at % CW == 0 else at
    return pl.pallas_call(
        functools.partial(weight_kernel, n_dp, spans),
        out_shape=(
            jax.ShapeDtypeStruct((at, width), F32),
            jax.ShapeDtypeStruct((width // 128, 128), F32),
            jax.ShapeDtypeStruct((width // 128, 128), F32),
        ),
        in_specs=[SMEM] + [VMEM] * (3 + n_dp) + [ANY] * (1 + len(pieces)),
        out_specs=(ANY, VMEM, VMEM),
        scratch_shapes=[
            pltpu.VMEM(contexts.shape, BF16),
            pltpu.VMEM((rows, at), BF16),
            pltpu.VMEM((2, step, width), F32),
            pltpu.SemaphoreType.DMA((n_dp,)),
            pltpu.SemaphoreType.DMA((len(pieces),)),
            pltpu.SemaphoreType.DMA((2,)),
        ],
        compiler_params=params(60),
        name="weight_grad",
    )(pos, gw_col, norm_gain, value_weight, *sums, contexts, *pieces)


def parts_kernel(chunks, resid_cols, pos_ref, context, weight, resid, *refs):
    outs, columns, sems = refs[-len(chunks) - 2 : -2], refs[-2], refs[-1]
    fetch = [
        pltpu.make_async_copy(weight.at[:, pl.ds(at, CW)], columns.at[k], sems.at[k])
        for k, (_, at) in enumerate(chunks)
    ]
    for copy in fetch:
        copy.start()
    for k, (j, _) in enumerate(chunks):
        fetch[k].wait()
        part = jnp.dot(context[...], columns[k], preferred_element_type=F32)
        own = jnp.where(pos_ref[1] == j, resid[:, resid_cols].astype(F32), 0.0)
        outs[k][...] = (part + own).astype(BF16)


def partial_sums(pos, context, out_weight, resid, at, chunks, tie):
    piece = jax.ShapeDtypeStruct((CAPB, CW), BF16)
    n = len(chunks)
    return pl.pallas_call(
        functools.partial(parts_kernel, chunks, slice(at * CW, (at + 1) * CW)),
        out_shape=(piece,) * n,
        in_specs=[SMEM, VMEM, ANY, VMEM] + [ANY] * len(tie),
        out_specs=(VMEM,) * n,
        scratch_shapes=[
            pltpu.VMEM((n, out_weight.shape[0], CW), BF16),
            pltpu.SemaphoreType.DMA((n,)),
        ],
        compiler_params=params(52),
        cost_estimate=pl.CostEstimate(flops=0, bytes_accessed=0, transcendentals=0),
        name="partial_sums",
    )(pos, context, out_weight, resid, *tie)


def step_kernel(part, joins, totals, ends, n_tie, pos_ref, *refs):
    refs = list(refs)
    take = lambda n=1: [refs.pop(0) for _ in range(n)]
    mid = pos_ref[2] == 1
    add = lambda a, b: (a[...].astype(F32) + b[...].astype(F32)).astype(BF16)
    (new,) = take() if part else (None,)
    pair = take(2) if joins else None
    halves = take(2) if totals else None
    last = take(2) if ends else None
    take(n_tie)
    if joins:
        take()[0][...] = add(*pair)
    if totals:
        total = add(*halves)
        take()[0][...] = total if new is None else jnp.where(mid, total, new[...])
    if ends:
        take()[0][...] = jnp.where(mid, last[0][...], last[1][...])


def pair_kernel(first, second, *refs):
    for part, arrived, out in zip((first, second), refs[:2], refs[-2:]):
        out[...] = (part[...].astype(F32) + arrived[...].astype(F32)).astype(BF16)


def join_pair(parts, arrived, tie):
    piece = jax.ShapeDtypeStruct((CAPB, CW), BF16)
    return pl.pallas_call(
        pair_kernel,
        out_shape=(piece, piece),
        in_specs=[VMEM] * 4 + [ANY] * len(tie),
        out_specs=(VMEM, VMEM),
        compiler_params=params(16),
        cost_estimate=pl.CostEstimate(flops=0, bytes_accessed=0, transcendentals=0),
        name="join_pair",
    )(*parts, *arrived, *tie)


def line_sum(context, resid_of, out_weight, pos, order, first_pair, after_step):
    edge = [(0, 1), (1, 0), (2, 3), (3, 2)]
    middle = [(1, 2), (2, 1)]
    width = context.shape[1]
    n, n_blk = len(order), 4
    piece = jax.ShapeDtypeStruct((CAPB, CW), BF16)
    parts, joined, from_edge, from_mid, payloads, hidden = {}, {}, {}, {}, {}, {}

    def make_parts(first, count, tie):
        r = order[first][1]
        resid, at = resid_of(r)
        chunks = [(j, j * width + r * CW) for j, _ in order[first : first + count]]
        made = partial_sums(pos, context, out_weight, resid, at, chunks, tie)
        parts.update(zip(range(first, first + count), made))

    arrived = [lax.ppermute(part, "tensor", edge) for part in first_pair]
    make_parts(2, 2, tuple(first_pair[1:]))
    for s in (2, 3):
        payloads[s] = parts[s]
        from_edge[s] = lax.ppermute(parts[s], "tensor", edge)
    joined[0], joined[1] = join_pair(first_pair, arrived, (parts[3],))
    for s in (0, 1):
        from_mid[s] = lax.ppermute(joined[s], "tensor", middle)
    tie = after_step(1, hidden, (joined[1],))
    make_parts(4, 2, tie)
    for s in range(2, n + 4):
        joins, totals, ends = s < n, s < n + 2, s >= 4
        part = totals and s + 2 < n
        outs, args = {}, [pos]
        if part:
            args.append(parts[s + 2])
        if joins:
            args += [parts[s], from_edge[s]]
            outs["joined"] = piece
        if totals:
            args += [joined[s - 2], from_mid[s - 2]]
            outs["payload"] = piece
        if ends:
            args += [payloads[s], from_edge[s]]
            outs["hidden"] = piece
        made = pl.pallas_call(
            functools.partial(step_kernel, part, joins, totals, ends, len(tie)),
            out_shape=tuple(outs.values()),
            in_specs=[SMEM] + [VMEM] * (len(args) - 1) + [ANY] * len(tie),
            out_specs=(VMEM,) * len(outs),
            compiler_params=params(16),
            cost_estimate=pl.CostEstimate(flops=0, bytes_accessed=0, transcendentals=0),
            name="line_step",
        )(*args, *tie)
        made = dict(zip(outs, made))
        tie = (next(iter(made.values())),)
        if joins:
            joined[s] = made["joined"]
            from_mid[s] = lax.ppermute(joined[s], "tensor", middle)
        if s + 2 < n + 4:
            payloads[s + 2] = made["payload"]
            from_edge[s + 2] = lax.ppermute(payloads[s + 2], "tensor", edge)
        if ends:
            hidden[order[s - 4]] = made["hidden"]
        tie = after_step(s, hidden, tie)
        if s % 2 == 0 and s + n_blk < n:
            make_parts(s + n_blk, 2, tie)


def on_device(
    query_states,
    key_states,
    value_states,
    residual,
    returns,
    lengths,
    balance_list,
    out_weight,
    norm_gain,
    value_weight,
):
    n_dp, n_tensor = lax.axis_size("dp"), lax.axis_size("tensor")
    me, col = lax.axis_index("dp"), lax.axis_index("tensor")
    per_dev = query_states.shape[0]
    width = query_states.shape[2]
    model_width = out_weight.shape[1]
    kv = key_states.shape[2] // HD

    seq_len = query_states.shape[1]
    cap = per_dev // n_dp
    first = CW if width > CW else width
    pick, start, size = route(me.reshape(1), lengths, balance_list, n_dp, per_dev)
    parts_in = (query_states, key_states, value_states, residual)
    used = width + 2 * kv * HD + first
    start_spans = ((0, 0, width), (1, 0, kv * HD), (2, 0, kv * HD), (3, 0, first))
    rest_span = (3, first, width)
    far = range(2, n_dp)
    blocks, rest = [None] * n_dp, [None] * n_dp
    sent = gather_rollouts(
        pick, parts_in, returns, tuple((d, start_spans, None) for d in far), n_dp
    )
    for d, payload in zip(far, sent):
        blocks[d] = xor_move(payload, d, n_dp)
    near = tuple((d, start_spans + (rest_span,), used) for d in (0, 1))
    sent = gather_rollouts(
        pick, parts_in, returns, near + tuple((d, (rest_span,), 0) for d in far), n_dp, sent[:1]
    )
    blocks[0], blocks[1] = sent[0], xor_move(sent[1], 1, n_dp)
    rest[:2] = blocks[:2]
    for d, payload in zip(far, sent[2:]):
        rest[d] = xor_move(payload, d, n_dp)
    rest_cols = (used, used) + (0,) * len(far)
    place, fetch = spread(start, size, seq_len)
    gw_own = norm_gain * value_weight
    gw = lax.all_gather(gw_own, "tensor", axis=0, tiled=True)
    gw_high = gw.astype(BF16)
    gw_low = (gw - gw_high.astype(F32)).astype(BF16)
    pair = jnp.stack([gw_high, gw_low])
    wgw = jnp.sum(mm(pair, out_weight, ((1,), (1,))), axis=0, keepdims=True)
    block = model_width // n_dp
    gw_col = lax.dynamic_slice_in_dim(gw, me * block, block).reshape(block, 1)
    is_mid = (col == 1) | (col == 2)
    pos = jnp.stack([me, col, is_mid.astype(jnp.int32)]).astype(jnp.int32)
    on_line = n_tensor == 4 and n_dp == 4
    per_block = width // CW
    order = [(j, r) for r in range(per_block) for j in (1, 2, 0, 3)]
    chunks = tuple((j, j * width + r * CW) for j, r in order[:2]) if on_line else ()
    context, resid_first, probs, parts = attention_forward(
        size, place, blocks, first, kv, seq_len, cap, (wgw, gw_col), pos, out_weight, chunks
    )
    gw_row, gw_mine = gw.reshape(1, model_width), gw_own.reshape(1, width)

    if on_line:
        later, owns, pieces = {}, [], []

        def move(held, tie):
            rounds = later["rounds"]
            bundle = bundle_pieces(
                [held[j, r] for j in range(n_tensor) for r in rounds], len(rounds), tie
            )
            moved = lax.all_to_all(bundle, "dp", split_axis=0, concat_axis=0, tiled=True)
            pieces.append(moved.reshape(n_dp * CAPB, bundle.shape[2]))
            return (bundle,)

        def after_step(s, hidden, tie):
            if s == 1:
                later["resid"], later["target"], later["context"] = pack(
                    place, rest, rest_cols, seq_len, cap, context, tie
                )
            if s in (20, 21):
                r, count = {20: (0, 2), 21: (2, 2)}[s]
                *later["state"], own = row_products(
                    pos,
                    out_weight,
                    gw_row,
                    [hidden[j, r + k] for j in range(n_tensor) for k in range(count)],
                    count,
                    r * CW,
                    width,
                    later.get("state"),
                    tie,
                )
                owns.append(own)
                return (own,)
            if s in (17, len(order) + 3):
                later["rounds"] = (0, 1, 2) if s == 17 else tuple(range(3, per_block))
                later["last"] = [hidden.get((j, per_block - 1)) for j in range(n_tensor)]
                later["tie"] = move(hidden, tie)
                return later["tie"]
            return tie

        line_sum(
            context,
            lambda r: (resid_first, 0) if r == 0 else (later["resid"], r - 1),
            out_weight,
            pos,
            order,
            parts,
            after_step,
        )
        acc, resid_out, sums, critic_row, a, b = last_products(
            pos,
            out_weight,
            gw_row,
            gw_mine,
            context,
            later["target"],
            later["last"],
            4 * CW,
            later["state"],
            owns,
            later["tie"],
        )
        contexts = lax.all_gather(later["context"], "dp", axis=0, tiled=True)
    else:
        resid_rest, target, _ = pack(place, rest, rest_cols, seq_len, cap, context)
        contexts = lax.all_gather(context, "dp", axis=0, tiled=True)
        resid = jnp.concatenate([resid_first, resid_rest], axis=1)
        part = jnp.dot(context, out_weight, preferred_element_type=F32)
        mine = lax.dynamic_slice_in_dim(part, col * width, width, axis=1) + resid.astype(F32)
        part = lax.dynamic_update_slice_in_dim(part, mine, col * width, axis=1)
        hidden = lax.psum(part.astype(BF16), "tensor")
        wide = hidden.astype(F32)
        sq = jnp.sum(wide * wide, axis=1, keepdims=True)
        vd = jnp.sum(wide * gw[None, :], axis=1, keepdims=True)
        acc = mm(hidden, out_weight, ((1,), (1,)))
        own = lax.dynamic_slice_in_dim(hidden, col * width, width, axis=1)
        pieces = [lax.all_to_all(hidden, "dp", split_axis=1, concat_axis=0, tiled=True)]
        resid_out, sums, critic_row, a, b = finish(
            sq, vd, target, gw_mine, context, own, model_width
        )

    all_sums = [sums] + [xor_move(sums, d, n_dp) for d in range(1, n_dp)]
    query_out, key_out, value_out = attention_backward(
        place, fetch, a, b, wgw, acc, probs, blocks, kv, seq_len, cap
    )
    weight_out, gain_out, value_weight_out = weight_grad(
        pos,
        gw_col,
        norm_gain.reshape(1, width),
        value_weight.reshape(1, width),
        all_sums,
        contexts,
        pieces,
    )
    return (
        critic_row.reshape(CAPB).astype(BF16),
        query_out,
        key_out,
        value_out,
        resid_out,
        weight_out,
        gain_out.reshape(width),
        value_weight_out.reshape(width),
    )


def solution(mesh):
    rows = P(("groups", "dp"), None, "tensor")
    packed = P(("groups", "dp"), "tensor")
    placed = (rows, rows, rows, rows, P(("groups", "dp"), None), P("groups"), P("groups"))
    placed += (P("tensor", None), P("tensor"), P("tensor"))
    return jax.shard_map(
        on_device,
        mesh=mesh,
        in_specs=placed,
        out_specs=(
            P(("groups", "dp")),
            packed,
            packed,
            packed,
            packed,
            packed,
            P(("groups", "tensor")),
            P(("groups", "tensor")),
        ),
        check_vma=False,
    )
```

```python
import functools
import math

import jax
import jax.numpy as jnp
from jax import lax
from jax.experimental import pallas as pl
from jax.experimental.pallas import tpu as pltpu
from jax.sharding import PartitionSpec as P

H = 40
KVH = 8
HD = 128
RATIO = H // KVH
CAPB = 576
EPS = 1e-06
NEG = -1e30
CW = 256
TAIL = 16
F32 = jnp.float32
BF16 = jnp.bfloat16
VMEM = pl.BlockSpec(memory_space=pltpu.VMEM)
SMEM = pl.BlockSpec(memory_space=pltpu.SMEM)
ANY = pl.BlockSpec(memory_space=pl.ANY)
HBM = pl.BlockSpec(memory_space=pltpu.HBM)


def params(mib):
    return pltpu.CompilerParams(vmem_limit_bytes=mib * 1024 * 1024)


def mm(a, b, dims):
    return lax.dot_general(a, b, (dims, ((), ())), preferred_element_type=F32)


def route_kernel(n_dp, per_dev, me_ref, len_ref, bal_ref, pick_ref, start_ref, size_ref, cnt_ref):
    cap = per_dev // n_dp
    me = me_ref[0]
    for d in range(n_dp):
        target = jnp.bitwise_xor(me, d)

        def outgoing(s, count):
            b = bal_ref[target * per_dev + s]
            home = lax.div(b, per_dev)

            @pl.when(home == me)
            def _():
                pick_ref[d * cap + count] = lax.rem(b, per_dev)

            return count + (home == me).astype(jnp.int32)

        lax.fori_loop(0, per_dev, outgoing, jnp.int32(0))
        cnt_ref[d] = jnp.int32(0)

    def incoming(s, run):
        b = bal_ref[me * per_dev + s]
        d = jnp.bitwise_xor(lax.div(b, per_dev), me)
        count = cnt_ref[d]
        size = len_ref[b]
        start_ref[d * cap + count] = run
        size_ref[d * cap + count] = size
        cnt_ref[d] = count + 1
        return run + size

    lax.fori_loop(0, per_dev, incoming, jnp.int32(0))


def route(me, lengths, balance_list, n_dp, per_dev):
    table = jax.ShapeDtypeStruct((per_dev,), jnp.int32)
    return pl.pallas_call(
        functools.partial(route_kernel, n_dp, per_dev),
        out_shape=(table, table, table),
        in_specs=[SMEM] * 3,
        out_specs=(SMEM, SMEM, SMEM),
        scratch_shapes=[pltpu.SMEM((n_dp,), jnp.int32)],
        name="route",
    )(me, lengths, balance_list)


def gather_kernel(cap, seq_len, outputs, n_part, pick_ref, *refs):
    parts, returns, outs, sems = refs[:n_part], refs[n_part], refs[-1 - len(outputs) : -1], refs[-1]
    copies = []
    for (d, spans, _), out in zip(outputs, outs):
        for i in range(cap):
            row = pick_ref[d * cap + i]
            col = 0
            for p, lo, hi in spans:
                copies.append(
                    pltpu.make_async_copy(
                        parts[p].at[row, :, pl.ds(lo, hi - lo)],
                        out.at[pl.ds(i * seq_len, seq_len), pl.ds(col, hi - lo)],
                        sems.at[len(copies)],
                    )
                )
                copies[-1].start()
                col += hi - lo
    for (d, _, at), out in zip(outputs, outs):
        if at is not None:
            rows = returns[...].astype(F32)
            home = lax.broadcasted_iota(jnp.int32, rows.shape, 0)
            picked = [
                jnp.sum(jnp.where(home == pick_ref[d * cap + i], rows, 0.0), axis=0, keepdims=True)
                for i in range(cap)
            ]
            picked.append(jnp.zeros((TAIL - cap, seq_len), F32))
            tail = jnp.concatenate(picked, axis=0).astype(BF16)
            out[cap * seq_len :, :] = jnp.zeros((TAIL, out.shape[1]), BF16)
            out[cap * seq_len :, at : at + seq_len] = tail
    for copy in copies:
        copy.wait()


def gather_rollouts(pick, parts, returns, outputs, n_dp, tie=()):
    per_dev, seq_len = parts[0].shape[:2]
    cap = per_dev // n_dp
    shapes = [
        (cap * seq_len + (0 if at is None else TAIL), sum(hi - lo for _, lo, hi in spans))
        for _, spans, at in outputs
    ]
    n_copy = sum(cap * len(spans) for _, spans, _ in outputs)
    return pl.pallas_call(
        functools.partial(gather_kernel, cap, seq_len, outputs, len(parts)),
        out_shape=tuple(jax.ShapeDtypeStruct(shape, BF16) for shape in shapes),
        in_specs=[SMEM] + [ANY] * len(parts) + [VMEM] + [ANY] * len(tie),
        out_specs=(VMEM,) * len(outputs),
        scratch_shapes=[pltpu.SemaphoreType.DMA((n_copy,))],
        compiler_params=params(60),
        name="gather_rollouts",
    )(pick, *parts, returns, *tie)


def xor_move(value, d, n_dp):
    return lax.ppermute(value, "dp", [(i, i ^ d) for i in range(n_dp)])


def pack_kernel(n_dp, cap, seq_len, cols, place, ctx_ref, *refs):
    blocks = refs[:n_dp]
    out, target, ctx_copy, rolled = refs[-4:]
    ctx_copy[...] = ctx_ref[...]
    returned = 0.0
    width = cap * seq_len
    for d in range(n_dp):
        lo = cols[d]
        rolled[d * width : (d + 1) * width, :] = blocks[d][:width, lo:]
        tail = blocks[d][width:, lo : lo + seq_len].astype(F32)
        line = jnp.concatenate([tail[i : i + 1, :] for i in range(cap)], axis=1)
        spots = place[:, d * width : (d + 1) * width].astype(F32)
        returned = returned + jnp.sum(spots * line, axis=1, keepdims=True)
    target[...] = returned
    out[...] = mm(place[...], rolled[...], ((1,), (0,))).astype(BF16)


def pack(place, blocks, cols, seq_len, cap, context, tie=()):
    n_dp = len(blocks)
    width = blocks[-1].shape[1] - cols[-1]
    return pl.pallas_call(
        functools.partial(pack_kernel, n_dp, cap, seq_len, cols),
        out_shape=(
            jax.ShapeDtypeStruct((CAPB, width), BF16),
            jax.ShapeDtypeStruct((CAPB, 1), F32),
            jax.ShapeDtypeStruct(context.shape, BF16),
        ),
        in_specs=[VMEM] * (2 + n_dp) + [ANY] * len(tie),
        out_specs=(VMEM,) * 3,
        scratch_shapes=[pltpu.VMEM((n_dp * cap * seq_len, width), BF16)],
        compiler_params=params(24),
        cost_estimate=pl.CostEstimate(flops=0, bytes_accessed=0, transcendentals=0),
        name="pack",
    )(place, context, *blocks, *tie)


def heads_of(rows, first):
    return jnp.concatenate(
        [rows[:, (first + r) * HD : (first + r + 1) * HD] for r in range(RATIO)], axis=0
    )


def spread_kernel(n_rollout, seq_len, start_ref, size_ref, place, fetch):
    iota = lambda shape, axis: lax.broadcasted_iota(jnp.int32, shape, axis)
    pair = (CAPB, 2 * seq_len)
    lane = iota(pair, 1)
    second = lane >= seq_len
    within = jnp.where(second, lane - seq_len, lane)
    offset = iota(pair, 0) - within
    turned = iota((seq_len, CAPB), 1) - iota((seq_len, CAPB), 0)
    row = iota((seq_len, CAPB), 0)
    for k in range(0, n_rollout, 2):
        first = (offset == start_ref[k]) & (within < size_ref[k]) & ~second
        other = (offset == start_ref[k + 1]) & (within < size_ref[k + 1]) & second
        place[:, k * seq_len : (k + 2) * seq_len] = (first | other).astype(BF16)
        for i in (k, k + 1):
            hit = (turned == start_ref[i]) & (row < size_ref[i])
            fetch[i * seq_len : (i + 1) * seq_len, :] = hit.astype(BF16)


def spread(start, size, seq_len):
    n_rollout = start.shape[0]
    rows = n_rollout * seq_len
    return pl.pallas_call(
        functools.partial(spread_kernel, n_rollout, seq_len),
        out_shape=(
            jax.ShapeDtypeStruct((CAPB, rows), BF16),
            jax.ShapeDtypeStruct((rows, CAPB), BF16),
        ),
        in_specs=[SMEM, SMEM],
        out_specs=(VMEM, VMEM),
        compiler_params=params(16),
        name="spread",
    )(start, size)


def forward_kernel(first, count, cap, seq_len, kv, chunks, size_ref, place, *refs):
    blocks, refs = refs[:count], refs[count:]
    if first == 0:
        probs_ref, room, rolled = refs[-3:]
    else:
        before, pos_ref, weight, out, extra, probs_ref, *part_refs = refs[:-3]
        rolled, columns, sems = refs[-3:]
        fetch = [
            pltpu.make_async_copy(weight.at[:, pl.ds(at, CW)], columns.at[k], sems.at[k])
            for k, (_, at) in enumerate(chunks)
        ]
        for copy in fetch:
            copy.start()
    qw = kv * RATIO * HD
    scale = 1.0 / math.sqrt(HD)
    span = RATIO * seq_len
    at_u = lax.broadcasted_iota(jnp.int32, (seq_len, span), 0)
    at_t = lax.rem(lax.broadcasted_iota(jnp.int32, (seq_len, span), 1), seq_len)
    at_t1 = lax.rem(lax.broadcasted_iota(jnp.int32, (1, span), 1), seq_len)
    causal = at_u <= at_t
    for d in range(count):
        for i in range(cap):
            size = size_ref[(first + d) * cap + i]
            rows = slice(i * seq_len, (i + 1) * seq_len)
            to = slice((d * cap + i) * seq_len, (d * cap + i + 1) * seq_len)
            keep = causal & (at_u < size)
            parts = []
            for g in range(kv):
                queries = heads_of(blocks[d][rows, g * RATIO * HD : (g + 1) * RATIO * HD], 0)
                keys = blocks[d][rows, qw + g * HD : qw + (g + 1) * HD]
                values = blocks[d][rows, qw + (kv + g) * HD : qw + (kv + g + 1) * HD]
                scores = jnp.where(keep, mm(keys, queries, ((1,), (1,))) * scale, NEG)
                top = jnp.max(scores, axis=0, keepdims=True)
                weights = jnp.exp(scores - top)
                total = jnp.sum(weights, axis=0, keepdims=True)
                probs = (weights * jnp.where(at_t1 < size, 1.0 / total, 0.0)).astype(BF16)
                probs_ref[d * cap + i, g] = probs
                mixed = mm(probs, values, ((0,), (0,)))
                parts += [mixed[r * seq_len : (r + 1) * seq_len] for r in range(RATIO)]
            rolled[to, :qw] = jnp.concatenate(parts, axis=1).astype(BF16)
            beside_from = qw + 2 * kv * HD
            beside_to = beside_from + rolled.shape[1] - qw
            rolled[to, qw:] = blocks[d][rows, beside_from:beside_to]
    packed = mm(place[:, first * cap * seq_len : (first + count) * cap * seq_len], rolled[...], ((1,), (0,)))
    if first == 0:
        room[...] = packed
    else:
        packed = packed + before[...]
        mixed = packed[:, :qw].astype(BF16)
        beside = packed[:, qw:]
        out[...] = mixed
        extra[...] = beside.astype(BF16)
        for k, (j, _) in enumerate(chunks):
            fetch[k].wait()
            own = jnp.where(pos_ref[1] == j, beside, 0.0)
            part = jnp.dot(mixed, columns[k], preferred_element_type=F32)
            part_refs[k][...] = (part + own).astype(BF16)


def attention_forward(size, place, blocks, extra, kv, seq_len, cap, ahead, pos, out_weight, chunks):
    n_dp = len(blocks)
    half = n_dp // 2
    width = kv * RATIO * HD
    shape = jax.ShapeDtypeStruct
    probs = shape((half * cap, kv, seq_len, RATIO * seq_len), BF16)
    rolled = pltpu.VMEM((half * cap * seq_len, width + extra), BF16)
    call = lambda first, outs, scratch, specs, more: pl.pallas_call(
        functools.partial(forward_kernel, first, half, cap, seq_len, kv, chunks),
        out_shape=outs,
        in_specs=[SMEM] + [VMEM] * (1 + half) + specs,
        out_specs=(VMEM,) * len(outs),
        scratch_shapes=scratch,
        compiler_params=params(52),
        name="attention_forward",
    )(size, place, *blocks[first : first + half], *more)
    probs_low, room = call(
        0, (probs, shape((CAPB, width + extra), F32)), [rolled], [ANY] * len(ahead), ahead
    )
    context, beside, probs_high, *parts = call(
        half,
        (shape((CAPB, width), BF16), shape((CAPB, extra), BF16), probs)
        + (shape((CAPB, CW), BF16),) * len(chunks),
        [
            rolled,
            pltpu.VMEM((max(1, len(chunks)), width, CW), BF16),
            pltpu.SemaphoreType.DMA((max(1, len(chunks)),)),
        ],
        [VMEM, SMEM, ANY],
        (room, pos, out_weight),
    )
    return context, beside, (probs_low, probs_high), parts


def backward_kernel(n_dp, cap, seq_len, kv, place, fetch, a_ref, b_ref, wgw_ref, acc_ref, *refs):
    all_probs, refs = refs[:2], refs[2:]
    blocks = refs[:n_dp]
    dq_out, dk_out, dv_out, grads, dq_all, dk_all, dv_all = refs[n_dp:]
    half = n_dp // 2
    qw = kv * RATIO * HD
    scale = 1.0 / math.sqrt(HD)
    packed = (a_ref[...] * wgw_ref[...] - b_ref[...] * acc_ref[...]).astype(BF16)
    grads[...] = mm(fetch[...], packed, ((1,), (0,))).astype(BF16)
    for d in range(n_dp):
        for i in range(cap):
            rows = slice(i * seq_len, (i + 1) * seq_len)
            to = slice((d * cap + i) * seq_len, (d * cap + i + 1) * seq_len)
            dq_parts, dk_parts, dv_parts = [], [], []
            for g in range(kv):
                cols = slice(g * RATIO * HD, (g + 1) * RATIO * HD)
                queries = heads_of(blocks[d][rows, cols], 0)
                keys = blocks[d][rows, qw + g * HD : qw + (g + 1) * HD]
                values = blocks[d][rows, qw + (kv + g) * HD : qw + (kv + g + 1) * HD]
                out_grad = heads_of(grads[to, cols], 0)
                probs_low = all_probs[d // half][d % half * cap + i, g]
                probs = probs_low.astype(F32)
                prob_grad = mm(values, out_grad, ((1,), (1,)))
                row_dot = jnp.sum(probs * prob_grad, axis=0, keepdims=True)
                score_grad = (probs * (prob_grad - row_dot) * scale).astype(BF16)
                dq = mm(score_grad, keys, ((0,), (0,)))
                dq_parts += [dq[r * seq_len : (r + 1) * seq_len] for r in range(RATIO)]
                dk_parts.append(mm(score_grad, queries, ((1,), (0,))))
                dv_parts.append(mm(probs_low, out_grad, ((1,), (0,))))
            for kept, parts in ((dq_all, dq_parts), (dk_all, dk_parts), (dv_all, dv_parts)):
                kept[to, :] = jnp.concatenate(parts, axis=1).astype(BF16)
    for out, kept in ((dq_out, dq_all), (dk_out, dk_all), (dv_out, dv_all)):
        out[...] = mm(place[...], kept[...], ((1,), (0,))).astype(BF16)


def attention_backward(place, fetch, a, b, wgw, acc, probs, blocks, kv, seq_len, cap):
    n_dp = len(blocks)
    qw, kw = kv * RATIO * HD, kv * HD
    rows = n_dp * cap * seq_len
    return pl.pallas_call(
        functools.partial(backward_kernel, n_dp, cap, seq_len, kv),
        out_shape=tuple(jax.ShapeDtypeStruct((CAPB, w), BF16) for w in (qw, kw, kw)),
        in_specs=[VMEM] * (8 + n_dp),
        out_specs=(VMEM,) * 3,
        scratch_shapes=[pltpu.VMEM((rows, w), BF16) for w in (qw, qw, kw, kw)],
        compiler_params=params(60),
        name="attention_backward",
    )(place, fetch, a, b, wgw, acc, *probs, *blocks)


def select(index, options):
    out = options[0]
    for k in range(1, len(options)):
        out = jnp.where(index == k, options[k], out)
    return out


def bundle_kernel(n_blk, n_round, *refs):
    pieces, out = refs[: n_blk * n_round], refs[-1]
    for j in range(n_blk):
        for k in range(n_round):
            out[j, :, k * CW : (k + 1) * CW] = pieces[j * n_round + k][...]


def bundle_pieces(pieces, n_round, tie):
    n_blk = len(pieces) // n_round
    return pl.pallas_call(
        functools.partial(bundle_kernel, n_blk, n_round),
        out_shape=jax.ShapeDtypeStruct((n_blk, CAPB, n_round * CW), BF16),
        in_specs=[VMEM] * len(pieces) + [ANY] * len(tie),
        out_specs=VMEM,
        compiler_params=params(16),
        cost_estimate=pl.CostEstimate(flops=0, bytes_accessed=0, transcendentals=0),
        name="bundle_pieces",
    )(*pieces, *tie)


def products(starts, n_cols, col, weight, gw_ref, piece, before, acc, sq, vd, own, columns, sems):
    n_blk = len(starts)
    cut = lambda j: slice(j * n_cols, (j + 1) * n_cols)
    fetch = [
        pltpu.make_async_copy(
            weight.at[:, pl.ds(at, n_cols)], columns.at[:, pl.ds(j * n_cols, n_cols)], sems.at[j]
        )
        for j, at in enumerate(starts)
    ]
    for copy in fetch:
        copy.start()
    tile = CAPB // 9
    for t in range(CAPB // tile):
        rows = slice(t * tile, (t + 1) * tile)
        pieces = [piece(j, rows) for j in range(n_blk)]
        own[rows, :] = select(col, pieces)
        squares = 0.0 if before is None else before[1][rows, :]
        dots = 0.0 if before is None else before[2][rows, :]
        for j, part in enumerate(pieces):
            wide = part.astype(F32)
            gain = gw_ref[:, starts[j] : starts[j] + n_cols]
            squares = squares + jnp.sum(wide * wide, axis=1, keepdims=True)
            dots = dots + jnp.sum(wide * gain, axis=1, keepdims=True)
        sq[rows, :] = squares
        vd[rows, :] = dots
    for copy in fetch:
        copy.wait()
    left = jnp.concatenate([piece(j, slice(0, CAPB)) for j in range(n_blk)], axis=1)
    total = mm(left, columns[...], ((1,), (1,)))
    acc[...] = total if before is None else total + before[0][...]


def rows_kernel(starts, n_cols, first, n_tie, pos_ref, weight, gw_ref, *refs):
    n_round = n_cols // CW
    held, refs = refs[: len(starts) * n_round], refs[len(starts) * n_round :]
    before, refs = (None, refs) if first else (refs[:3], refs[3:])
    piece = lambda j, rows: jnp.concatenate(
        [held[j * n_round + k][rows, :] for k in range(n_round)], axis=1
    )
    products(starts, n_cols, pos_ref[1], weight, gw_ref, piece, before, *refs[n_tie:])


def row_products(pos, out_weight, gw_row, pieces, n_round, first_col, width, state, tie):
    n_blk, n_cols = len(pieces) // n_round, n_round * CW
    depth = out_weight.shape[0]
    starts = [j * width + first_col for j in range(n_blk)]
    shape = jax.ShapeDtypeStruct
    column = shape((CAPB, 1), F32)
    before = [] if state is None else list(state)
    return pl.pallas_call(
        functools.partial(rows_kernel, starts, n_cols, state is None, len(tie)),
        out_shape=(shape((CAPB, depth), F32), column, column, shape((CAPB, n_cols), BF16)),
        in_specs=[SMEM, ANY] + [VMEM] * (1 + len(pieces) + len(before)) + [ANY] * len(tie),
        out_specs=(VMEM,) * 4,
        scratch_shapes=[
            pltpu.VMEM((depth, n_blk * n_cols), BF16),
            pltpu.SemaphoreType.DMA((n_blk,)),
        ],
        compiler_params=params(52),
        cost_estimate=pl.CostEstimate(flops=0, bytes_accessed=0, transcendentals=0),
        name="row_products",
    )(pos, out_weight, gw_row, *pieces, *before, *tie)


def row_of(column):
    return jnp.transpose(jnp.broadcast_to(column, (column.shape[0], 128)))[0:1, :]


def column_of(row):
    return jnp.transpose(jnp.broadcast_to(row, (128, row.shape[1])))[:, 0:1]


def norm_grads(model_width, sq, vd, target, gw_ref, ctx_ref, owns, outs):
    resid_out, sums, critic_row, a_col, b_col = outs
    inv_rms = lax.rsqrt(sq / model_width + EPS)
    critic = inv_rms * vd
    err = critic - target
    a = inv_rms * err
    b = inv_rms * inv_rms * inv_rms * err * vd / model_width
    a_col[...] = a
    b_col[...] = b
    critic_row[...] = row_of(critic)
    sums[...] = jnp.zeros_like(sums)
    sums[2:3, :CAPB] = row_of(b)
    at = 0
    for own in owns:
        cols = slice(at, at + own.shape[1])
        at += own.shape[1]
        hidden = own[...].astype(F32)
        resid_out[:, cols] = (a * gw_ref[:, cols] - b * hidden).astype(BF16)
        sums[0:1, cols] = jnp.sum(a * hidden, axis=0, keepdims=True)
    sums[1:2, :] = jnp.sum(a * ctx_ref[...].astype(F32), axis=0, keepdims=True)


def norm_shapes(width):
    shape = jax.ShapeDtypeStruct
    column = shape((CAPB, 1), F32)
    return (shape((CAPB, width), BF16), shape((8, width), F32), shape((1, CAPB), F32), column, column)


def last_kernel(starts, model_width, n_own, n_tie, pos_ref, weight, gw_ref, gw_own, ctx, target, *refs):
    n_blk = len(starts)
    pieces, refs = refs[:n_blk], refs[n_blk:]
    before, owns, refs = refs[:3], refs[3 : 3 + n_own], refs[3 + n_own + n_tie :]
    acc, outs, refs = refs[0], refs[1:6], refs[6:]
    sq, vd, own, columns, sems = refs
    piece = lambda j, rows: pieces[j][rows, :]
    products(
        starts, CW, pos_ref[1], weight, gw_ref, piece, before, acc, sq, vd, own, columns, sems
    )
    norm_grads(model_width, sq[...], vd[...], target[...], gw_own, ctx, (*owns, own), outs)


def last_products(
    pos, out_weight, gw_row, gw_own, context, target, pieces, first_col, state, owns, tie
):
    n_blk = len(pieces)
    depth, model_width = out_weight.shape
    width = context.shape[1]
    starts = [j * width + first_col for j in range(n_blk)]
    shape = jax.ShapeDtypeStruct
    return pl.pallas_call(
        functools.partial(last_kernel, starts, model_width, len(owns), len(tie)),
        out_shape=(shape((CAPB, depth), F32),) + norm_shapes(width),
        in_specs=[SMEM, ANY] + [VMEM] * (4 + n_blk + 3 + len(owns)) + [ANY] * len(tie),
        out_specs=(VMEM,) * 6,
        scratch_shapes=[
            pltpu.VMEM((CAPB, 1), F32),
            pltpu.VMEM((CAPB, 1), F32),
            pltpu.VMEM((CAPB, CW), BF16),
            pltpu.VMEM((depth, n_blk * CW), BF16),
            pltpu.SemaphoreType.DMA((n_blk,)),
        ],
        compiler_params=params(52),
        name="last_products",
    )(pos, out_weight, gw_row, gw_own, context, target, *pieces, *state, *owns, *tie)


def finish_kernel(model_width, sq, vd, target, gw_ref, ctx_ref, own, *outs):
    norm_grads(model_width, sq[...], vd[...], target[...], gw_ref, ctx_ref, (own,), outs)


def finish(sq, vd, target, gw_own, context, own, model_width):
    return pl.pallas_call(
        functools.partial(finish_kernel, model_width),
        out_shape=norm_shapes(context.shape[1]),
        in_specs=[VMEM] * 6,
        out_specs=(VMEM,) * 5,
        compiler_params=params(32),
        name="finish",
    )(sq, vd, target, gw_own, context, own)


def paired_sum(terms):
    while len(terms) > 1:
        terms = [terms[k] + terms[k + 1] for k in range(0, len(terms), 2)]
    return terms[0]


def weight_kernel(n_dp, spans, pos_ref, gw_ref, norm_gain, value_weight, *refs):
    n_piece = len(spans)
    sums, (ctx_hbm,) = refs[:n_dp], refs[n_dp : n_dp + 1]
    pieces = refs[n_dp + 1 : n_dp + 1 + n_piece]
    out, gain_out, value_out, *refs = refs[n_dp + 1 + n_piece :]
    ctx, held, made, ctx_sems, in_sems, out_sems = refs
    me = pos_ref[0]
    gain_sum = paired_sum([s[0:1, :] for s in sums])
    context_sum = paired_sum([s[1:2, :] for s in sums])
    for ref, row in ((gain_out, value_weight[...] * gain_sum), (value_out, norm_gain[...] * gain_sum)):
        ref[...] = jnp.concatenate([row[:, k * 128 : (k + 1) * 128] for k in range(ref.shape[0])], axis=0)
    rows_of = lambda d: pl.ds(pl.multiple_of(jnp.bitwise_xor(me, d) * CAPB, CAPB), CAPB)
    ctx_in = [
        pltpu.make_async_copy(ctx_hbm.at[rows_of(d)], ctx.at[rows_of(d)], ctx_sems.at[d])
        for d in range(n_dp)
    ]
    piece_in = [
        pltpu.make_async_copy(pieces[r], held.at[:, pl.ds(lo, hi - lo)], in_sems.at[r])
        for r, (lo, hi) in enumerate(spans)
    ]
    for copy in ctx_in + piece_in:
        copy.start()
    for d in range(n_dp):
        ctx_in[d].wait()
        factor = column_of(sums[d][2:3, :CAPB])
        rows = rows_of(d)
        ctx[rows, :] = (factor * ctx[rows, :].astype(F32)).astype(BF16)
    store, arrived = [], 0
    step = made.shape[1]
    for t in range(spans[-1][1] // step):
        lo, hi = t * step, (t + 1) * step
        while arrived < n_piece and spans[arrived][0] < hi:
            piece_in[arrived].wait()
            arrived += 1
        if t >= 2:
            store[t - 2].wait()
        rank_one = gw_ref[lo:hi, :] * context_sum
        made[t % 2] = rank_one - mm(held[:, lo:hi], ctx[...], ((0,), (0,)))
        store.append(
            pltpu.make_async_copy(made.at[t % 2], out.at[pl.ds(lo, step)], out_sems.at[t % 2])
        )
        store[t].start()
    for copy in store[-2:]:
        copy.wait()


def weight_grad(pos, gw_col, norm_gain, value_weight, sums, contexts, pieces):
    n_dp = len(sums)
    width = contexts.shape[1]
    rows = pieces[0].shape[0]
    spans, at = [], 0
    for piece in pieces:
        spans.append((at, at + piece.shape[1]))
        at += piece.shape[1]
    step = CW if at % CW == 0 else at
    return pl.pallas_call(
        functools.partial(weight_kernel, n_dp, spans),
        out_shape=(
            jax.ShapeDtypeStruct((at, width), F32),
            jax.ShapeDtypeStruct((width // 128, 128), F32),
            jax.ShapeDtypeStruct((width // 128, 128), F32),
        ),
        in_specs=[SMEM] + [VMEM] * (3 + n_dp) + [ANY] * (1 + len(pieces)),
        out_specs=(ANY, VMEM, VMEM),
        scratch_shapes=[
            pltpu.VMEM(contexts.shape, BF16),
            pltpu.VMEM((rows, at), BF16),
            pltpu.VMEM((2, step, width), F32),
            pltpu.SemaphoreType.DMA((n_dp,)),
            pltpu.SemaphoreType.DMA((len(pieces),)),
            pltpu.SemaphoreType.DMA((2,)),
        ],
        compiler_params=params(60),
        name="weight_grad",
    )(pos, gw_col, norm_gain, value_weight, *sums, contexts, *pieces)


def parts_kernel(chunks, resid_cols, pos_ref, context, weight, resid, *refs):
    outs, columns, sems = refs[-len(chunks) - 2 : -2], refs[-2], refs[-1]
    fetch = [
        pltpu.make_async_copy(weight.at[:, pl.ds(at, CW)], columns.at[k], sems.at[k])
        for k, (_, at) in enumerate(chunks)
    ]
    for copy in fetch:
        copy.start()
    for k, (j, _) in enumerate(chunks):
        fetch[k].wait()
        part = jnp.dot(context[...], columns[k], preferred_element_type=F32)
        own = jnp.where(pos_ref[1] == j, resid[:, resid_cols].astype(F32), 0.0)
        outs[k][...] = (part + own).astype(BF16)


def partial_sums(pos, context, out_weight, resid, at, chunks, tie):
    piece = jax.ShapeDtypeStruct((CAPB, CW), BF16)
    n = len(chunks)
    return pl.pallas_call(
        functools.partial(parts_kernel, chunks, slice(at * CW, (at + 1) * CW)),
        out_shape=(piece,) * n,
        in_specs=[SMEM, VMEM, ANY, VMEM] + [ANY] * len(tie),
        out_specs=(VMEM,) * n,
        scratch_shapes=[
            pltpu.VMEM((n, out_weight.shape[0], CW), BF16),
            pltpu.SemaphoreType.DMA((n,)),
        ],
        compiler_params=params(52),
        cost_estimate=pl.CostEstimate(flops=0, bytes_accessed=0, transcendentals=0),
        name="partial_sums",
    )(pos, context, out_weight, resid, *tie)


def step_kernel(part, joins, totals, ends, n_tie, pos_ref, *refs):
    refs = list(refs)
    take = lambda n=1: [refs.pop(0) for _ in range(n)]
    mid = pos_ref[2] == 1
    add = lambda a, b: (a[...].astype(F32) + b[...].astype(F32)).astype(BF16)
    (new,) = take() if part else (None,)
    pair = take(2) if joins else None
    halves = take(2) if totals else None
    last = take(2) if ends else None
    take(n_tie)
    if joins:
        take()[0][...] = add(*pair)
    if totals:
        total = add(*halves)
        take()[0][...] = total if new is None else jnp.where(mid, total, new[...])
    if ends:
        take()[0][...] = jnp.where(mid, last[0][...], last[1][...])


def pair_kernel(first, second, *refs):
    for part, arrived, out in zip((first, second), refs[:2], refs[-2:]):
        out[...] = (part[...].astype(F32) + arrived[...].astype(F32)).astype(BF16)


def join_pair(parts, arrived, tie):
    piece = jax.ShapeDtypeStruct((CAPB, CW), BF16)
    return pl.pallas_call(
        pair_kernel,
        out_shape=(piece, piece),
        in_specs=[VMEM] * 4 + [ANY] * len(tie),
        out_specs=(VMEM, VMEM),
        compiler_params=params(16),
        cost_estimate=pl.CostEstimate(flops=0, bytes_accessed=0, transcendentals=0),
        name="join_pair",
    )(*parts, *arrived, *tie)


def line_sum(context, resid_of, out_weight, pos, order, first_pair, after_step):
    edge = [(0, 1), (1, 0), (2, 3), (3, 2)]
    middle = [(1, 2), (2, 1)]
    width = context.shape[1]
    n, n_blk = len(order), 4
    piece = jax.ShapeDtypeStruct((CAPB, CW), BF16)
    parts, joined, from_edge, from_mid, payloads, hidden = {}, {}, {}, {}, {}, {}

    def make_parts(first, count, tie):
        r = order[first][1]
        resid, at = resid_of(r)
        chunks = [(j, j * width + r * CW) for j, _ in order[first : first + count]]
        made = partial_sums(pos, context, out_weight, resid, at, chunks, tie)
        parts.update(zip(range(first, first + count), made))

    arrived = [lax.ppermute(part, "tensor", edge) for part in first_pair]
    make_parts(2, 2, tuple(first_pair[1:]))
    for s in (2, 3):
        payloads[s] = parts[s]
        from_edge[s] = lax.ppermute(parts[s], "tensor", edge)
    tie = after_step(1, hidden, (parts[3],))
    joined[0], joined[1] = join_pair(first_pair, arrived, tie)
    for s in (0, 1):
        from_mid[s] = lax.ppermute(joined[s], "tensor", middle)
    tie = (joined[1],)
    make_parts(4, 2, tie)
    for s in range(2, n + 4):
        joins, totals, ends = s < n, s < n + 2, s >= 4
        part = totals and s + 2 < n
        outs, args = {}, [pos]
        if part:
            args.append(parts[s + 2])
        if joins:
            args += [parts[s], from_edge[s]]
            outs["joined"] = piece
        if totals:
            args += [joined[s - 2], from_mid[s - 2]]
            outs["payload"] = piece
        if ends:
            args += [payloads[s], from_edge[s]]
            outs["hidden"] = piece
        made = pl.pallas_call(
            functools.partial(step_kernel, part, joins, totals, ends, len(tie)),
            out_shape=tuple(outs.values()),
            in_specs=[SMEM] + [VMEM] * (len(args) - 1) + [ANY] * len(tie),
            out_specs=(VMEM,) * len(outs),
            compiler_params=params(16),
            cost_estimate=pl.CostEstimate(flops=0, bytes_accessed=0, transcendentals=0),
            name="line_step",
        )(*args, *tie)
        made = dict(zip(outs, made))
        tie = (next(iter(made.values())),)
        if joins:
            joined[s] = made["joined"]
            from_mid[s] = lax.ppermute(joined[s], "tensor", middle)
        if s + 2 < n + 4:
            payloads[s + 2] = made["payload"]
            from_edge[s + 2] = lax.ppermute(payloads[s + 2], "tensor", edge)
        if ends:
            hidden[order[s - 4]] = made["hidden"]
        tie = after_step(s, hidden, tie)
        if s % 2 == 0 and s + n_blk < n:
            make_parts(s + n_blk, 2, tie)


def on_device(
    query_states,
    key_states,
    value_states,
    residual,
    returns,
    lengths,
    balance_list,
    out_weight,
    norm_gain,
    value_weight,
):
    n_dp, n_tensor = lax.axis_size("dp"), lax.axis_size("tensor")
    me, col = lax.axis_index("dp"), lax.axis_index("tensor")
    per_dev = query_states.shape[0]
    width = query_states.shape[2]
    model_width = out_weight.shape[1]
    kv = key_states.shape[2] // HD

    seq_len = query_states.shape[1]
    cap = per_dev // n_dp
    first = CW if width > CW else width
    pick, start, size = route(me.reshape(1), lengths, balance_list, n_dp, per_dev)
    parts_in = (query_states, key_states, value_states, residual)
    used = width + 2 * kv * HD + first
    start_spans = ((0, 0, width), (1, 0, kv * HD), (2, 0, kv * HD), (3, 0, first))
    rest_span = (3, first, width)
    far = range(2, n_dp)
    blocks, rest = [None] * n_dp, [None] * n_dp
    sent = gather_rollouts(
        pick, parts_in, returns, tuple((d, start_spans, None) for d in far), n_dp
    )
    for d, payload in zip(far, sent):
        blocks[d] = xor_move(payload, d, n_dp)
    gw_own = norm_gain * value_weight
    gw = lax.all_gather(gw_own, "tensor", axis=0, tiled=True)
    near = tuple((d, start_spans + (rest_span,), used) for d in (0, 1))
    sent = gather_rollouts(
        pick, parts_in, returns, near + tuple((d, (rest_span,), 0) for d in far), n_dp, (*sent[:1], gw)
    )
    blocks[0], blocks[1] = sent[0], xor_move(sent[1], 1, n_dp)
    rest[:2] = blocks[:2]
    for d, payload in zip(far, sent[2:]):
        rest[d] = xor_move(payload, d, n_dp)
    rest_cols = (used, used) + (0,) * len(far)
    place, fetch = spread(start, size, seq_len)
    gw_high = gw.astype(BF16)
    gw_low = (gw - gw_high.astype(F32)).astype(BF16)
    pair = jnp.stack([gw_high, gw_low])
    wgw = jnp.sum(mm(pair, out_weight, ((1,), (1,))), axis=0, keepdims=True)
    block = model_width // n_dp
    gw_col = lax.dynamic_slice_in_dim(gw, me * block, block).reshape(block, 1)
    is_mid = (col == 1) | (col == 2)
    pos = jnp.stack([me, col, is_mid.astype(jnp.int32)]).astype(jnp.int32)
    on_line = n_tensor == 4 and n_dp == 4
    per_block = width // CW
    order = [(j, r) for r in range(per_block) for j in (1, 2, 0, 3)]
    chunks = tuple((j, j * width + r * CW) for j, r in order[:2]) if on_line else ()
    context, resid_first, probs, parts = attention_forward(
        size, place, blocks, first, kv, seq_len, cap, (wgw, gw_col), pos, out_weight, chunks
    )
    gw_row, gw_mine = gw.reshape(1, model_width), gw_own.reshape(1, width)

    if on_line:
        later, owns, pieces = {}, [], []

        def move(held, tie):
            rounds = later["rounds"]
            bundle = bundle_pieces(
                [held[j, r] for j in range(n_tensor) for r in rounds], len(rounds), tie
            )
            moved = lax.all_to_all(bundle, "dp", split_axis=0, concat_axis=0, tiled=True)
            pieces.append(moved.reshape(n_dp * CAPB, bundle.shape[2]))
            return (bundle,)

        def after_step(s, hidden, tie):
            if s == 1:
                later["resid"], later["target"], later["context"] = pack(
                    place, rest, rest_cols, seq_len, cap, context, tie
                )
                return (later["target"],)
            if s in (20, 21):
                r, count = {20: (0, 2), 21: (2, 2)}[s]
                *later["state"], own = row_products(
                    pos,
                    out_weight,
                    gw_row,
                    [hidden[j, r + k] for j in range(n_tensor) for k in range(count)],
                    count,
                    r * CW,
                    width,
                    later.get("state"),
                    tie,
                )
                owns.append(own)
                return (own,)
            if s in (17, len(order) + 3):
                later["rounds"] = (0, 1, 2) if s == 17 else tuple(range(3, per_block))
                later["last"] = [hidden.get((j, per_block - 1)) for j in range(n_tensor)]
                later["tie"] = move(hidden, tie)
                return later["tie"]
            return tie

        line_sum(
            context,
            lambda r: (resid_first, 0) if r == 0 else (later["resid"], r - 1),
            out_weight,
            pos,
            order,
            parts,
            after_step,
        )
        acc, resid_out, sums, critic_row, a, b = last_products(
            pos,
            out_weight,
            gw_row,
            gw_mine,
            context,
            later["target"],
            later["last"],
            4 * CW,
            later["state"],
            owns,
            later["tie"],
        )
        contexts = lax.all_gather(later["context"], "dp", axis=0, tiled=True)
    else:
        resid_rest, target, _ = pack(place, rest, rest_cols, seq_len, cap, context)
        contexts = lax.all_gather(context, "dp", axis=0, tiled=True)
        resid = jnp.concatenate([resid_first, resid_rest], axis=1)
        part = jnp.dot(context, out_weight, preferred_element_type=F32)
        mine = lax.dynamic_slice_in_dim(part, col * width, width, axis=1) + resid.astype(F32)
        part = lax.dynamic_update_slice_in_dim(part, mine, col * width, axis=1)
        hidden = lax.psum(part.astype(BF16), "tensor")
        wide = hidden.astype(F32)
        sq = jnp.sum(wide * wide, axis=1, keepdims=True)
        vd = jnp.sum(wide * gw[None, :], axis=1, keepdims=True)
        acc = mm(hidden, out_weight, ((1,), (1,)))
        own = lax.dynamic_slice_in_dim(hidden, col * width, width, axis=1)
        pieces = [lax.all_to_all(hidden, "dp", split_axis=1, concat_axis=0, tiled=True)]
        resid_out, sums, critic_row, a, b = finish(
            sq, vd, target, gw_mine, context, own, model_width
        )

    all_sums = [sums] + [xor_move(sums, d, n_dp) for d in range(1, n_dp)]
    query_out, key_out, value_out = attention_backward(
        place, fetch, a, b, wgw, acc, probs, blocks, kv, seq_len, cap
    )
    weight_out, gain_out, value_weight_out = weight_grad(
        pos,
        gw_col,
        norm_gain.reshape(1, width),
        value_weight.reshape(1, width),
        all_sums,
        contexts,
        pieces,
    )
    return (
        critic_row.reshape(CAPB).astype(BF16),
        query_out,
        key_out,
        value_out,
        resid_out,
        weight_out,
        gain_out.reshape(width),
        value_weight_out.reshape(width),
    )


def solution(mesh):
    rows = P(("groups", "dp"), None, "tensor")
    packed = P(("groups", "dp"), "tensor")
    placed = (rows, rows, rows, rows, P(("groups", "dp"), None), P("groups"), P("groups"))
    placed += (P("tensor", None), P("tensor"), P("tensor"))
    return jax.shard_map(
        on_device,
        mesh=mesh,
        in_specs=placed,
        out_specs=(
            P(("groups", "dp")),
            packed,
            packed,
            packed,
            packed,
            packed,
            P(("groups", "tensor")),
            P(("groups", "tensor")),
        ),
        check_vma=False,
    )
```

```python
import functools
import math

import jax
import jax.numpy as jnp
from jax import lax
from jax.experimental import pallas as pl
from jax.experimental.pallas import tpu as pltpu
from jax.sharding import PartitionSpec as P

H = 40
KVH = 8
HD = 128
RATIO = H // KVH
CAPB = 576
EPS = 1e-06
NEG = -1e30
CW = 256
TAIL = 16
F32 = jnp.float32
BF16 = jnp.bfloat16
VMEM = pl.BlockSpec(memory_space=pltpu.VMEM)
SMEM = pl.BlockSpec(memory_space=pltpu.SMEM)
ANY = pl.BlockSpec(memory_space=pl.ANY)
HBM = pl.BlockSpec(memory_space=pltpu.HBM)


def params(mib):
    return pltpu.CompilerParams(vmem_limit_bytes=mib * 1024 * 1024)


def mm(a, b, dims):
    return lax.dot_general(a, b, (dims, ((), ())), preferred_element_type=F32)


def route_kernel(n_dp, per_dev, me_ref, len_ref, bal_ref, pick_ref, start_ref, size_ref, cnt_ref):
    cap = per_dev // n_dp
    me = me_ref[0]
    for d in range(n_dp):
        target = jnp.bitwise_xor(me, d)

        def outgoing(s, count):
            b = bal_ref[target * per_dev + s]
            home = lax.div(b, per_dev)

            @pl.when(home == me)
            def _():
                pick_ref[d * cap + count] = lax.rem(b, per_dev)

            return count + (home == me).astype(jnp.int32)

        lax.fori_loop(0, per_dev, outgoing, jnp.int32(0))
        cnt_ref[d] = jnp.int32(0)

    def incoming(s, run):
        b = bal_ref[me * per_dev + s]
        d = jnp.bitwise_xor(lax.div(b, per_dev), me)
        count = cnt_ref[d]
        size = len_ref[b]
        start_ref[d * cap + count] = run
        size_ref[d * cap + count] = size
        cnt_ref[d] = count + 1
        return run + size

    lax.fori_loop(0, per_dev, incoming, jnp.int32(0))


def route(me, lengths, balance_list, n_dp, per_dev):
    table = jax.ShapeDtypeStruct((per_dev,), jnp.int32)
    return pl.pallas_call(
        functools.partial(route_kernel, n_dp, per_dev),
        out_shape=(table, table, table),
        in_specs=[SMEM] * 3,
        out_specs=(SMEM, SMEM, SMEM),
        scratch_shapes=[pltpu.SMEM((n_dp,), jnp.int32)],
        name="route",
    )(me, lengths, balance_list)


def gather_kernel(cap, seq_len, outputs, n_part, pick_ref, *refs):
    parts, returns, outs, sems = refs[:n_part], refs[n_part], refs[-1 - len(outputs) : -1], refs[-1]
    copies = []
    for (d, spans, _), out in zip(outputs, outs):
        for i in range(cap):
            row = pick_ref[d * cap + i]
            col = 0
            for p, lo, hi in spans:
                copies.append(
                    pltpu.make_async_copy(
                        parts[p].at[row, :, pl.ds(lo, hi - lo)],
                        out.at[pl.ds(i * seq_len, seq_len), pl.ds(col, hi - lo)],
                        sems.at[len(copies)],
                    )
                )
                copies[-1].start()
                col += hi - lo
    for (d, _, at), out in zip(outputs, outs):
        if at is not None:
            rows = returns[...].astype(F32)
            home = lax.broadcasted_iota(jnp.int32, rows.shape, 0)
            picked = [
                jnp.sum(jnp.where(home == pick_ref[d * cap + i], rows, 0.0), axis=0, keepdims=True)
                for i in range(cap)
            ]
            picked.append(jnp.zeros((TAIL - cap, seq_len), F32))
            tail = jnp.concatenate(picked, axis=0).astype(BF16)
            out[cap * seq_len :, :] = jnp.zeros((TAIL, out.shape[1]), BF16)
            out[cap * seq_len :, at : at + seq_len] = tail
    for copy in copies:
        copy.wait()


def gather_rollouts(pick, parts, returns, outputs, n_dp, tie=()):
    per_dev, seq_len = parts[0].shape[:2]
    cap = per_dev // n_dp
    shapes = [
        (cap * seq_len + (0 if at is None else TAIL), sum(hi - lo for _, lo, hi in spans))
        for _, spans, at in outputs
    ]
    n_copy = sum(cap * len(spans) for _, spans, _ in outputs)
    return pl.pallas_call(
        functools.partial(gather_kernel, cap, seq_len, outputs, len(parts)),
        out_shape=tuple(jax.ShapeDtypeStruct(shape, BF16) for shape in shapes),
        in_specs=[SMEM] + [ANY] * len(parts) + [VMEM] + [ANY] * len(tie),
        out_specs=(VMEM,) * len(outputs),
        scratch_shapes=[pltpu.SemaphoreType.DMA((n_copy,))],
        compiler_params=params(60),
        name="gather_rollouts",
    )(pick, *parts, returns, *tie)


def xor_move(value, d, n_dp):
    return lax.ppermute(value, "dp", [(i, i ^ d) for i in range(n_dp)])


def pack_kernel(n_dp, cap, seq_len, cols, place, ctx_ref, *refs):
    blocks = refs[:n_dp]
    out, target, ctx_copy, rolled = refs[-4:]
    ctx_copy[...] = ctx_ref[...]
    returned = 0.0
    width = cap * seq_len
    for d in range(n_dp):
        lo = cols[d]
        rolled[d * width : (d + 1) * width, :] = blocks[d][:width, lo:]
        tail = blocks[d][width:, lo : lo + seq_len].astype(F32)
        line = jnp.concatenate([tail[i : i + 1, :] for i in range(cap)], axis=1)
        spots = place[:, d * width : (d + 1) * width].astype(F32)
        returned = returned + jnp.sum(spots * line, axis=1, keepdims=True)
    target[...] = returned
    out[...] = mm(place[...], rolled[...], ((1,), (0,))).astype(BF16)


def pack(place, blocks, cols, seq_len, cap, context, tie=()):
    n_dp = len(blocks)
    width = blocks[-1].shape[1] - cols[-1]
    return pl.pallas_call(
        functools.partial(pack_kernel, n_dp, cap, seq_len, cols),
        out_shape=(
            jax.ShapeDtypeStruct((CAPB, width), BF16),
            jax.ShapeDtypeStruct((CAPB, 1), F32),
            jax.ShapeDtypeStruct(context.shape, BF16),
        ),
        in_specs=[VMEM] * (2 + n_dp) + [ANY] * len(tie),
        out_specs=(VMEM,) * 3,
        scratch_shapes=[pltpu.VMEM((n_dp * cap * seq_len, width), BF16)],
        compiler_params=params(24),
        cost_estimate=pl.CostEstimate(flops=0, bytes_accessed=0, transcendentals=0),
        name="pack",
    )(place, context, *blocks, *tie)


def heads_of(rows, first):
    return jnp.concatenate(
        [rows[:, (first + r) * HD : (first + r + 1) * HD] for r in range(RATIO)], axis=0
    )


def spread_kernel(n_rollout, seq_len, start_ref, size_ref, place, fetch):
    iota = lambda shape, axis: lax.broadcasted_iota(jnp.int32, shape, axis)
    pair = (CAPB, 2 * seq_len)
    lane = iota(pair, 1)
    second = lane >= seq_len
    within = jnp.where(second, lane - seq_len, lane)
    offset = iota(pair, 0) - within
    turned = iota((seq_len, CAPB), 1) - iota((seq_len, CAPB), 0)
    row = iota((seq_len, CAPB), 0)
    for k in range(0, n_rollout, 2):
        first = (offset == start_ref[k]) & (within < size_ref[k]) & ~second
        other = (offset == start_ref[k + 1]) & (within < size_ref[k + 1]) & second
        place[:, k * seq_len : (k + 2) * seq_len] = (first | other).astype(BF16)
        for i in (k, k + 1):
            hit = (turned == start_ref[i]) & (row < size_ref[i])
            fetch[i * seq_len : (i + 1) * seq_len, :] = hit.astype(BF16)


def spread(start, size, seq_len):
    n_rollout = start.shape[0]
    rows = n_rollout * seq_len
    return pl.pallas_call(
        functools.partial(spread_kernel, n_rollout, seq_len),
        out_shape=(
            jax.ShapeDtypeStruct((CAPB, rows), BF16),
            jax.ShapeDtypeStruct((rows, CAPB), BF16),
        ),
        in_specs=[SMEM, SMEM],
        out_specs=(VMEM, VMEM),
        compiler_params=params(16),
        name="spread",
    )(start, size)


def forward_kernel(first, count, cap, seq_len, kv, chunks, size_ref, place, *refs):
    blocks, refs = refs[:count], refs[count:]
    if first == 0:
        probs_ref, room, rolled = refs[-3:]
    else:
        before, pos_ref, weight, out, extra, probs_ref, *part_refs = refs[:-3]
        rolled, columns, sems = refs[-3:]
        fetch = [
            pltpu.make_async_copy(weight.at[:, pl.ds(at, CW)], columns.at[k], sems.at[k])
            for k, (_, at) in enumerate(chunks)
        ]
        for copy in fetch:
            copy.start()
    qw = kv * RATIO * HD
    scale = 1.0 / math.sqrt(HD)
    span = RATIO * seq_len
    at_u = lax.broadcasted_iota(jnp.int32, (seq_len, span), 0)
    at_t = lax.rem(lax.broadcasted_iota(jnp.int32, (seq_len, span), 1), seq_len)
    at_t1 = lax.rem(lax.broadcasted_iota(jnp.int32, (1, span), 1), seq_len)
    causal = at_u <= at_t
    for d in range(count):
        for i in range(cap):
            size = size_ref[(first + d) * cap + i]
            rows = slice(i * seq_len, (i + 1) * seq_len)
            to = slice((d * cap + i) * seq_len, (d * cap + i + 1) * seq_len)
            keep = causal & (at_u < size)
            parts = []
            for g in range(kv):
                queries = heads_of(blocks[d][rows, g * RATIO * HD : (g + 1) * RATIO * HD], 0)
                keys = blocks[d][rows, qw + g * HD : qw + (g + 1) * HD]
                values = blocks[d][rows, qw + (kv + g) * HD : qw + (kv + g + 1) * HD]
                scores = jnp.where(keep, mm(keys, queries, ((1,), (1,))) * scale, NEG)
                top = jnp.max(scores, axis=0, keepdims=True)
                weights = jnp.exp(scores - top)
                total = jnp.sum(weights, axis=0, keepdims=True)
                probs = (weights * jnp.where(at_t1 < size, 1.0 / total, 0.0)).astype(BF16)
                probs_ref[d * cap + i, g] = probs
                mixed = mm(probs, values, ((0,), (0,)))
                parts += [mixed[r * seq_len : (r + 1) * seq_len] for r in range(RATIO)]
            rolled[to, :qw] = jnp.concatenate(parts, axis=1).astype(BF16)
            beside_from = qw + 2 * kv * HD
            beside_to = beside_from + rolled.shape[1] - qw
            rolled[to, qw:] = blocks[d][rows, beside_from:beside_to]
    packed = mm(place[:, first * cap * seq_len : (first + count) * cap * seq_len], rolled[...], ((1,), (0,)))
    if first == 0:
        room[...] = packed
    else:
        packed = packed + before[...]
        mixed = packed[:, :qw].astype(BF16)
        beside = packed[:, qw:]
        out[...] = mixed
        extra[...] = beside.astype(BF16)
        for k, (j, _) in enumerate(chunks):
            fetch[k].wait()
            own = jnp.where(pos_ref[1] == j, beside, 0.0)
            part = jnp.dot(mixed, columns[k], preferred_element_type=F32)
            part_refs[k][...] = (part + own).astype(BF16)


def attention_forward(size, place, blocks, extra, kv, seq_len, cap, ahead, pos, out_weight, chunks):
    n_dp = len(blocks)
    half = n_dp // 2
    width = kv * RATIO * HD
    shape = jax.ShapeDtypeStruct
    probs = shape((half * cap, kv, seq_len, RATIO * seq_len), BF16)
    rolled = pltpu.VMEM((half * cap * seq_len, width + extra), BF16)
    call = lambda first, outs, scratch, specs, more: pl.pallas_call(
        functools.partial(forward_kernel, first, half, cap, seq_len, kv, chunks),
        out_shape=outs,
        in_specs=[SMEM] + [VMEM] * (1 + half) + specs,
        out_specs=(VMEM,) * len(outs),
        scratch_shapes=scratch,
        compiler_params=params(52),
        name="attention_forward",
    )(size, place, *blocks[first : first + half], *more)
    probs_low, room = call(
        0, (probs, shape((CAPB, width + extra), F32)), [rolled], [ANY] * len(ahead), ahead
    )
    context, beside, probs_high, *parts = call(
        half,
        (shape((CAPB, width), BF16), shape((CAPB, extra), BF16), probs)
        + (shape((CAPB, CW), BF16),) * len(chunks),
        [
            rolled,
            pltpu.VMEM((max(1, len(chunks)), width, CW), BF16),
            pltpu.SemaphoreType.DMA((max(1, len(chunks)),)),
        ],
        [VMEM, SMEM, ANY],
        (room, pos, out_weight),
    )
    return context, beside, (probs_low, probs_high), parts


def backward_kernel(n_dp, cap, seq_len, kv, place, fetch, a_ref, b_ref, wgw_ref, acc_ref, *refs):
    all_probs, refs = refs[:2], refs[2:]
    blocks = refs[:n_dp]
    dq_out, dk_out, dv_out, grads, dq_all, dk_all, dv_all = refs[n_dp:]
    half = n_dp // 2
    qw = kv * RATIO * HD
    scale = 1.0 / math.sqrt(HD)
    packed = (a_ref[...] * wgw_ref[...] - b_ref[...] * acc_ref[...]).astype(BF16)
    grads[...] = mm(fetch[...], packed, ((1,), (0,))).astype(BF16)
    for d in range(n_dp):
        for i in range(cap):
            rows = slice(i * seq_len, (i + 1) * seq_len)
            to = slice((d * cap + i) * seq_len, (d * cap + i + 1) * seq_len)
            dq_parts, dk_parts, dv_parts = [], [], []
            for g in range(kv):
                cols = slice(g * RATIO * HD, (g + 1) * RATIO * HD)
                queries = heads_of(blocks[d][rows, cols], 0)
                keys = blocks[d][rows, qw + g * HD : qw + (g + 1) * HD]
                values = blocks[d][rows, qw + (kv + g) * HD : qw + (kv + g + 1) * HD]
                out_grad = heads_of(grads[to, cols], 0)
                probs_low = all_probs[d // half][d % half * cap + i, g]
                probs = probs_low.astype(F32)
                prob_grad = mm(values, out_grad, ((1,), (1,)))
                row_dot = jnp.sum(probs * prob_grad, axis=0, keepdims=True)
                score_grad = (probs * (prob_grad - row_dot) * scale).astype(BF16)
                dq = mm(score_grad, keys, ((0,), (0,)))
                dq_parts += [dq[r * seq_len : (r + 1) * seq_len] for r in range(RATIO)]
                dk_parts.append(mm(score_grad, queries, ((1,), (0,))))
                dv_parts.append(mm(probs_low, out_grad, ((1,), (0,))))
            for kept, parts in ((dq_all, dq_parts), (dk_all, dk_parts), (dv_all, dv_parts)):
                kept[to, :] = jnp.concatenate(parts, axis=1).astype(BF16)
    for out, kept in ((dq_out, dq_all), (dk_out, dk_all), (dv_out, dv_all)):
        out[...] = mm(place[...], kept[...], ((1,), (0,))).astype(BF16)


def attention_backward(place, fetch, a, b, wgw, acc, probs, blocks, kv, seq_len, cap):
    n_dp = len(blocks)
    qw, kw = kv * RATIO * HD, kv * HD
    rows = n_dp * cap * seq_len
    return pl.pallas_call(
        functools.partial(backward_kernel, n_dp, cap, seq_len, kv),
        out_shape=tuple(jax.ShapeDtypeStruct((CAPB, w), BF16) for w in (qw, kw, kw)),
        in_specs=[VMEM] * (8 + n_dp),
        out_specs=(VMEM,) * 3,
        scratch_shapes=[pltpu.VMEM((rows, w), BF16) for w in (qw, qw, kw, kw)],
        compiler_params=params(60),
        name="attention_backward",
    )(place, fetch, a, b, wgw, acc, *probs, *blocks)


def select(index, options):
    out = options[0]
    for k in range(1, len(options)):
        out = jnp.where(index == k, options[k], out)
    return out


def bundle_kernel(n_blk, n_round, *refs):
    pieces, out = refs[: n_blk * n_round], refs[-1]
    for j in range(n_blk):
        for k in range(n_round):
            out[j, :, k * CW : (k + 1) * CW] = pieces[j * n_round + k][...]


def bundle_pieces(pieces, n_round, tie, cost):
    n_blk = len(pieces) // n_round
    return pl.pallas_call(
        functools.partial(bundle_kernel, n_blk, n_round),
        out_shape=jax.ShapeDtypeStruct((n_blk, CAPB, n_round * CW), BF16),
        in_specs=[VMEM] * len(pieces) + [ANY] * len(tie),
        out_specs=VMEM,
        compiler_params=params(16),
        cost_estimate=pl.CostEstimate(flops=0, bytes_accessed=cost, transcendentals=0),
        name="bundle_pieces",
    )(*pieces, *tie)


def products(starts, n_cols, col, weight, gw_ref, piece, before, acc, sq, vd, own, columns, sems):
    n_blk = len(starts)
    cut = lambda j: slice(j * n_cols, (j + 1) * n_cols)
    fetch = [
        pltpu.make_async_copy(
            weight.at[:, pl.ds(at, n_cols)], columns.at[:, pl.ds(j * n_cols, n_cols)], sems.at[j]
        )
        for j, at in enumerate(starts)
    ]
    for copy in fetch:
        copy.start()
    tile = CAPB // 9
    for t in range(CAPB // tile):
        rows = slice(t * tile, (t + 1) * tile)
        pieces = [piece(j, rows) for j in range(n_blk)]
        own[rows, :] = select(col, pieces)
        squares = 0.0 if before is None else before[1][rows, :]
        dots = 0.0 if before is None else before[2][rows, :]
        for j, part in enumerate(pieces):
            wide = part.astype(F32)
            gain = gw_ref[:, starts[j] : starts[j] + n_cols]
            squares = squares + jnp.sum(wide * wide, axis=1, keepdims=True)
            dots = dots + jnp.sum(wide * gain, axis=1, keepdims=True)
        sq[rows, :] = squares
        vd[rows, :] = dots
    for copy in fetch:
        copy.wait()
    left = jnp.concatenate([piece(j, slice(0, CAPB)) for j in range(n_blk)], axis=1)
    total = mm(left, columns[...], ((1,), (1,)))
    acc[...] = total if before is None else total + before[0][...]


def rows_kernel(starts, n_cols, first, n_tie, pos_ref, weight, gw_ref, *refs):
    n_round = n_cols // CW
    held, refs = refs[: len(starts) * n_round], refs[len(starts) * n_round :]
    before, refs = (None, refs) if first else (refs[:3], refs[3:])
    piece = lambda j, rows: jnp.concatenate(
        [held[j * n_round + k][rows, :] for k in range(n_round)], axis=1
    )
    products(starts, n_cols, pos_ref[1], weight, gw_ref, piece, before, *refs[n_tie:])


def row_products(pos, out_weight, gw_row, pieces, n_round, first_col, width, state, tie):
    n_blk, n_cols = len(pieces) // n_round, n_round * CW
    depth = out_weight.shape[0]
    starts = [j * width + first_col for j in range(n_blk)]
    shape = jax.ShapeDtypeStruct
    column = shape((CAPB, 1), F32)
    before = [] if state is None else list(state)
    return pl.pallas_call(
        functools.partial(rows_kernel, starts, n_cols, state is None, len(tie)),
        out_shape=(shape((CAPB, depth), F32), column, column, shape((CAPB, n_cols), BF16)),
        in_specs=[SMEM, ANY] + [VMEM] * (1 + len(pieces) + len(before)) + [ANY] * len(tie),
        out_specs=(VMEM,) * 4,
        scratch_shapes=[
            pltpu.VMEM((depth, n_blk * n_cols), BF16),
            pltpu.SemaphoreType.DMA((n_blk,)),
        ],
        compiler_params=params(52),
        cost_estimate=pl.CostEstimate(flops=0, bytes_accessed=0, transcendentals=0),
        name="row_products",
    )(pos, out_weight, gw_row, *pieces, *before, *tie)


def row_of(column):
    return jnp.transpose(jnp.broadcast_to(column, (column.shape[0], 128)))[0:1, :]


def column_of(row):
    return jnp.transpose(jnp.broadcast_to(row, (128, row.shape[1])))[:, 0:1]


def norm_grads(model_width, sq, vd, target, gw_ref, ctx_ref, owns, outs):
    resid_out, sums, critic_row, a_col, b_col = outs
    inv_rms = lax.rsqrt(sq / model_width + EPS)
    critic = inv_rms * vd
    err = critic - target
    a = inv_rms * err
    b = inv_rms * inv_rms * inv_rms * err * vd / model_width
    a_col[...] = a
    b_col[...] = b
    critic_row[...] = row_of(critic)
    sums[...] = jnp.zeros_like(sums)
    sums[2:3, :CAPB] = row_of(b)
    at = 0
    for own in owns:
        cols = slice(at, at + own.shape[1])
        at += own.shape[1]
        hidden = own[...].astype(F32)
        resid_out[:, cols] = (a * gw_ref[:, cols] - b * hidden).astype(BF16)
        sums[0:1, cols] = jnp.sum(a * hidden, axis=0, keepdims=True)
    sums[1:2, :] = jnp.sum(a * ctx_ref[...].astype(F32), axis=0, keepdims=True)


def norm_shapes(width):
    shape = jax.ShapeDtypeStruct
    column = shape((CAPB, 1), F32)
    return (shape((CAPB, width), BF16), shape((8, width), F32), shape((1, CAPB), F32), column, column)


def last_kernel(starts, model_width, n_own, n_tie, pos_ref, weight, gw_ref, gw_own, ctx, target, *refs):
    n_blk = len(starts)
    pieces, refs = refs[:n_blk], refs[n_blk:]
    before, owns, refs = refs[:3], refs[3 : 3 + n_own], refs[3 + n_own + n_tie :]
    acc, outs, refs = refs[0], refs[1:6], refs[6:]
    sq, vd, own, columns, sems = refs
    piece = lambda j, rows: pieces[j][rows, :]
    products(
        starts, CW, pos_ref[1], weight, gw_ref, piece, before, acc, sq, vd, own, columns, sems
    )
    norm_grads(model_width, sq[...], vd[...], target[...], gw_own, ctx, (*owns, own), outs)


def last_products(
    pos, out_weight, gw_row, gw_own, context, target, pieces, first_col, state, owns, tie
):
    n_blk = len(pieces)
    depth, model_width = out_weight.shape
    width = context.shape[1]
    starts = [j * width + first_col for j in range(n_blk)]
    shape = jax.ShapeDtypeStruct
    return pl.pallas_call(
        functools.partial(last_kernel, starts, model_width, len(owns), len(tie)),
        out_shape=(shape((CAPB, depth), F32),) + norm_shapes(width),
        in_specs=[SMEM, ANY] + [VMEM] * (4 + n_blk + 3 + len(owns)) + [ANY] * len(tie),
        out_specs=(VMEM,) * 6,
        scratch_shapes=[
            pltpu.VMEM((CAPB, 1), F32),
            pltpu.VMEM((CAPB, 1), F32),
            pltpu.VMEM((CAPB, CW), BF16),
            pltpu.VMEM((depth, n_blk * CW), BF16),
            pltpu.SemaphoreType.DMA((n_blk,)),
        ],
        compiler_params=params(52),
        name="last_products",
    )(pos, out_weight, gw_row, gw_own, context, target, *pieces, *state, *owns, *tie)


def finish_kernel(model_width, sq, vd, target, gw_ref, ctx_ref, own, *outs):
    norm_grads(model_width, sq[...], vd[...], target[...], gw_ref, ctx_ref, (own,), outs)


def finish(sq, vd, target, gw_own, context, own, model_width):
    return pl.pallas_call(
        functools.partial(finish_kernel, model_width),
        out_shape=norm_shapes(context.shape[1]),
        in_specs=[VMEM] * 6,
        out_specs=(VMEM,) * 5,
        compiler_params=params(32),
        name="finish",
    )(sq, vd, target, gw_own, context, own)


def paired_sum(terms):
    while len(terms) > 1:
        terms = [terms[k] + terms[k + 1] for k in range(0, len(terms), 2)]
    return terms[0]


def weight_kernel(n_dp, spans, pos_ref, gw_ref, norm_gain, value_weight, *refs):
    n_piece = len(spans)
    sums, (ctx_hbm,) = refs[:n_dp], refs[n_dp : n_dp + 1]
    pieces = refs[n_dp + 1 : n_dp + 1 + n_piece]
    out, gain_out, value_out, *refs = refs[n_dp + 1 + n_piece :]
    ctx, held, made, ctx_sems, in_sems, out_sems = refs
    me = pos_ref[0]
    gain_sum = paired_sum([s[0:1, :] for s in sums])
    context_sum = paired_sum([s[1:2, :] for s in sums])
    for ref, row in ((gain_out, value_weight[...] * gain_sum), (value_out, norm_gain[...] * gain_sum)):
        ref[...] = jnp.concatenate([row[:, k * 128 : (k + 1) * 128] for k in range(ref.shape[0])], axis=0)
    rows_of = lambda d: pl.ds(pl.multiple_of(jnp.bitwise_xor(me, d) * CAPB, CAPB), CAPB)
    ctx_in = [
        pltpu.make_async_copy(ctx_hbm.at[rows_of(d)], ctx.at[rows_of(d)], ctx_sems.at[d])
        for d in range(n_dp)
    ]
    piece_in = [
        pltpu.make_async_copy(pieces[r], held.at[:, pl.ds(lo, hi - lo)], in_sems.at[r])
        for r, (lo, hi) in enumerate(spans)
    ]
    for copy in ctx_in + piece_in:
        copy.start()
    for d in range(n_dp):
        ctx_in[d].wait()
        factor = column_of(sums[d][2:3, :CAPB])
        rows = rows_of(d)
        ctx[rows, :] = (factor * ctx[rows, :].astype(F32)).astype(BF16)
    store, arrived = [], 0
    step = made.shape[1]
    for t in range(spans[-1][1] // step):
        lo, hi = t * step, (t + 1) * step
        while arrived < n_piece and spans[arrived][0] < hi:
            piece_in[arrived].wait()
            arrived += 1
        if t >= 2:
            store[t - 2].wait()
        rank_one = gw_ref[lo:hi, :] * context_sum
        made[t % 2] = rank_one - mm(held[:, lo:hi], ctx[...], ((0,), (0,)))
        store.append(
            pltpu.make_async_copy(made.at[t % 2], out.at[pl.ds(lo, step)], out_sems.at[t % 2])
        )
        store[t].start()
    for copy in store[-2:]:
        copy.wait()


def weight_grad(pos, gw_col, norm_gain, value_weight, sums, contexts, pieces):
    n_dp = len(sums)
    width = contexts.shape[1]
    rows = pieces[0].shape[0]
    spans, at = [], 0
    for piece in pieces:
        spans.append((at, at + piece.shape[1]))
        at += piece.shape[1]
    step = CW if at % CW == 0 else at
    return pl.pallas_call(
        functools.partial(weight_kernel, n_dp, spans),
        out_shape=(
            jax.ShapeDtypeStruct((at, width), F32),
            jax.ShapeDtypeStruct((width // 128, 128), F32),
            jax.ShapeDtypeStruct((width // 128, 128), F32),
        ),
        in_specs=[SMEM] + [VMEM] * (3 + n_dp) + [ANY] * (1 + len(pieces)),
        out_specs=(ANY, VMEM, VMEM),
        scratch_shapes=[
            pltpu.VMEM(contexts.shape, BF16),
            pltpu.VMEM((rows, at), BF16),
            pltpu.VMEM((2, step, width), F32),
            pltpu.SemaphoreType.DMA((n_dp,)),
            pltpu.SemaphoreType.DMA((len(pieces),)),
            pltpu.SemaphoreType.DMA((2,)),
        ],
        compiler_params=params(60),
        name="weight_grad",
    )(pos, gw_col, norm_gain, value_weight, *sums, contexts, *pieces)


def parts_kernel(chunks, resid_cols, pos_ref, context, weight, resid, *refs):
    outs, columns, sems = refs[-len(chunks) - 2 : -2], refs[-2], refs[-1]
    fetch = [
        pltpu.make_async_copy(weight.at[:, pl.ds(at, CW)], columns.at[k], sems.at[k])
        for k, (_, at) in enumerate(chunks)
    ]
    for copy in fetch:
        copy.start()
    for k, (j, _) in enumerate(chunks):
        fetch[k].wait()
        part = jnp.dot(context[...], columns[k], preferred_element_type=F32)
        own = jnp.where(pos_ref[1] == j, resid[:, resid_cols].astype(F32), 0.0)
        outs[k][...] = (part + own).astype(BF16)


def partial_sums(pos, context, out_weight, resid, at, chunks, tie):
    piece = jax.ShapeDtypeStruct((CAPB, CW), BF16)
    n = len(chunks)
    return pl.pallas_call(
        functools.partial(parts_kernel, chunks, slice(at * CW, (at + 1) * CW)),
        out_shape=(piece,) * n,
        in_specs=[SMEM, VMEM, ANY, VMEM] + [ANY] * len(tie),
        out_specs=(VMEM,) * n,
        scratch_shapes=[
            pltpu.VMEM((n, out_weight.shape[0], CW), BF16),
            pltpu.SemaphoreType.DMA((n,)),
        ],
        compiler_params=params(52),
        cost_estimate=pl.CostEstimate(flops=0, bytes_accessed=0, transcendentals=0),
        name="partial_sums",
    )(pos, context, out_weight, resid, *tie)


def step_kernel(part, joins, totals, ends, n_tie, pos_ref, *refs):
    refs = list(refs)
    take = lambda n=1: [refs.pop(0) for _ in range(n)]
    mid = pos_ref[2] == 1
    add = lambda a, b: (a[...].astype(F32) + b[...].astype(F32)).astype(BF16)
    (new,) = take() if part else (None,)
    pair = take(2) if joins else None
    halves = take(2) if totals else None
    last = take(2) if ends else None
    take(n_tie)
    if joins:
        take()[0][...] = add(*pair)
    if totals:
        total = add(*halves)
        take()[0][...] = total if new is None else jnp.where(mid, total, new[...])
    if ends:
        take()[0][...] = jnp.where(mid, last[0][...], last[1][...])


def pair_kernel(first, second, *refs):
    for part, arrived, out in zip((first, second), refs[:2], refs[-2:]):
        out[...] = (part[...].astype(F32) + arrived[...].astype(F32)).astype(BF16)


def join_pair(parts, arrived, tie):
    piece = jax.ShapeDtypeStruct((CAPB, CW), BF16)
    return pl.pallas_call(
        pair_kernel,
        out_shape=(piece, piece),
        in_specs=[VMEM] * 4 + [ANY] * len(tie),
        out_specs=(VMEM, VMEM),
        compiler_params=params(16),
        cost_estimate=pl.CostEstimate(flops=0, bytes_accessed=0, transcendentals=0),
        name="join_pair",
    )(*parts, *arrived, *tie)


def line_sum(context, resid_of, out_weight, pos, order, first_pair, after_step):
    edge = [(0, 1), (1, 0), (2, 3), (3, 2)]
    middle = [(1, 2), (2, 1)]
    width = context.shape[1]
    n, n_blk = len(order), 4
    piece = jax.ShapeDtypeStruct((CAPB, CW), BF16)
    parts, joined, from_edge, from_mid, payloads, hidden = {}, {}, {}, {}, {}, {}

    def make_parts(first, count, tie):
        r = order[first][1]
        resid, at = resid_of(r)
        chunks = [(j, j * width + r * CW) for j, _ in order[first : first + count]]
        made = partial_sums(pos, context, out_weight, resid, at, chunks, tie)
        parts.update(zip(range(first, first + count), made))

    arrived = [lax.ppermute(part, "tensor", edge) for part in first_pair]
    make_parts(2, 2, tuple(first_pair[1:]))
    for s in (2, 3):
        payloads[s] = parts[s]
        from_edge[s] = lax.ppermute(parts[s], "tensor", edge)
    joined[0], joined[1] = join_pair(first_pair, arrived, (parts[3],))
    for s in (0, 1):
        from_mid[s] = lax.ppermute(joined[s], "tensor", middle)
    tie = after_step(1, hidden, (joined[1],))
    make_parts(4, 2, tie)
    for s in range(2, n + 4):
        joins, totals, ends = s < n, s < n + 2, s >= 4
        part = totals and s + 2 < n
        outs, args = {}, [pos]
        if part:
            args.append(parts[s + 2])
        if joins:
            args += [parts[s], from_edge[s]]
            outs["joined"] = piece
        if totals:
            args += [joined[s - 2], from_mid[s - 2]]
            outs["payload"] = piece
        if ends:
            args += [payloads[s], from_edge[s]]
            outs["hidden"] = piece
        made = pl.pallas_call(
            functools.partial(step_kernel, part, joins, totals, ends, len(tie)),
            out_shape=tuple(outs.values()),
            in_specs=[SMEM] + [VMEM] * (len(args) - 1) + [ANY] * len(tie),
            out_specs=(VMEM,) * len(outs),
            compiler_params=params(16),
            cost_estimate=pl.CostEstimate(flops=0, bytes_accessed=0, transcendentals=0),
            name="line_step",
        )(*args, *tie)
        made = dict(zip(outs, made))
        tie = (next(iter(made.values())),)
        if joins:
            joined[s] = made["joined"]
            from_mid[s] = lax.ppermute(joined[s], "tensor", middle)
        if s + 2 < n + 4:
            payloads[s + 2] = made["payload"]
            from_edge[s + 2] = lax.ppermute(payloads[s + 2], "tensor", edge)
        if ends:
            hidden[order[s - 4]] = made["hidden"]
        tie = after_step(s, hidden, tie)
        if s % 2 == 0 and s + n_blk < n:
            make_parts(s + n_blk, 2, tie)


def on_device(
    query_states,
    key_states,
    value_states,
    residual,
    returns,
    lengths,
    balance_list,
    out_weight,
    norm_gain,
    value_weight,
):
    n_dp, n_tensor = lax.axis_size("dp"), lax.axis_size("tensor")
    me, col = lax.axis_index("dp"), lax.axis_index("tensor")
    per_dev = query_states.shape[0]
    width = query_states.shape[2]
    model_width = out_weight.shape[1]
    kv = key_states.shape[2] // HD

    seq_len = query_states.shape[1]
    cap = per_dev // n_dp
    first = CW if width > CW else width
    pick, start, size = route(me.reshape(1), lengths, balance_list, n_dp, per_dev)
    parts_in = (query_states, key_states, value_states, residual)
    used = width + 2 * kv * HD + first
    start_spans = ((0, 0, width), (1, 0, kv * HD), (2, 0, kv * HD), (3, 0, first))
    rest_span = (3, first, width)
    far = range(2, n_dp)
    blocks, rest = [None] * n_dp, [None] * n_dp
    sent = gather_rollouts(
        pick, parts_in, returns, tuple((d, start_spans, None) for d in far), n_dp
    )
    for d, payload in zip(far, sent):
        blocks[d] = xor_move(payload, d, n_dp)
    near = tuple((d, start_spans + (rest_span,), used) for d in (0, 1))
    sent = gather_rollouts(
        pick, parts_in, returns, near + tuple((d, (rest_span,), 0) for d in far), n_dp, sent[:1]
    )
    blocks[0], blocks[1] = sent[0], xor_move(sent[1], 1, n_dp)
    rest[:2] = blocks[:2]
    for d, payload in zip(far, sent[2:]):
        rest[d] = xor_move(payload, d, n_dp)
    rest_cols = (used, used) + (0,) * len(far)
    place, fetch = spread(start, size, seq_len)
    gw_own = norm_gain * value_weight
    gw = lax.all_gather(gw_own, "tensor", axis=0, tiled=True)
    gw_high = gw.astype(BF16)
    gw_low = (gw - gw_high.astype(F32)).astype(BF16)
    pair = jnp.stack([gw_high, gw_low])
    wgw = jnp.sum(mm(pair, out_weight, ((1,), (1,))), axis=0, keepdims=True)
    block = model_width // n_dp
    gw_col = lax.dynamic_slice_in_dim(gw, me * block, block).reshape(block, 1)
    is_mid = (col == 1) | (col == 2)
    pos = jnp.stack([me, col, is_mid.astype(jnp.int32)]).astype(jnp.int32)
    on_line = n_tensor == 4 and n_dp == 4
    per_block = width // CW
    order = [(j, r) for r in range(per_block) for j in (1, 2, 0, 3)]
    chunks = tuple((j, j * width + r * CW) for j, r in order[:2]) if on_line else ()
    context, resid_first, probs, parts = attention_forward(
        size, place, blocks, first, kv, seq_len, cap, (wgw, gw_col), pos, out_weight, chunks
    )
    gw_row, gw_mine = gw.reshape(1, model_width), gw_own.reshape(1, width)

    if on_line:
        later, owns, pieces = {}, [], []

        def move(held, tie):
            rounds = later["rounds"]
            bundle = bundle_pieces(
                [held[j, r] for j in range(n_tensor) for r in rounds],
                len(rounds),
                tie,
                200_000_000 if rounds[-1] == per_block - 1 else 0,
            )
            moved = lax.all_to_all(bundle, "dp", split_axis=0, concat_axis=0, tiled=True)
            pieces.append(moved.reshape(n_dp * CAPB, bundle.shape[2]))
            return (bundle,)

        def after_step(s, hidden, tie):
            if s == 1:
                later["resid"], later["target"], later["context"] = pack(
                    place, rest, rest_cols, seq_len, cap, context, tie
                )
            if s in (20, 21):
                r, count = {20: (0, 2), 21: (2, 2)}[s]
                *later["state"], own = row_products(
                    pos,
                    out_weight,
                    gw_row,
                    [hidden[j, r + k] for j in range(n_tensor) for k in range(count)],
                    count,
                    r * CW,
                    width,
                    later.get("state"),
                    tie,
                )
                owns.append(own)
                return (own,)
            if s in (17, len(order) + 3):
                later["rounds"] = (0, 1, 2) if s == 17 else tuple(range(3, per_block))
                later["last"] = [hidden.get((j, per_block - 1)) for j in range(n_tensor)]
                later["tie"] = move(hidden, tie)
                return later["tie"]
            return tie

        line_sum(
            context,
            lambda r: (resid_first, 0) if r == 0 else (later["resid"], r - 1),
            out_weight,
            pos,
            order,
            parts,
            after_step,
        )
        acc, resid_out, sums, critic_row, a, b = last_products(
            pos,
            out_weight,
            gw_row,
            gw_mine,
            context,
            later["target"],
            later["last"],
            4 * CW,
            later["state"],
            owns,
            later["tie"],
        )
        contexts = lax.all_gather(later["context"], "dp", axis=0, tiled=True)
    else:
        resid_rest, target, _ = pack(place, rest, rest_cols, seq_len, cap, context)
        contexts = lax.all_gather(context, "dp", axis=0, tiled=True)
        resid = jnp.concatenate([resid_first, resid_rest], axis=1)
        part = jnp.dot(context, out_weight, preferred_element_type=F32)
        mine = lax.dynamic_slice_in_dim(part, col * width, width, axis=1) + resid.astype(F32)
        part = lax.dynamic_update_slice_in_dim(part, mine, col * width, axis=1)
        hidden = lax.psum(part.astype(BF16), "tensor")
        wide = hidden.astype(F32)
        sq = jnp.sum(wide * wide, axis=1, keepdims=True)
        vd = jnp.sum(wide * gw[None, :], axis=1, keepdims=True)
        acc = mm(hidden, out_weight, ((1,), (1,)))
        own = lax.dynamic_slice_in_dim(hidden, col * width, width, axis=1)
        pieces = [lax.all_to_all(hidden, "dp", split_axis=1, concat_axis=0, tiled=True)]
        resid_out, sums, critic_row, a, b = finish(
            sq, vd, target, gw_mine, context, own, model_width
        )

    all_sums = [sums] + [xor_move(sums, d, n_dp) for d in range(1, n_dp)]
    query_out, key_out, value_out = attention_backward(
        place, fetch, a, b, wgw, acc, probs, blocks, kv, seq_len, cap
    )
    weight_out, gain_out, value_weight_out = weight_grad(
        pos,
        gw_col,
        norm_gain.reshape(1, width),
        value_weight.reshape(1, width),
        all_sums,
        contexts,
        pieces,
    )
    return (
        critic_row.reshape(CAPB).astype(BF16),
        query_out,
        key_out,
        value_out,
        resid_out,
        weight_out,
        gain_out.reshape(width),
        value_weight_out.reshape(width),
    )


def solution(mesh):
    rows = P(("groups", "dp"), None, "tensor")
    packed = P(("groups", "dp"), "tensor")
    placed = (rows, rows, rows, rows, P(("groups", "dp"), None), P("groups"), P("groups"))
    placed += (P("tensor", None), P("tensor"), P("tensor"))
    return jax.shard_map(
        on_device,
        mesh=mesh,
        in_specs=placed,
        out_specs=(
            P(("groups", "dp")),
            packed,
            packed,
            packed,
            packed,
            packed,
            P(("groups", "tensor")),
            P(("groups", "tensor")),
        ),
        check_vma=False,
    )
```

```python
import functools
import math

import jax
import jax.numpy as jnp
from jax import lax
from jax.experimental import pallas as pl
from jax.experimental.pallas import tpu as pltpu
from jax.sharding import PartitionSpec as P

H = 40
KVH = 8
HD = 128
RATIO = H // KVH
CAPB = 576
EPS = 1e-06
NEG = -1e30
CW = 256
TAIL = 16
F32 = jnp.float32
BF16 = jnp.bfloat16
VMEM = pl.BlockSpec(memory_space=pltpu.VMEM)
SMEM = pl.BlockSpec(memory_space=pltpu.SMEM)
ANY = pl.BlockSpec(memory_space=pl.ANY)
HBM = pl.BlockSpec(memory_space=pltpu.HBM)


def params(mib):
    return pltpu.CompilerParams(vmem_limit_bytes=mib * 1024 * 1024)


def mm(a, b, dims):
    return lax.dot_general(a, b, (dims, ((), ())), preferred_element_type=F32)


def route_kernel(n_dp, per_dev, me_ref, len_ref, bal_ref, pick_ref, start_ref, size_ref, cnt_ref):
    cap = per_dev // n_dp
    me = me_ref[0]
    for d in range(n_dp):
        target = jnp.bitwise_xor(me, d)

        def outgoing(s, count):
            b = bal_ref[target * per_dev + s]
            home = lax.div(b, per_dev)

            @pl.when(home == me)
            def _():
                pick_ref[d * cap + count] = lax.rem(b, per_dev)

            return count + (home == me).astype(jnp.int32)

        lax.fori_loop(0, per_dev, outgoing, jnp.int32(0))
        cnt_ref[d] = jnp.int32(0)

    def incoming(s, run):
        b = bal_ref[me * per_dev + s]
        d = jnp.bitwise_xor(lax.div(b, per_dev), me)
        count = cnt_ref[d]
        size = len_ref[b]
        start_ref[d * cap + count] = run
        size_ref[d * cap + count] = size
        cnt_ref[d] = count + 1
        return run + size

    lax.fori_loop(0, per_dev, incoming, jnp.int32(0))


def route(me, lengths, balance_list, n_dp, per_dev):
    table = jax.ShapeDtypeStruct((per_dev,), jnp.int32)
    return pl.pallas_call(
        functools.partial(route_kernel, n_dp, per_dev),
        out_shape=(table, table, table),
        in_specs=[SMEM] * 3,
        out_specs=(SMEM, SMEM, SMEM),
        scratch_shapes=[pltpu.SMEM((n_dp,), jnp.int32)],
        name="route",
    )(me, lengths, balance_list)


def gather_kernel(cap, seq_len, outputs, n_part, pick_ref, *refs):
    parts, returns, outs, sems = refs[:n_part], refs[n_part], refs[-1 - len(outputs) : -1], refs[-1]
    copies = []
    for (d, spans, _), out in zip(outputs, outs):
        for i in range(cap):
            row = pick_ref[d * cap + i]
            col = 0
            for p, lo, hi in spans:
                copies.append(
                    pltpu.make_async_copy(
                        parts[p].at[row, :, pl.ds(lo, hi - lo)],
                        out.at[pl.ds(i * seq_len, seq_len), pl.ds(col, hi - lo)],
                        sems.at[len(copies)],
                    )
                )
                copies[-1].start()
                col += hi - lo
    for (d, _, at), out in zip(outputs, outs):
        if at is not None:
            rows = returns[...].astype(F32)
            home = lax.broadcasted_iota(jnp.int32, rows.shape, 0)
            picked = [
                jnp.sum(jnp.where(home == pick_ref[d * cap + i], rows, 0.0), axis=0, keepdims=True)
                for i in range(cap)
            ]
            picked.append(jnp.zeros((TAIL - cap, seq_len), F32))
            tail = jnp.concatenate(picked, axis=0).astype(BF16)
            out[cap * seq_len :, :] = jnp.zeros((TAIL, out.shape[1]), BF16)
            out[cap * seq_len :, at : at + seq_len] = tail
    for copy in copies:
        copy.wait()


def gather_rollouts(pick, parts, returns, outputs, n_dp, tie=()):
    per_dev, seq_len = parts[0].shape[:2]
    cap = per_dev // n_dp
    shapes = [
        (cap * seq_len + (0 if at is None else TAIL), sum(hi - lo for _, lo, hi in spans))
        for _, spans, at in outputs
    ]
    n_copy = sum(cap * len(spans) for _, spans, _ in outputs)
    return pl.pallas_call(
        functools.partial(gather_kernel, cap, seq_len, outputs, len(parts)),
        out_shape=tuple(jax.ShapeDtypeStruct(shape, BF16) for shape in shapes),
        in_specs=[SMEM] + [ANY] * len(parts) + [VMEM] + [ANY] * len(tie),
        out_specs=(VMEM,) * len(outputs),
        scratch_shapes=[pltpu.SemaphoreType.DMA((n_copy,))],
        compiler_params=params(60),
        name="gather_rollouts",
    )(pick, *parts, returns, *tie)


def xor_move(value, d, n_dp):
    return lax.ppermute(value, "dp", [(i, i ^ d) for i in range(n_dp)])


def pack_kernel(n_dp, cap, seq_len, cols, place, ctx_ref, *refs):
    blocks = refs[:n_dp]
    out, target, ctx_copy, rolled = refs[-4:]
    ctx_copy[...] = ctx_ref[...]
    returned = 0.0
    width = cap * seq_len
    for d in range(n_dp):
        lo = cols[d]
        rolled[d * width : (d + 1) * width, :] = blocks[d][:width, lo:]
        tail = blocks[d][width:, lo : lo + seq_len].astype(F32)
        line = jnp.concatenate([tail[i : i + 1, :] for i in range(cap)], axis=1)
        spots = place[:, d * width : (d + 1) * width].astype(F32)
        returned = returned + jnp.sum(spots * line, axis=1, keepdims=True)
    target[...] = returned
    out[...] = mm(place[...], rolled[...], ((1,), (0,))).astype(BF16)


def pack(place, blocks, cols, seq_len, cap, context, tie=()):
    n_dp = len(blocks)
    width = blocks[-1].shape[1] - cols[-1]
    return pl.pallas_call(
        functools.partial(pack_kernel, n_dp, cap, seq_len, cols),
        out_shape=(
            jax.ShapeDtypeStruct((CAPB, width), BF16),
            jax.ShapeDtypeStruct((CAPB, 1), F32),
            jax.ShapeDtypeStruct(context.shape, BF16),
        ),
        in_specs=[VMEM] * (2 + n_dp) + [ANY] * len(tie),
        out_specs=(VMEM,) * 3,
        scratch_shapes=[pltpu.VMEM((n_dp * cap * seq_len, width), BF16)],
        compiler_params=params(24),
        cost_estimate=pl.CostEstimate(flops=0, bytes_accessed=0, transcendentals=0),
        name="pack",
    )(place, context, *blocks, *tie)


def heads_of(rows, first):
    return jnp.concatenate(
        [rows[:, (first + r) * HD : (first + r + 1) * HD] for r in range(RATIO)], axis=0
    )


def spread_kernel(n_rollout, seq_len, start_ref, size_ref, place, fetch):
    iota = lambda shape, axis: lax.broadcasted_iota(jnp.int32, shape, axis)
    pair = (CAPB, 2 * seq_len)
    lane = iota(pair, 1)
    second = lane >= seq_len
    within = jnp.where(second, lane - seq_len, lane)
    offset = iota(pair, 0) - within
    turned = iota((seq_len, CAPB), 1) - iota((seq_len, CAPB), 0)
    row = iota((seq_len, CAPB), 0)
    for k in range(0, n_rollout, 2):
        first = (offset == start_ref[k]) & (within < size_ref[k]) & ~second
        other = (offset == start_ref[k + 1]) & (within < size_ref[k + 1]) & second
        place[:, k * seq_len : (k + 2) * seq_len] = (first | other).astype(BF16)
        for i in (k, k + 1):
            hit = (turned == start_ref[i]) & (row < size_ref[i])
            fetch[i * seq_len : (i + 1) * seq_len, :] = hit.astype(BF16)


def spread(start, size, seq_len):
    n_rollout = start.shape[0]
    rows = n_rollout * seq_len
    return pl.pallas_call(
        functools.partial(spread_kernel, n_rollout, seq_len),
        out_shape=(
            jax.ShapeDtypeStruct((CAPB, rows), BF16),
            jax.ShapeDtypeStruct((rows, CAPB), BF16),
        ),
        in_specs=[SMEM, SMEM],
        out_specs=(VMEM, VMEM),
        compiler_params=params(16),
        name="spread",
    )(start, size)


def forward_kernel(first, count, cap, seq_len, kv, chunks, size_ref, place, *refs):
    blocks, refs = refs[:count], refs[count:]
    if first == 0:
        probs_ref, room, rolled = refs[-3:]
    else:
        before, pos_ref, weight, out, extra, probs_ref, *part_refs = refs[:-3]
        rolled, columns, sems = refs[-3:]
        fetch = [
            pltpu.make_async_copy(weight.at[:, pl.ds(at, CW)], columns.at[k], sems.at[k])
            for k, (_, at) in enumerate(chunks)
        ]
        for copy in fetch:
            copy.start()
    qw = kv * RATIO * HD
    scale = 1.0 / math.sqrt(HD)
    span = RATIO * seq_len
    at_u = lax.broadcasted_iota(jnp.int32, (seq_len, span), 0)
    at_t = lax.rem(lax.broadcasted_iota(jnp.int32, (seq_len, span), 1), seq_len)
    at_t1 = lax.rem(lax.broadcasted_iota(jnp.int32, (1, span), 1), seq_len)
    causal = at_u <= at_t
    for d in range(count):
        for i in range(cap):
            size = size_ref[(first + d) * cap + i]
            rows = slice(i * seq_len, (i + 1) * seq_len)
            to = slice((d * cap + i) * seq_len, (d * cap + i + 1) * seq_len)
            keep = causal & (at_u < size)
            parts = []
            for g in range(kv):
                queries = heads_of(blocks[d][rows, g * RATIO * HD : (g + 1) * RATIO * HD], 0)
                keys = blocks[d][rows, qw + g * HD : qw + (g + 1) * HD]
                values = blocks[d][rows, qw + (kv + g) * HD : qw + (kv + g + 1) * HD]
                scores = jnp.where(keep, mm(keys, queries, ((1,), (1,))) * scale, NEG)
                top = jnp.max(scores, axis=0, keepdims=True)
                weights = jnp.exp(scores - top)
                total = jnp.sum(weights, axis=0, keepdims=True)
                probs = (weights * jnp.where(at_t1 < size, 1.0 / total, 0.0)).astype(BF16)
                probs_ref[d * cap + i, g] = probs
                mixed = mm(probs, values, ((0,), (0,)))
                parts += [mixed[r * seq_len : (r + 1) * seq_len] for r in range(RATIO)]
            rolled[to, :qw] = jnp.concatenate(parts, axis=1).astype(BF16)
            beside_from = qw + 2 * kv * HD
            beside_to = beside_from + rolled.shape[1] - qw
            rolled[to, qw:] = blocks[d][rows, beside_from:beside_to]
    packed = mm(place[:, first * cap * seq_len : (first + count) * cap * seq_len], rolled[...], ((1,), (0,)))
    if first == 0:
        room[...] = packed
    else:
        packed = packed + before[...]
        mixed = packed[:, :qw].astype(BF16)
        beside = packed[:, qw:]
        out[...] = mixed
        extra[...] = beside.astype(BF16)
        for k, (j, _) in enumerate(chunks):
            fetch[k].wait()
            own = jnp.where(pos_ref[1] == j, beside, 0.0)
            part = jnp.dot(mixed, columns[k], preferred_element_type=F32)
            part_refs[k][...] = (part + own).astype(BF16)


def attention_forward(size, place, blocks, extra, kv, seq_len, cap, ahead, pos, out_weight, chunks):
    n_dp = len(blocks)
    half = n_dp // 2
    width = kv * RATIO * HD
    shape = jax.ShapeDtypeStruct
    probs = shape((half * cap, kv, seq_len, RATIO * seq_len), BF16)
    rolled = pltpu.VMEM((half * cap * seq_len, width + extra), BF16)
    call = lambda first, outs, scratch, specs, more: pl.pallas_call(
        functools.partial(forward_kernel, first, half, cap, seq_len, kv, chunks),
        out_shape=outs,
        in_specs=[SMEM] + [VMEM] * (1 + half) + specs,
        out_specs=(VMEM,) * len(outs),
        scratch_shapes=scratch,
        compiler_params=params(52),
        name="attention_forward",
    )(size, place, *blocks[first : first + half], *more)
    probs_low, room = call(
        0, (probs, shape((CAPB, width + extra), F32)), [rolled], [ANY] * len(ahead), ahead
    )
    context, beside, probs_high, *parts = call(
        half,
        (shape((CAPB, width), BF16), shape((CAPB, extra), BF16), probs)
        + (shape((CAPB, CW), BF16),) * len(chunks),
        [
            rolled,
            pltpu.VMEM((max(1, len(chunks)), width, CW), BF16),
            pltpu.SemaphoreType.DMA((max(1, len(chunks)),)),
        ],
        [VMEM, SMEM, ANY],
        (room, pos, out_weight),
    )
    return context, beside, (probs_low, probs_high), parts


def backward_kernel(n_dp, cap, seq_len, kv, place, fetch, a_ref, b_ref, wgw_ref, acc_ref, *refs):
    all_probs, refs = refs[:2], refs[2:]
    blocks = refs[:n_dp]
    dq_out, dk_out, dv_out, grads, dq_all, dk_all, dv_all = refs[n_dp:]
    half = n_dp // 2
    qw = kv * RATIO * HD
    scale = 1.0 / math.sqrt(HD)
    packed = (a_ref[...] * wgw_ref[...] - b_ref[...] * acc_ref[...]).astype(BF16)
    grads[...] = mm(fetch[...], packed, ((1,), (0,))).astype(BF16)
    for d in range(n_dp):
        for i in range(cap):
            rows = slice(i * seq_len, (i + 1) * seq_len)
            to = slice((d * cap + i) * seq_len, (d * cap + i + 1) * seq_len)
            dq_parts, dk_parts, dv_parts = [], [], []
            for g in range(kv):
                cols = slice(g * RATIO * HD, (g + 1) * RATIO * HD)
                queries = heads_of(blocks[d][rows, cols], 0)
                keys = blocks[d][rows, qw + g * HD : qw + (g + 1) * HD]
                values = blocks[d][rows, qw + (kv + g) * HD : qw + (kv + g + 1) * HD]
                out_grad = heads_of(grads[to, cols], 0)
                probs_low = all_probs[d // half][d % half * cap + i, g]
                probs = probs_low.astype(F32)
                prob_grad = mm(values, out_grad, ((1,), (1,)))
                row_dot = jnp.sum(probs * prob_grad, axis=0, keepdims=True)
                score_grad = (probs * (prob_grad - row_dot) * scale).astype(BF16)
                dq = mm(score_grad, keys, ((0,), (0,)))
                dq_parts += [dq[r * seq_len : (r + 1) * seq_len] for r in range(RATIO)]
                dk_parts.append(mm(score_grad, queries, ((1,), (0,))))
                dv_parts.append(mm(probs_low, out_grad, ((1,), (0,))))
            for kept, parts in ((dq_all, dq_parts), (dk_all, dk_parts), (dv_all, dv_parts)):
                kept[to, :] = jnp.concatenate(parts, axis=1).astype(BF16)
    for out, kept in ((dq_out, dq_all), (dk_out, dk_all), (dv_out, dv_all)):
        out[...] = mm(place[...], kept[...], ((1,), (0,))).astype(BF16)


def attention_backward(place, fetch, a, b, wgw, acc, probs, blocks, kv, seq_len, cap):
    n_dp = len(blocks)
    qw, kw = kv * RATIO * HD, kv * HD
    rows = n_dp * cap * seq_len
    return pl.pallas_call(
        functools.partial(backward_kernel, n_dp, cap, seq_len, kv),
        out_shape=tuple(jax.ShapeDtypeStruct((CAPB, w), BF16) for w in (qw, kw, kw)),
        in_specs=[VMEM] * (8 + n_dp),
        out_specs=(VMEM,) * 3,
        scratch_shapes=[pltpu.VMEM((rows, w), BF16) for w in (qw, qw, kw, kw)],
        compiler_params=params(60),
        name="attention_backward",
    )(place, fetch, a, b, wgw, acc, *probs, *blocks)


def select(index, options):
    out = options[0]
    for k in range(1, len(options)):
        out = jnp.where(index == k, options[k], out)
    return out


def bundle_kernel(n_blk, n_round, *refs):
    pieces, out = refs[: n_blk * n_round], refs[-1]
    for j in range(n_blk):
        for k in range(n_round):
            out[j, :, k * CW : (k + 1) * CW] = pieces[j * n_round + k][...]


def bundle_pieces(pieces, n_round, tie):
    n_blk = len(pieces) // n_round
    return pl.pallas_call(
        functools.partial(bundle_kernel, n_blk, n_round),
        out_shape=jax.ShapeDtypeStruct((n_blk, CAPB, n_round * CW), BF16),
        in_specs=[VMEM] * len(pieces) + [ANY] * len(tie),
        out_specs=VMEM,
        compiler_params=params(16),
        cost_estimate=pl.CostEstimate(flops=0, bytes_accessed=0, transcendentals=0),
        name="bundle_pieces",
    )(*pieces, *tie)


def products(starts, n_cols, col, weight, gw_ref, piece, before, acc, sq, vd, own, columns, sems):
    n_blk = len(starts)
    cut = lambda j: slice(j * n_cols, (j + 1) * n_cols)
    fetch = [
        pltpu.make_async_copy(
            weight.at[:, pl.ds(at, n_cols)], columns.at[:, pl.ds(j * n_cols, n_cols)], sems.at[j]
        )
        for j, at in enumerate(starts)
    ]
    for copy in fetch:
        copy.start()
    tile = CAPB // 9
    for t in range(CAPB // tile):
        rows = slice(t * tile, (t + 1) * tile)
        pieces = [piece(j, rows) for j in range(n_blk)]
        own[rows, :] = select(col, pieces)
        squares = 0.0 if before is None else before[1][rows, :]
        dots = 0.0 if before is None else before[2][rows, :]
        for j, part in enumerate(pieces):
            wide = part.astype(F32)
            gain = gw_ref[:, starts[j] : starts[j] + n_cols]
            squares = squares + jnp.sum(wide * wide, axis=1, keepdims=True)
            dots = dots + jnp.sum(wide * gain, axis=1, keepdims=True)
        sq[rows, :] = squares
        vd[rows, :] = dots
    for copy in fetch:
        copy.wait()
    left = jnp.concatenate([piece(j, slice(0, CAPB)) for j in range(n_blk)], axis=1)
    total = mm(left, columns[...], ((1,), (1,)))
    acc[...] = total if before is None else total + before[0][...]


def rows_kernel(starts, n_cols, first, n_tie, pos_ref, weight, gw_ref, *refs):
    n_round = n_cols // CW
    held, refs = refs[: len(starts) * n_round], refs[len(starts) * n_round :]
    before, refs = (None, refs) if first else (refs[:3], refs[3:])
    piece = lambda j, rows: jnp.concatenate(
        [held[j * n_round + k][rows, :] for k in range(n_round)], axis=1
    )
    products(starts, n_cols, pos_ref[1], weight, gw_ref, piece, before, *refs[n_tie:])


def row_products(pos, out_weight, gw_row, pieces, n_round, first_col, width, state, tie):
    n_blk, n_cols = len(pieces) // n_round, n_round * CW
    depth = out_weight.shape[0]
    starts = [j * width + first_col for j in range(n_blk)]
    shape = jax.ShapeDtypeStruct
    column = shape((CAPB, 1), F32)
    before = [] if state is None else list(state)
    return pl.pallas_call(
        functools.partial(rows_kernel, starts, n_cols, state is None, len(tie)),
        out_shape=(shape((CAPB, depth), F32), column, column, shape((CAPB, n_cols), BF16)),
        in_specs=[SMEM, ANY] + [VMEM] * (1 + len(pieces) + len(before)) + [ANY] * len(tie),
        out_specs=(VMEM,) * 4,
        scratch_shapes=[
            pltpu.VMEM((depth, n_blk * n_cols), BF16),
            pltpu.SemaphoreType.DMA((n_blk,)),
        ],
        compiler_params=params(52),
        cost_estimate=pl.CostEstimate(flops=0, bytes_accessed=0, transcendentals=0),
        name="row_products",
    )(pos, out_weight, gw_row, *pieces, *before, *tie)


def row_of(column):
    return jnp.transpose(jnp.broadcast_to(column, (column.shape[0], 128)))[0:1, :]


def column_of(row):
    return jnp.transpose(jnp.broadcast_to(row, (128, row.shape[1])))[:, 0:1]


def norm_grads(model_width, sq, vd, target, gw_ref, ctx_ref, owns, outs):
    resid_out, sums, critic_row, a_col, b_col = outs
    inv_rms = lax.rsqrt(sq / model_width + EPS)
    critic = inv_rms * vd
    err = critic - target
    a = inv_rms * err
    b = inv_rms * inv_rms * inv_rms * err * vd / model_width
    a_col[...] = a
    b_col[...] = b
    critic_row[...] = row_of(critic)
    sums[...] = jnp.zeros_like(sums)
    sums[2:3, :CAPB] = row_of(b)
    at = 0
    for own in owns:
        cols = slice(at, at + own.shape[1])
        at += own.shape[1]
        hidden = own[...].astype(F32)
        resid_out[:, cols] = (a * gw_ref[:, cols] - b * hidden).astype(BF16)
        sums[0:1, cols] = jnp.sum(a * hidden, axis=0, keepdims=True)
    sums[1:2, :] = jnp.sum(a * ctx_ref[...].astype(F32), axis=0, keepdims=True)


def norm_shapes(width):
    shape = jax.ShapeDtypeStruct
    column = shape((CAPB, 1), F32)
    return (shape((CAPB, width), BF16), shape((8, width), F32), shape((1, CAPB), F32), column, column)


def last_kernel(starts, model_width, n_own, n_tie, pos_ref, weight, gw_ref, gw_own, ctx, target, *refs):
    n_blk = len(starts)
    pieces, refs = refs[:n_blk], refs[n_blk:]
    before, owns, refs = refs[:3], refs[3 : 3 + n_own], refs[3 + n_own + n_tie :]
    acc, outs, refs = refs[0], refs[1:6], refs[6:]
    sq, vd, own, columns, sems = refs
    piece = lambda j, rows: pieces[j][rows, :]
    products(
        starts, CW, pos_ref[1], weight, gw_ref, piece, before, acc, sq, vd, own, columns, sems
    )
    norm_grads(model_width, sq[...], vd[...], target[...], gw_own, ctx, (*owns, own), outs)


def last_products(
    pos, out_weight, gw_row, gw_own, context, target, pieces, first_col, state, owns, tie
):
    n_blk = len(pieces)
    depth, model_width = out_weight.shape
    width = context.shape[1]
    starts = [j * width + first_col for j in range(n_blk)]
    shape = jax.ShapeDtypeStruct
    return pl.pallas_call(
        functools.partial(last_kernel, starts, model_width, len(owns), len(tie)),
        out_shape=(shape((CAPB, depth), F32),) + norm_shapes(width),
        in_specs=[SMEM, ANY] + [VMEM] * (4 + n_blk + 3 + len(owns)) + [ANY] * len(tie),
        out_specs=(VMEM,) * 6,
        scratch_shapes=[
            pltpu.VMEM((CAPB, 1), F32),
            pltpu.VMEM((CAPB, 1), F32),
            pltpu.VMEM((CAPB, CW), BF16),
            pltpu.VMEM((depth, n_blk * CW), BF16),
            pltpu.SemaphoreType.DMA((n_blk,)),
        ],
        compiler_params=params(52),
        name="last_products",
    )(pos, out_weight, gw_row, gw_own, context, target, *pieces, *state, *owns, *tie)


def finish_kernel(model_width, sq, vd, target, gw_ref, ctx_ref, own, *outs):
    norm_grads(model_width, sq[...], vd[...], target[...], gw_ref, ctx_ref, (own,), outs)


def finish(sq, vd, target, gw_own, context, own, model_width):
    return pl.pallas_call(
        functools.partial(finish_kernel, model_width),
        out_shape=norm_shapes(context.shape[1]),
        in_specs=[VMEM] * 6,
        out_specs=(VMEM,) * 5,
        compiler_params=params(32),
        name="finish",
    )(sq, vd, target, gw_own, context, own)


def paired_sum(terms):
    while len(terms) > 1:
        terms = [terms[k] + terms[k + 1] for k in range(0, len(terms), 2)]
    return terms[0]


def weight_kernel(n_dp, spans, pos_ref, gw_ref, norm_gain, value_weight, *refs):
    n_piece = len(spans)
    sums, (ctx_hbm,) = refs[:n_dp], refs[n_dp : n_dp + 1]
    pieces = refs[n_dp + 1 : n_dp + 1 + n_piece]
    out, gain_out, value_out, *refs = refs[n_dp + 1 + n_piece :]
    ctx, held, made, ctx_sems, in_sems, out_sems = refs
    me = pos_ref[0]
    gain_sum = paired_sum([s[0:1, :] for s in sums])
    context_sum = paired_sum([s[1:2, :] for s in sums])
    for ref, row in ((gain_out, value_weight[...] * gain_sum), (value_out, norm_gain[...] * gain_sum)):
        ref[...] = jnp.concatenate([row[:, k * 128 : (k + 1) * 128] for k in range(ref.shape[0])], axis=0)
    rows_of = lambda d: pl.ds(pl.multiple_of(jnp.bitwise_xor(me, d) * CAPB, CAPB), CAPB)
    ctx_in = [
        pltpu.make_async_copy(ctx_hbm.at[rows_of(d)], ctx.at[rows_of(d)], ctx_sems.at[d])
        for d in range(n_dp)
    ]
    piece_in = [
        pltpu.make_async_copy(pieces[r], held.at[:, pl.ds(lo, hi - lo)], in_sems.at[r])
        for r, (lo, hi) in enumerate(spans)
    ]
    for copy in ctx_in + piece_in:
        copy.start()
    for d in range(n_dp):
        ctx_in[d].wait()
        factor = column_of(sums[d][2:3, :CAPB])
        rows = rows_of(d)
        ctx[rows, :] = (factor * ctx[rows, :].astype(F32)).astype(BF16)
    store, arrived = [], 0
    step = made.shape[1]
    for t in range(spans[-1][1] // step):
        lo, hi = t * step, (t + 1) * step
        while arrived < n_piece and spans[arrived][0] < hi:
            piece_in[arrived].wait()
            arrived += 1
        if t >= 2:
            store[t - 2].wait()
        rank_one = gw_ref[lo:hi, :] * context_sum
        made[t % 2] = rank_one - mm(held[:, lo:hi], ctx[...], ((0,), (0,)))
        store.append(
            pltpu.make_async_copy(made.at[t % 2], out.at[pl.ds(lo, step)], out_sems.at[t % 2])
        )
        store[t].start()
    for copy in store[-2:]:
        copy.wait()


def weight_grad(pos, gw_col, norm_gain, value_weight, sums, contexts, pieces):
    n_dp = len(sums)
    width = contexts.shape[1]
    rows = pieces[0].shape[0]
    spans, at = [], 0
    for piece in pieces:
        spans.append((at, at + piece.shape[1]))
        at += piece.shape[1]
    step = CW if at % CW == 0 else at
    return pl.pallas_call(
        functools.partial(weight_kernel, n_dp, spans),
        out_shape=(
            jax.ShapeDtypeStruct((at, width), F32),
            jax.ShapeDtypeStruct((width // 128, 128), F32),
            jax.ShapeDtypeStruct((width // 128, 128), F32),
        ),
        in_specs=[SMEM] + [VMEM] * (3 + n_dp) + [ANY] * (1 + len(pieces)),
        out_specs=(ANY, VMEM, VMEM),
        scratch_shapes=[
            pltpu.VMEM(contexts.shape, BF16),
            pltpu.VMEM((rows, at), BF16),
            pltpu.VMEM((2, step, width), F32),
            pltpu.SemaphoreType.DMA((n_dp,)),
            pltpu.SemaphoreType.DMA((len(pieces),)),
            pltpu.SemaphoreType.DMA((2,)),
        ],
        compiler_params=params(60),
        name="weight_grad",
    )(pos, gw_col, norm_gain, value_weight, *sums, contexts, *pieces)


def parts_kernel(chunks, resid_cols, pos_ref, context, weight, resid, *refs):
    outs, columns, sems = refs[-len(chunks) - 2 : -2], refs[-2], refs[-1]
    fetch = [
        pltpu.make_async_copy(weight.at[:, pl.ds(at, CW)], columns.at[k], sems.at[k])
        for k, (_, at) in enumerate(chunks)
    ]
    for copy in fetch:
        copy.start()
    for k, (j, _) in enumerate(chunks):
        fetch[k].wait()
        part = jnp.dot(context[...], columns[k], preferred_element_type=F32)
        own = jnp.where(pos_ref[1] == j, resid[:, resid_cols].astype(F32), 0.0)
        outs[k][...] = (part + own).astype(BF16)


def partial_sums(pos, context, out_weight, resid, at, chunks, tie):
    piece = jax.ShapeDtypeStruct((CAPB, CW), BF16)
    n = len(chunks)
    return pl.pallas_call(
        functools.partial(parts_kernel, chunks, slice(at * CW, (at + 1) * CW)),
        out_shape=(piece,) * n,
        in_specs=[SMEM, VMEM, ANY, VMEM] + [ANY] * len(tie),
        out_specs=(VMEM,) * n,
        scratch_shapes=[
            pltpu.VMEM((n, out_weight.shape[0], CW), BF16),
            pltpu.SemaphoreType.DMA((n,)),
        ],
        compiler_params=params(52),
        cost_estimate=pl.CostEstimate(flops=0, bytes_accessed=0, transcendentals=0),
        name="partial_sums",
    )(pos, context, out_weight, resid, *tie)


def step_kernel(part, joins, totals, ends, n_tie, pos_ref, *refs):
    refs = list(refs)
    take = lambda n=1: [refs.pop(0) for _ in range(n)]
    mid = pos_ref[2] == 1
    add = lambda a, b: (a[...].astype(F32) + b[...].astype(F32)).astype(BF16)
    (new,) = take() if part else (None,)
    pair = take(2) if joins else None
    halves = take(2) if totals else None
    last = take(2) if ends else None
    take(n_tie)
    if joins:
        take()[0][...] = add(*pair)
    if totals:
        total = add(*halves)
        take()[0][...] = total if new is None else jnp.where(mid, total, new[...])
    if ends:
        take()[0][...] = jnp.where(mid, last[0][...], last[1][...])


def pair_kernel(first, second, *refs):
    for part, arrived, out in zip((first, second), refs[:2], refs[-2:]):
        out[...] = (part[...].astype(F32) + arrived[...].astype(F32)).astype(BF16)


def join_pair(parts, arrived, tie):
    piece = jax.ShapeDtypeStruct((CAPB, CW), BF16)
    return pl.pallas_call(
        pair_kernel,
        out_shape=(piece, piece),
        in_specs=[VMEM] * 4 + [ANY] * len(tie),
        out_specs=(VMEM, VMEM),
        compiler_params=params(16),
        cost_estimate=pl.CostEstimate(flops=0, bytes_accessed=0, transcendentals=0),
        name="join_pair",
    )(*parts, *arrived, *tie)


def line_sum(context, resid_of, out_weight, pos, order, first_pair, after_step):
    edge = [(0, 1), (1, 0), (2, 3), (3, 2)]
    middle = [(1, 2), (2, 1)]
    width = context.shape[1]
    n, n_blk = len(order), 4
    piece = jax.ShapeDtypeStruct((CAPB, CW), BF16)
    parts, joined, from_edge, from_mid, payloads, hidden = {}, {}, {}, {}, {}, {}

    def make_parts(first, count, tie):
        r = order[first][1]
        resid, at = resid_of(r)
        chunks = [(j, j * width + r * CW) for j, _ in order[first : first + count]]
        made = partial_sums(pos, context, out_weight, resid, at, chunks, tie)
        parts.update(zip(range(first, first + count), made))

    arrived = [lax.ppermute(part, "tensor", edge) for part in first_pair]
    make_parts(2, 2, tuple(first_pair[1:]))
    for s in (2, 3):
        payloads[s] = parts[s]
        from_edge[s] = lax.ppermute(parts[s], "tensor", edge)
    joined[0], joined[1] = join_pair(first_pair, arrived, (parts[3],))
    for s in (0, 1):
        from_mid[s] = lax.ppermute(joined[s], "tensor", middle)
    tie = after_step(1, hidden, (joined[1],))
    make_parts(4, 2, tie)
    for s in range(2, n + 4):
        joins, totals, ends = s < n, s < n + 2, s >= 4
        part = totals and s + 2 < n
        outs, args = {}, [pos]
        if part:
            args.append(parts[s + 2])
        if joins:
            args += [parts[s], from_edge[s]]
            outs["joined"] = piece
        if totals:
            args += [joined[s - 2], from_mid[s - 2]]
            outs["payload"] = piece
        if ends:
            args += [payloads[s], from_edge[s]]
            outs["hidden"] = piece
        made = pl.pallas_call(
            functools.partial(step_kernel, part, joins, totals, ends, len(tie)),
            out_shape=tuple(outs.values()),
            in_specs=[SMEM] + [VMEM] * (len(args) - 1) + [ANY] * len(tie),
            out_specs=(VMEM,) * len(outs),
            compiler_params=params(16),
            cost_estimate=pl.CostEstimate(flops=0, bytes_accessed=0, transcendentals=0),
            name="line_step",
        )(*args, *tie)
        made = dict(zip(outs, made))
        tie = (next(iter(made.values())),)
        if joins:
            joined[s] = made["joined"]
            from_mid[s] = lax.ppermute(joined[s], "tensor", middle)
        if s + 2 < n + 4:
            payloads[s + 2] = made["payload"]
            from_edge[s + 2] = lax.ppermute(payloads[s + 2], "tensor", edge)
        if ends:
            hidden[order[s - 4]] = made["hidden"]
        tie = after_step(s, hidden, tie)
        if s % 2 == 0 and s + n_blk < n:
            make_parts(s + n_blk, 2, tie)


def on_device(
    query_states,
    key_states,
    value_states,
    residual,
    returns,
    lengths,
    balance_list,
    out_weight,
    norm_gain,
    value_weight,
):
    n_dp, n_tensor = lax.axis_size("dp"), lax.axis_size("tensor")
    me, col = lax.axis_index("dp"), lax.axis_index("tensor")
    per_dev = query_states.shape[0]
    width = query_states.shape[2]
    model_width = out_weight.shape[1]
    kv = key_states.shape[2] // HD

    seq_len = query_states.shape[1]
    cap = per_dev // n_dp
    first = CW if width > CW else width
    pick, start, size = route(me.reshape(1), lengths, balance_list, n_dp, per_dev)
    parts_in = (query_states, key_states, value_states, residual)
    used = width + 2 * kv * HD + first
    start_spans = ((0, 0, width), (1, 0, kv * HD), (2, 0, kv * HD), (3, 0, first))
    rest_span = (3, first, width)
    far = range(2, n_dp)
    blocks, rest = [None] * n_dp, [None] * n_dp
    sent = gather_rollouts(
        pick, parts_in, returns, tuple((d, start_spans, None) for d in far), n_dp
    )
    for d, payload in zip(far, sent):
        blocks[d] = xor_move(payload, d, n_dp)
    near = tuple((d, start_spans + (rest_span,), used) for d in (0, 1))
    sent = gather_rollouts(
        pick, parts_in, returns, near + tuple((d, (rest_span,), 0) for d in far), n_dp, sent[:1]
    )
    blocks[0], blocks[1] = sent[0], xor_move(sent[1], 1, n_dp)
    rest[:2] = blocks[:2]
    for d, payload in zip(far, sent[2:]):
        rest[d] = xor_move(payload, d, n_dp)
    rest_cols = (used, used) + (0,) * len(far)
    place, fetch = spread(start, size, seq_len)
    gw_own = norm_gain * value_weight
    gw = lax.all_gather(gw_own, "tensor", axis=0, tiled=True)
    gw_high = gw.astype(BF16)
    gw_low = (gw - gw_high.astype(F32)).astype(BF16)
    pair = jnp.stack([gw_high, gw_low])
    wgw = jnp.sum(mm(pair, out_weight, ((1,), (1,))), axis=0, keepdims=True)
    block = model_width // n_dp
    gw_col = lax.dynamic_slice_in_dim(gw, me * block, block).reshape(block, 1)
    is_mid = (col == 1) | (col == 2)
    pos = jnp.stack([me, col, is_mid.astype(jnp.int32)]).astype(jnp.int32)
    on_line = n_tensor == 4 and n_dp == 4
    per_block = width // CW
    order = [(j, r) for r in range(per_block) for j in (1, 2, 0, 3)]
    chunks = tuple((j, j * width + r * CW) for j, r in order[:2]) if on_line else ()
    context, resid_first, probs, parts = attention_forward(
        size, place, blocks, first, kv, seq_len, cap, (wgw, gw_col), pos, out_weight, chunks
    )
    gw_row, gw_mine = gw.reshape(1, model_width), gw_own.reshape(1, width)

    if on_line:
        later, owns, pieces = {}, [], []

        def move(held, tie):
            rounds = later["rounds"]
            bundle = bundle_pieces(
                [held[j, r] for j in range(n_tensor) for r in rounds], len(rounds), tie
            )
            moved = lax.all_to_all(bundle, "dp", split_axis=0, concat_axis=0, tiled=True)
            pieces.append(moved.reshape(n_dp * CAPB, bundle.shape[2]))
            return (bundle,)

        def after_step(s, hidden, tie):
            if s == 1:
                later["resid"], later["target"], later["context"] = pack(
                    place, rest, rest_cols, seq_len, cap, context, tie
                )
            if s in (20, 21):
                r, count = {20: (0, 2), 21: (2, 2)}[s]
                *later["state"], own = row_products(
                    pos,
                    out_weight,
                    gw_row,
                    [hidden[j, r + k] for j in range(n_tensor) for k in range(count)],
                    count,
                    r * CW,
                    width,
                    later.get("state"),
                    tie,
                )
                owns.append(own)
                return (own,)
            if s in (11, len(order) + 3):
                later["rounds"] = (0, 1) if s == 11 else tuple(range(2, per_block))
                later["last"] = [hidden.get((j, per_block - 1)) for j in range(n_tensor)]
                later["tie"] = move(hidden, tie)
                return later["tie"]
            return tie

        line_sum(
            context,
            lambda r: (resid_first, 0) if r == 0 else (later["resid"], r - 1),
            out_weight,
            pos,
            order,
            parts,
            after_step,
        )
        acc, resid_out, sums, critic_row, a, b = last_products(
            pos,
            out_weight,
            gw_row,
            gw_mine,
            context,
            later["target"],
            later["last"],
            4 * CW,
            later["state"],
            owns,
            later["tie"],
        )
        contexts = lax.all_gather(later["context"], "dp", axis=0, tiled=True)
    else:
        resid_rest, target, _ = pack(place, rest, rest_cols, seq_len, cap, context)
        contexts = lax.all_gather(context, "dp", axis=0, tiled=True)
        resid = jnp.concatenate([resid_first, resid_rest], axis=1)
        part = jnp.dot(context, out_weight, preferred_element_type=F32)
        mine = lax.dynamic_slice_in_dim(part, col * width, width, axis=1) + resid.astype(F32)
        part = lax.dynamic_update_slice_in_dim(part, mine, col * width, axis=1)
        hidden = lax.psum(part.astype(BF16), "tensor")
        wide = hidden.astype(F32)
        sq = jnp.sum(wide * wide, axis=1, keepdims=True)
        vd = jnp.sum(wide * gw[None, :], axis=1, keepdims=True)
        acc = mm(hidden, out_weight, ((1,), (1,)))
        own = lax.dynamic_slice_in_dim(hidden, col * width, width, axis=1)
        pieces = [lax.all_to_all(hidden, "dp", split_axis=1, concat_axis=0, tiled=True)]
        resid_out, sums, critic_row, a, b = finish(
            sq, vd, target, gw_mine, context, own, model_width
        )

    all_sums = [sums] + [xor_move(sums, d, n_dp) for d in range(1, n_dp)]
    query_out, key_out, value_out = attention_backward(
        place, fetch, a, b, wgw, acc, probs, blocks, kv, seq_len, cap
    )
    weight_out, gain_out, value_weight_out = weight_grad(
        pos,
        gw_col,
        norm_gain.reshape(1, width),
        value_weight.reshape(1, width),
        all_sums,
        contexts,
        pieces,
    )
    return (
        critic_row.reshape(CAPB).astype(BF16),
        query_out,
        key_out,
        value_out,
        resid_out,
        weight_out,
        gain_out.reshape(width),
        value_weight_out.reshape(width),
    )


def solution(mesh):
    rows = P(("groups", "dp"), None, "tensor")
    packed = P(("groups", "dp"), "tensor")
    placed = (rows, rows, rows, rows, P(("groups", "dp"), None), P("groups"), P("groups"))
    placed += (P("tensor", None), P("tensor"), P("tensor"))
    return jax.shard_map(
        on_device,
        mesh=mesh,
        in_specs=placed,
        out_specs=(
            P(("groups", "dp")),
            packed,
            packed,
            packed,
            packed,
            packed,
            P(("groups", "tensor")),
            P(("groups", "tensor")),
        ),
        check_vma=False,
    )
```
